32 devices in a mesh: ctx: 16 (over z, y, core), fsdp: 2 (over x).
Axes of the slice: x: 2, y: 2, z: 4, core: 2. Of those that a mesh axis runs over, the one named last changes fastest.
Arguments:
- tokens: bfloat16 [4, 2048, 1536], P('fsdp', 'ctx'), may hold values from -6 to 6
- attn_gain: float32 [1536], replicated, may hold values from 0.25 to 1.75
- w_query: bfloat16 [1536, 1536], P('fsdp'), may hold values from -0.21875 to 0.21875
- w_key: bfloat16 [1536, 768], P('fsdp'), may hold values from -0.15625 to 0.15625
- w_value: bfloat16 [1536, 768], P('fsdp'), may hold values from -0.15625 to 0.15625
- w_out: bfloat16 [1536, 1536], P('fsdp'), may hold values from -0.4375 to 0.4375
- mlp_gain: float32 [1536], replicated, may hold values from 0.25 to 1.75
- w_gate: bfloat16 [1536, 4096], P('fsdp'), may hold values from -0.15625 to 0.15625
- w_up: bfloat16 [1536, 4096], P('fsdp'), may hold values from -0.15625 to 0.15625
- w_down: bfloat16 [4096, 1536], P('fsdp'), may hold values from -0.125 to 0.125
- cotangent: bfloat16 [4, 2048, 1536], P('fsdp', 'ctx'), may hold values from -6 to 6
Outputs:
- mixed: bfloat16 [4, 2048, 1536], P('fsdp', 'ctx')
- tokens_grad: bfloat16 [4, 2048, 1536], P('fsdp', 'ctx')
- attn_gain_grad: float32 [1536], replicated
- w_query_grad: float32 [1536, 1536], P('fsdp', 'ctx')
- w_key_grad: float32 [1536, 768], P('fsdp', 'ctx')
- w_value_grad: float32 [1536, 768], P('fsdp', 'ctx')
- w_out_grad: float32 [1536, 1536], P('fsdp', 'ctx')
- mlp_gain_grad: float32 [1536], replicated
- w_gate_grad: float32 [1536, 4096], P('fsdp', 'ctx')
- w_up_grad: float32 [1536, 4096], P('fsdp', 'ctx')
- w_down_grad: float32 [4096, 1536], P('fsdp', 'ctx')
The draws below stay inside these ranges and needn't reach their ends.
All inputs are finite; a program needn't handle non-finite values.
Results may differ from the reference program's by a relative error of at most 0.024.
Values may be sent and summed in bfloat16 or wider, within the bound.
A program may use at most 384 MiB of HBM per device.

```python
import jax
import jax.numpy as jnp
from jax import lax

D = 1536
HQ = 16
HK = 8
HD = 96
FF = 4096
L = 2048
SEQS = 4


def block_levels(rng, extent, shards, smallest, top_value):
    def one(dim, shards_of):
        steps = jax.random.uniform(jax.random.fold_in(jax.random.fold_in(rng, 6), dim), (shards_of,), jnp.float32, smallest / len(shards), top_value / len(shards))
        return jnp.repeat(jnp.exp(steps), extent[dim] // shards_of).reshape((-1,) + (1,) * (len(extent) - dim - 1))

    loudness = one(*shards[0])
    for cut in shards[1:]:
        loudness = loudness * one(*cut)
    return loudness


def scatter_about(stream_key, extent, deviation, reach, split=(), kind=jnp.bfloat16):
    loudness = block_levels(stream_key, extent, split, -0.22, 0.18) if split else 1.0
    entries = jax.random.normal(stream_key, extent, jnp.float32) * deviation * loudness
    return jnp.minimum(jnp.maximum(entries, -reach), reach).astype(kind)


def setup_inputs(seed: int = 0) -> dict:
    seeds = jax.random.split(jax.random.key(seed), 12)
    tokens = scatter_about(seeds[0], (SEQS, L, D), 1.0, 6.0, ((0, 2), (1, 16)))
    attn_gain = jnp.clip(1.0 + 0.15 * jax.random.normal(seeds[1], (D,), jnp.float32), 0.25, 1.75)
    w_query = scatter_about(seeds[2], (D, HQ * HD), (D // 2) ** -0.5, 0.21875, ((0, 2),))
    w_key = scatter_about(seeds[3], (D, HK * HD), D ** -0.5, 0.15625, ((0, 2),))
    w_value = scatter_about(seeds[4], (D, HK * HD), D ** -0.5, 0.15625, ((0, 2),))
    w_out = scatter_about(seeds[5], (HQ * HD, D), (HQ * HD // 8) ** -0.5, 0.4375, ((0, 2),))
    mlp_gain = jnp.clip(1.0 + 0.15 * jax.random.normal(seeds[6], (D,), jnp.float32), 0.25, 1.75)
    w_gate = scatter_about(seeds[7], (D, FF), D ** -0.5, 0.15625, ((0, 2),))
    w_up = scatter_about(seeds[8], (D, FF), D ** -0.5, 0.15625, ((0, 2),))
    w_down = scatter_about(seeds[9], (FF, D), (FF // 2) ** -0.5, 0.125, ((0, 2),))
    cotangent = scatter_about(seeds[10], (SEQS, L, D), 1.0, 6.0, ((0, 2), (1, 16)))
    return {"tokens": tokens, "attn_gain": attn_gain, "w_query": w_query, "w_key": w_key, "w_value": w_value, "w_out": w_out, "mlp_gain": mlp_gain, "w_gate": w_gate, "w_up": w_up, "w_down": w_down, "cotangent": cotangent}


@jax.custom_vjp
def low(v):
    return lax.optimization_barrier(v.astype(jnp.bfloat16)).astype(jnp.float32)

@jax.custom_vjp
def low_back(v):
    return v

def low_keep(v):
    return (low(v), None)

def low_pass(kept, grad):
    return (grad,)

def back_keep(v):
    return (v, None)

def back_low(kept, grad):
    return (low(grad),)
low.defvjp(low_keep, low_pass)
low_back.defvjp(back_keep, back_low)
EPSILON = 1e-05
ROPE_BASE = 100000.0
MASK_FILL = -1e+30
HIGHEST = lax.Precision.HIGHEST

def matmul(left, right):
    return jnp.dot(left, right, precision=HIGHEST, preferred_element_type=jnp.float32)

def rms_unit(values):
    return values * lax.rsqrt(lax.optimization_barrier(jnp.mean(values * values, axis=-1, keepdims=True)) + EPSILON)

def rotate(values, cosine, sine_rows):
    half_dim = values.shape[-1] // 2
    front = values[..., :half_dim]
    back_half = values[..., half_dim:]
    return jnp.concatenate([front * cosine - back_half * sine_rows, back_half * cosine + front * sine_rows], axis=-1)

def rope_tables(length):
    half_dim = HD // 2
    inv_freq = 1.0 / ROPE_BASE ** (jnp.arange(half_dim, dtype=jnp.float32) * 2.0 / HD)
    angles = jnp.arange(length, dtype=jnp.int32).astype(jnp.float32)[:, None] * inv_freq[None, :]
    return (jnp.cos(angles)[:, None, :], jnp.sin(angles)[:, None, :])

def attend(queries, keys, values):
    length = queries.shape[0]
    block_rows = min(512, length)
    block_count = length // block_rows
    grouped = queries.reshape(block_count, block_rows, HK, HQ // HK, HD)
    starts = jnp.arange(block_count, dtype=jnp.int32) * block_rows
    key_pos = jnp.arange(length, dtype=jnp.int32)

    def one_block(pair):
        rows_in, row_start = pair
        scores = jnp.einsum('cgrd,lgd->grcl', rows_in, keys, precision=HIGHEST, preferred_element_type=jnp.float32)
        scores = low_back(scores)
        query_pos = row_start + jnp.arange(block_rows, dtype=jnp.int32)
        allowed = key_pos[None, :] <= query_pos[:, None]
        scores = jnp.where(allowed, scores, MASK_FILL)
        row_top = lax.optimization_barrier(jnp.max(scores, axis=-1, keepdims=True))
        shifted_exp = jnp.exp(scores - row_top)
        probs = low(shifted_exp / lax.optimization_barrier(jnp.sum(shifted_exp, axis=-1, keepdims=True)))
        mixed_rows = jnp.einsum('grcl,lgd->cgrd', probs, values, precision=HIGHEST, preferred_element_type=jnp.float32)
        return mixed_rows.reshape(block_rows, HQ * HD)
    mixed_blocks = lax.map(jax.checkpoint(one_block), (grouped, starts))
    return mixed_blocks.reshape(length, HQ * HD)

def layer_forward(hidden_in, attn_gain, w_query, w_key, w_value, w_out, mlp_gain, w_gate, w_up, w_down):
    length = hidden_in.shape[0]
    cosine, sine_rows = rope_tables(length)
    normed = low(rms_unit(hidden_in) * attn_gain)
    query_raw = low_back(matmul(normed, w_query)).reshape(length, HQ, HD)
    key_raw = low_back(matmul(normed, w_key)).reshape(length, HK, HD)
    values = low_back(low(matmul(normed, w_value))).reshape(length, HK, HD)
    queries = low(rotate(query_raw, cosine, sine_rows) * HD ** (-0.5))
    keys = low(rotate(key_raw, cosine, sine_rows))
    attended = low_back(low(attend(queries, keys, values)))
    branch = low_back(matmul(attended, w_out))
    resid = hidden_in + branch
    normed_two = low(rms_unit(resid) * mlp_gain)
    gate_proj = low_back(matmul(normed_two, w_gate))
    up_proj = low_back(matmul(normed_two, w_up))
    hidden_act = low(gate_proj * jax.nn.sigmoid(gate_proj) * up_proj)
    return resid + low_back(matmul(hidden_act, w_down))

def reference(tokens, attn_gain, w_query, w_key, w_value, w_out, mlp_gain, w_gate, w_up, w_down, cotangent):
    params = tuple((weight.astype(jnp.float32) for weight in (attn_gain, w_query, w_key, w_value, w_out, mlp_gain, w_gate, w_up, w_down)))

    def one_seq(totals, pair):
        seq_in, seq_cot = pair
        result, pullback = jax.vjp(layer_forward, seq_in.astype(jnp.float32), *params)
        grads = pullback(seq_cot.astype(jnp.float32))
        totals = tuple((acc + grad_one for acc, grad_one in zip(totals, grads[1:])))
        return (totals, (result.astype(jnp.bfloat16), grads[0].astype(jnp.bfloat16)))
    zeros_init = tuple((jnp.zeros_like(weight) for weight in params))
    totals, outputs = lax.scan(one_seq, zeros_init, (tokens, cotangent))
    return (outputs[0], outputs[1], totals[0], totals[1], totals[2], totals[3], totals[4], totals[5], totals[6], totals[7], totals[8])
```

```python
import functools

import jax
import jax.numpy as jnp
import numpy as np
from jax import lax
from jax.experimental import pallas as pl
from jax.experimental.pallas import tpu as pltpu
from jax.sharding import PartitionSpec as P

HQ = 16
HK = 8
HD = 96
MICRO = 2
LANES = 128
HEAD_COLS = 4 * HD
BF = jnp.bfloat16


EPSILON = 1e-05
ROPE_BASE = 100000.0
MASK_FILL = -1e30


def matmul(left, right):
    return jnp.dot(left, right, preferred_element_type=jnp.float32)


def times_transposed(left, right):
    return lax.dot_general(
        left, right, (((1,), (1,)), ((), ())), preferred_element_type=jnp.float32
    )


def transposed_times(left, right):
    return lax.dot_general(
        left, right, (((0,), (0,)), ((), ())), preferred_element_type=jnp.float32
    )


def normalize(values):
    inv_rms = lax.rsqrt(jnp.mean(values * values, axis=-1, keepdims=True) + EPSILON)
    return (values * inv_rms, inv_rms)


def norm_back(grad_normed, gain_row, unit_rows, inv_rms):
    scaled = grad_normed * gain_row
    return inv_rms * (scaled - unit_rows * jnp.mean(scaled * unit_rows, axis=-1, keepdims=True))


def rotate(values, cosine, sine_rows):
    half_dim = values.shape[-1] // 2
    front = values[..., :half_dim]
    back_half = values[..., half_dim:]
    return jnp.concatenate(
        [front * cosine - back_half * sine_rows, back_half * cosine + front * sine_rows], axis=-1
    )


def attend_forward(query_rows, key_rows, value_rows, allowed):
    width_ct = query_rows.shape[0]
    grouped = query_rows.reshape(width_ct, HK, HQ // HK, HD)
    key_heads = key_rows.reshape(-1, HK, HD)
    value_heads = value_rows.reshape(-1, HK, HD)
    scores = jnp.einsum("cgrd,lgd->grcl", grouped, key_heads, preferred_element_type=jnp.float32)
    scores = jnp.where(allowed, scores, MASK_FILL)
    row_top = jnp.max(scores, axis=-1, keepdims=True)
    shifted_exp = jnp.exp(scores - row_top)
    row_total = jnp.sum(shifted_exp, axis=-1, keepdims=True)
    prob_low = (shifted_exp / row_total).astype(jnp.bfloat16)
    attended = jnp.einsum(
        "grcl,lgd->cgrd", prob_low, value_heads, preferred_element_type=jnp.float32
    )
    return (attended.reshape(width_ct, HQ * HD), row_top + jnp.log(row_total))


def attend_backward(query_rows, key_rows, value_rows, allowed, log_total, grad_rows):
    width_ct = query_rows.shape[0]
    grouped = query_rows.reshape(width_ct, HK, HQ // HK, HD)
    key_heads = key_rows.reshape(-1, HK, HD)
    value_heads = value_rows.reshape(-1, HK, HD)
    scores = jnp.einsum("cgrd,lgd->grcl", grouped, key_heads, preferred_element_type=jnp.float32)
    prob_full = jnp.exp(jnp.where(allowed, scores, MASK_FILL) - log_total)
    prob_low = prob_full.astype(jnp.bfloat16)
    grad_heads = grad_rows.reshape(width_ct, HK, HQ // HK, HD)
    grad_prob = jnp.einsum(
        "cgrd,lgd->grcl", grad_heads, value_heads, preferred_element_type=jnp.float32
    )
    row_inner = jnp.sum(prob_full * grad_prob, axis=-1, keepdims=True)
    grad_scores = (prob_full * (grad_prob - row_inner)).astype(jnp.bfloat16)
    grad_query = jnp.einsum(
        "grcl,lgd->cgrd", grad_scores, key_heads, preferred_element_type=jnp.float32
    )
    grad_key = jnp.einsum(
        "grcl,cgrd->lgd", grad_scores, grouped, preferred_element_type=jnp.float32
    )
    grad_value = jnp.einsum(
        "grcl,cgrd->lgd", prob_low, grad_heads, preferred_element_type=jnp.float32
    )
    return (
        grad_query.reshape(width_ct, HQ * HD),
        grad_key.reshape(-1, HK * HD),
        grad_value.reshape(-1, HK * HD),
        row_inner,
    )


def reduce_grad(full_grad):
    partial_grad = lax.psum_scatter(
        full_grad.astype(jnp.bfloat16), "fsdp", scatter_dimension=0, tiled=True
    )
    return lax.psum_scatter(partial_grad, "ctx", scatter_dimension=1, tiled=True).astype(
        jnp.float32
    )


def shards(
    tokens, attn_gain, w_query, w_key, w_value, w_out, mlp_gain, w_gate, w_up, w_down, cotangent
):
    seq_local, width_ct, model_width = tokens.shape
    seq_block = seq_local // MICRO
    row_count = seq_block * width_ct
    length = width_ct * lax.axis_size("ctx")
    half_dim = HD // 2
    offset = lax.axis_index("ctx") * width_ct
    query_pos = offset + jnp.arange(width_ct, dtype=jnp.int32)
    key_pos = jnp.arange(length, dtype=jnp.int32)
    allowed = key_pos[None, :] <= query_pos[:, None]
    inv_freq = 1.0 / ROPE_BASE ** (jnp.arange(half_dim, dtype=jnp.float32) * 2.0 / HD)
    angles = query_pos.astype(jnp.float32)[:, None] * inv_freq[None, :]
    cos_one = jnp.cos(angles)[:, None, :]
    sin_one = jnp.sin(angles)[:, None, :]
    cos_rows = jnp.tile(cos_one, (seq_block, 1, 1))
    sin_rows = jnp.tile(sin_one, (seq_block, 1, 1))
    head_scale = HD ** (-0.5)
    mixed_list, token_grad_list = ([], [])
    kept_normed_one, kept_grad_query, kept_grad_key, kept_grad_value = ([], [], [], [])
    kept_attended, kept_grad_branch, kept_normed_two = ([], [], [])
    kept_grad_gate, kept_grad_upper, kept_inner, kept_grad_down = ([], [], [], [])
    attn_gain_acc = jnp.zeros((model_width,), jnp.float32)
    mlp_gain_acc = jnp.zeros((model_width,), jnp.float32)
    for micro_at in range(MICRO):
        first_seq = micro_at * seq_block
        inputs = (
            tokens[first_seq : first_seq + seq_block]
            .reshape(row_count, model_width)
            .astype(jnp.float32)
        )
        outer_grad = (
            cotangent[first_seq : first_seq + seq_block]
            .reshape(row_count, model_width)
            .astype(jnp.float32)
        )
        attn_all = (
            lax.all_gather(w_query, "fsdp", axis=0, tiled=True),
            lax.all_gather(w_key, "fsdp", axis=0, tiled=True),
            lax.all_gather(w_value, "fsdp", axis=0, tiled=True),
            lax.all_gather(w_out, "fsdp", axis=0, tiled=True),
        )
        unit_one, inv_one = normalize(inputs)
        normed_one = (unit_one * attn_gain).astype(jnp.bfloat16)
        query_raw = matmul(normed_one, attn_all[0]).reshape(row_count, HQ, HD)
        key_raw = matmul(normed_one, attn_all[1]).reshape(row_count, HK, HD)
        value_raw = matmul(normed_one, attn_all[2])
        queries = (
            (rotate(query_raw, cos_rows, sin_rows) * head_scale)
            .astype(jnp.bfloat16)
            .reshape(seq_block, width_ct, HQ * HD)
        )
        keys = (
            rotate(key_raw, cos_rows, sin_rows)
            .astype(jnp.bfloat16)
            .reshape(seq_block, width_ct, HK * HD)
        )
        values = value_raw.astype(jnp.bfloat16).reshape(seq_block, width_ct, HK * HD)
        key_all, value_all = (
            lax.all_gather(keys, "ctx", axis=1, tiled=True),
            lax.all_gather(values, "ctx", axis=1, tiled=True),
        )
        attended_parts, lse_parts = ([], [])
        seq_at = 0
        attended_one, lse_one = attend_forward(
            queries[seq_at], key_all[seq_at], value_all[seq_at], allowed
        )
        attended_parts.append(attended_one)
        lse_parts.append(lse_one)
        attended = attended_parts[0].astype(jnp.bfloat16)
        resid = inputs + matmul(attended, attn_all[3])
        unit_two, inv_two = normalize(resid)
        normed_two = (unit_two * mlp_gain).astype(jnp.bfloat16)
        gate_proj = matmul(normed_two, lax.all_gather(w_gate, "fsdp", axis=0, tiled=True))
        up_proj = matmul(normed_two, lax.all_gather(w_up, "fsdp", axis=0, tiled=True))
        sigma = jax.nn.sigmoid(gate_proj)
        active = gate_proj * sigma
        hidden_act = (active * up_proj).astype(jnp.bfloat16)
        down_out = matmul(hidden_act, lax.all_gather(w_down, "fsdp", axis=0, tiled=True))
        mixed_list.append((resid + down_out).astype(jnp.bfloat16))
        grad_down = outer_grad.astype(jnp.bfloat16)
        grad_hidden = times_transposed(
            grad_down, lax.all_gather(w_down, "fsdp", axis=0, tiled=True)
        )
        grad_gate = (grad_hidden * up_proj * sigma * (1.0 + gate_proj * (1.0 - sigma))).astype(
            jnp.bfloat16
        )
        grad_upper = (grad_hidden * active).astype(jnp.bfloat16)
        pair_pieces = lax.all_gather((w_gate, w_up), "fsdp", axis=0, tiled=True)
        grad_normed_two = times_transposed(grad_gate, pair_pieces[0]) + times_transposed(
            grad_upper, pair_pieces[1]
        )
        mlp_gain_acc = mlp_gain_acc + jnp.sum(grad_normed_two * unit_two, axis=0)
        grad_resid = outer_grad + norm_back(grad_normed_two, mlp_gain, unit_two, inv_two)
        grad_branch = grad_resid.astype(jnp.bfloat16)
        attn_back = (
            lax.all_gather(w_query, "fsdp", axis=0, tiled=True),
            lax.all_gather(w_key, "fsdp", axis=0, tiled=True),
            lax.all_gather(w_value, "fsdp", axis=0, tiled=True),
            lax.all_gather(w_out, "fsdp", axis=0, tiled=True),
        )
        grad_attended = times_transposed(grad_branch, attn_back[3]).astype(jnp.bfloat16)
        key_back, value_back = (
            lax.all_gather(keys, "ctx", axis=1, tiled=True),
            lax.all_gather(values, "ctx", axis=1, tiled=True),
        )
        query_parts, key_parts, value_parts = ([], [], [])
        seq_at = 0
        query_one = queries[seq_at]
        key_one = key_back[seq_at]
        value_one = value_back[seq_at]
        lse_one = lse_parts[seq_at]
        grad_query, grad_key, grad_value, row_inner = attend_backward(
            query_one, key_one, value_one, allowed, lse_one, grad_attended
        )
        own_key = lax.psum_scatter(
            grad_key.astype(jnp.bfloat16), "ctx", scatter_dimension=0, tiled=True
        ).astype(jnp.float32)
        own_value = lax.psum_scatter(
            grad_value.astype(jnp.bfloat16), "ctx", scatter_dimension=0, tiled=True
        ).astype(jnp.float32)
        query_parts.append(
            rotate((grad_query * head_scale).reshape(width_ct, HQ, HD), cos_one, -sin_one).reshape(
                width_ct, HQ * HD
            )
        )
        key_parts.append(
            rotate(own_key.reshape(width_ct, HK, HD), cos_one, -sin_one).reshape(width_ct, HK * HD)
        )
        value_parts.append(own_value)
        grad_query_raw = query_parts[0].astype(jnp.bfloat16)
        grad_key_raw = key_parts[0].astype(jnp.bfloat16)
        grad_value_raw = value_parts[0].astype(jnp.bfloat16)
        grad_normed_one = (
            times_transposed(grad_query_raw, attn_back[0])
            + times_transposed(grad_key_raw, attn_back[1])
            + times_transposed(grad_value_raw, attn_back[2])
        )
        attn_gain_acc = attn_gain_acc + jnp.sum(grad_normed_one * unit_one, axis=0)
        token_grad_list.append(
            (grad_resid + norm_back(grad_normed_one, attn_gain, unit_one, inv_one)).astype(
                jnp.bfloat16
            )
        )
        kept_normed_one.append(normed_one)
        kept_grad_query.append(grad_query_raw)
        kept_grad_key.append(grad_key_raw)
        kept_grad_value.append(grad_value_raw)
        kept_attended.append(attended)
        kept_grad_branch.append(grad_branch)
        kept_normed_two.append(normed_two)
        kept_grad_gate.append(grad_gate)
        kept_grad_upper.append(grad_upper)
        kept_inner.append(hidden_act)
        kept_grad_down.append(grad_down)
    normed_one_all = jnp.concatenate(kept_normed_one, axis=0)
    normed_two_all = jnp.concatenate(kept_normed_two, axis=0)
    w_query_grad = reduce_grad(
        transposed_times(normed_one_all, jnp.concatenate(kept_grad_query, axis=0))
    )
    w_key_grad = reduce_grad(
        transposed_times(normed_one_all, jnp.concatenate(kept_grad_key, axis=0))
    )
    w_value_grad = reduce_grad(
        transposed_times(normed_one_all, jnp.concatenate(kept_grad_value, axis=0))
    )
    w_out_grad = reduce_grad(
        transposed_times(
            jnp.concatenate(kept_attended, axis=0), jnp.concatenate(kept_grad_branch, axis=0)
        )
    )
    w_gate_grad = reduce_grad(
        transposed_times(normed_two_all, jnp.concatenate(kept_grad_gate, axis=0))
    )
    w_up_grad = reduce_grad(
        transposed_times(normed_two_all, jnp.concatenate(kept_grad_upper, axis=0))
    )
    w_down_grad = reduce_grad(
        transposed_times(
            jnp.concatenate(kept_inner, axis=0), jnp.concatenate(kept_grad_down, axis=0)
        )
    )
    attn_gain_grad, mlp_gain_grad = lax.psum((attn_gain_acc, mlp_gain_acc), ("ctx", "fsdp"))
    mixed = jnp.concatenate(mixed_list, axis=0).reshape(seq_local, width_ct, model_width)
    tokens_grad = jnp.concatenate(token_grad_list, axis=0).reshape(seq_local, width_ct, model_width)
    return (
        mixed,
        tokens_grad,
        attn_gain_grad,
        w_query_grad,
        w_key_grad,
        w_value_grad,
        w_out_grad,
        mlp_gain_grad,
        w_gate_grad,
        w_up_grad,
        w_down_grad,
    )


def nt(a,b):
    return lax.dot_general(a,b,(((1,),(1,)),((),())),preferred_element_type=jnp.float32)
def nn(a,b):
    return jnp.dot(a,b,preferred_element_type=jnp.float32)

def turn(v,cosine,sine):
    return v*cosine+pltpu.roll(v,LANES//2,1)*sine

def forward_kernel(rows,step_rows,raw_ref,cos_ref,sin_ref,qkv_ref,out_ref,lse_ref,key_ref,val_t_ref):
    at=pl.program_id(0)
    here=pl.ds(pl.multiple_of(at*rows,rows),rows)
    cosine,sine=cos_ref[...],sin_ref[...]
    raw=raw_ref[...]
    @pl.when(at==0)
    def _():
        val_t_ref[...]=jnp.zeros_like(val_t_ref)
    scale=HD**-0.5
    parts=[(turn(raw[:,j*LANES:(j+1)*LANES],cosine,sine)*(scale if j<2 else 1.0)).astype(BF) for j in range(3)]
    value=raw[:,3*LANES:].astype(BF)
    for j in range(3):
        qkv_ref[:,j*LANES:(j+1)*LANES]=parts[j]
    qkv_ref[:,3*LANES:]=value
    key_ref[here,:]=parts[2]
    val_t_ref[:,here]=value.T
    query=jnp.concatenate(parts[:2],axis=0)
    length=key_ref.shape[0]
    per=step_rows//rows
    for band in range(length//step_rows):
        @pl.when(at//per==band)
        def _():
            extent=(band+1)*step_rows
            scores=nt(key_ref[0:extent,:],query)
            tail=scores[band*step_rows:,:]
            key_pos=lax.broadcasted_iota(jnp.int32,tail.shape,0)
            query_pos=(at%per)*rows+lax.broadcasted_iota(jnp.int32,tail.shape,1)%rows
            tail=jnp.where(key_pos<=query_pos,tail,MASK_FILL)
            pieces=[scores[b*step_rows:(b+1)*step_rows,:] for b in range(band)]+[tail]
            top=functools.reduce(jnp.maximum,[jnp.max(p,axis=0,keepdims=True) for p in pieces])
            total=0.0; acc=0.0
            for b,p in enumerate(pieces):
                e=jnp.exp(p-top)
                total=total+jnp.sum(e,axis=0,keepdims=True)
                acc=acc+nn(val_t_ref[:,b*step_rows:(b+1)*step_rows],e.astype(BF))
            acc=acc/total
            out_ref[:,0:LANES]=acc[:,0:rows].T.astype(BF)
            out_ref[:,LANES:]=acc[:,rows:].T.astype(BF)
            lse_ref[0]=top+jnp.log(total)

def head_forward(raw,cosine,sine,rows=512,step_rows=512):
    length=raw.shape[0]
    steps=length//rows
    return pl.pallas_call(
        functools.partial(forward_kernel,rows,step_rows),
        grid=(steps,),
        in_specs=[pl.BlockSpec((rows,4*LANES),lambda i:(i,0)),
                  pl.BlockSpec((rows,LANES),lambda i:(i,0)),
                  pl.BlockSpec((rows,LANES),lambda i:(i,0))],
        out_specs=[pl.BlockSpec((rows,4*LANES),lambda i:(i,0)),
                   pl.BlockSpec((rows,2*LANES),lambda i:(i,0)),
                   pl.BlockSpec((1,1,2*rows),lambda i:(i,0,0))],
        out_shape=[jax.ShapeDtypeStruct((length,4*LANES),BF),
                   jax.ShapeDtypeStruct((length,2*LANES),BF),
                   jax.ShapeDtypeStruct((steps,1,2*rows),jnp.float32)],
        scratch_shapes=[pltpu.VMEM((length,LANES),BF),pltpu.VMEM((LANES,length),BF)],
        compiler_params=pltpu.CompilerParams(vmem_limit_bytes=48*1024*1024),
    )(raw,cosine,sine)

def backward_kernel(rows,step_rows,qkv_ref,out_ref,grad_ref,lse_ref,cos_ref,sin_ref,pick_ref,res_ref,
                    key_t_ref,grad_key_ref,grad_val_ref,rows_ref):
    at=pl.program_id(0)
    here=pl.ds(pl.multiple_of(at*rows,rows),rows)
    length=qkv_ref.shape[0]
    scale=HD**-0.5
    @pl.when(at==0)
    def _():
        grad_key_ref[...]=jnp.zeros_like(grad_key_ref)
        grad_val_ref[...]=jnp.zeros_like(grad_val_ref)
        for b in range(length//rows):
            key_t_ref[:,b*rows:(b+1)*rows]=qkv_ref[b*rows:(b+1)*rows,2*LANES:3*LANES].T
    query=jnp.concatenate([qkv_ref[here,0:LANES],qkv_ref[here,LANES:2*LANES]],axis=0)
    grad=jnp.concatenate([grad_ref[:,0:LANES],grad_ref[:,LANES:]],axis=0)
    out=jnp.concatenate([out_ref[:,0:LANES],out_ref[:,LANES:]],axis=0)
    inner=jnp.sum((grad.astype(jnp.float32)*out.astype(jnp.float32)).T,axis=0,keepdims=True)
    lse=lse_ref[0]
    per=step_rows//rows
    for band in range(length//step_rows):
        @pl.when(at//per==band)
        def _():
            grad_query=0.0
            for b in range(band+1):
                span=slice(b*step_rows,(b+1)*step_rows)
                scores=nt(qkv_ref[span,2*LANES:3*LANES],query)
                prob=jnp.exp(scores-lse)
                if b==band:
                    key_pos=lax.broadcasted_iota(jnp.int32,scores.shape,0)
                    query_pos=(at%per)*rows+lax.broadcasted_iota(jnp.int32,scores.shape,1)%rows
                    prob=jnp.where(key_pos<=query_pos,prob,0.0)
                grad_prob=nt(qkv_ref[span,3*LANES:],grad)
                grad_scores=(prob*(grad_prob-inner)).astype(BF)
                grad_val_ref[span,:]+=nn(prob.astype(BF),grad)
                grad_key_ref[span,:]+=nn(grad_scores,query)
                grad_query=grad_query+nn(key_t_ref[:,span],grad_scores)
            for j in range(2):
                back=grad_query[:,j*rows:(j+1)*rows].T*scale
                rows_ref[here,j*LANES:(j+1)*LANES]=turn(back,cos_ref[here,:],-sin_ref[here,:]).astype(BF)
    @pl.when(at==length//rows-1)
    def _():
        for b in range(length//step_rows):
            span=slice(b*step_rows,(b+1)*step_rows)
            rows_ref[span,2*LANES:3*LANES]=turn(grad_key_ref[span,:],cos_ref[span,:],-sin_ref[span,:]).astype(BF)
            rows_ref[span,3*LANES:]=grad_val_ref[span,:].astype(BF)
            res_ref[span,:]=nn(rows_ref[span,:],pick_ref[...]).astype(BF)

def head_backward(qkv,out,grad,lse,cosine,sine,pick,rows=256,step_rows=256):
    length=qkv.shape[0]
    steps=length//rows
    lse=lse.reshape(-1,2,lse.shape[2]//2).transpose(1,0,2).reshape(2,steps,rows).transpose(1,0,2).reshape(steps,1,2*rows)
    whole=lambda a:pl.BlockSpec(a.shape,lambda i:(0,)*a.ndim)
    return pl.pallas_call(
        functools.partial(backward_kernel,rows,step_rows),
        grid=(steps,),
        in_specs=[whole(qkv),
                  pl.BlockSpec((rows,2*LANES),lambda i:(i,0)),
                  pl.BlockSpec((rows,2*LANES),lambda i:(i,0)),
                  pl.BlockSpec((1,1,2*rows),lambda i:(i,0,0)),
                  whole(cosine),whole(sine),whole(pick)],
        out_specs=pl.BlockSpec((length,4*HD),lambda i:(0,0)),
        out_shape=jax.ShapeDtypeStruct((length,4*HD),BF),
        scratch_shapes=[pltpu.VMEM((LANES,length),BF),pltpu.VMEM((length,LANES),jnp.float32),
                        pltpu.VMEM((length,LANES),jnp.float32),pltpu.VMEM((length,4*LANES),BF)],
        compiler_params=pltpu.CompilerParams(vmem_limit_bytes=48*1024*1024),
    )(qkv,out,grad,lse,cosine,sine,pick)

def pad_columns():
    half=HD//2
    lanes=np.arange(4*LANES); block=lanes//LANES; lane=lanes%LANES
    split=np.where(lane<half,lane,np.where((lane>=LANES//2)&(lane<LANES//2+half),lane-LANES//2+half,-1))
    plain=np.where(lane<HD,lane,-1)
    column=np.where(block<3,split,plain)
    return np.where(column>=0,column+block*HD,-1)

CORES, LINES, PLANES = 2, 2, 4
CHIPS = LINES * PLANES
RANKS = CORES * CHIPS


def swap_fsdp(value):
    return lax.ppermute(value, "fsdp", [(0, 1), (1, 0)])


def swap_ctx(value, bit):
    return lax.ppermute(value, "ctx", [(i, i ^ bit) for i in range(RANKS)])


def swap_core(value):
    return swap_ctx(value, 1)


def swap_line(value):
    return swap_ctx(value, CORES)


def plane_up(value, sources):
    step = CORES * LINES
    return lax.ppermute(value, "ctx", [(z * step + i, z * step + step + i) for z in sources for i in range(step)])


def plane_down(value, sources):
    step = CORES * LINES
    return lax.ppermute(value, "ctx", [(z * step + i, z * step - step + i) for z in sources for i in range(step)])


def at(value, index, axis=0):
    return lax.dynamic_index_in_dim(value, index, axis, keepdims=False)


def in_order(which, mine, other):
    first = which == 0
    return jnp.concatenate([jnp.where(first, mine, other), jnp.where(first, other, mine)], axis=0)


def after(value, earlier):
    return lax.optimization_barrier((value, earlier))[0]


def plane_scatter(pieces, plane):
    up = down = None
    last = PLANES - 1
    for step in range(last):
        term_up = at(pieces, jnp.clip(plane + last - step, 0, last))
        term_down = at(pieces, jnp.clip(plane - last + step, 0, last))
        if up is not None:
            term_up = (term_up.astype(jnp.float32) + up.astype(jnp.float32)).astype(BF)
            term_down = (term_down.astype(jnp.float32) + down.astype(jnp.float32)).astype(BF)
        up = plane_up(term_up, range(0, step + 1))
        down = plane_down(term_down, range(last - step, last + 1))
    own = at(pieces, plane).astype(jnp.float32)
    return own + up.astype(jnp.float32) + down.astype(jnp.float32)


def line_scatter(kept, sent):
    return (kept.astype(jnp.float32) + swap_line(sent).astype(jnp.float32)).astype(BF)


def rope_rows(length):
    lane = jnp.arange(LANES)
    half = LANES // 2
    entry = jnp.where(lane < half, lane, lane - half)
    used = entry < HD // 2
    inv_freq = 1.0 / ROPE_BASE ** (entry.astype(jnp.float32) * 2.0 / HD)
    angles = jnp.arange(length, dtype=jnp.int32).astype(jnp.float32)[:, None] * inv_freq[None, :]
    sign = jnp.where(lane < half, -1.0, 1.0)
    return jnp.where(used, jnp.cos(angles), 0.0), jnp.where(used, jnp.sin(angles) * sign, 0.0)


def mlp_part(normed, grad_rows, gate_up, down):
    both = matmul(normed, gate_up)
    half = both.shape[1] // 2
    gate, upper = both[:, :half], both[:, half:]
    sigma = jax.nn.sigmoid(gate)
    active = gate * sigma
    inner = (active * upper).astype(BF)
    grad_inner = times_transposed(grad_rows, down)
    grad_gate = (grad_inner * upper * sigma * (1.0 + gate * (1.0 - sigma))).astype(BF)
    grad_upper = (grad_inner * active).astype(BF)
    grad_both = jnp.concatenate([grad_gate, grad_upper], axis=1)
    return inner, grad_both, matmul(inner, down), times_transposed(grad_both, gate_up)


def head_shards(
    tokens, attn_gain, w_query, w_key, w_value, w_out, mlp_gain, w_gate, w_up, w_down, cotangent
):
    seqs, width, model = tokens.shape
    length = width * RANKS
    rows = seqs * width
    half_model = model // 2
    hidden = w_gate.shape[1]
    half_hidden = hidden // 2
    chunk = hidden // (2 * RANKS)
    rank = lax.axis_index("ctx")
    side = lax.axis_index("fsdp")
    core = rank % CORES
    line = (rank // CORES) % LINES
    plane = rank // (CORES * LINES)
    chip = rank // CORES
    pick = jnp.asarray((pad_columns()[:, None] == np.arange(HEAD_COLS)[None, :]).astype(np.float32)).astype(BF)
    cosine, sine = rope_rows(length)

    mine = at(tokens, core)
    own_block = in_order(core, mine, swap_core(at(tokens, 1 - core)))
    ups, downs = [], []
    up = down = own_block
    for step in range(PLANES - 1):
        up = plane_up(up, range(step, PLANES - 1))
        down = plane_down(down, range(1, PLANES - step))
        ups.append(up)
        downs.append(down)
    low = plane < PLANES // 2
    slots = [
        own_block,
        jnp.where(low, downs[0], ups[0]),
        jnp.where(low, downs[1], ups[1]),
        jnp.where(plane == 0, downs[2], jnp.where(plane == 1, ups[0], jnp.where(plane == 2, downs[0], ups[2]))),
    ]

    packed = jnp.concatenate(
        [w_query.reshape(half_model, HK, -1), w_key.reshape(half_model, HK, -1), w_value.reshape(half_model, HK, -1)],
        axis=2,
    )
    head_rows = at(packed, chip, 1)
    head_got = swap_fsdp(head_rows)
    head_weight = in_order(side, head_rows, head_got)
    head_padded = times_transposed(head_weight, pick).astype(BF)

    def fetch(block, earlier):
        part = at(block.reshape((CORES, block.shape[0] // CORES) + block.shape[1:]), core)
        got = swap_fsdp(after(part, earlier))
        return in_order(core, got, swap_core(got)), got

    out_other, done = fetch(w_out, head_got)
    out_full = in_order(side, w_out, out_other)
    out_padded = jnp.pad(out_full.reshape(HQ, HD, model), ((0, 0), (0, LANES - HD), (0, 0))).reshape(HQ * LANES, model)

    def columns_of(block, which):
        cut = block.reshape(half_model, PLANES, LINES, CORES, 2, chunk)
        return at(cut, which, 4).transpose(0, 3, 2, 1, 4).reshape(half_model, half_hidden)

    first = core == 0
    sent = jnp.where(first, columns_of(w_gate, 1 - side), columns_of(w_up, 1 - side))
    got = swap_fsdp(after(sent, done))
    other = swap_core(got)
    gate_up = in_order(
        side,
        jnp.concatenate([columns_of(w_gate, side), columns_of(w_up, side)], axis=1),
        jnp.concatenate([jnp.where(first, got, other), jnp.where(first, other, got)], axis=1),
    )
    down_cut = w_down.reshape(PLANES // 2, LINES, CORES, 2, chunk, model)
    down_other, done = fetch(at(down_cut, 1 - side, 3).reshape(-1, model), got)
    down_rows = in_order(side, at(down_cut, side, 3).reshape(-1, model), down_other)
    down_weight = (
        down_rows.reshape(PLANES, LINES, CORES, chunk, model).transpose(2, 1, 0, 3, 4).reshape(half_hidden, model)
    )
    grad_down = cotangent.reshape(rows, model)
    grad_down_other = swap_fsdp(after(grad_down, done))

    normed_seq = jnp.zeros((CHIPS, 2 * width, model), BF)
    raw_seq = jnp.zeros((CHIPS, 2 * width, 4 * LANES), jnp.float32)
    for number, piece in enumerate(slots):
        place = jnp.where(low, plane + number, plane - number) % PLANES
        for across in range(LINES):
            block = swap_line(piece) if across else piece
            spot = place * LINES + (line if across == 0 else 1 - line)
            normed = (normalize(block.astype(jnp.float32))[0] * attn_gain).astype(BF)
            normed_seq = lax.dynamic_update_index_in_dim(normed_seq, normed, spot, 0)
            raw_seq = lax.dynamic_update_index_in_dim(raw_seq, matmul(normed, head_padded), spot, 0)
    normed_seq = normed_seq.reshape(length, model)
    qkv, attended_seq, lse = head_forward(raw_seq.reshape(length, 4 * LANES), cosine, sine)

    def exchange(value):
        return lax.all_to_all(value.reshape(RANKS, width, -1), "ctx", 0, 0, tiled=True)

    attended = (
        exchange(attended_seq).reshape(CHIPS, CORES, width, 2 * LANES).transpose(1, 2, 0, 3).reshape(rows, HQ * LANES)
    )
    inputs = tokens.reshape(rows, model).astype(jnp.float32)
    resid = inputs + matmul(attended, out_padded)
    unit_two, inv_two = normalize(resid)
    normed_two = (unit_two * mlp_gain).astype(BF)

    normed_other = swap_fsdp(normed_two)
    inner_own, grad_both_own, mixed_own, back_own = mlp_part(normed_two, grad_down, gate_up, down_weight)
    inner_other, grad_both_other, mixed_other, back_other = mlp_part(
        normed_other, grad_down_other, gate_up, down_weight
    )
    back_got = swap_fsdp(back_other.astype(BF))
    mixed_got = swap_fsdp(after(mixed_other.astype(BF), back_got))
    mixed = (resid + mixed_own + mixed_got.astype(jnp.float32)).astype(BF)
    grad_normed_two = back_own + back_got.astype(jnp.float32)
    grad_resid = grad_down.astype(jnp.float32) + norm_back(grad_normed_two, mlp_gain, unit_two, inv_two)
    mlp_gain_part = jnp.sum(grad_normed_two * unit_two, axis=0)
    grad_branch = grad_resid.astype(BF)
    grad_attended = times_transposed(grad_branch, out_padded).astype(BF)
    grad_att_seq = exchange(grad_attended.reshape(CORES, width, CHIPS, 2 * LANES).transpose(2, 0, 1, 3)).reshape(
        length, 2 * LANES
    )

    acts = jnp.concatenate(
        [
            jnp.concatenate([inner_own, grad_both_own], axis=1),
            jnp.concatenate([inner_other, grad_both_other], axis=1),
        ],
        axis=0,
    ).reshape(2 * rows, 3, CORES, half_hidden // CORES)
    acts_got = swap_core(at(acts, 1 - core, 2))
    acts_all = jnp.concatenate([at(acts, core, 2), acts_got], axis=0)
    normed_pair = jnp.concatenate([normed_two, normed_other], axis=0)
    normed_all = jnp.concatenate([normed_pair, swap_core(normed_pair)], axis=0)
    cot_pair = jnp.concatenate([grad_down, grad_down_other], axis=0)
    cot_all = jnp.concatenate([cot_pair, swap_core(cot_pair)], axis=0)
    part_hidden = half_hidden // CORES
    grad_down_weight = transposed_times(cot_all, acts_all[:, 0]).astype(BF)
    grad_gate_up = transposed_times(acts_all[:, 1:].reshape(-1, 2 * part_hidden), normed_all).astype(BF)

    per_chip = model // CHIPS
    cut = grad_down_weight.reshape(PLANES, LINES, per_chip, part_hidden)
    reduced = plane_scatter(line_scatter(at(cut, line, 1), at(cut, 1 - line, 1)), plane)
    cut = grad_gate_up.reshape(2, LINES, PLANES, chunk, model)
    halves = line_scatter(at(cut, line, 1), at(cut, 1 - line, 1))
    gate_up_reduced = plane_scatter(halves.transpose(1, 0, 2, 3), plane).astype(BF)
    cut = gate_up_reduced.reshape(2, chunk, 2, half_model)
    gate_up_got = swap_fsdp(at(cut, 1 - side, 2))
    gate_up_keep = at(cut, side, 2)
    low_side = side == 0
    gate_up_grad = jnp.concatenate(
        [jnp.where(low_side, gate_up_keep, gate_up_got), jnp.where(low_side, gate_up_got, gate_up_keep)], axis=1
    ).astype(jnp.float32)
    w_gate_grad, w_up_grad = gate_up_grad[0].T, gate_up_grad[1].T

    cut = reduced.astype(BF).reshape(CORES, model // RANKS, LINES, 2, PLANES // 2, chunk)
    keep, got = at(cut, core), swap_core(at(cut, 1 - core))
    by_core = jnp.stack([jnp.where(first, keep, got), jnp.where(first, got, keep)], axis=3)
    keep, got = at(by_core, side, 2), swap_fsdp(at(by_core, 1 - side, 2))
    by_side = jnp.stack([jnp.where(low_side, keep, got), jnp.where(low_side, got, keep)], axis=4)
    w_down_grad = by_side.transpose(0, 3, 1, 2, 4, 5).reshape(model // RANKS, -1).T.astype(jnp.float32)

    att_cut = attended.reshape(rows, 2, HK * LANES)
    att_other, branch_other = swap_fsdp((at(att_cut, 1 - side, 1), grad_branch))
    att_pair = jnp.concatenate([at(att_cut, side, 1), att_other], axis=0)
    branch_pair = jnp.concatenate([grad_branch, branch_other], axis=0)
    cut = transposed_times(branch_pair, att_pair).astype(BF).reshape(CHIPS, CORES, model // RANKS, HK * LANES)
    got = swap_core(at(cut, 1 - core, 1))
    pair_sum = (at(cut, core, 1).astype(jnp.float32) + got.astype(jnp.float32)).astype(BF)
    cut = pair_sum.reshape(PLANES, LINES, model // RANKS, HK * LANES)
    reduced = plane_scatter(line_scatter(at(cut, line, 1), at(cut, 1 - line, 1)), plane)
    w_out_grad = reduced.reshape(model // RANKS, HK, LANES)[:, :, :HD].reshape(model // RANKS, half_model).T

    grad_qkv = head_backward(qkv, attended_seq, grad_att_seq, lse, cosine, sine, pick)
    grad_own = exchange(grad_qkv).reshape(CHIPS, CORES, width, HEAD_COLS).transpose(1, 2, 0, 3).reshape(rows, -1)

    head_grad = transposed_times(grad_qkv, normed_seq)
    gain_part = jnp.sum(head_grad * head_weight.T.astype(jnp.float32), axis=0) / attn_gain
    query_cut = head_grad[: 2 * HD].reshape(CORES, HD, model)
    key_cut = head_grad[2 * HD :].reshape(2, CORES, HD // 2, model)

    def of_core(which):
        return jnp.concatenate([at(query_cut, which), at(key_cut, which, 1).reshape(HD, model)], axis=0)

    two = of_core(core) + swap_core(of_core(1 - core).astype(BF)).astype(jnp.float32)
    cut = two.reshape(2 * HD, 2, half_model)
    four = at(cut, side, 1) + swap_fsdp(at(cut, 1 - side, 1).astype(BF)).astype(jnp.float32)
    w_query_grad = four[:HD].T
    w_key_grad = four[HD : HD + HD // 2].T
    w_value_grad = four[HD + HD // 2 :].T

    gains = jnp.stack([gain_part, mlp_gain_part])
    gains = gains + swap_fsdp(gains)
    for bit in (1, 2, 4, 8):
        gains = gains + swap_ctx(gains, bit)

    packed_other, _ = fetch(packed.reshape(half_model, HK * HEAD_COLS), back_got)
    packed_full = in_order(side, packed.reshape(half_model, HK * HEAD_COLS), packed_other)
    grad_normed_one = times_transposed(grad_own, packed_full)
    unit_one, inv_one = normalize(inputs)
    tokens_grad = (grad_resid + norm_back(grad_normed_one, attn_gain, unit_one, inv_one)).astype(BF)
    return (
        mixed.reshape(seqs, width, model),
        tokens_grad.reshape(seqs, width, model),
        gains[0],
        w_query_grad,
        w_key_grad,
        w_value_grad,
        w_out_grad,
        gains[1],
        w_gate_grad,
        w_up_grad,
        w_down_grad,
    )


def solution(mesh):
    by_heads = mesh.shape["ctx"] == RANKS and mesh.shape["fsdp"] == 2
    placed = (
        P("fsdp", "ctx", None),
        P(),
        P("fsdp", None),
        P("fsdp", None),
        P("fsdp", None),
        P("fsdp", None),
        P(),
        P("fsdp", None),
        P("fsdp", None),
        P("fsdp", None),
        P("fsdp", "ctx", None),
    )
    return jax.shard_map(
        head_shards if by_heads else shards,
        mesh=mesh,
        in_specs=placed,
        out_specs=(
            P("fsdp", "ctx", None),
            P("fsdp", "ctx", None),
            P(),
            P("fsdp", "ctx"),
            P("fsdp", "ctx"),
            P("fsdp", "ctx"),
            P("fsdp", "ctx"),
            P(),
            P("fsdp", "ctx"),
            P("fsdp", "ctx"),
            P("fsdp", "ctx"),
        ),
        check_vma=False,
    )
```

```python
import functools

import jax
import jax.numpy as jnp
import numpy as np
from jax import lax
from jax.experimental import pallas as pl
from jax.experimental.pallas import tpu as pltpu
from jax.sharding import PartitionSpec as P

HQ = 16
HK = 8
HD = 96
MICRO = 2
LANES = 128
HEAD_COLS = 4 * HD
BF = jnp.bfloat16
VMEM_LIMIT = 48 * 1024 * 1024


EPSILON = 1e-05
ROPE_BASE = 100000.0
MASK_FILL = -1e30


def matmul(left, right):
    return jnp.dot(left, right, preferred_element_type=jnp.float32)


def times_transposed(left, right):
    return lax.dot_general(
        left, right, (((1,), (1,)), ((), ())), preferred_element_type=jnp.float32
    )


def transposed_times(left, right):
    return lax.dot_general(
        left, right, (((0,), (0,)), ((), ())), preferred_element_type=jnp.float32
    )


def normalize(values):
    inv_rms = lax.rsqrt(jnp.mean(values * values, axis=-1, keepdims=True) + EPSILON)
    return (values * inv_rms, inv_rms)


def norm_back(grad_normed, gain_row, unit_rows, inv_rms):
    scaled = grad_normed * gain_row
    return inv_rms * (scaled - unit_rows * jnp.mean(scaled * unit_rows, axis=-1, keepdims=True))


def rotate(values, cosine, sine_rows):
    half_dim = values.shape[-1] // 2
    front = values[..., :half_dim]
    back_half = values[..., half_dim:]
    return jnp.concatenate(
        [front * cosine - back_half * sine_rows, back_half * cosine + front * sine_rows], axis=-1
    )


def attend_forward(query_rows, key_rows, value_rows, allowed):
    width_ct = query_rows.shape[0]
    grouped = query_rows.reshape(width_ct, HK, HQ // HK, HD)
    key_heads = key_rows.reshape(-1, HK, HD)
    value_heads = value_rows.reshape(-1, HK, HD)
    scores = jnp.einsum("cgrd,lgd->grcl", grouped, key_heads, preferred_element_type=jnp.float32)
    scores = jnp.where(allowed, scores, MASK_FILL)
    row_top = jnp.max(scores, axis=-1, keepdims=True)
    shifted_exp = jnp.exp(scores - row_top)
    row_total = jnp.sum(shifted_exp, axis=-1, keepdims=True)
    prob_low = (shifted_exp / row_total).astype(jnp.bfloat16)
    attended = jnp.einsum(
        "grcl,lgd->cgrd", prob_low, value_heads, preferred_element_type=jnp.float32
    )
    return (attended.reshape(width_ct, HQ * HD), row_top + jnp.log(row_total))


def attend_backward(query_rows, key_rows, value_rows, allowed, log_total, grad_rows):
    width_ct = query_rows.shape[0]
    grouped = query_rows.reshape(width_ct, HK, HQ // HK, HD)
    key_heads = key_rows.reshape(-1, HK, HD)
    value_heads = value_rows.reshape(-1, HK, HD)
    scores = jnp.einsum("cgrd,lgd->grcl", grouped, key_heads, preferred_element_type=jnp.float32)
    prob_full = jnp.exp(jnp.where(allowed, scores, MASK_FILL) - log_total)
    prob_low = prob_full.astype(jnp.bfloat16)
    grad_heads = grad_rows.reshape(width_ct, HK, HQ // HK, HD)
    grad_prob = jnp.einsum(
        "cgrd,lgd->grcl", grad_heads, value_heads, preferred_element_type=jnp.float32
    )
    row_inner = jnp.sum(prob_full * grad_prob, axis=-1, keepdims=True)
    grad_scores = (prob_full * (grad_prob - row_inner)).astype(jnp.bfloat16)
    grad_query = jnp.einsum(
        "grcl,lgd->cgrd", grad_scores, key_heads, preferred_element_type=jnp.float32
    )
    grad_key = jnp.einsum(
        "grcl,cgrd->lgd", grad_scores, grouped, preferred_element_type=jnp.float32
    )
    grad_value = jnp.einsum(
        "grcl,cgrd->lgd", prob_low, grad_heads, preferred_element_type=jnp.float32
    )
    return (
        grad_query.reshape(width_ct, HQ * HD),
        grad_key.reshape(-1, HK * HD),
        grad_value.reshape(-1, HK * HD),
        row_inner,
    )


def reduce_grad(full_grad):
    partial_grad = lax.psum_scatter(
        full_grad.astype(jnp.bfloat16), "fsdp", scatter_dimension=0, tiled=True
    )
    return lax.psum_scatter(partial_grad, "ctx", scatter_dimension=1, tiled=True).astype(
        jnp.float32
    )


def shards(
    tokens, attn_gain, w_query, w_key, w_value, w_out, mlp_gain, w_gate, w_up, w_down, cotangent
):
    seq_local, width_ct, model_width = tokens.shape
    seq_block = seq_local // MICRO
    row_count = seq_block * width_ct
    length = width_ct * lax.axis_size("ctx")
    half_dim = HD // 2
    offset = lax.axis_index("ctx") * width_ct
    query_pos = offset + jnp.arange(width_ct, dtype=jnp.int32)
    key_pos = jnp.arange(length, dtype=jnp.int32)
    allowed = key_pos[None, :] <= query_pos[:, None]
    inv_freq = 1.0 / ROPE_BASE ** (jnp.arange(half_dim, dtype=jnp.float32) * 2.0 / HD)
    angles = query_pos.astype(jnp.float32)[:, None] * inv_freq[None, :]
    cos_one = jnp.cos(angles)[:, None, :]
    sin_one = jnp.sin(angles)[:, None, :]
    cos_rows = jnp.tile(cos_one, (seq_block, 1, 1))
    sin_rows = jnp.tile(sin_one, (seq_block, 1, 1))
    head_scale = HD ** (-0.5)
    mixed_list, token_grad_list = ([], [])
    kept_normed_one, kept_grad_query, kept_grad_key, kept_grad_value = ([], [], [], [])
    kept_attended, kept_grad_branch, kept_normed_two = ([], [], [])
    kept_grad_gate, kept_grad_upper, kept_inner, kept_grad_down = ([], [], [], [])
    attn_gain_acc = jnp.zeros((model_width,), jnp.float32)
    mlp_gain_acc = jnp.zeros((model_width,), jnp.float32)
    for micro_at in range(MICRO):
        first_seq = micro_at * seq_block
        inputs = (
            tokens[first_seq : first_seq + seq_block]
            .reshape(row_count, model_width)
            .astype(jnp.float32)
        )
        outer_grad = (
            cotangent[first_seq : first_seq + seq_block]
            .reshape(row_count, model_width)
            .astype(jnp.float32)
        )
        attn_all = (
            lax.all_gather(w_query, "fsdp", axis=0, tiled=True),
            lax.all_gather(w_key, "fsdp", axis=0, tiled=True),
            lax.all_gather(w_value, "fsdp", axis=0, tiled=True),
            lax.all_gather(w_out, "fsdp", axis=0, tiled=True),
        )
        unit_one, inv_one = normalize(inputs)
        normed_one = (unit_one * attn_gain).astype(jnp.bfloat16)
        query_raw = matmul(normed_one, attn_all[0]).reshape(row_count, HQ, HD)
        key_raw = matmul(normed_one, attn_all[1]).reshape(row_count, HK, HD)
        value_raw = matmul(normed_one, attn_all[2])
        queries = (
            (rotate(query_raw, cos_rows, sin_rows) * head_scale)
            .astype(jnp.bfloat16)
            .reshape(seq_block, width_ct, HQ * HD)
        )
        keys = (
            rotate(key_raw, cos_rows, sin_rows)
            .astype(jnp.bfloat16)
            .reshape(seq_block, width_ct, HK * HD)
        )
        values = value_raw.astype(jnp.bfloat16).reshape(seq_block, width_ct, HK * HD)
        key_all, value_all = (
            lax.all_gather(keys, "ctx", axis=1, tiled=True),
            lax.all_gather(values, "ctx", axis=1, tiled=True),
        )
        attended_parts, lse_parts = ([], [])
        seq_at = 0
        attended_one, lse_one = attend_forward(
            queries[seq_at], key_all[seq_at], value_all[seq_at], allowed
        )
        attended_parts.append(attended_one)
        lse_parts.append(lse_one)
        attended = attended_parts[0].astype(jnp.bfloat16)
        resid = inputs + matmul(attended, attn_all[3])
        unit_two, inv_two = normalize(resid)
        normed_two = (unit_two * mlp_gain).astype(jnp.bfloat16)
        gate_proj = matmul(normed_two, lax.all_gather(w_gate, "fsdp", axis=0, tiled=True))
        up_proj = matmul(normed_two, lax.all_gather(w_up, "fsdp", axis=0, tiled=True))
        sigma = jax.nn.sigmoid(gate_proj)
        active = gate_proj * sigma
        hidden_act = (active * up_proj).astype(jnp.bfloat16)
        down_out = matmul(hidden_act, lax.all_gather(w_down, "fsdp", axis=0, tiled=True))
        mixed_list.append((resid + down_out).astype(jnp.bfloat16))
        grad_down = outer_grad.astype(jnp.bfloat16)
        grad_hidden = times_transposed(
            grad_down, lax.all_gather(w_down, "fsdp", axis=0, tiled=True)
        )
        grad_gate = (grad_hidden * up_proj * sigma * (1.0 + gate_proj * (1.0 - sigma))).astype(
            jnp.bfloat16
        )
        grad_upper = (grad_hidden * active).astype(jnp.bfloat16)
        pair_pieces = lax.all_gather((w_gate, w_up), "fsdp", axis=0, tiled=True)
        grad_normed_two = times_transposed(grad_gate, pair_pieces[0]) + times_transposed(
            grad_upper, pair_pieces[1]
        )
        mlp_gain_acc = mlp_gain_acc + jnp.sum(grad_normed_two * unit_two, axis=0)
        grad_resid = outer_grad + norm_back(grad_normed_two, mlp_gain, unit_two, inv_two)
        grad_branch = grad_resid.astype(jnp.bfloat16)
        attn_back = (
            lax.all_gather(w_query, "fsdp", axis=0, tiled=True),
            lax.all_gather(w_key, "fsdp", axis=0, tiled=True),
            lax.all_gather(w_value, "fsdp", axis=0, tiled=True),
            lax.all_gather(w_out, "fsdp", axis=0, tiled=True),
        )
        grad_attended = times_transposed(grad_branch, attn_back[3]).astype(jnp.bfloat16)
        key_back, value_back = (
            lax.all_gather(keys, "ctx", axis=1, tiled=True),
            lax.all_gather(values, "ctx", axis=1, tiled=True),
        )
        query_parts, key_parts, value_parts = ([], [], [])
        seq_at = 0
        query_one = queries[seq_at]
        key_one = key_back[seq_at]
        value_one = value_back[seq_at]
        lse_one = lse_parts[seq_at]
        grad_query, grad_key, grad_value, row_inner = attend_backward(
            query_one, key_one, value_one, allowed, lse_one, grad_attended
        )
        own_key = lax.psum_scatter(
            grad_key.astype(jnp.bfloat16), "ctx", scatter_dimension=0, tiled=True
        ).astype(jnp.float32)
        own_value = lax.psum_scatter(
            grad_value.astype(jnp.bfloat16), "ctx", scatter_dimension=0, tiled=True
        ).astype(jnp.float32)
        query_parts.append(
            rotate((grad_query * head_scale).reshape(width_ct, HQ, HD), cos_one, -sin_one).reshape(
                width_ct, HQ * HD
            )
        )
        key_parts.append(
            rotate(own_key.reshape(width_ct, HK, HD), cos_one, -sin_one).reshape(width_ct, HK * HD)
        )
        value_parts.append(own_value)
        grad_query_raw = query_parts[0].astype(jnp.bfloat16)
        grad_key_raw = key_parts[0].astype(jnp.bfloat16)
        grad_value_raw = value_parts[0].astype(jnp.bfloat16)
        grad_normed_one = (
            times_transposed(grad_query_raw, attn_back[0])
            + times_transposed(grad_key_raw, attn_back[1])
            + times_transposed(grad_value_raw, attn_back[2])
        )
        attn_gain_acc = attn_gain_acc + jnp.sum(grad_normed_one * unit_one, axis=0)
        token_grad_list.append(
            (grad_resid + norm_back(grad_normed_one, attn_gain, unit_one, inv_one)).astype(
                jnp.bfloat16
            )
        )
        kept_normed_one.append(normed_one)
        kept_grad_query.append(grad_query_raw)
        kept_grad_key.append(grad_key_raw)
        kept_grad_value.append(grad_value_raw)
        kept_attended.append(attended)
        kept_grad_branch.append(grad_branch)
        kept_normed_two.append(normed_two)
        kept_grad_gate.append(grad_gate)
        kept_grad_upper.append(grad_upper)
        kept_inner.append(hidden_act)
        kept_grad_down.append(grad_down)
    normed_one_all = jnp.concatenate(kept_normed_one, axis=0)
    normed_two_all = jnp.concatenate(kept_normed_two, axis=0)
    w_query_grad = reduce_grad(
        transposed_times(normed_one_all, jnp.concatenate(kept_grad_query, axis=0))
    )
    w_key_grad = reduce_grad(
        transposed_times(normed_one_all, jnp.concatenate(kept_grad_key, axis=0))
    )
    w_value_grad = reduce_grad(
        transposed_times(normed_one_all, jnp.concatenate(kept_grad_value, axis=0))
    )
    w_out_grad = reduce_grad(
        transposed_times(
            jnp.concatenate(kept_attended, axis=0), jnp.concatenate(kept_grad_branch, axis=0)
        )
    )
    w_gate_grad = reduce_grad(
        transposed_times(normed_two_all, jnp.concatenate(kept_grad_gate, axis=0))
    )
    w_up_grad = reduce_grad(
        transposed_times(normed_two_all, jnp.concatenate(kept_grad_upper, axis=0))
    )
    w_down_grad = reduce_grad(
        transposed_times(
            jnp.concatenate(kept_inner, axis=0), jnp.concatenate(kept_grad_down, axis=0)
        )
    )
    attn_gain_grad, mlp_gain_grad = lax.psum((attn_gain_acc, mlp_gain_acc), ("ctx", "fsdp"))
    mixed = jnp.concatenate(mixed_list, axis=0).reshape(seq_local, width_ct, model_width)
    tokens_grad = jnp.concatenate(token_grad_list, axis=0).reshape(seq_local, width_ct, model_width)
    return (
        mixed,
        tokens_grad,
        attn_gain_grad,
        w_query_grad,
        w_key_grad,
        w_value_grad,
        w_out_grad,
        mlp_gain_grad,
        w_gate_grad,
        w_up_grad,
        w_down_grad,
    )


def nt(a,b):
    return lax.dot_general(a,b,(((1,),(1,)),((),())),preferred_element_type=jnp.float32)
def nn(a,b):
    return jnp.dot(a,b,preferred_element_type=jnp.float32)

def turn(v,cosine,sine):
    return v*cosine+pltpu.roll(v,LANES//2,1)*sine

def forward_kernel(rows,step_rows,raw_ref,cos_ref,sin_ref,qkv_ref,out_ref,lse_ref,key_ref,val_t_ref):
    at=pl.program_id(0)
    here=pl.ds(pl.multiple_of(at*rows,rows),rows)
    cosine,sine=cos_ref[...],sin_ref[...]
    raw=raw_ref[...]
    @pl.when(at==0)
    def _():
        val_t_ref[...]=jnp.zeros_like(val_t_ref)
    scale=HD**-0.5
    parts=[(turn(raw[:,j*LANES:(j+1)*LANES],cosine,sine)*(scale if j<2 else 1.0)).astype(BF) for j in range(3)]
    value=raw[:,3*LANES:].astype(BF)
    for j in range(3):
        qkv_ref[:,j*LANES:(j+1)*LANES]=parts[j]
    qkv_ref[:,3*LANES:]=value
    key_ref[here,:]=parts[2]
    val_t_ref[:,here]=value.T
    query=jnp.concatenate(parts[:2],axis=0)
    length=key_ref.shape[0]
    per=step_rows//rows
    for band in range(length//step_rows):
        @pl.when(at//per==band)
        def _():
            extent=(band+1)*step_rows
            scores=nt(key_ref[0:extent,:],query)
            tail=scores[band*step_rows:,:]
            key_pos=lax.broadcasted_iota(jnp.int32,tail.shape,0)
            query_pos=(at%per)*rows+lax.broadcasted_iota(jnp.int32,tail.shape,1)%rows
            tail=jnp.where(key_pos<=query_pos,tail,MASK_FILL)
            pieces=[scores[b*step_rows:(b+1)*step_rows,:] for b in range(band)]+[tail]
            top=functools.reduce(jnp.maximum,[jnp.max(p,axis=0,keepdims=True) for p in pieces])
            total=0.0; acc=0.0
            for b,p in enumerate(pieces):
                e=jnp.exp(p-top)
                total=total+jnp.sum(e,axis=0,keepdims=True)
                acc=acc+nn(val_t_ref[:,b*step_rows:(b+1)*step_rows],e.astype(BF))
            acc=acc/total
            out_ref[:,0:LANES]=acc[:,0:rows].T.astype(BF)
            out_ref[:,LANES:]=acc[:,rows:].T.astype(BF)
            lse_ref[0]=top+jnp.log(total)

def head_forward(raw,cosine,sine,rows=512,step_rows=512):
    length=raw.shape[0]
    steps=length//rows
    return pl.pallas_call(
        functools.partial(forward_kernel,rows,step_rows),
        grid=(steps,),
        in_specs=[pl.BlockSpec((rows,4*LANES),lambda i:(i,0)),
                  pl.BlockSpec((rows,LANES),lambda i:(i,0)),
                  pl.BlockSpec((rows,LANES),lambda i:(i,0))],
        out_specs=[pl.BlockSpec((rows,4*LANES),lambda i:(i,0)),
                   pl.BlockSpec((rows,2*LANES),lambda i:(i,0)),
                   pl.BlockSpec((1,1,2*rows),lambda i:(i,0,0))],
        out_shape=[jax.ShapeDtypeStruct((length,4*LANES),BF),
                   jax.ShapeDtypeStruct((length,2*LANES),BF),
                   jax.ShapeDtypeStruct((steps,1,2*rows),jnp.float32)],
        scratch_shapes=[pltpu.VMEM((length,LANES),BF),pltpu.VMEM((LANES,length),BF)],
        compiler_params=pltpu.CompilerParams(vmem_limit_bytes=VMEM_LIMIT),
    )(raw,cosine,sine)

def backward_kernel(rows,step_rows,qkv_ref,out_ref,grad_ref,lse_ref,cos_ref,sin_ref,pick_ref,res_ref,
                    key_t_ref,grad_key_ref,grad_val_ref,rows_ref):
    at=pl.program_id(0)
    here=pl.ds(pl.multiple_of(at*rows,rows),rows)
    length=qkv_ref.shape[0]
    scale=HD**-0.5
    @pl.when(at==0)
    def _():
        grad_key_ref[...]=jnp.zeros_like(grad_key_ref)
        grad_val_ref[...]=jnp.zeros_like(grad_val_ref)
        for b in range(length//rows):
            key_t_ref[:,b*rows:(b+1)*rows]=qkv_ref[b*rows:(b+1)*rows,2*LANES:3*LANES].T
    query=jnp.concatenate([qkv_ref[here,0:LANES],qkv_ref[here,LANES:2*LANES]],axis=0)
    grad=jnp.concatenate([grad_ref[:,0:LANES],grad_ref[:,LANES:]],axis=0)
    out=jnp.concatenate([out_ref[:,0:LANES],out_ref[:,LANES:]],axis=0)
    inner=jnp.sum((grad.astype(jnp.float32)*out.astype(jnp.float32)).T,axis=0,keepdims=True)
    lse=lse_ref[0]
    per=step_rows//rows
    for band in range(length//step_rows):
        @pl.when(at//per==band)
        def _():
            grad_query=0.0
            for b in range(band+1):
                span=slice(b*step_rows,(b+1)*step_rows)
                scores=nt(qkv_ref[span,2*LANES:3*LANES],query)
                prob=jnp.exp(scores-lse)
                if b==band:
                    key_pos=lax.broadcasted_iota(jnp.int32,scores.shape,0)
                    query_pos=(at%per)*rows+lax.broadcasted_iota(jnp.int32,scores.shape,1)%rows
                    prob=jnp.where(key_pos<=query_pos,prob,0.0)
                grad_prob=nt(qkv_ref[span,3*LANES:],grad)
                grad_scores=(prob*(grad_prob-inner)).astype(BF)
                grad_val_ref[span,:]+=nn(prob.astype(BF),grad)
                grad_key_ref[span,:]+=nn(grad_scores,query)
                grad_query=grad_query+nn(key_t_ref[:,span],grad_scores)
            for j in range(2):
                back=grad_query[:,j*rows:(j+1)*rows].T*scale
                rows_ref[here,j*LANES:(j+1)*LANES]=turn(back,cos_ref[here,:],-sin_ref[here,:]).astype(BF)
    @pl.when(at==length//rows-1)
    def _():
        for b in range(length//step_rows):
            span=slice(b*step_rows,(b+1)*step_rows)
            rows_ref[span,2*LANES:3*LANES]=turn(grad_key_ref[span,:],cos_ref[span,:],-sin_ref[span,:]).astype(BF)
            rows_ref[span,3*LANES:]=grad_val_ref[span,:].astype(BF)
            res_ref[span,:]=nn(rows_ref[span,:],pick_ref[...]).astype(BF)

def head_backward(qkv,out,grad,lse,cosine,sine,pick,rows=256,step_rows=256):
    length=qkv.shape[0]
    steps=length//rows
    lse=lse.reshape(-1,2,lse.shape[2]//2).transpose(1,0,2).reshape(2,steps,rows).transpose(1,0,2).reshape(steps,1,2*rows)
    whole=lambda a:pl.BlockSpec(a.shape,lambda i:(0,)*a.ndim)
    return pl.pallas_call(
        functools.partial(backward_kernel,rows,step_rows),
        grid=(steps,),
        in_specs=[whole(qkv),
                  pl.BlockSpec((rows,2*LANES),lambda i:(i,0)),
                  pl.BlockSpec((rows,2*LANES),lambda i:(i,0)),
                  pl.BlockSpec((1,1,2*rows),lambda i:(i,0,0)),
                  whole(cosine),whole(sine),whole(pick)],
        out_specs=pl.BlockSpec((length,4*HD),lambda i:(0,0)),
        out_shape=jax.ShapeDtypeStruct((length,4*HD),BF),
        scratch_shapes=[pltpu.VMEM((LANES,length),BF),pltpu.VMEM((length,LANES),jnp.float32),
                        pltpu.VMEM((length,LANES),jnp.float32),pltpu.VMEM((length,4*LANES),BF)],
        compiler_params=pltpu.CompilerParams(vmem_limit_bytes=VMEM_LIMIT),
    )(qkv,out,grad,lse,cosine,sine,pick)

def pad_columns():
    half=HD//2
    lanes=np.arange(4*LANES); block=lanes//LANES; lane=lanes%LANES
    split=np.where(lane<half,lane,np.where((lane>=LANES//2)&(lane<LANES//2+half),lane-LANES//2+half,-1))
    plain=np.where(lane<HD,lane,-1)
    column=np.where(block<3,split,plain)
    return np.where(column>=0,column+block*HD,-1)

CORES, LINES, PLANES = 2, 2, 4
CHIPS = LINES * PLANES
RANKS = CORES * CHIPS


def swap_fsdp(value):
    return lax.ppermute(value, "fsdp", [(0, 1), (1, 0)])


def swap_ctx(value, bit):
    return lax.ppermute(value, "ctx", [(i, i ^ bit) for i in range(RANKS)])


def swap_core(value):
    return swap_ctx(value, 1)


def swap_line(value):
    return swap_ctx(value, CORES)


def plane_up(value, sources):
    step = CORES * LINES
    return lax.ppermute(value, "ctx", [(z * step + i, z * step + step + i) for z in sources for i in range(step)])


def plane_down(value, sources):
    step = CORES * LINES
    return lax.ppermute(value, "ctx", [(z * step + i, z * step - step + i) for z in sources for i in range(step)])


def at(value, index, axis=0):
    return lax.dynamic_index_in_dim(value, index, axis, keepdims=False)


def in_order(which, mine, other):
    first = which == 0
    return jnp.concatenate([jnp.where(first, mine, other), jnp.where(first, other, mine)], axis=0)


def after(value, earlier):
    return lax.optimization_barrier((value, earlier))[0]


def rope_rows(length):
    lane = jnp.arange(LANES)
    half = LANES // 2
    entry = jnp.where(lane < half, lane, lane - half)
    used = entry < HD // 2
    inv_freq = 1.0 / ROPE_BASE ** (entry.astype(jnp.float32) * 2.0 / HD)
    angles = jnp.arange(length, dtype=jnp.int32).astype(jnp.float32)[:, None] * inv_freq[None, :]
    sign = jnp.where(lane < half, -1.0, 1.0)
    return jnp.where(used, jnp.cos(angles), 0.0), jnp.where(used, jnp.sin(angles) * sign, 0.0)


def take_kernel(info, gate_a, gate_b, up_a, up_b, out_ref):
    @pl.when(info[1] == 0)
    def _():
        out_ref[:, :LANES] = gate_a[...]
        out_ref[:, LANES:] = gate_b[...]

    @pl.when(info[1] != 0)
    def _():
        out_ref[:, :LANES] = up_a[...]
        out_ref[:, LANES:] = up_b[...]


def take_columns(info, w_gate, w_up):
    depth, hidden = w_gate.shape
    part = depth // LINES
    steps = hidden // (4 * LANES)

    def spec(core, odd):
        return pl.BlockSpec(
            (part, LANES), lambda j, info: (info[2], jnp.where(info[1] == core, 4 * j + 2 * odd + 1 - info[0], 0))
        )

    return pl.pallas_call(
        take_kernel,
        grid_spec=pltpu.PrefetchScalarGridSpec(
            num_scalar_prefetch=1,
            grid=(steps,),
            in_specs=[spec(0, 0), spec(0, 1), spec(1, 0), spec(1, 1)],
            out_specs=pl.BlockSpec((part, 2 * LANES), lambda j, info: (0, j)),
        ),
        out_shape=jax.ShapeDtypeStruct((part, hidden // 2), BF),
        compiler_params=pltpu.CompilerParams(vmem_limit_bytes=VMEM_LIMIT),
        cost_estimate=pl.CostEstimate(flops=0, bytes_accessed=2 * depth * hidden, transcendentals=0),
    )(info, w_gate, w_gate, w_up, w_up)


def mlp_kernel(
    info, normed, grad_rows, gate_a, gate_b, up_a, up_b, got, other, down_a, down_b, down_got, down_other,
    inner_ref, grad_gate_ref, grad_up_ref, mixed_ref, back_ref,
    gate_far, up_far, down, mixed_acc, back_acc,
):
    step = pl.program_id(0)
    half_steps = pl.num_programs(0) // 2
    side, core = info[0], info[1]
    depth = gate_a.shape[0]
    near = pl.ds(pl.multiple_of(side * depth, LANES), depth)
    far = pl.ds(pl.multiple_of((1 - side) * depth, LANES), depth)

    @pl.when(step == 0)
    def _():
        mixed_acc[...] = jnp.zeros_like(mixed_acc)
        back_acc[...] = jnp.zeros_like(back_acc)

    @pl.when(core == 0)
    def _():
        gate_far[...] = got[...]
        up_far[...] = other[...]

    @pl.when(core != 0)
    def _():
        gate_far[...] = other[...]
        up_far[...] = got[...]

    @pl.when(step < half_steps)
    def _():
        down[:LANES, :] = down_a[...]
        down[LANES:, :] = down_b[...]

    far_half = (step - half_steps) * 2 // half_steps

    @pl.when((step >= half_steps) & (far_half == core))
    def _():
        down[...] = down_got[...]

    @pl.when((step >= half_steps) & (far_half != core))
    def _():
        down[...] = down_other[...]

    gate_near = jnp.concatenate([gate_a[...], gate_b[...]], axis=1)
    up_near = jnp.concatenate([up_a[...], up_b[...]], axis=1)
    gate = nn(normed[:, near], gate_near) + nn(normed[:, far], gate_far[...])
    upper = nn(normed[:, near], up_near) + nn(normed[:, far], up_far[...])
    sigma = jax.nn.sigmoid(gate)
    active = gate * sigma
    inner = (active * upper).astype(BF)
    grad_inner = nt(grad_rows[...], down[...])
    grad_gate = (grad_inner * upper * sigma * (1.0 + gate * (1.0 - sigma))).astype(BF)
    grad_up = (grad_inner * active).astype(BF)
    for which in range(CORES):
        span = slice(which * LANES, (which + 1) * LANES)
        inner_ref[which] = inner[:, span]
        grad_gate_ref[which] = grad_gate[:, span]
        grad_up_ref[which] = grad_up[:, span]
    mixed_acc[...] += nn(inner, down[...])
    back_acc[:, near] += nt(grad_gate, gate_near) + nt(grad_up, up_near)
    back_acc[:, far] += nt(grad_gate, gate_far[...]) + nt(grad_up, up_far[...])

    @pl.when(step == 2 * half_steps - 1)
    def _():
        mixed_ref[...] = mixed_acc[...].astype(mixed_ref.dtype)
        back_ref[...] = back_acc[...].astype(back_ref.dtype)


def mlp_part(info, normed, grad_rows, weights, kind):
    w_gate, w_up, got, other, w_down, down_got, down_other = weights
    rows, model = normed.shape
    depth, hidden = w_gate.shape
    half = hidden // 2
    steps = half // (2 * LANES)
    part = steps // 2

    def pair_of(j, info):
        return jnp.where(j < part, info[0] * part + j, (1 - info[0]) * part + j - part)

    def whole(shape):
        return pl.BlockSpec(shape, lambda j, info: (0, 0))

    def column(odd):
        return pl.BlockSpec((depth, LANES), lambda j, info: (0, 4 * pair_of(j, info) + 2 * odd + info[0]))

    def row(odd):
        return pl.BlockSpec((LANES, model), lambda j, info: (4 * jnp.minimum(j, part - 1) + 2 * odd + info[0], 0))

    def far_row(which):
        def block(j, info):
            half_at = jnp.where(which == 0, info[1], 1 - info[1])
            return (jnp.clip(j - part - half_at * (part // 2), 0, part // 2 - 1), 0)

        return pl.BlockSpec((2 * LANES, model), block)

    far = pl.BlockSpec((depth, 2 * LANES), lambda j, info: (0, pair_of(j, info)))

    def place(j, info):
        pair = pair_of(j, info)
        return (0, 0, (pair % LINES) * PLANES + pair // LINES)

    act = pl.BlockSpec((CORES, rows, LANES), place)
    act_shape = jax.ShapeDtypeStruct((CORES, rows, half // CORES), BF)
    return pl.pallas_call(
        mlp_kernel,
        grid_spec=pltpu.PrefetchScalarGridSpec(
            num_scalar_prefetch=1,
            grid=(steps,),
            in_specs=[
                whole((rows, model)), whole((rows, model)),
                column(0), column(1), column(0), column(1), far, far,
                row(0), row(1), far_row(0), far_row(1),
            ],
            out_specs=[act, act, act, whole((rows, model)), whole((rows, model))],
            scratch_shapes=[
                pltpu.VMEM((depth, 2 * LANES), BF),
                pltpu.VMEM((depth, 2 * LANES), BF),
                pltpu.VMEM((2 * LANES, model), BF),
                pltpu.VMEM((rows, model), jnp.float32),
                pltpu.VMEM((rows, model), jnp.float32),
            ],
        ),
        out_shape=[act_shape, act_shape, act_shape] + [jax.ShapeDtypeStruct((rows, model), kind)] * 2,
        compiler_params=pltpu.CompilerParams(vmem_limit_bytes=VMEM_LIMIT),
        cost_estimate=pl.CostEstimate(
            flops=12 * rows * model * half, bytes_accessed=6 * model * half, transcendentals=rows * half
        ),
    )(info, normed, grad_rows, w_gate, w_gate, w_up, w_up, got, other, w_down, w_down, down_got, down_other)


def ctx_copy(source, target, sems, number, rank):
    return pltpu.make_async_remote_copy(
        src_ref=source,
        dst_ref=target,
        send_sem=sems.at[0, number],
        recv_sem=sems.at[1, number],
        device_id={"ctx": rank},
        device_id_type=pl.DeviceIdType.MESH,
    )


def side_copy(source, target, sems, number, side):
    return pltpu.make_async_remote_copy(
        src_ref=source,
        dst_ref=target,
        send_sem=sems.at[0, number],
        recv_sem=sems.at[1, number],
        device_id={"fsdp": side},
        device_id_type=pl.DeviceIdType.MESH,
    )


def greet(rank, side):
    barrier = pltpu.get_barrier_semaphore()
    for away in range(1, RANKS):
        pl.semaphore_signal(
            barrier,
            inc=1,
            device_id={"ctx": lax.rem(rank + away, RANKS)},
            device_id_type=pl.DeviceIdType.MESH,
        )
    pl.semaphore_signal(barrier, inc=1, device_id={"fsdp": 1 - side}, device_id_type=pl.DeviceIdType.MESH)
    pl.semaphore_wait(barrier, RANKS)


def wide(value):
    return value.astype(jnp.float32)


def reduce_kernel(
    rows_in, down_keep, down_got, gate_keep, gate_got, up_keep, up_sent, out_keep, out_sent, head_keep, head_sent, gains_in,
    rows_out, down_mine, down_theirs, down_side, gate_mine, gate_side, up_mine, up_side, out_mine, head_out, gains_out,
    up_got, out_got, down_acc, gate_acc, up_acc, out_acc, down_in, gate_in, up_in, out_in,
    head_got, head_two, head_side, head_last, gain_buf, gain_in, exchange_sems, plane_sems, sems, local_sem,
):
    rank = lax.axis_index("ctx")
    side = lax.axis_index("fsdp")
    core = lax.rem(rank, CORES)
    line = lax.rem(lax.div(rank, CORES), LINES)
    plane = lax.div(rank, CORES * LINES)
    step_rank = CORES * LINES
    last = PLANES - 1
    other_line = rank + CORES * (1 - 2 * line)
    other_core = rank + 1 - 2 * core
    greet(rank, side)

    up_line = ctx_copy(up_sent, up_got, sems, 0, other_line)
    out_line = ctx_copy(out_sent, out_got, sems, 1, other_line)
    head_line = ctx_copy(head_sent, head_got, sems, 2, other_line)

    weights = (
        (down_keep, down_got, down_acc, down_in, 0),
        (gate_keep, gate_got, gate_acc, gate_in, 1),
        (up_keep, up_got, up_acc, up_in, 2),
        (out_keep, out_got, out_acc, out_in, 3),
    )

    def message(weight, direction, step):
        _, _, acc, landed, number = weight
        slot = direction * last + step
        target = rank + step_rank * (1 - 2 * direction)
        return ctx_copy(acc.at[slot], landed.at[slot], plane_sems, number * 2 * last + slot, target)

    def hop(weight, step):
        keep, got, acc, landed, _ = weight
        for direction in range(2):
            depth = plane if direction == 0 else last - plane
            piece = plane + (last - step) * (1 - 2 * direction)
            slot = direction * last + step

            if step:
                @pl.when((depth >= 1) & (depth <= step))
                def _():
                    message(weight, direction, step - 1).wait_recv()

                @pl.when((depth >= 1) & (depth <= step) & (depth < last))
                def _():
                    acc[slot] = (wide(keep[piece]) + wide(got[piece]) + wide(landed[slot - 1])).astype(BF)

            @pl.when(depth == 0)
            def _():
                acc[slot] = (wide(keep[piece]) + wide(got[piece])).astype(BF)

            @pl.when((depth <= step) & (depth < last))
            def _():
                message(weight, direction, step).start()

    def finish(weight, result):
        keep, got, _, landed, _ = weight
        for direction in range(2):
            depth = plane if direction == 0 else last - plane

            @pl.when(depth >= 1)
            def _():
                message(weight, direction, last - 1).wait_recv()

        base = wide(keep[plane]) + wide(got[plane])
        above, below = landed.at[last - 1], landed.at[2 * last - 1]

        @pl.when(plane == 0)
        def _():
            result[...] = (base + wide(below[...])).astype(BF)

        @pl.when(plane == last)
        def _():
            result[...] = (base + wide(above[...])).astype(BF)

        @pl.when((plane > 0) & (plane < last))
        def _():
            result[...] = (base + wide(above[...]) + wide(below[...])).astype(BF)

    def sent(weight):
        for step in range(last):
            for direction in range(2):
                depth = plane if direction == 0 else last - plane

                @pl.when((depth <= step) & (depth < last))
                def _():
                    message(weight, direction, step).wait_send()

    down, gate, up, out = weights
    hop(down, 0)
    hop(gate, 0)
    up_line.start()
    head_line.start()
    copies = []
    for away in range(1, RANKS):
        to = lax.rem(rank + away, RANKS)
        copy = ctx_copy(rows_in.at[to], rows_out.at[rank], exchange_sems, away, to)
        copy.start()
        copies.append(copy)
    own = pltpu.make_async_copy(rows_in.at[rank], rows_out.at[rank], local_sem)
    own.start()
    out_line.start()

    gain_partners = (None, other_core, other_line, rank + step_rank * (1 - 2 * lax.rem(plane, 2)),
                     rank + 2 * step_rank * (1 - 2 * lax.div(plane, 2)))

    def gain_copy(number):
        if number == 0:
            return side_copy(gain_buf.at[0], gain_in.at[0], sems, 3, 1 - side)
        return ctx_copy(gain_buf.at[number], gain_in.at[number], sems, 3 + number, gain_partners[number])

    def gain_hop(number):
        if number:
            gain_copy(number - 1).wait_recv()
            gain_buf[number] = gain_buf[number - 1] + gain_in[number - 1]
        else:
            gain_buf[0] = gains_in[...]
        if number < 5:
            gain_copy(number).start()

    gain_hop(0)
    hop(down, 1)
    hop(gate, 1)
    gain_hop(1)

    model = head_keep.shape[1]
    half = model // 2
    near = pl.ds(pl.multiple_of(side * half, LANES), half)
    far = pl.ds(pl.multiple_of((1 - side) * half, LANES), half)
    head_line.wait_recv()
    head_two[...] = (head_keep[...] + wide(head_got[...])).astype(BF)
    head_cross = side_copy(head_two.at[:, far], head_side, sems, 8, 1 - side)
    head_cross.start()
    gain_hop(2)

    up_line.wait_recv()
    out_line.wait_recv()
    hop(up, 0)
    hop(out, 0)
    hop(down, 2)
    hop(gate, 2)
    gain_hop(3)
    head_cross.wait_recv()
    head_last[...] = (wide(head_two[:, near]) + wide(head_side[...])).astype(BF)
    turned = rank - CORES * line - core + CORES * core + line
    head_turn = ctx_copy(head_last, head_out, sems, 9, turned)

    @pl.when(line != core)
    def _():
        head_turn.start()

    @pl.when(line == core)
    def _():
        head_out[...] = head_last[...]

    hop(up, 1)
    hop(out, 1)
    gain_hop(4)

    finish(down, down_mine)
    per_core = down_mine.shape[0] // CORES
    theirs = pl.ds(pl.multiple_of((1 - core) * per_core, 16), per_core)
    mine = pl.ds(pl.multiple_of(core * per_core, 16), per_core)
    down_core = ctx_copy(down_mine.at[theirs], down_theirs, sems, 10, other_core)
    down_core.start()
    finish(gate, gate_mine)
    gate_cross = side_copy(gate_mine.at[:, far], gate_side, sems, 11, 1 - side)
    gate_cross.start()

    hop(up, 2)
    hop(out, 2)
    gain_hop(5)
    gains_out[...] = gain_buf[5]

    down_core.wait_recv()
    crosses = []
    span = down_mine.shape[1] // 4
    for which in range(2):
        block = down_mine.at[mine] if which == 0 else down_theirs
        for at_line in range(LINES):
            lanes = pl.ds(pl.multiple_of(at_line * 2 * span + (1 - side) * span, LANES), span)
            cross = side_copy(block.at[:, lanes], down_side.at[which, at_line], sems, 13 + which * LINES + at_line, 1 - side)
            cross.start()
            crosses.append(cross)

    finish(up, up_mine)
    up_cross = side_copy(up_mine.at[:, far], up_side, sems, 12, 1 - side)
    up_cross.start()
    finish(out, out_mine)

    @pl.when(line != core)
    def _():
        head_turn.wait()

    for copy in copies:
        copy.wait()
    own.wait()
    for cross in crosses + [gate_cross, up_cross]:
        cross.wait()
    for copy in (up_line, out_line, head_line, head_cross, down_core):
        copy.wait_send()
    for number in range(5):
        gain_copy(number).wait_send()
    for weight in weights:
        sent(weight)


def reduce_all(rows_in, down, gate, up, out, head, gains):
    (down_keep, down_got), (gate_keep, gate_got), (up_keep, up_sent), (out_keep, out_sent) = down, gate, up, out
    head_keep, head_sent = head
    hops = 2 * (PLANES - 1)
    vmem = pl.BlockSpec(memory_space=pltpu.VMEM)
    hbm = pl.BlockSpec(memory_space=pl.ANY)

    def piece(keep):
        return keep.shape[1:]

    def half_lanes(keep):
        return (keep.shape[1], keep.shape[2] // 2)

    def shape(dims, kind=BF):
        return jax.ShapeDtypeStruct(dims, kind)

    down_rows, down_cols = piece(down_keep)
    keeps = (down_keep, gate_keep, up_keep, out_keep)
    return pl.pallas_call(
        reduce_kernel,
        in_specs=[hbm] + [vmem] * 5 + [hbm, vmem, hbm, vmem, hbm, vmem],
        out_specs=[hbm] + [vmem] * 10,
        out_shape=[
            shape(rows_in.shape),
            shape((down_rows, down_cols)),
            shape((down_rows // CORES, down_cols)),
            shape((2, LINES, down_rows // CORES, down_cols // 4)),
            shape(piece(gate_keep)),
            shape(half_lanes(gate_keep)),
            shape(piece(up_keep)),
            shape(half_lanes(up_keep)),
            shape(piece(out_keep)),
            shape((head_keep.shape[0], head_keep.shape[1] // 2)),
            shape(gains.shape, jnp.float32),
        ],
        scratch_shapes=[pltpu.VMEM(up_keep.shape, BF), pltpu.VMEM(out_keep.shape, BF)]
        + [pltpu.VMEM((hops,) + piece(keep), BF) for keep in keeps]
        + [pltpu.VMEM((hops,) + piece(keep), BF) for keep in keeps]
        + [
            pltpu.VMEM(head_keep.shape, BF),
            pltpu.VMEM(head_keep.shape, BF),
            pltpu.VMEM((head_keep.shape[0], head_keep.shape[1] // 2), BF),
            pltpu.VMEM((head_keep.shape[0], head_keep.shape[1] // 2), BF),
            pltpu.VMEM((6,) + gains.shape, jnp.float32),
            pltpu.VMEM((5,) + gains.shape, jnp.float32),
            pltpu.SemaphoreType.DMA((2, RANKS)),
            pltpu.SemaphoreType.DMA((2, 4 * hops)),
            pltpu.SemaphoreType.DMA((2, 17)),
            pltpu.SemaphoreType.DMA,
        ],
        compiler_params=pltpu.CompilerParams(
            collective_id=0, has_side_effects=True, vmem_limit_bytes=VMEM_LIMIT
        ),
    )(
        rows_in, down_keep, down_got, gate_keep, gate_got, up_keep, up_sent, out_keep, out_sent, head_keep, head_sent, gains
    )


def head_shards(
    tokens, attn_gain, w_query, w_key, w_value, w_out, mlp_gain, w_gate, w_up, w_down, cotangent
):
    seqs, width, model = tokens.shape
    length = width * RANKS
    rows = seqs * width
    half_model = model // 2
    hidden = w_gate.shape[1]
    half_hidden = hidden // 2
    part_hidden = half_hidden // CORES
    chunk = hidden // (2 * RANKS)
    rank = lax.axis_index("ctx")
    side = lax.axis_index("fsdp")
    core = rank % CORES
    line = (rank // CORES) % LINES
    plane = rank // (CORES * LINES)
    head = plane * CORES + core
    low_side = side == 0
    info = jnp.stack([side, core, line]).astype(jnp.int32)
    pick = jnp.asarray((pad_columns()[:, None] == np.arange(HEAD_COLS)[None, :]).astype(np.float32)).astype(BF)

    near = at(tokens, line)
    across = swap_line(at(tokens, 1 - line))
    low = plane < PLANES // 2
    streams = []
    for start in (near, across):
        ups, downs = [], []
        up = down = start
        for step in range(PLANES - 1):
            up = plane_up(up, range(step, PLANES - 1))
            down = plane_down(down, range(1, PLANES - step))
            ups.append(up)
            downs.append(down)
        streams.append([
            start,
            jnp.where(low, downs[0], ups[0]),
            jnp.where(low, downs[1], ups[1]),
            jnp.where(plane == 0, downs[2], jnp.where(plane == 1, ups[0], jnp.where(plane == 2, downs[0], ups[2]))),
        ])

    def head_slice(weight, size):
        return lax.dynamic_slice_in_dim(weight, head * size, size, 1)

    head_rows = jnp.concatenate(
        [head_slice(w_query, 2 * HD), head_slice(w_key, HD), head_slice(w_value, HD)], axis=1
    )
    head_got = swap_fsdp(head_rows)
    head_weight = in_order(side, head_rows, head_got)
    head_padded = times_transposed(head_weight, pick).astype(BF)
    cosine, sine = rope_rows(length)

    def fetch(part, earlier):
        crossed = swap_fsdp(after(part, earlier))
        got = in_order(line, crossed, swap_line(crossed))
        return got, swap_core(got), crossed

    def quarter(block):
        return at(block.reshape((CORES * LINES, block.shape[0] // 4) + block.shape[1:]), 2 * core + line)

    out_got, out_other, crossed = fetch(quarter(w_out), head_got)
    gate_got, gate_other, crossed = fetch(take_columns(info, w_gate, w_up), crossed)
    cut = w_down.reshape(CORES * LINES, -1, 2, chunk, model)
    down_got, down_other, crossed = fetch(at(at(cut, 2 * core + line), 1 - side, 1).reshape(-1, model), crossed)
    weights = (w_gate, w_up, gate_got, gate_other, w_down, down_got, down_other)
    grad_down = cotangent.reshape(rows, model)

    normed_seq = jnp.zeros((PLANES, CHIPS // PLANES * 2 * width, model), BF)
    raw_seq = jnp.zeros((PLANES, CHIPS // PLANES * 2 * width, 4 * LANES), jnp.float32)
    for number in range(PLANES):
        place = jnp.where(low, plane + number, plane - number) % PLANES
        both = jnp.stack([streams[0][number], streams[1][number]])
        theirs = swap_core(both)
        block = jnp.stack(
            [
                jnp.where(core == 0, both, theirs),
                jnp.where(core == 0, theirs, both),
            ],
            axis=1,
        )
        block = jnp.where(line == 0, block, block[::-1]).reshape(-1, model)
        normed = (normalize(block.astype(jnp.float32))[0] * attn_gain).astype(BF)
        normed_seq = lax.dynamic_update_index_in_dim(normed_seq, normed, place, 0)
        raw_seq = lax.dynamic_update_index_in_dim(raw_seq, matmul(normed, head_padded), place, 0)
    normed_seq = normed_seq.reshape(length, model)
    qkv, attended_seq, lse = head_forward(raw_seq.reshape(length, 4 * LANES), cosine, sine)

    def exchange(value):
        return lax.all_to_all(value.reshape(RANKS, width, -1), "ctx", 0, 0, tiled=True)

    def by_token(value):
        cut = value.reshape(PLANES, LINES, CORES, width, value.shape[-1])
        return cut.transpose(1, 3, 0, 2, 4).reshape(rows, HK * value.shape[-1])

    attended = by_token(exchange(attended_seq))
    out_far = in_order(core, out_got, out_other)
    out_full = in_order(side, w_out, out_far)
    out_padded = jnp.pad(out_full.reshape(HQ, HD, model), ((0, 0), (0, LANES - HD), (0, 0))).reshape(HQ * LANES, model)
    inputs = tokens.reshape(rows, model).astype(jnp.float32)
    resid = inputs + matmul(attended, out_padded)
    unit_two, inv_two = normalize(resid)
    normed_two = (unit_two * mlp_gain).astype(BF)

    normed_other, grad_down_other = swap_fsdp((normed_two, after(grad_down, crossed)))
    inner_own, gate_own, up_own, mixed_own, back_own = mlp_part(info, normed_two, grad_down, weights, jnp.float32)
    normed_other, grad_down_other = after((normed_other, grad_down_other), mixed_own)
    inner_far, gate_far, up_far, mixed_far, back_far = mlp_part(info, normed_other, grad_down_other, weights, BF)
    back_got = swap_fsdp(back_far)
    mixed_got = swap_fsdp(after(mixed_far, back_got))

    normed_pair = jnp.concatenate([normed_two, normed_other], axis=0)
    normed_sib = swap_core(normed_pair)
    cot_pair = jnp.concatenate([grad_down, grad_down_other], axis=0)
    cot_sib = swap_core(cot_pair)

    def pair_acts(own, far):
        pair = jnp.concatenate([own, far], axis=1)
        return at(pair, core), swap_core(at(pair, 1 - core))

    inner_pair, inner_sib = pair_acts(inner_own, inner_far)
    grad_down_weight = (transposed_times(cot_pair, inner_pair) + transposed_times(cot_sib, inner_sib)).astype(BF)
    gate_pair, gate_sib = pair_acts(gate_own, gate_far)
    grad_gate_weight = (transposed_times(gate_pair, normed_pair) + transposed_times(gate_sib, normed_sib)).astype(BF)
    up_pair, up_sib = pair_acts(up_own, up_far)
    grad_up_weight = (transposed_times(up_pair, normed_pair) + transposed_times(up_sib, normed_sib)).astype(BF)

    mixed = (resid + mixed_own + mixed_got.astype(jnp.float32)).astype(BF)
    back_got = after(back_got, (grad_down_weight, grad_gate_weight, grad_up_weight))
    grad_normed_two = back_own + back_got.astype(jnp.float32)
    grad_resid = grad_down.astype(jnp.float32) + norm_back(grad_normed_two, mlp_gain, unit_two, inv_two)
    mlp_gain_part = jnp.sum(grad_normed_two * unit_two, axis=0)
    grad_branch = grad_resid.astype(BF)
    grad_attended = times_transposed(grad_branch, out_padded).astype(BF)
    cut = grad_attended.reshape(LINES, width, PLANES, CORES, 2 * LANES)
    grad_att_seq = exchange(cut.transpose(2, 0, 3, 1, 4)).reshape(length, 2 * LANES)

    att_cut = attended.reshape(rows, 2, HK * LANES)
    att_other, branch_other = swap_fsdp((at(att_cut, 1 - side, 1), grad_branch))
    att_pair = jnp.concatenate([at(att_cut, side, 1), att_other], axis=0)
    branch_pair = jnp.concatenate([grad_branch, branch_other], axis=0)
    cut = transposed_times(branch_pair, att_pair).astype(BF).reshape(CHIPS, CORES, model // RANKS, HK * LANES)
    got = swap_core(at(cut, 1 - core, 1))
    out_pair = (at(cut, core, 1).astype(jnp.float32) + got.astype(jnp.float32)).astype(BF)

    per_chip = model // CHIPS
    down_cut = grad_down_weight.reshape(PLANES, LINES, per_chip, part_hidden)
    gate_cut = grad_gate_weight.reshape(LINES, PLANES, chunk, model)
    up_cut = grad_up_weight.reshape(LINES, PLANES, chunk, model)
    out_cut = out_pair.reshape(PLANES, LINES, model // RANKS, HK * LANES)
    down_got = swap_line(at(down_cut, 1 - line, 1))
    gate_got = swap_line(at(gate_cut, 1 - line))

    grad_qkv = head_backward(qkv, attended_seq, grad_att_seq, lse, cosine, sine, pick)
    head_grad = transposed_times(grad_qkv, normed_seq)
    gain_part = jnp.sum(head_grad * head_weight.T.astype(jnp.float32), axis=0) / attn_gain
    query_cut = head_grad[: 2 * HD].reshape(2, HD, model)
    key_cut = head_grad[2 * HD :].reshape(2, 2, HD // 2, model)

    def half_columns(which):
        return jnp.concatenate([at(query_cut, which), at(key_cut, which, 1).reshape(HD, model)], axis=0)

    gains = jnp.concatenate([jnp.stack([gain_part, mlp_gain_part]), jnp.zeros((6, model), jnp.float32)], axis=0)
    (
        grad_rows, down_mine, down_theirs, down_side, gate_mine, gate_side, up_mine, up_side, out_mine, head_mine, gains
    ) = reduce_all(
        grad_qkv.reshape(RANKS, width, HEAD_COLS),
        (at(down_cut, line, 1), after(down_got, grad_qkv)),
        (at(gate_cut, line), after(gate_got, grad_qkv)),
        (at(up_cut, line), at(up_cut, 1 - line)),
        (at(out_cut, line, 1), at(out_cut, 1 - line, 1)),
        (half_columns(line), half_columns(1 - line).astype(BF)),
        gains,
    )
    grad_own = by_token(grad_rows)

    def by_columns(mine, theirs):
        cut = mine.reshape(chunk, 2, half_model)
        return in_order(side, at(cut, side, 1), theirs).astype(jnp.float32).T

    w_gate_grad = by_columns(gate_mine, gate_side)
    w_up_grad = by_columns(up_mine, up_side)
    shape = (model // RANKS, LINES, 2, PLANES // 2, chunk)
    parts = [at(down_mine.reshape((CORES,) + shape), core), down_theirs.reshape(shape)]
    kept = [at(part, side, 2) for part in parts]
    sided = [down_side[i].reshape(LINES, model // RANKS, PLANES // 2, chunk).transpose(1, 0, 2, 3) for i in range(2)]
    by_side = [
        jnp.stack([jnp.where(low_side, k, g), jnp.where(low_side, g, k)], axis=3) for k, g in zip(kept, sided)
    ]
    first = core == 0
    by_core = jnp.stack(
        [jnp.where(first, by_side[0], by_side[1]), jnp.where(first, by_side[1], by_side[0])], axis=3
    )
    w_down_grad = by_core.transpose(0, 2, 1, 3, 4, 5).reshape(model // RANKS, -1).T.astype(jnp.float32)
    w_out_grad = (
        out_mine.reshape(model // RANKS, HK, LANES)[:, :, :HD].reshape(model // RANKS, half_model).T.astype(jnp.float32)
    )
    head_mine = head_mine.astype(jnp.float32)
    w_query_grad = head_mine[:HD].T
    w_key_grad = head_mine[HD : HD + HD // 2].T
    w_value_grad = head_mine[HD + HD // 2 :].T

    late = after((w_query, w_key, w_value), attended_seq)
    packed = jnp.concatenate([part.reshape(half_model, HK, -1) for part in late], axis=2).reshape(half_model, -1)
    packed_got, packed_other, _ = fetch(quarter(packed), mixed_got)
    packed_full = in_order(side, packed, in_order(core, packed_got, packed_other))
    grad_normed_one = times_transposed(grad_own, packed_full)
    unit_one, inv_one = normalize(inputs)
    tokens_grad = (grad_resid + norm_back(grad_normed_one, attn_gain, unit_one, inv_one)).astype(BF)
    return (
        mixed.reshape(seqs, width, model),
        tokens_grad.reshape(seqs, width, model),
        gains[0],
        w_query_grad,
        w_key_grad,
        w_value_grad,
        w_out_grad,
        gains[1],
        w_gate_grad,
        w_up_grad,
        w_down_grad,
    )


def solution(mesh):
    by_heads = mesh.shape["ctx"] == RANKS and mesh.shape["fsdp"] == 2
    placed = (
        P("fsdp", "ctx", None),
        P(),
        P("fsdp", None),
        P("fsdp", None),
        P("fsdp", None),
        P("fsdp", None),
        P(),
        P("fsdp", None),
        P("fsdp", None),
        P("fsdp", None),
        P("fsdp", "ctx", None),
    )
    return jax.shard_map(
        head_shards if by_heads else shards,
        mesh=mesh,
        in_specs=placed,
        out_specs=(
            P("fsdp", "ctx", None),
            P("fsdp", "ctx", None),
            P(),
            P("fsdp", "ctx"),
            P("fsdp", "ctx"),
            P("fsdp", "ctx"),
            P("fsdp", "ctx"),
            P(),
            P("fsdp", "ctx"),
            P("fsdp", "ctx"),
            P("fsdp", "ctx"),
        ),
        check_vma=False,
    )
```

```python
import functools

import jax
import jax.numpy as jnp
import numpy as np
from jax import lax
from jax.experimental import pallas as pl
from jax.experimental.pallas import tpu as pltpu
from jax.sharding import PartitionSpec as P

HQ = 16
HK = 8
HD = 96
MICRO = 2
LANES = 128
HEAD_COLS = 4 * HD
BF = jnp.bfloat16
VMEM_LIMIT = 48 * 1024 * 1024


EPSILON = 1e-05
ROPE_BASE = 100000.0
MASK_FILL = -1e30


def matmul(left, right):
    return jnp.dot(left, right, preferred_element_type=jnp.float32)


def times_transposed(left, right):
    return lax.dot_general(
        left, right, (((1,), (1,)), ((), ())), preferred_element_type=jnp.float32
    )


def transposed_times(left, right):
    return lax.dot_general(
        left, right, (((0,), (0,)), ((), ())), preferred_element_type=jnp.float32
    )


def normalize(values):
    inv_rms = lax.rsqrt(jnp.mean(values * values, axis=-1, keepdims=True) + EPSILON)
    return (values * inv_rms, inv_rms)


def norm_back(grad_normed, gain_row, unit_rows, inv_rms):
    scaled = grad_normed * gain_row
    return inv_rms * (scaled - unit_rows * jnp.mean(scaled * unit_rows, axis=-1, keepdims=True))


def rotate(values, cosine, sine_rows):
    half_dim = values.shape[-1] // 2
    front = values[..., :half_dim]
    back_half = values[..., half_dim:]
    return jnp.concatenate(
        [front * cosine - back_half * sine_rows, back_half * cosine + front * sine_rows], axis=-1
    )


def attend_forward(query_rows, key_rows, value_rows, allowed):
    width_ct = query_rows.shape[0]
    grouped = query_rows.reshape(width_ct, HK, HQ // HK, HD)
    key_heads = key_rows.reshape(-1, HK, HD)
    value_heads = value_rows.reshape(-1, HK, HD)
    scores = jnp.einsum("cgrd,lgd->grcl", grouped, key_heads, preferred_element_type=jnp.float32)
    scores = jnp.where(allowed, scores, MASK_FILL)
    row_top = jnp.max(scores, axis=-1, keepdims=True)
    shifted_exp = jnp.exp(scores - row_top)
    row_total = jnp.sum(shifted_exp, axis=-1, keepdims=True)
    prob_low = (shifted_exp / row_total).astype(jnp.bfloat16)
    attended = jnp.einsum(
        "grcl,lgd->cgrd", prob_low, value_heads, preferred_element_type=jnp.float32
    )
    return (attended.reshape(width_ct, HQ * HD), row_top + jnp.log(row_total))


def attend_backward(query_rows, key_rows, value_rows, allowed, log_total, grad_rows):
    width_ct = query_rows.shape[0]
    grouped = query_rows.reshape(width_ct, HK, HQ // HK, HD)
    key_heads = key_rows.reshape(-1, HK, HD)
    value_heads = value_rows.reshape(-1, HK, HD)
    scores = jnp.einsum("cgrd,lgd->grcl", grouped, key_heads, preferred_element_type=jnp.float32)
    prob_full = jnp.exp(jnp.where(allowed, scores, MASK_FILL) - log_total)
    prob_low = prob_full.astype(jnp.bfloat16)
    grad_heads = grad_rows.reshape(width_ct, HK, HQ // HK, HD)
    grad_prob = jnp.einsum(
        "cgrd,lgd->grcl", grad_heads, value_heads, preferred_element_type=jnp.float32
    )
    row_inner = jnp.sum(prob_full * grad_prob, axis=-1, keepdims=True)
    grad_scores = (prob_full * (grad_prob - row_inner)).astype(jnp.bfloat16)
    grad_query = jnp.einsum(
        "grcl,lgd->cgrd", grad_scores, key_heads, preferred_element_type=jnp.float32
    )
    grad_key = jnp.einsum(
        "grcl,cgrd->lgd", grad_scores, grouped, preferred_element_type=jnp.float32
    )
    grad_value = jnp.einsum(
        "grcl,cgrd->lgd", prob_low, grad_heads, preferred_element_type=jnp.float32
    )
    return (
        grad_query.reshape(width_ct, HQ * HD),
        grad_key.reshape(-1, HK * HD),
        grad_value.reshape(-1, HK * HD),
        row_inner,
    )


def reduce_grad(full_grad):
    partial_grad = lax.psum_scatter(
        full_grad.astype(jnp.bfloat16), "fsdp", scatter_dimension=0, tiled=True
    )
    return lax.psum_scatter(partial_grad, "ctx", scatter_dimension=1, tiled=True).astype(
        jnp.float32
    )


def shards(
    tokens, attn_gain, w_query, w_key, w_value, w_out, mlp_gain, w_gate, w_up, w_down, cotangent
):
    seq_local, width_ct, model_width = tokens.shape
    seq_block = seq_local // MICRO
    row_count = seq_block * width_ct
    length = width_ct * lax.axis_size("ctx")
    half_dim = HD // 2
    offset = lax.axis_index("ctx") * width_ct
    query_pos = offset + jnp.arange(width_ct, dtype=jnp.int32)
    key_pos = jnp.arange(length, dtype=jnp.int32)
    allowed = key_pos[None, :] <= query_pos[:, None]
    inv_freq = 1.0 / ROPE_BASE ** (jnp.arange(half_dim, dtype=jnp.float32) * 2.0 / HD)
    angles = query_pos.astype(jnp.float32)[:, None] * inv_freq[None, :]
    cos_one = jnp.cos(angles)[:, None, :]
    sin_one = jnp.sin(angles)[:, None, :]
    cos_rows = jnp.tile(cos_one, (seq_block, 1, 1))
    sin_rows = jnp.tile(sin_one, (seq_block, 1, 1))
    head_scale = HD ** (-0.5)
    mixed_list, token_grad_list = ([], [])
    kept_normed_one, kept_grad_query, kept_grad_key, kept_grad_value = ([], [], [], [])
    kept_attended, kept_grad_branch, kept_normed_two = ([], [], [])
    kept_grad_gate, kept_grad_upper, kept_inner, kept_grad_down = ([], [], [], [])
    attn_gain_acc = jnp.zeros((model_width,), jnp.float32)
    mlp_gain_acc = jnp.zeros((model_width,), jnp.float32)
    for micro_at in range(MICRO):
        first_seq = micro_at * seq_block
        inputs = (
            tokens[first_seq : first_seq + seq_block]
            .reshape(row_count, model_width)
            .astype(jnp.float32)
        )
        outer_grad = (
            cotangent[first_seq : first_seq + seq_block]
            .reshape(row_count, model_width)
            .astype(jnp.float32)
        )
        attn_all = (
            lax.all_gather(w_query, "fsdp", axis=0, tiled=True),
            lax.all_gather(w_key, "fsdp", axis=0, tiled=True),
            lax.all_gather(w_value, "fsdp", axis=0, tiled=True),
            lax.all_gather(w_out, "fsdp", axis=0, tiled=True),
        )
        unit_one, inv_one = normalize(inputs)
        normed_one = (unit_one * attn_gain).astype(jnp.bfloat16)
        query_raw = matmul(normed_one, attn_all[0]).reshape(row_count, HQ, HD)
        key_raw = matmul(normed_one, attn_all[1]).reshape(row_count, HK, HD)
        value_raw = matmul(normed_one, attn_all[2])
        queries = (
            (rotate(query_raw, cos_rows, sin_rows) * head_scale)
            .astype(jnp.bfloat16)
            .reshape(seq_block, width_ct, HQ * HD)
        )
        keys = (
            rotate(key_raw, cos_rows, sin_rows)
            .astype(jnp.bfloat16)
            .reshape(seq_block, width_ct, HK * HD)
        )
        values = value_raw.astype(jnp.bfloat16).reshape(seq_block, width_ct, HK * HD)
        key_all, value_all = (
            lax.all_gather(keys, "ctx", axis=1, tiled=True),
            lax.all_gather(values, "ctx", axis=1, tiled=True),
        )
        attended_parts, lse_parts = ([], [])
        seq_at = 0
        attended_one, lse_one = attend_forward(
            queries[seq_at], key_all[seq_at], value_all[seq_at], allowed
        )
        attended_parts.append(attended_one)
        lse_parts.append(lse_one)
        attended = attended_parts[0].astype(jnp.bfloat16)
        resid = inputs + matmul(attended, attn_all[3])
        unit_two, inv_two = normalize(resid)
        normed_two = (unit_two * mlp_gain).astype(jnp.bfloat16)
        gate_proj = matmul(normed_two, lax.all_gather(w_gate, "fsdp", axis=0, tiled=True))
        up_proj = matmul(normed_two, lax.all_gather(w_up, "fsdp", axis=0, tiled=True))
        sigma = jax.nn.sigmoid(gate_proj)
        active = gate_proj * sigma
        hidden_act = (active * up_proj).astype(jnp.bfloat16)
        down_out = matmul(hidden_act, lax.all_gather(w_down, "fsdp", axis=0, tiled=True))
        mixed_list.append((resid + down_out).astype(jnp.bfloat16))
        grad_down = outer_grad.astype(jnp.bfloat16)
        grad_hidden = times_transposed(
            grad_down, lax.all_gather(w_down, "fsdp", axis=0, tiled=True)
        )
        grad_gate = (grad_hidden * up_proj * sigma * (1.0 + gate_proj * (1.0 - sigma))).astype(
            jnp.bfloat16
        )
        grad_upper = (grad_hidden * active).astype(jnp.bfloat16)
        pair_pieces = lax.all_gather((w_gate, w_up), "fsdp", axis=0, tiled=True)
        grad_normed_two = times_transposed(grad_gate, pair_pieces[0]) + times_transposed(
            grad_upper, pair_pieces[1]
        )
        mlp_gain_acc = mlp_gain_acc + jnp.sum(grad_normed_two * unit_two, axis=0)
        grad_resid = outer_grad + norm_back(grad_normed_two, mlp_gain, unit_two, inv_two)
        grad_branch = grad_resid.astype(jnp.bfloat16)
        attn_back = (
            lax.all_gather(w_query, "fsdp", axis=0, tiled=True),
            lax.all_gather(w_key, "fsdp", axis=0, tiled=True),
            lax.all_gather(w_value, "fsdp", axis=0, tiled=True),
            lax.all_gather(w_out, "fsdp", axis=0, tiled=True),
        )
        grad_attended = times_transposed(grad_branch, attn_back[3]).astype(jnp.bfloat16)
        key_back, value_back = (
            lax.all_gather(keys, "ctx", axis=1, tiled=True),
            lax.all_gather(values, "ctx", axis=1, tiled=True),
        )
        query_parts, key_parts, value_parts = ([], [], [])
        seq_at = 0
        query_one = queries[seq_at]
        key_one = key_back[seq_at]
        value_one = value_back[seq_at]
        lse_one = lse_parts[seq_at]
        grad_query, grad_key, grad_value, row_inner = attend_backward(
            query_one, key_one, value_one, allowed, lse_one, grad_attended
        )
        own_key = lax.psum_scatter(
            grad_key.astype(jnp.bfloat16), "ctx", scatter_dimension=0, tiled=True
        ).astype(jnp.float32)
        own_value = lax.psum_scatter(
            grad_value.astype(jnp.bfloat16), "ctx", scatter_dimension=0, tiled=True
        ).astype(jnp.float32)
        query_parts.append(
            rotate((grad_query * head_scale).reshape(width_ct, HQ, HD), cos_one, -sin_one).reshape(
                width_ct, HQ * HD
            )
        )
        key_parts.append(
            rotate(own_key.reshape(width_ct, HK, HD), cos_one, -sin_one).reshape(width_ct, HK * HD)
        )
        value_parts.append(own_value)
        grad_query_raw = query_parts[0].astype(jnp.bfloat16)
        grad_key_raw = key_parts[0].astype(jnp.bfloat16)
        grad_value_raw = value_parts[0].astype(jnp.bfloat16)
        grad_normed_one = (
            times_transposed(grad_query_raw, attn_back[0])
            + times_transposed(grad_key_raw, attn_back[1])
            + times_transposed(grad_value_raw, attn_back[2])
        )
        attn_gain_acc = attn_gain_acc + jnp.sum(grad_normed_one * unit_one, axis=0)
        token_grad_list.append(
            (grad_resid + norm_back(grad_normed_one, attn_gain, unit_one, inv_one)).astype(
                jnp.bfloat16
            )
        )
        kept_normed_one.append(normed_one)
        kept_grad_query.append(grad_query_raw)
        kept_grad_key.append(grad_key_raw)
        kept_grad_value.append(grad_value_raw)
        kept_attended.append(attended)
        kept_grad_branch.append(grad_branch)
        kept_normed_two.append(normed_two)
        kept_grad_gate.append(grad_gate)
        kept_grad_upper.append(grad_upper)
        kept_inner.append(hidden_act)
        kept_grad_down.append(grad_down)
    normed_one_all = jnp.concatenate(kept_normed_one, axis=0)
    normed_two_all = jnp.concatenate(kept_normed_two, axis=0)
    w_query_grad = reduce_grad(
        transposed_times(normed_one_all, jnp.concatenate(kept_grad_query, axis=0))
    )
    w_key_grad = reduce_grad(
        transposed_times(normed_one_all, jnp.concatenate(kept_grad_key, axis=0))
    )
    w_value_grad = reduce_grad(
        transposed_times(normed_one_all, jnp.concatenate(kept_grad_value, axis=0))
    )
    w_out_grad = reduce_grad(
        transposed_times(
            jnp.concatenate(kept_attended, axis=0), jnp.concatenate(kept_grad_branch, axis=0)
        )
    )
    w_gate_grad = reduce_grad(
        transposed_times(normed_two_all, jnp.concatenate(kept_grad_gate, axis=0))
    )
    w_up_grad = reduce_grad(
        transposed_times(normed_two_all, jnp.concatenate(kept_grad_upper, axis=0))
    )
    w_down_grad = reduce_grad(
        transposed_times(
            jnp.concatenate(kept_inner, axis=0), jnp.concatenate(kept_grad_down, axis=0)
        )
    )
    attn_gain_grad, mlp_gain_grad = lax.psum((attn_gain_acc, mlp_gain_acc), ("ctx", "fsdp"))
    mixed = jnp.concatenate(mixed_list, axis=0).reshape(seq_local, width_ct, model_width)
    tokens_grad = jnp.concatenate(token_grad_list, axis=0).reshape(seq_local, width_ct, model_width)
    return (
        mixed,
        tokens_grad,
        attn_gain_grad,
        w_query_grad,
        w_key_grad,
        w_value_grad,
        w_out_grad,
        mlp_gain_grad,
        w_gate_grad,
        w_up_grad,
        w_down_grad,
    )


def nt(a,b):
    return lax.dot_general(a,b,(((1,),(1,)),((),())),preferred_element_type=jnp.float32)
def nn(a,b):
    return jnp.dot(a,b,preferred_element_type=jnp.float32)

def turn(v,cosine,sine):
    return v*cosine+pltpu.roll(v,LANES//2,1)*sine

def forward_kernel(tokens_ref,gain_ref,weight_ref,cos_ref,sin_ref,normed_ref,qkv_ref,out_ref,lse_ref,key_ref,val_t_ref):
    at=pl.program_id(0)
    rows=tokens_ref.shape[0]
    here=pl.ds(pl.multiple_of(at*rows,rows),rows)
    cosine,sine=cos_ref[...],sin_ref[...]
    @pl.when(at==0)
    def _():
        val_t_ref[...]=jnp.zeros_like(val_t_ref)
    unit,_=normalize(tokens_ref[...].astype(jnp.float32))
    normed=(unit*gain_ref[...]).astype(BF)
    normed_ref[...]=normed
    raw=nn(normed,weight_ref[...])
    scale=HD**-0.5
    parts=[(turn(raw[:,j*LANES:(j+1)*LANES],cosine,sine)*(scale if j<2 else 1.0)).astype(BF) for j in range(3)]
    value=raw[:,3*LANES:].astype(BF)
    for j in range(3):
        qkv_ref[:,j*LANES:(j+1)*LANES]=parts[j]
    qkv_ref[:,3*LANES:]=value
    key_ref[here,:]=parts[2]
    val_t_ref[:,here]=value.T
    query=jnp.concatenate(parts[:2],axis=0)
    length=key_ref.shape[0]
    for band in range(length//rows):
        @pl.when(at==band)
        def _():
            scores=nt(key_ref[0:(band+1)*rows,:],query)
            tail=scores[band*rows:,:]
            key_pos=lax.broadcasted_iota(jnp.int32,tail.shape,0)
            query_pos=lax.broadcasted_iota(jnp.int32,tail.shape,1)%rows
            tail=jnp.where(key_pos<=query_pos,tail,MASK_FILL)
            pieces=[scores[b*rows:(b+1)*rows,:] for b in range(band)]+[tail]
            top=functools.reduce(jnp.maximum,[jnp.max(p,axis=0,keepdims=True) for p in pieces])
            total=0.0; acc=0.0
            for b,p in enumerate(pieces):
                e=jnp.exp(p-top)
                total=total+jnp.sum(e,axis=0,keepdims=True)
                acc=acc+nn(val_t_ref[:,b*rows:(b+1)*rows],e.astype(BF))
            acc=acc/total
            out_ref[:,0:LANES]=acc[:,0:rows].T.astype(BF)
            out_ref[:,LANES:]=acc[:,rows:].T.astype(BF)
            lse_ref[0]=top+jnp.log(total)

def head_forward(tokens,gain,weight,cosine,sine,rows=512):
    length,model=tokens.shape
    steps=length//rows
    block=lambda cols:pl.BlockSpec((rows,cols),lambda i:(i,0))
    return pl.pallas_call(
        forward_kernel,
        grid=(steps,),
        in_specs=[block(model),pl.BlockSpec((1,model),lambda i:(0,0)),pl.BlockSpec(weight.shape,lambda i:(0,0)),
                  block(LANES),block(LANES)],
        out_specs=[block(model),block(4*LANES),block(2*LANES),pl.BlockSpec((1,1,2*rows),lambda i:(i,0,0))],
        out_shape=[jax.ShapeDtypeStruct((length,model),BF),
                   jax.ShapeDtypeStruct((length,4*LANES),BF),
                   jax.ShapeDtypeStruct((length,2*LANES),BF),
                   jax.ShapeDtypeStruct((steps,1,2*rows),jnp.float32)],
        scratch_shapes=[pltpu.VMEM((length,LANES),BF),pltpu.VMEM((LANES,length),BF)],
        compiler_params=pltpu.CompilerParams(vmem_limit_bytes=VMEM_LIMIT),
    )(tokens,gain,weight,cosine,sine)

def backward_kernel(rows,step_rows,qkv_ref,out_ref,grad_ref,lse_ref,cos_ref,sin_ref,pick_ref,sent_ref,res_ref,got_ref,
                    key_t_ref,grad_key_ref,grad_val_ref,rows_ref,line_sems):
    at=pl.program_id(0)
    rank=lax.axis_index("ctx")
    other_line=rank+CORES*(1-2*lax.rem(lax.div(rank,CORES),LINES))
    copies=[ctx_copy(sent_ref.at[number],got_ref.at[slot],line_sems,slot,other_line)
            for slot,number in enumerate((PLANES-1,0))]
    @pl.when(at==0)
    def _():
        barrier=pltpu.get_barrier_semaphore()
        pl.semaphore_signal(barrier,inc=1,device_id={"ctx":other_line},device_id_type=pl.DeviceIdType.MESH)
        pl.semaphore_wait(barrier,1)
        for copy in copies:
            copy.start()
    here=pl.ds(pl.multiple_of(at*rows,rows),rows)
    length=qkv_ref.shape[0]
    scale=HD**-0.5
    @pl.when(at==0)
    def _():
        grad_key_ref[...]=jnp.zeros_like(grad_key_ref)
        grad_val_ref[...]=jnp.zeros_like(grad_val_ref)
        for b in range(length//rows):
            key_t_ref[:,b*rows:(b+1)*rows]=qkv_ref[b*rows:(b+1)*rows,2*LANES:3*LANES].T
    query=jnp.concatenate([qkv_ref[here,0:LANES],qkv_ref[here,LANES:2*LANES]],axis=0)
    grad=jnp.concatenate([grad_ref[:,0:LANES],grad_ref[:,LANES:]],axis=0)
    out=jnp.concatenate([out_ref[:,0:LANES],out_ref[:,LANES:]],axis=0)
    inner=jnp.sum((grad.astype(jnp.float32)*out.astype(jnp.float32)).T,axis=0,keepdims=True)
    lse=lse_ref[0]
    per=step_rows//rows
    for band in range(length//step_rows):
        @pl.when(at//per==band)
        def _():
            grad_query=0.0
            for b in range(band+1):
                span=slice(b*step_rows,(b+1)*step_rows)
                scores=nt(qkv_ref[span,2*LANES:3*LANES],query)
                prob=jnp.exp(scores-lse)
                if b==band:
                    key_pos=lax.broadcasted_iota(jnp.int32,scores.shape,0)
                    query_pos=(at%per)*rows+lax.broadcasted_iota(jnp.int32,scores.shape,1)%rows
                    prob=jnp.where(key_pos<=query_pos,prob,0.0)
                grad_prob=nt(qkv_ref[span,3*LANES:],grad)
                grad_scores=(prob*(grad_prob-inner)).astype(BF)
                grad_val_ref[span,:]+=nn(prob.astype(BF),grad)
                grad_key_ref[span,:]+=nn(grad_scores,query)
                grad_query=grad_query+nn(key_t_ref[:,span],grad_scores)
            for j in range(2):
                back=grad_query[:,j*rows:(j+1)*rows].T*scale
                rows_ref[here,j*LANES:(j+1)*LANES]=turn(back,cos_ref[here,:],-sin_ref[here,:]).astype(BF)
    @pl.when(at==length//rows-1)
    def _():
        for b in range(length//step_rows):
            span=slice(b*step_rows,(b+1)*step_rows)
            rows_ref[span,2*LANES:3*LANES]=turn(grad_key_ref[span,:],cos_ref[span,:],-sin_ref[span,:]).astype(BF)
            rows_ref[span,3*LANES:]=grad_val_ref[span,:].astype(BF)
            res_ref[span,:]=nn(rows_ref[span,:],pick_ref[...]).astype(BF)
        for copy in copies:
            copy.wait()

def head_backward(qkv,out,grad,lse,cosine,sine,pick,sent,rows=256,step_rows=256):
    length=qkv.shape[0]
    steps=length//rows
    lse=lse.reshape(-1,2,lse.shape[2]//2).transpose(1,0,2).reshape(2,steps,rows).transpose(1,0,2).reshape(steps,1,2*rows)
    whole=lambda a:pl.BlockSpec(a.shape,lambda i:(0,)*a.ndim)
    return pl.pallas_call(
        functools.partial(backward_kernel,rows,step_rows),
        grid=(steps,),
        in_specs=[whole(qkv),
                  pl.BlockSpec((rows,2*LANES),lambda i:(i,0)),
                  pl.BlockSpec((rows,2*LANES),lambda i:(i,0)),
                  pl.BlockSpec((1,1,2*rows),lambda i:(i,0,0)),
                  whole(cosine),whole(sine),whole(pick),pl.BlockSpec(memory_space=pl.ANY)],
        out_specs=[pl.BlockSpec((length,4*HD),lambda i:(0,0)),pl.BlockSpec(memory_space=pl.ANY)],
        out_shape=[jax.ShapeDtypeStruct((length,4*HD),BF),jax.ShapeDtypeStruct((2,)+sent.shape[1:],BF)],
        scratch_shapes=[pltpu.VMEM((LANES,length),BF),pltpu.VMEM((length,LANES),jnp.float32),
                        pltpu.VMEM((length,LANES),jnp.float32),pltpu.VMEM((length,4*LANES),BF),
                        pltpu.SemaphoreType.DMA((2,2))],
        compiler_params=pltpu.CompilerParams(collective_id=3,has_side_effects=True,vmem_limit_bytes=VMEM_LIMIT),
    )(qkv,out,grad,lse,cosine,sine,pick,sent)

def pad_columns():
    half=HD//2
    lanes=np.arange(4*LANES); block=lanes//LANES; lane=lanes%LANES
    split=np.where(lane<half,lane,np.where((lane>=LANES//2)&(lane<LANES//2+half),lane-LANES//2+half,-1))
    plain=np.where(lane<HD,lane,-1)
    column=np.where(block<3,split,plain)
    return np.where(column>=0,column+block*HD,-1)

CORES, LINES, PLANES = 2, 2, 4
CHIPS = LINES * PLANES
RANKS = CORES * CHIPS


def swap_fsdp(value):
    return lax.ppermute(value, "fsdp", [(0, 1), (1, 0)])


def swap_ctx(value, bit):
    return lax.ppermute(value, "ctx", [(i, i ^ bit) for i in range(RANKS)])


def swap_core(value):
    return swap_ctx(value, 1)


def swap_line(value):
    return swap_ctx(value, CORES)


def plane_up(value, sources):
    step = CORES * LINES
    return lax.ppermute(value, "ctx", [(z * step + i, z * step + step + i) for z in sources for i in range(step)])


def plane_down(value, sources):
    step = CORES * LINES
    return lax.ppermute(value, "ctx", [(z * step + i, z * step - step + i) for z in sources for i in range(step)])


def at(value, index, axis=0):
    return lax.dynamic_index_in_dim(value, index, axis, keepdims=False)


def in_order(which, mine, other):
    first = which == 0
    return jnp.concatenate([jnp.where(first, mine, other), jnp.where(first, other, mine)], axis=0)


def after(value, earlier):
    return lax.optimization_barrier((value, earlier))[0]


def rope_rows(length):
    lane = jnp.arange(LANES)
    half = LANES // 2
    entry = jnp.where(lane < half, lane, lane - half)
    used = entry < HD // 2
    inv_freq = 1.0 / ROPE_BASE ** (entry.astype(jnp.float32) * 2.0 / HD)
    angles = jnp.arange(length, dtype=jnp.int32).astype(jnp.float32)[:, None] * inv_freq[None, :]
    sign = jnp.where(lane < half, -1.0, 1.0)
    return jnp.where(used, jnp.cos(angles), 0.0), jnp.where(used, jnp.sin(angles) * sign, 0.0)


def mlp_kernel(
    info, normed, grad_rows, gate_a, gate_b, up_a, up_b, gate_far, up_far, down_a, down_b, down_far,
    inner_ref, grad_gate_ref, grad_up_ref, mixed_ref, back_ref,
    down, mixed_acc, back_acc,
):
    step = pl.program_id(0)
    half_steps = pl.num_programs(0) // 2
    side = info[0]
    depth = gate_a.shape[0]
    near = pl.ds(pl.multiple_of(side * depth, LANES), depth)
    far = pl.ds(pl.multiple_of((1 - side) * depth, LANES), depth)

    @pl.when(step == 0)
    def _():
        mixed_acc[...] = jnp.zeros_like(mixed_acc)
        back_acc[...] = jnp.zeros_like(back_acc)

    @pl.when(step < half_steps)
    def _():
        down[:LANES, :] = down_a[...]
        down[LANES:, :] = down_b[...]

    @pl.when(step >= half_steps)
    def _():
        down[...] = down_far[...]

    gate_near = jnp.concatenate([gate_a[...], gate_b[...]], axis=1)
    up_near = jnp.concatenate([up_a[...], up_b[...]], axis=1)
    gate = nn(normed[:, near], gate_near) + nn(normed[:, far], gate_far[...])
    upper = nn(normed[:, near], up_near) + nn(normed[:, far], up_far[...])
    sigma = jax.nn.sigmoid(gate)
    active = gate * sigma
    inner = (active * upper).astype(BF)
    grad_inner = nt(grad_rows[...], down[...])
    grad_gate = (grad_inner * upper * sigma * (1.0 + gate * (1.0 - sigma))).astype(BF)
    grad_up = (grad_inner * active).astype(BF)
    for which in range(CORES):
        span = slice(which * LANES, (which + 1) * LANES)
        inner_ref[which] = inner[:, span]
        grad_gate_ref[which] = grad_gate[:, span]
        grad_up_ref[which] = grad_up[:, span]
    mixed_acc[...] += nn(inner, down[...])
    back_acc[:, near] += nt(grad_gate, gate_near) + nt(grad_up, up_near)
    back_acc[:, far] += nt(grad_gate, gate_far[...]) + nt(grad_up, up_far[...])

    @pl.when(step == 2 * half_steps - 1)
    def _():
        mixed_ref[...] = mixed_acc[...].astype(mixed_ref.dtype)
        back_ref[...] = back_acc[...].astype(back_ref.dtype)


def mlp_part(info, normed, grad_rows, weights, kind):
    w_gate, w_up, far, w_down, down_far = weights
    rows, model = normed.shape
    depth, hidden = w_gate.shape
    half = hidden // 2
    steps = half // (2 * LANES)
    part = steps // 2

    def pair_of(j, info):
        return jnp.where(j < part, info[0] * part + j, (1 - info[0]) * part + j - part)

    def whole(shape):
        return pl.BlockSpec(shape, lambda j, info: (0, 0))

    def column(odd):
        return pl.BlockSpec((depth, LANES), lambda j, info: (0, 4 * pair_of(j, info) + 2 * odd + info[0]))

    def row(odd):
        return pl.BlockSpec((LANES, model), lambda j, info: (4 * jnp.minimum(j, part - 1) + 2 * odd + info[0], 0))

    def far_column(which):
        return pl.BlockSpec((None, depth, 2 * LANES), lambda j, info: (which, 0, pair_of(j, info)))

    far_row = pl.BlockSpec((2 * LANES, model), lambda j, info: (jnp.maximum(j - part, 0), 0))

    def place(j, info):
        pair = pair_of(j, info)
        return (0, 0, (pair % LINES) * PLANES + pair // LINES)

    act = pl.BlockSpec((CORES, rows, LANES), place)
    act_shape = jax.ShapeDtypeStruct((CORES, rows, half // CORES), BF)
    return pl.pallas_call(
        mlp_kernel,
        grid_spec=pltpu.PrefetchScalarGridSpec(
            num_scalar_prefetch=1,
            grid=(steps,),
            in_specs=[
                whole((rows, model)), whole((rows, model)),
                column(0), column(1), column(0), column(1), far_column(0), far_column(1),
                row(0), row(1), far_row,
            ],
            out_specs=[act, act, act, whole((rows, model)), whole((rows, model))],
            scratch_shapes=[
                pltpu.VMEM((2 * LANES, model), BF),
                pltpu.VMEM((rows, model), jnp.float32),
                pltpu.VMEM((rows, model), jnp.float32),
            ],
        ),
        out_shape=[act_shape, act_shape, act_shape] + [jax.ShapeDtypeStruct((rows, model), kind)] * 2,
        compiler_params=pltpu.CompilerParams(vmem_limit_bytes=VMEM_LIMIT),
        cost_estimate=pl.CostEstimate(
            flops=12 * rows * model * half, bytes_accessed=6 * model * half, transcendentals=rows * half
        ),
    )(info, normed, grad_rows, w_gate, w_gate, w_up, w_up, far, far, w_down, w_down, down_far)


def head_rows_of(info, number, out_near, out_far):
    heads = []
    for is_far in range(2):
        for at_plane in range(PLANES // 2):
            for at_core in range(CORES):
                plane = 2 * (info[0] if is_far == 0 else 1 - info[0]) + at_plane
                heads.append((plane, at_core, out_far if is_far else out_near, (2 * at_plane + at_core) * 2 * HD))
    return heads


def post_kernel(info, att, tokens, out_near, out_far, gain, resid_ref, normed_ref):
    width = att.shape[1]
    total = tokens[...].astype(jnp.float32)
    for plane, core, weight, first in head_rows_of(info, 0, out_near, out_far):
        both = [att[plane * CORES * LINES + seq * CORES + core] for seq in range(LINES)]
        for head in range(2):
            rows = jnp.concatenate([block[:, head * LANES : head * LANES + HD] for block in both], axis=0)
            total = total + nn(rows, weight[first + head * HD : first + (head + 1) * HD, :])
    resid_ref[...] = total
    normed_ref[...] = (normalize(total)[0] * gain[...]).astype(BF)


def local_call(kernel, info, operands, outs):
    def spec(shape):
        return pl.BlockSpec(shape, lambda i, info: (0,) * len(shape))

    return pl.pallas_call(
        kernel,
        grid_spec=pltpu.PrefetchScalarGridSpec(
            num_scalar_prefetch=1,
            grid=(1,),
            in_specs=[spec(operand.shape) for operand in operands],
            out_specs=[spec(out.shape) for out in outs],
        ),
        out_shape=outs,
        compiler_params=pltpu.CompilerParams(vmem_limit_bytes=VMEM_LIMIT),
    )(info, *operands)


def pre_kernel(
    info, back_own, back_got, grad_rows, resid, gain, out_near, out_far, grad_ref, branch_ref, att_ref, gain_ref
):
    width = att_ref.shape[1]
    grad_normed = back_own[...] + back_got[...].astype(jnp.float32)
    unit, inv = normalize(resid[...])
    gain_ref[...] = jnp.sum(grad_normed * unit, axis=0, keepdims=True)
    grad = grad_rows[...].astype(jnp.float32) + norm_back(grad_normed, gain[...], unit, inv)
    grad_ref[...] = grad
    branch = grad.astype(BF)
    branch_ref[...] = branch
    blank = jnp.zeros((width, LANES - HD), BF)
    for plane, core, weight, first in head_rows_of(info, 0, out_near, out_far):
        for head in range(2):
            back = nt(branch, weight[first + head * HD : first + (head + 1) * HD, :]).astype(BF)
            for seq in range(LINES):
                number = plane * CORES * LINES + seq * CORES + core
                att_ref[number, :, head * LANES : head * LANES + HD] = back[seq * width : (seq + 1) * width]
                att_ref[number, :, head * LANES + HD : (head + 1) * LANES] = blank


def last_kernel(info, rows_in, tokens, gain, grad, query, key, value, query_far, key_far, value_far, out_ref, total):
    width = rows_in.shape[1]
    half = query.shape[0]
    for is_far, weights in enumerate(((query, key, value), (query_far, key_far, value_far))):
        here = pl.ds(pl.multiple_of((info[0] if is_far == 0 else 1 - info[0]) * half, LANES), half)
        acc = 0.0
        for head in range(HK):
            first = head // CORES * CORES * LINES + head % CORES
            rows = jnp.concatenate([rows_in[first + seq * CORES] for seq in range(LINES)], axis=0)
            for weight, start, size in zip(weights, (0, 2 * HD, 3 * HD), (2 * HD, HD, HD)):
                acc = acc + nt(rows[:, start : start + size], weight[:, head * size : (head + 1) * size])
        total[:, here] = acc
    unit, inv = normalize(tokens[...].astype(jnp.float32))
    out_ref[...] = (grad[...] + norm_back(total[...], gain[...], unit, inv)).astype(BF)


def gather_kernel(
    tokens, head_in, w_gate, w_up, w_out, seq_out, head_out, far, out_far, sems_in, sems_up, sems_down, sems_core, weight_sems, column_sems, group_sems, local_sem
):
    rank = lax.axis_index("ctx")
    side = lax.axis_index("fsdp")
    core = lax.rem(rank, CORES)
    line = lax.rem(lax.div(rank, CORES), LINES)
    plane = lax.div(rank, CORES * LINES)
    step_rank = CORES * LINES
    last = PLANES - 1
    other_line = rank + CORES * (1 - 2 * line)
    other_core = rank + 1 - 2 * core
    greet(rank, side)

    def spot(at_plane, at_line):
        return at_plane * step_rank + at_line * CORES + core

    def move(index, send_sems, to, source=None):
        return pltpu.make_async_remote_copy(
            src_ref=seq_out.at[index] if source is None else source,
            dst_ref=seq_out.at[index],
            send_sem=send_sems.at[index],
            recv_sem=sems_in.at[index],
            device_id={"ctx": to},
            device_id_type=pl.DeviceIdType.MESH,
        )

    near, across = spot(plane, line), spot(plane, 1 - line)
    mine = tokens.at[line]
    to_line = pltpu.make_async_remote_copy(
        src_ref=tokens.at[1 - line],
        dst_ref=seq_out.at[near],
        send_sem=local_sem.at[1],
        recv_sem=sems_in.at[near],
        device_id={"ctx": other_line},
        device_id_type=pl.DeviceIdType.MESH,
    )
    landed_line = pltpu.make_async_remote_copy(
        src_ref=tokens.at[1 - line],
        dst_ref=seq_out.at[across],
        send_sem=local_sem.at[1],
        recv_sem=sems_in.at[across],
        device_id={"ctx": other_line},
        device_id_type=pl.DeviceIdType.MESH,
    )
    own = pltpu.make_async_copy(mine, seq_out.at[near], local_sem.at[0])

    def spread(index, up, down, source=None):
        if up:
            @pl.when(plane < last)
            def _():
                move(index, sems_up, rank + step_rank, source).start()

        if down:
            @pl.when(plane > 0)
            def _():
                move(index, sems_down, rank - step_rank, source).start()

        move(index, sems_core, other_core, source).start()

    to_line.start()
    spread(near, True, True, mine)
    own.start()

    head_cross = side_copy(head_in, head_out, weight_sems, 0, 1 - side)
    depth = w_gate.shape[0] // LINES
    rows = pl.ds(pl.multiple_of(line * depth, 16), depth)
    other_rows = pl.ds(pl.multiple_of((1 - line) * depth, 16), depth)
    groups = 4
    group_columns = far.shape[2] // groups
    per_group = group_columns // LANES

    def column(weight, number):
        there = pl.ds(number * LANES, LANES)
        here = pl.ds(pl.multiple_of((2 * number + 1 - side) * LANES, LANES), LANES)
        return side_copy(weight.at[rows, here], far.at[core, rows, there], column_sems, number, 1 - side)

    def send_group(group):
        for number in range(group * per_group, (group + 1) * per_group):
            @pl.when(core == 0)
            def _():
                column(w_gate, number).start()

            @pl.when(core != 0)
            def _():
                column(w_up, number).start()

    def group_copy(group, which_rows, kind, to):
        block = far.at[core, which_rows, pl.ds(group * group_columns, group_columns)]
        return ctx_copy(block, block, group_sems, kind * groups + group, to)

    def pass_group(group):
        for number in range(group * per_group, (group + 1) * per_group):
            column(w_gate, number).wait_recv()
        group_copy(group, rows, 0, other_line).start()
        group_copy(group, rows, 1, other_core).start()

    def pass_line(group):
        group_copy(group, rows, 0, other_line).wait_recv()
        group_copy(group, other_rows, 2, other_core).start()

    quarter = 2 * core + line
    out_rows = w_out.shape[0] // 4

    def out_slice(ref, which):
        return ref.at[pl.ds(pl.multiple_of(which * out_rows, 16), out_rows)]

    out_mine, out_got = out_slice(out_far, quarter), out_slice(out_far, 2 * core + 1 - line)
    out_cross = side_copy(out_slice(w_out, quarter), out_mine, weight_sems, 1, 1 - side)
    out_line = ctx_copy(out_mine, out_mine, weight_sems, 2, other_line)
    out_core = ctx_copy(out_mine, out_mine, weight_sems, 3, other_core)
    out_more = ctx_copy(out_got, out_got, weight_sems, 4, other_core)
    send_group(0)
    send_group(1)

    def forward(index, up, down):
        move(index, sems_core, other_core).wait_recv()
        spread(index, up, down)

    landed_line.wait_recv()
    spread(across, True, True)

    def pass_on(away, at_line):
        @pl.when(plane >= away)
        def _():
            forward(spot(plane - away, at_line), True, False)

        @pl.when(plane + away <= last)
        def _():
            forward(spot(plane + away, at_line), False, True)

    pass_on(1, line)
    pass_group(0)
    send_group(2)
    pass_group(1)
    send_group(3)
    pass_on(1, 1 - line)
    pass_line(0)
    pass_on(2, line)
    pass_group(2)
    out_cross.start()
    pass_group(3)
    head_cross.start()
    pass_line(1)
    pass_on(2, 1 - line)
    pass_line(2)
    pass_on(3, line)
    out_cross.wait_recv()
    out_line.start()
    out_core.start()
    pass_line(3)
    pass_on(3, 1 - line)
    out_line.wait_recv()
    out_more.start()

    for at_plane in range(PLANES):
        for at_line in range(LINES):
            index = at_plane * step_rank + at_line * CORES + 1 - core
            move(index, sems_core, other_core).wait_recv()
    head_cross.wait_recv()
    out_core.wait_recv()
    out_more.wait_recv()
    for group in range(groups):
        group_copy(group, rows, 1, other_core).wait_recv()
        group_copy(group, other_rows, 2, other_core).wait_recv()

    own.wait()
    to_line.wait_send()
    for at_plane in range(PLANES):
        for at_line in range(LINES):
            index = at_plane * step_rank + at_line * CORES + core
            move(index, sems_core, other_core).wait_send()

            @pl.when((plane < last) & (at_plane <= plane))
            def _():
                move(index, sems_up, rank + step_rank).wait_send()

            @pl.when((plane > 0) & (at_plane >= plane))
            def _():
                move(index, sems_down, rank - step_rank).wait_send()

    for copy in (head_cross, out_cross, out_line, out_core, out_more):
        copy.wait_send()
    for number in range(groups * per_group):
        column(w_gate, number).wait_send()
    for group in range(groups):
        group_copy(group, rows, 0, other_line).wait_send()
        group_copy(group, rows, 1, other_core).wait_send()
        group_copy(group, other_rows, 2, other_core).wait_send()


def gather_all(tokens, head_rows, w_gate, w_up, w_out):
    width, model = tokens.shape[1:]
    depth, hidden = w_gate.shape
    hbm = pl.BlockSpec(memory_space=pl.ANY)
    dma = pltpu.SemaphoreType.DMA
    return pl.pallas_call(
        gather_kernel,
        in_specs=[hbm] * 5,
        out_specs=[hbm] * 4,
        out_shape=[
            jax.ShapeDtypeStruct((RANKS, width, model), BF),
            jax.ShapeDtypeStruct(head_rows.shape, BF),
            jax.ShapeDtypeStruct((2, depth, hidden // 2), BF),
            jax.ShapeDtypeStruct(w_out.shape, BF),
        ],
        scratch_shapes=[dma((RANKS,)), dma((RANKS,)), dma((RANKS,)), dma((RANKS,)), dma((2, 5)), dma((2, RANKS)), dma((2, 12)), dma((2,))],
        compiler_params=pltpu.CompilerParams(collective_id=1, has_side_effects=True, vmem_limit_bytes=VMEM_LIMIT),
    )(tokens, head_rows, w_gate, w_up, w_out)


def scatter_kernel(rows_in, w_down, rows_out, down_far, exchange_sems, weight_sems, local_sem):
    rank = lax.axis_index("ctx")
    side = lax.axis_index("fsdp")
    core = lax.rem(rank, CORES)
    line = lax.rem(lax.div(rank, CORES), LINES)
    other_line = rank + CORES * (1 - 2 * line)
    other_core = rank + 1 - 2 * core
    greet(rank, side)
    chunk = w_down.shape[0] // RANKS
    quarter = 2 * core + line
    crosses = []
    for part in range(2):
        number = 2 * quarter + part
        source = w_down.at[pl.ds(pl.multiple_of((2 * number + 1 - side) * chunk, chunk), chunk)]
        target = down_far.at[pl.ds(pl.multiple_of(number * chunk, chunk), chunk)]
        crosses.append(side_copy(source, target, weight_sems, part, 1 - side))
    copies = []
    for away in range(1, RANKS):
        to = lax.rem(rank + away, RANKS)
        copy = ctx_copy(rows_in.at[to], rows_out.at[rank], exchange_sems, away, to)
        copy.start()
        copies.append(copy)
    crosses[0].start()
    own = pltpu.make_async_copy(rows_in.at[rank], rows_out.at[rank], local_sem)
    own.start()

    def down_slice(which, part):
        return down_far.at[pl.ds(pl.multiple_of((2 * which + part) * chunk, chunk), chunk)]

    here = [down_slice(quarter, part) for part in range(2)]
    there = [down_slice(2 * core + 1 - line, part) for part in range(2)]
    lines = [ctx_copy(here[i], here[i], weight_sems, 2 + i, other_line) for i in range(2)]
    cores = [ctx_copy(here[i], here[i], weight_sems, 4 + i, other_core) for i in range(2)]
    mores = [ctx_copy(there[i], there[i], weight_sems, 6 + i, other_core) for i in range(2)]
    for number in range(2):
        crosses[number].wait_recv()
        if number == 0:
            crosses[1].start()
        lines[number].start()
        cores[number].start()
    for number in range(2):
        lines[number].wait_recv()
        mores[number].start()
    for copy in cores + mores:
        copy.wait_recv()
    for copy in copies:
        copy.wait()
    own.wait()
    for copy in crosses + lines + cores + mores:
        copy.wait_send()


def scatter_rows(rows_in, w_down):
    hbm = pl.BlockSpec(memory_space=pl.ANY)
    dma = pltpu.SemaphoreType.DMA
    return pl.pallas_call(
        scatter_kernel,
        in_specs=[hbm] * 2,
        out_specs=[hbm] * 2,
        out_shape=[
            jax.ShapeDtypeStruct(rows_in.shape, BF),
            jax.ShapeDtypeStruct((w_down.shape[0] // 2, w_down.shape[1]), BF),
        ],
        scratch_shapes=[dma((2, RANKS)), dma((2, 8)), dma],
        compiler_params=pltpu.CompilerParams(collective_id=2, has_side_effects=True, vmem_limit_bytes=VMEM_LIMIT),
    )(rows_in, w_down)


def ctx_copy(source, target, sems, number, rank):
    return pltpu.make_async_remote_copy(
        src_ref=source,
        dst_ref=target,
        send_sem=sems.at[0, number],
        recv_sem=sems.at[1, number],
        device_id={"ctx": rank},
        device_id_type=pl.DeviceIdType.MESH,
    )


def side_copy(source, target, sems, number, side):
    return pltpu.make_async_remote_copy(
        src_ref=source,
        dst_ref=target,
        send_sem=sems.at[0, number],
        recv_sem=sems.at[1, number],
        device_id={"fsdp": side},
        device_id_type=pl.DeviceIdType.MESH,
    )


def greet(rank, side):
    barrier = pltpu.get_barrier_semaphore()
    for away in range(1, RANKS):
        pl.semaphore_signal(
            barrier,
            inc=1,
            device_id={"ctx": lax.rem(rank + away, RANKS)},
            device_id_type=pl.DeviceIdType.MESH,
        )
    pl.semaphore_signal(barrier, inc=1, device_id={"fsdp": 1 - side}, device_id_type=pl.DeviceIdType.MESH)
    pl.semaphore_wait(barrier, RANKS)


def wide(value):
    return value.astype(jnp.float32)


def reduce_kernel(
    rows_in, down_keep, down_got, gate_keep, gate_first, gate_sent, up_keep, up_sent, out_part, out_sent, head_keep, head_sent, gains_in,
    w_query, w_key, w_value, rows_out, down_mine, down_theirs, down_side, gate_mine, gate_side, up_mine, up_side, out_mine, head_out, gains_out,
    query_far, key_far, value_far, gate_got, up_got, out_core, out_side, out_sum, out_got, down_acc, gate_acc, up_acc, out_acc, down_in, gate_in, up_in, out_in,
    head_got, head_two, head_side, head_last, gain_buf, gain_in, exchange_sems, plane_sems, sems, line_sems, fetch_sems, local_sem,
):
    rank = lax.axis_index("ctx")
    side = lax.axis_index("fsdp")
    core = lax.rem(rank, CORES)
    line = lax.rem(lax.div(rank, CORES), LINES)
    plane = lax.div(rank, CORES * LINES)
    step_rank = CORES * LINES
    last = PLANES - 1
    other_line = rank + CORES * (1 - 2 * line)
    other_core = rank + 1 - 2 * core
    greet(rank, side)


    def gate_line(number):
        return ctx_copy(gate_sent.at[number], gate_got.at[number], line_sems, number, other_line)

    def up_line(number):
        return ctx_copy(up_sent.at[number], up_got.at[number], line_sems, PLANES + number, other_line)

    out_cross_core = ctx_copy(out_sent, out_core, sems, 1, other_core)
    model = head_keep.shape[1]
    half = model // 2
    near = pl.ds(pl.multiple_of(side * half, LANES), half)
    far = pl.ds(pl.multiple_of((1 - side) * half, LANES), half)
    half_out = out_sum.shape[3]
    out_near = pl.ds(pl.multiple_of(side * half_out, LANES), half_out)
    out_away = pl.ds(pl.multiple_of((1 - side) * half_out, LANES), half_out)
    out_cross = side_copy(out_core.at[:, :, :, out_away], out_side, sems, 17, 1 - side)
    out_line = ctx_copy(out_sum.at[1 - line], out_got, sems, 18, other_line)
    head_line = ctx_copy(head_sent, head_got, sems, 2, other_line)

    weights = (
        (down_keep, down_got, down_acc, down_in, 0, None),
        (gate_keep, gate_got, gate_acc, gate_in, 1, gate_line),
        (up_keep, up_got, up_acc, up_in, 2, up_line),
        (out_sum.at[line], out_got, out_acc, out_in, 3, None),
    )

    def arrives(arrival, piece):
        return (piece >= 0) if arrival is up_line else (piece > 0) & (piece < last)

    def message(weight, direction, step):
        _, _, acc, landed, number, _ = weight
        slot = direction * last + step
        target = rank + step_rank * (1 - 2 * direction)
        place = jnp.clip(step - direction * (last - plane), 0, last - 1)
        return ctx_copy(acc.at[place], landed.at[slot], plane_sems, number * 2 * last + slot, target)

    def hop(weight, step):
        keep, got, acc, landed, _, arrival = weight
        for direction in range(2):
            depth = plane if direction == 0 else last - plane
            piece = plane + (last - step) * (1 - 2 * direction)
            slot = direction * last + step
            place = step - direction * (last - plane)

            if arrival is not None:
                @pl.when((depth <= step) & (depth < last) & arrives(arrival, piece))
                def _():
                    arrival(piece).wait_recv()

            if step:
                @pl.when((depth >= 1) & (depth <= step))
                def _():
                    message(weight, direction, step - 1).wait_recv()

                @pl.when((depth >= 1) & (depth <= step) & (depth < last))
                def _():
                    acc[place] = (wide(keep[piece]) + wide(got[piece]) + wide(landed[slot - 1])).astype(BF)

            @pl.when(depth == 0)
            def _():
                acc[place] = (wide(keep[piece]) + wide(got[piece])).astype(BF)

            @pl.when((depth <= step) & (depth < last))
            def _():
                message(weight, direction, step).start()

    def finish(weight, result):
        keep, got, _, landed, _, arrival = weight
        for direction in range(2):
            depth = plane if direction == 0 else last - plane

            @pl.when(depth >= 1)
            def _():
                message(weight, direction, last - 1).wait_recv()

        if arrival is not None:
            @pl.when(arrives(arrival, plane))
            def _():
                arrival(plane).wait_recv()

        base = wide(keep[plane]) + wide(got[plane])
        above, below = landed.at[last - 1], landed.at[2 * last - 1]

        @pl.when(plane == 0)
        def _():
            result[...] = (base + wide(below[...])).astype(BF)

        @pl.when(plane == last)
        def _():
            result[...] = (base + wide(above[...])).astype(BF)

        @pl.when((plane > 0) & (plane < last))
        def _():
            result[...] = (base + wide(above[...]) + wide(below[...])).astype(BF)

    def sent(weight):
        for step in range(last):
            for direction in range(2):
                depth = plane if direction == 0 else last - plane

                @pl.when((depth <= step) & (depth < last))
                def _():
                    message(weight, direction, step).wait_send()

    down, gate, up, out = weights
    hop(down, 0)
    for number in (2, 1):
        gate_line(number).start()
    gate_got[0] = gate_first[1]
    gate_got[PLANES - 1] = gate_first[0]
    hop(gate, 0)
    head_line.start()
    copies = []
    for away in range(1, RANKS):
        to = lax.rem(rank + away, RANKS)
        copy = ctx_copy(rows_in.at[to], rows_out.at[rank], exchange_sems, away, to)
        copy.start()
        copies.append(copy)
    own = pltpu.make_async_copy(rows_in.at[rank], rows_out.at[rank], local_sem)
    own.start()
    out_cross_core.start()
    fetched = []
    for number, (source, target) in enumerate(((w_query, query_far), (w_key, key_far), (w_value, value_far))):
        per = source.shape[0] // CORES
        part = pl.ds(pl.multiple_of(core * per, 16), per)
        cross = side_copy(source.at[part], target.at[part], fetch_sems, number, 1 - side)
        fetched.append((cross, ctx_copy(target.at[part], target.at[part], fetch_sems, 3 + number, other_core)))

    gain_partners = (None, other_core, other_line, rank + step_rank * (1 - 2 * lax.rem(plane, 2)),
                     rank + 2 * step_rank * (1 - 2 * lax.div(plane, 2)))

    def gain_copy(number):
        if number == 0:
            return side_copy(gain_buf.at[0], gain_in.at[0], sems, 3, 1 - side)
        return ctx_copy(gain_buf.at[number], gain_in.at[number], sems, 3 + number, gain_partners[number])

    def gain_hop(number):
        if number:
            gain_copy(number - 1).wait_recv()
            gain_buf[number] = gain_buf[number - 1] + gain_in[number - 1]
        else:
            gain_buf[0] = gains_in[...]
        if number < 5:
            gain_copy(number).start()

    gain_hop(0)
    hop(down, 1)
    gain_hop(1)
    for number in (3, 0, 2, 1):
        up_line(number).start()

    out_cross_core.wait_recv()

    @pl.loop(0, PLANES)
    def _(index):
        for at_line in range(LINES):
            out_core[at_line, index] = (wide(out_part[at_line, index]) + wide(out_core[at_line, index])).astype(BF)

    out_cross.start()
    hop(gate, 1)
    hop(down, 2)
    head_line.wait_recv()
    head_two[...] = (head_keep[...] + wide(head_got[...])).astype(BF)
    head_cross = side_copy(head_two.at[:, far], head_side, sems, 8, 1 - side)
    head_cross.start()
    gain_hop(2)
    hop(gate, 2)
    hop(up, 0)
    out_cross.wait_recv()
    for cross, _ in fetched:
        cross.start()

    @pl.loop(0, PLANES)
    def _(index):
        for at_line in range(LINES):
            out_sum[at_line, index] = (
                wide(out_core[at_line, index, :, out_near]) + wide(out_side[at_line, index])
            ).astype(BF)

    out_line.start()
    gain_hop(3)
    head_cross.wait_recv()
    head_last[...] = (wide(head_two[:, near]) + wide(head_side[...])).astype(BF)
    turned = rank - CORES * line - core + CORES * core + line
    head_turn = ctx_copy(head_last, head_out, sems, 9, turned)

    @pl.when(line != core)
    def _():
        head_turn.start()

    @pl.when(line == core)
    def _():
        head_out[...] = head_last[...]

    hop(up, 1)
    out_line.wait_recv()
    hop(out, 0)
    gain_hop(4)
    finish(down, down_mine)
    per_core = down_mine.shape[0] // CORES
    theirs = pl.ds(pl.multiple_of((1 - core) * per_core, 16), per_core)
    mine = pl.ds(pl.multiple_of(core * per_core, 16), per_core)
    down_core = ctx_copy(down_mine.at[theirs], down_theirs, sems, 10, other_core)
    down_core.start()
    hop(out, 1)
    finish(gate, gate_mine)
    gate_cross = side_copy(gate_mine.at[:, far], gate_side, sems, 11, 1 - side)
    gate_cross.start()

    hop(up, 2)
    gain_hop(5)
    for cross, onward in fetched:
        cross.wait_recv()
        onward.start()
    gains_out[...] = gain_buf[5]

    down_core.wait_recv()
    crosses = []
    span = down_mine.shape[1] // 4
    for which in range(2):
        block = down_mine.at[mine] if which == 0 else down_theirs
        for at_line in range(LINES):
            lanes = pl.ds(pl.multiple_of(at_line * 2 * span + (1 - side) * span, LANES), span)
            cross = side_copy(block.at[:, lanes], down_side.at[which, at_line], sems, 13 + which * LINES + at_line, 1 - side)
            cross.start()
            crosses.append(cross)

    hop(out, 2)
    finish(up, up_mine)
    up_cross = side_copy(up_mine.at[:, far], up_side, sems, 12, 1 - side)
    up_cross.start()
    finish(out, out_mine)

    @pl.when(line != core)
    def _():
        head_turn.wait()

    for copy in copies:
        copy.wait()
    own.wait()
    for cross in crosses + [gate_cross, up_cross]:
        cross.wait()
    for copy in (out_cross_core, out_cross, out_line, head_line, head_cross, down_core):
        copy.wait_send()
    for cross, onward in fetched:
        cross.wait_send()
        onward.wait()
    for number in range(5):
        gain_copy(number).wait_send()
    for number in range(PLANES):
        up_line(number).wait_send()
    for number in (2, 1):
        gate_line(number).wait_send()
    for weight in weights:
        sent(weight)


def reduce_all(rows_in, down, gate, up, out, head, gains, attn_weights):
    (down_keep, down_got), (gate_keep, gate_first, gate_sent), (up_keep, up_sent), (out_part, out_sent) = down, gate, up, out
    head_keep, head_sent = head
    hops = 2 * (PLANES - 1)
    vmem = pl.BlockSpec(memory_space=pltpu.VMEM)
    hbm = pl.BlockSpec(memory_space=pl.ANY)

    def piece(keep):
        return keep.shape[1:]

    def half_lanes(keep):
        return (keep.shape[1], keep.shape[2] // 2)

    def shape(dims, kind=BF):
        return jax.ShapeDtypeStruct(dims, kind)

    down_rows, down_cols = piece(down_keep)
    out_half = out_part.shape[1:3] + (out_part.shape[3] // 2,)
    keeps = (down_keep, gate_keep, up_keep, jax.ShapeDtypeStruct(out_half, BF))
    return pl.pallas_call(
        reduce_kernel,
        in_specs=[hbm] + [vmem] * 4 + [hbm, vmem] * 4 + [hbm] * 3,
        out_specs=[hbm] + [vmem] * 10 + [hbm] * 3,
        out_shape=[
            shape(rows_in.shape),
            shape((down_rows, down_cols)),
            shape((down_rows // CORES, down_cols)),
            shape((2, LINES, down_rows // CORES, down_cols // 4)),
            shape(piece(gate_keep)),
            shape(half_lanes(gate_keep)),
            shape(piece(up_keep)),
            shape(half_lanes(up_keep)),
            shape(out_half[1:]),
            shape((head_keep.shape[0], head_keep.shape[1] // 2)),
            shape(gains.shape, jnp.float32),
        ]
        + [shape(weight.shape) for weight in attn_weights],
        scratch_shapes=[
            pltpu.VMEM(gate_keep.shape, BF),
            pltpu.VMEM(up_keep.shape, BF),
            pltpu.VMEM(out_part.shape, BF),
            pltpu.VMEM(out_part.shape[:1] + out_half, BF),
            pltpu.VMEM(out_part.shape[:1] + out_half, BF),
            pltpu.VMEM(out_half, BF),
        ]
        + [pltpu.VMEM((PLANES - 1,) + piece(keep), BF) for keep in keeps]
        + [pltpu.VMEM((hops,) + piece(keep), BF) for keep in keeps]
        + [
            pltpu.VMEM(head_keep.shape, BF),
            pltpu.VMEM(head_keep.shape, BF),
            pltpu.VMEM((head_keep.shape[0], head_keep.shape[1] // 2), BF),
            pltpu.VMEM((head_keep.shape[0], head_keep.shape[1] // 2), BF),
            pltpu.VMEM((6,) + gains.shape, jnp.float32),
            pltpu.VMEM((5,) + gains.shape, jnp.float32),
            pltpu.SemaphoreType.DMA((2, RANKS)),
            pltpu.SemaphoreType.DMA((2, 4 * hops)),
            pltpu.SemaphoreType.DMA((2, 19)),
            pltpu.SemaphoreType.DMA((2, 2 * PLANES)),
            pltpu.SemaphoreType.DMA((2, 6)),
            pltpu.SemaphoreType.DMA,
        ],
        compiler_params=pltpu.CompilerParams(
            collective_id=0, has_side_effects=True, vmem_limit_bytes=VMEM_LIMIT
        ),
    )(
        rows_in, down_keep, down_got, gate_keep, gate_first, gate_sent, up_keep, up_sent, out_part, out_sent, head_keep, head_sent, gains,
        *attn_weights,
    )


def local_last(info, operands):
    rows, model = operands[1].shape

    def spec(shape):
        return pl.BlockSpec(shape, lambda i, info: (0,) * len(shape))

    return pl.pallas_call(
        last_kernel,
        grid_spec=pltpu.PrefetchScalarGridSpec(
            num_scalar_prefetch=1,
            grid=(1,),
            in_specs=[spec(operand.shape) for operand in operands],
            out_specs=spec((rows, model)),
            scratch_shapes=[pltpu.VMEM((rows, model), jnp.float32)],
        ),
        out_shape=jax.ShapeDtypeStruct((rows, model), BF),
        compiler_params=pltpu.CompilerParams(vmem_limit_bytes=VMEM_LIMIT),
    )(info, *operands)


def head_shards(
    tokens, attn_gain, w_query, w_key, w_value, w_out, mlp_gain, w_gate, w_up, w_down, cotangent
):
    seqs, width, model = tokens.shape
    length = width * RANKS
    rows = seqs * width
    half_model = model // 2
    hidden = w_gate.shape[1]
    half_hidden = hidden // 2
    part_hidden = half_hidden // CORES
    chunk = hidden // (2 * RANKS)
    rank = lax.axis_index("ctx")
    side = lax.axis_index("fsdp")
    core = rank % CORES
    line = (rank // CORES) % LINES
    plane = rank // (CORES * LINES)
    head = plane * CORES + core
    low_side = side == 0
    info = jnp.stack([side, core, line]).astype(jnp.int32)
    pick = jnp.asarray((pad_columns()[:, None] == np.arange(HEAD_COLS)[None, :]).astype(np.float32)).astype(BF)

    def head_slice(weight, size):
        return lax.dynamic_slice_in_dim(weight, head * size, size, 1)

    head_rows = jnp.concatenate(
        [head_slice(w_query, 2 * HD), head_slice(w_key, HD), head_slice(w_value, HD)], axis=1
    )
    tokens_seq, head_far, far, out_far = gather_all(tokens, head_rows, w_gate, w_up, w_out)
    grad_down = cotangent.reshape(rows, model)
    grad_down_other = swap_fsdp(after(grad_down, tokens_seq))
    head_weight = in_order(side, head_rows, head_far)
    head_padded = times_transposed(head_weight, pick).astype(BF)
    cosine, sine = rope_rows(length)
    attn_row, mlp_row = attn_gain[None], mlp_gain[None]
    normed_seq, qkv, attended_seq, lse = head_forward(
        tokens_seq.reshape(length, model), attn_row, head_padded, cosine, sine
    )
    attended_blocks, down_far = scatter_rows(attended_seq.reshape(RANKS, width, -1), w_down)
    weights = (w_gate, w_up, far, w_down, down_far)
    token_rows = tokens.reshape(rows, model)
    resid, normed_two = local_call(
        post_kernel,
        info,
        (attended_blocks, token_rows, w_out, out_far, mlp_row),
        [jax.ShapeDtypeStruct((rows, model), jnp.float32), jax.ShapeDtypeStruct((rows, model), BF)],
    )

    def exchange(value):
        return lax.all_to_all(value.reshape(RANKS, width, -1), "ctx", 0, 0, tiled=True)

    normed_other = swap_fsdp(normed_two)
    inner_own, gate_own, up_own, mixed_own, back_own = mlp_part(info, normed_two, grad_down, weights, jnp.float32)
    normed_other, grad_down_other = after((normed_other, grad_down_other), mixed_own)
    inner_far, gate_far, up_far, mixed_far, back_far = mlp_part(info, normed_other, grad_down_other, weights, BF)
    back_got = swap_fsdp(back_far)

    normed_pair = jnp.concatenate([normed_two, normed_other], axis=0)
    normed_sib = swap_core(normed_pair)
    cot_pair = jnp.concatenate([grad_down, grad_down_other], axis=0)
    cot_sib = swap_core(cot_pair)

    def pair_acts(own, far):
        pair = jnp.concatenate([own, far], axis=1)
        return at(pair, core), swap_core(at(pair, 1 - core))

    inner_pair, inner_sib = pair_acts(inner_own, inner_far)
    grad_down_weight = (transposed_times(cot_pair, inner_pair) + transposed_times(cot_sib, inner_sib)).astype(BF)
    gate_pair, gate_sib = pair_acts(gate_own, gate_far)
    grad_gate_weight = (transposed_times(gate_pair, normed_pair) + transposed_times(gate_sib, normed_sib)).astype(BF)
    up_pair, up_sib = pair_acts(up_own, up_far)
    grad_up_weight = (transposed_times(up_pair, normed_pair) + transposed_times(up_sib, normed_sib)).astype(BF)

    per_chip = model // CHIPS
    down_cut = grad_down_weight.reshape(PLANES, LINES, per_chip, part_hidden)
    gate_cut = grad_gate_weight.reshape(LINES, PLANES, chunk, model)
    up_cut = grad_up_weight.reshape(LINES, PLANES, chunk, model)
    down_sent, gate_sent, up_sent = at(down_cut, 1 - line, 1), at(gate_cut, 1 - line), at(up_cut, 1 - line)
    down_got = swap_line(down_sent)
    back_got, mixed_far = after((back_got, mixed_far), (down_sent, gate_sent))
    mixed_got = swap_fsdp(mixed_far)
    mixed = (resid + mixed_own + mixed_got.astype(jnp.float32)).astype(BF)
    grad_resid, grad_branch, grad_attended, mlp_gain_part = local_call(
        pre_kernel,
        info,
        (back_own, back_got, grad_down, resid, mlp_row, w_out, out_far),
        [
            jax.ShapeDtypeStruct((rows, model), jnp.float32),
            jax.ShapeDtypeStruct((rows, model), BF),
            jax.ShapeDtypeStruct(attended_blocks.shape, BF),
            jax.ShapeDtypeStruct((1, model), jnp.float32),
        ],
    )
    grad_att_seq = exchange(grad_attended).reshape(length, 2 * LANES)

    attended = attended_blocks.reshape(PLANES, LINES, CORES, width, 2 * LANES)
    attended = attended.transpose(1, 3, 0, 2, 4).reshape(rows, HQ * LANES)
    out_cut = transposed_times(grad_branch, attended).astype(BF)
    out_cut = out_cut.reshape(PLANES, LINES, CORES, model // RANKS, HQ * LANES)

    def of_lines(which):
        return at(out_cut, which, 2).transpose(1, 0, 2, 3)

    grad_qkv, gate_first = head_backward(qkv, attended_seq, grad_att_seq, lse, cosine, sine, pick, gate_sent)
    head_grad = transposed_times(grad_qkv, normed_seq)
    gain_part = jnp.sum(head_grad * head_weight.T.astype(jnp.float32), axis=0) / attn_gain
    query_cut = head_grad[: 2 * HD].reshape(2, HD, model)
    key_cut = head_grad[2 * HD :].reshape(2, 2, HD // 2, model)

    def half_columns(which):
        return jnp.concatenate([at(query_cut, which), at(key_cut, which, 1).reshape(HD, model)], axis=0)

    gains = jnp.concatenate([jnp.stack([gain_part, mlp_gain_part[0]]), jnp.zeros((6, model), jnp.float32)], axis=0)
    (
        grad_rows, down_mine, down_theirs, down_side, gate_mine, gate_side, up_mine, up_side, out_mine, head_mine, gains,
        *attn_far,
    ) = reduce_all(
        grad_qkv.reshape(RANKS, width, HEAD_COLS),
        (at(down_cut, line, 1), after(down_got, grad_qkv)),
        (at(gate_cut, line), gate_first, gate_sent),
        (at(up_cut, line), up_sent),
        (of_lines(core), of_lines(1 - core)),
        (half_columns(line), half_columns(1 - line).astype(BF)),
        gains,
        (w_query, w_key, w_value),
    )

    def by_columns(mine, theirs):
        cut = mine.reshape(chunk, 2, half_model)
        return in_order(side, at(cut, side, 1), theirs).astype(jnp.float32).T

    w_gate_grad = by_columns(gate_mine, gate_side)
    w_up_grad = by_columns(up_mine, up_side)
    shape = (model // RANKS, LINES, 2, PLANES // 2, chunk)
    parts = [at(down_mine.reshape((CORES,) + shape), core), down_theirs.reshape(shape)]
    kept = [at(part, side, 2) for part in parts]
    sided = [down_side[i].reshape(LINES, model // RANKS, PLANES // 2, chunk).transpose(1, 0, 2, 3) for i in range(2)]
    by_side = [
        jnp.stack([jnp.where(low_side, k, g), jnp.where(low_side, g, k)], axis=3) for k, g in zip(kept, sided)
    ]
    first = core == 0
    by_core = jnp.stack(
        [jnp.where(first, by_side[0], by_side[1]), jnp.where(first, by_side[1], by_side[0])], axis=3
    )
    w_down_grad = by_core.transpose(0, 2, 1, 3, 4, 5).reshape(model // RANKS, -1).T.astype(jnp.float32)
    w_out_grad = (
        out_mine.reshape(model // RANKS, HK, LANES)[:, :, :HD].reshape(model // RANKS, half_model).T.astype(jnp.float32)
    )
    head_mine = head_mine.astype(jnp.float32)
    w_query_grad = head_mine[:HD].T
    w_key_grad = head_mine[HD : HD + HD // 2].T
    w_value_grad = head_mine[HD + HD // 2 :].T

    tokens_grad = local_last(
        info, (grad_rows, token_rows, attn_row, grad_resid, w_query, w_key, w_value) + tuple(attn_far)
    )
    return (
        mixed.reshape(seqs, width, model),
        tokens_grad.reshape(seqs, width, model),
        gains[0],
        w_query_grad,
        w_key_grad,
        w_value_grad,
        w_out_grad,
        gains[1],
        w_gate_grad,
        w_up_grad,
        w_down_grad,
    )


def solution(mesh):
    by_heads = mesh.shape["ctx"] == RANKS and mesh.shape["fsdp"] == 2
    placed = (
        P("fsdp", "ctx", None),
        P(),
        P("fsdp", None),
        P("fsdp", None),
        P("fsdp", None),
        P("fsdp", None),
        P(),
        P("fsdp", None),
        P("fsdp", None),
        P("fsdp", None),
        P("fsdp", "ctx", None),
    )
    return jax.shard_map(
        head_shards if by_heads else shards,
        mesh=mesh,
        in_specs=placed,
        out_specs=(
            P("fsdp", "ctx", None),
            P("fsdp", "ctx", None),
            P(),
            P("fsdp", "ctx"),
            P("fsdp", "ctx"),
            P("fsdp", "ctx"),
            P("fsdp", "ctx"),
            P(),
            P("fsdp", "ctx"),
            P("fsdp", "ctx"),
            P("fsdp", "ctx"),
        ),
        check_vma=False,
    )
```

```python
import dataclasses
import functools
from typing import Any

import jax
import jax.numpy as jnp
import numpy as np
from jax import lax
from jax.experimental import pallas as pl
from jax.experimental.pallas import tpu as pltpu
from jax.sharding import PartitionSpec as P

HQ = 16
HK = 8
HD = 96
MICRO = 2
LANES = 128
HEAD_COLS = 4 * HD
BF = jnp.bfloat16
VMEM_LIMIT = 48 * 1024 * 1024


EPSILON = 1e-05
ROPE_BASE = 100000.0
MASK_FILL = -1e30


def matmul(left, right):
    return jnp.dot(left, right, preferred_element_type=jnp.float32)


def times_transposed(left, right):
    return lax.dot_general(
        left, right, (((1,), (1,)), ((), ())), preferred_element_type=jnp.float32
    )


def transposed_times(left, right):
    return lax.dot_general(
        left, right, (((0,), (0,)), ((), ())), preferred_element_type=jnp.float32
    )


def normalize(values):
    inv_rms = lax.rsqrt(jnp.mean(values * values, axis=-1, keepdims=True) + EPSILON)
    return (values * inv_rms, inv_rms)


def norm_back(grad_normed, gain_row, unit_rows, inv_rms):
    scaled = grad_normed * gain_row
    return inv_rms * (scaled - unit_rows * jnp.mean(scaled * unit_rows, axis=-1, keepdims=True))


def rotate(values, cosine, sine_rows):
    half_dim = values.shape[-1] // 2
    front = values[..., :half_dim]
    back_half = values[..., half_dim:]
    return jnp.concatenate(
        [front * cosine - back_half * sine_rows, back_half * cosine + front * sine_rows], axis=-1
    )


def attend_forward(query_rows, key_rows, value_rows, allowed):
    width_ct = query_rows.shape[0]
    grouped = query_rows.reshape(width_ct, HK, HQ // HK, HD)
    key_heads = key_rows.reshape(-1, HK, HD)
    value_heads = value_rows.reshape(-1, HK, HD)
    scores = jnp.einsum("cgrd,lgd->grcl", grouped, key_heads, preferred_element_type=jnp.float32)
    scores = jnp.where(allowed, scores, MASK_FILL)
    row_top = jnp.max(scores, axis=-1, keepdims=True)
    shifted_exp = jnp.exp(scores - row_top)
    row_total = jnp.sum(shifted_exp, axis=-1, keepdims=True)
    prob_low = (shifted_exp / row_total).astype(jnp.bfloat16)
    attended = jnp.einsum(
        "grcl,lgd->cgrd", prob_low, value_heads, preferred_element_type=jnp.float32
    )
    return (attended.reshape(width_ct, HQ * HD), row_top + jnp.log(row_total))


def attend_backward(query_rows, key_rows, value_rows, allowed, log_total, grad_rows):
    width_ct = query_rows.shape[0]
    grouped = query_rows.reshape(width_ct, HK, HQ // HK, HD)
    key_heads = key_rows.reshape(-1, HK, HD)
    value_heads = value_rows.reshape(-1, HK, HD)
    scores = jnp.einsum("cgrd,lgd->grcl", grouped, key_heads, preferred_element_type=jnp.float32)
    prob_full = jnp.exp(jnp.where(allowed, scores, MASK_FILL) - log_total)
    prob_low = prob_full.astype(jnp.bfloat16)
    grad_heads = grad_rows.reshape(width_ct, HK, HQ // HK, HD)
    grad_prob = jnp.einsum(
        "cgrd,lgd->grcl", grad_heads, value_heads, preferred_element_type=jnp.float32
    )
    row_inner = jnp.sum(prob_full * grad_prob, axis=-1, keepdims=True)
    grad_scores = (prob_full * (grad_prob - row_inner)).astype(jnp.bfloat16)
    grad_query = jnp.einsum(
        "grcl,lgd->cgrd", grad_scores, key_heads, preferred_element_type=jnp.float32
    )
    grad_key = jnp.einsum(
        "grcl,cgrd->lgd", grad_scores, grouped, preferred_element_type=jnp.float32
    )
    grad_value = jnp.einsum(
        "grcl,cgrd->lgd", prob_low, grad_heads, preferred_element_type=jnp.float32
    )
    return (
        grad_query.reshape(width_ct, HQ * HD),
        grad_key.reshape(-1, HK * HD),
        grad_value.reshape(-1, HK * HD),
        row_inner,
    )


def reduce_grad(full_grad):
    partial_grad = lax.psum_scatter(
        full_grad.astype(jnp.bfloat16), "fsdp", scatter_dimension=0, tiled=True
    )
    return lax.psum_scatter(partial_grad, "ctx", scatter_dimension=1, tiled=True).astype(
        jnp.float32
    )


def shards(
    tokens, attn_gain, w_query, w_key, w_value, w_out, mlp_gain, w_gate, w_up, w_down, cotangent
):
    seq_local, width_ct, model_width = tokens.shape
    seq_block = seq_local // MICRO
    row_count = seq_block * width_ct
    length = width_ct * lax.axis_size("ctx")
    half_dim = HD // 2
    offset = lax.axis_index("ctx") * width_ct
    query_pos = offset + jnp.arange(width_ct, dtype=jnp.int32)
    key_pos = jnp.arange(length, dtype=jnp.int32)
    allowed = key_pos[None, :] <= query_pos[:, None]
    inv_freq = 1.0 / ROPE_BASE ** (jnp.arange(half_dim, dtype=jnp.float32) * 2.0 / HD)
    angles = query_pos.astype(jnp.float32)[:, None] * inv_freq[None, :]
    cos_one = jnp.cos(angles)[:, None, :]
    sin_one = jnp.sin(angles)[:, None, :]
    cos_rows = jnp.tile(cos_one, (seq_block, 1, 1))
    sin_rows = jnp.tile(sin_one, (seq_block, 1, 1))
    head_scale = HD ** (-0.5)
    mixed_list, token_grad_list = ([], [])
    kept_normed_one, kept_grad_query, kept_grad_key, kept_grad_value = ([], [], [], [])
    kept_attended, kept_grad_branch, kept_normed_two = ([], [], [])
    kept_grad_gate, kept_grad_upper, kept_inner, kept_grad_down = ([], [], [], [])
    attn_gain_acc = jnp.zeros((model_width,), jnp.float32)
    mlp_gain_acc = jnp.zeros((model_width,), jnp.float32)
    for micro_at in range(MICRO):
        first_seq = micro_at * seq_block
        inputs = (
            tokens[first_seq : first_seq + seq_block]
            .reshape(row_count, model_width)
            .astype(jnp.float32)
        )
        outer_grad = (
            cotangent[first_seq : first_seq + seq_block]
            .reshape(row_count, model_width)
            .astype(jnp.float32)
        )
        attn_all = (
            lax.all_gather(w_query, "fsdp", axis=0, tiled=True),
            lax.all_gather(w_key, "fsdp", axis=0, tiled=True),
            lax.all_gather(w_value, "fsdp", axis=0, tiled=True),
            lax.all_gather(w_out, "fsdp", axis=0, tiled=True),
        )
        unit_one, inv_one = normalize(inputs)
        normed_one = (unit_one * attn_gain).astype(jnp.bfloat16)
        query_raw = matmul(normed_one, attn_all[0]).reshape(row_count, HQ, HD)
        key_raw = matmul(normed_one, attn_all[1]).reshape(row_count, HK, HD)
        value_raw = matmul(normed_one, attn_all[2])
        queries = (
            (rotate(query_raw, cos_rows, sin_rows) * head_scale)
            .astype(jnp.bfloat16)
            .reshape(seq_block, width_ct, HQ * HD)
        )
        keys = (
            rotate(key_raw, cos_rows, sin_rows)
            .astype(jnp.bfloat16)
            .reshape(seq_block, width_ct, HK * HD)
        )
        values = value_raw.astype(jnp.bfloat16).reshape(seq_block, width_ct, HK * HD)
        key_all, value_all = (
            lax.all_gather(keys, "ctx", axis=1, tiled=True),
            lax.all_gather(values, "ctx", axis=1, tiled=True),
        )
        attended_parts, lse_parts = ([], [])
        seq_at = 0
        attended_one, lse_one = attend_forward(
            queries[seq_at], key_all[seq_at], value_all[seq_at], allowed
        )
        attended_parts.append(attended_one)
        lse_parts.append(lse_one)
        attended = attended_parts[0].astype(jnp.bfloat16)
        resid = inputs + matmul(attended, attn_all[3])
        unit_two, inv_two = normalize(resid)
        normed_two = (unit_two * mlp_gain).astype(jnp.bfloat16)
        gate_proj = matmul(normed_two, lax.all_gather(w_gate, "fsdp", axis=0, tiled=True))
        up_proj = matmul(normed_two, lax.all_gather(w_up, "fsdp", axis=0, tiled=True))
        sigma = jax.nn.sigmoid(gate_proj)
        active = gate_proj * sigma
        hidden_act = (active * up_proj).astype(jnp.bfloat16)
        down_out = matmul(hidden_act, lax.all_gather(w_down, "fsdp", axis=0, tiled=True))
        mixed_list.append((resid + down_out).astype(jnp.bfloat16))
        grad_down = outer_grad.astype(jnp.bfloat16)
        grad_hidden = times_transposed(
            grad_down, lax.all_gather(w_down, "fsdp", axis=0, tiled=True)
        )
        grad_gate = (grad_hidden * up_proj * sigma * (1.0 + gate_proj * (1.0 - sigma))).astype(
            jnp.bfloat16
        )
        grad_upper = (grad_hidden * active).astype(jnp.bfloat16)
        pair_pieces = lax.all_gather((w_gate, w_up), "fsdp", axis=0, tiled=True)
        grad_normed_two = times_transposed(grad_gate, pair_pieces[0]) + times_transposed(
            grad_upper, pair_pieces[1]
        )
        mlp_gain_acc = mlp_gain_acc + jnp.sum(grad_normed_two * unit_two, axis=0)
        grad_resid = outer_grad + norm_back(grad_normed_two, mlp_gain, unit_two, inv_two)
        grad_branch = grad_resid.astype(jnp.bfloat16)
        attn_back = (
            lax.all_gather(w_query, "fsdp", axis=0, tiled=True),
            lax.all_gather(w_key, "fsdp", axis=0, tiled=True),
            lax.all_gather(w_value, "fsdp", axis=0, tiled=True),
            lax.all_gather(w_out, "fsdp", axis=0, tiled=True),
        )
        grad_attended = times_transposed(grad_branch, attn_back[3]).astype(jnp.bfloat16)
        key_back, value_back = (
            lax.all_gather(keys, "ctx", axis=1, tiled=True),
            lax.all_gather(values, "ctx", axis=1, tiled=True),
        )
        query_parts, key_parts, value_parts = ([], [], [])
        seq_at = 0
        query_one = queries[seq_at]
        key_one = key_back[seq_at]
        value_one = value_back[seq_at]
        lse_one = lse_parts[seq_at]
        grad_query, grad_key, grad_value, row_inner = attend_backward(
            query_one, key_one, value_one, allowed, lse_one, grad_attended
        )
        own_key = lax.psum_scatter(
            grad_key.astype(jnp.bfloat16), "ctx", scatter_dimension=0, tiled=True
        ).astype(jnp.float32)
        own_value = lax.psum_scatter(
            grad_value.astype(jnp.bfloat16), "ctx", scatter_dimension=0, tiled=True
        ).astype(jnp.float32)
        query_parts.append(
            rotate((grad_query * head_scale).reshape(width_ct, HQ, HD), cos_one, -sin_one).reshape(
                width_ct, HQ * HD
            )
        )
        key_parts.append(
            rotate(own_key.reshape(width_ct, HK, HD), cos_one, -sin_one).reshape(width_ct, HK * HD)
        )
        value_parts.append(own_value)
        grad_query_raw = query_parts[0].astype(jnp.bfloat16)
        grad_key_raw = key_parts[0].astype(jnp.bfloat16)
        grad_value_raw = value_parts[0].astype(jnp.bfloat16)
        grad_normed_one = (
            times_transposed(grad_query_raw, attn_back[0])
            + times_transposed(grad_key_raw, attn_back[1])
            + times_transposed(grad_value_raw, attn_back[2])
        )
        attn_gain_acc = attn_gain_acc + jnp.sum(grad_normed_one * unit_one, axis=0)
        token_grad_list.append(
            (grad_resid + norm_back(grad_normed_one, attn_gain, unit_one, inv_one)).astype(
                jnp.bfloat16
            )
        )
        kept_normed_one.append(normed_one)
        kept_grad_query.append(grad_query_raw)
        kept_grad_key.append(grad_key_raw)
        kept_grad_value.append(grad_value_raw)
        kept_attended.append(attended)
        kept_grad_branch.append(grad_branch)
        kept_normed_two.append(normed_two)
        kept_grad_gate.append(grad_gate)
        kept_grad_upper.append(grad_upper)
        kept_inner.append(hidden_act)
        kept_grad_down.append(grad_down)
    normed_one_all = jnp.concatenate(kept_normed_one, axis=0)
    normed_two_all = jnp.concatenate(kept_normed_two, axis=0)
    w_query_grad = reduce_grad(
        transposed_times(normed_one_all, jnp.concatenate(kept_grad_query, axis=0))
    )
    w_key_grad = reduce_grad(
        transposed_times(normed_one_all, jnp.concatenate(kept_grad_key, axis=0))
    )
    w_value_grad = reduce_grad(
        transposed_times(normed_one_all, jnp.concatenate(kept_grad_value, axis=0))
    )
    w_out_grad = reduce_grad(
        transposed_times(
            jnp.concatenate(kept_attended, axis=0), jnp.concatenate(kept_grad_branch, axis=0)
        )
    )
    w_gate_grad = reduce_grad(
        transposed_times(normed_two_all, jnp.concatenate(kept_grad_gate, axis=0))
    )
    w_up_grad = reduce_grad(
        transposed_times(normed_two_all, jnp.concatenate(kept_grad_upper, axis=0))
    )
    w_down_grad = reduce_grad(
        transposed_times(
            jnp.concatenate(kept_inner, axis=0), jnp.concatenate(kept_grad_down, axis=0)
        )
    )
    attn_gain_grad, mlp_gain_grad = lax.psum((attn_gain_acc, mlp_gain_acc), ("ctx", "fsdp"))
    mixed = jnp.concatenate(mixed_list, axis=0).reshape(seq_local, width_ct, model_width)
    tokens_grad = jnp.concatenate(token_grad_list, axis=0).reshape(seq_local, width_ct, model_width)
    return (
        mixed,
        tokens_grad,
        attn_gain_grad,
        w_query_grad,
        w_key_grad,
        w_value_grad,
        w_out_grad,
        mlp_gain_grad,
        w_gate_grad,
        w_up_grad,
        w_down_grad,
    )


def nt(a,b):
    return lax.dot_general(a,b,(((1,),(1,)),((),())),preferred_element_type=jnp.float32)
def tn(a,b):
    return lax.dot_general(a,b,(((0,),(0,)),((),())),preferred_element_type=jnp.float32)
def nn(a,b):
    return jnp.dot(a,b,preferred_element_type=jnp.float32)

def turn(v,cosine,sine):
    return v*cosine+pltpu.roll(v,LANES//2,1)*sine

def forward_kernel(
    tokens_ref, gain_ref, head_near, head_far, pick_ref, cos_ref, sin_ref, w_down, cot_in,
    normed_ref, qkv_ref, att_ref, lse_ref, rows_out, down_far, cot_out,
    weight_ref, key_ref, val_t_ref, exchange_sems, weight_sems, local_sem,
):
    at = pl.program_id(0)
    rank = lax.axis_index("ctx")
    side = lax.axis_index("fsdp")
    core = lax.rem(rank, CORES)
    line = lax.rem(lax.div(rank, CORES), LINES)
    other_line = rank + CORES * (1 - 2 * line)
    other_core = rank + 1 - 2 * core
    rows = tokens_ref.shape[0]
    width = att_ref.shape[1]
    blocks = rows // width
    here = pl.ds(pl.multiple_of(at * rows, rows), rows)

    chunk = w_down.shape[0] // RANKS
    quarter = 2 * core + line

    def down_slice(which, part):
        return down_far.at[pl.ds(pl.multiple_of((2 * which + part) * chunk, chunk), chunk)]

    def down_cross(part):
        number = 2 * quarter + part
        source = w_down.at[pl.ds(pl.multiple_of((2 * number + 1 - side) * chunk, chunk), chunk)]
        return side_copy(source, down_slice(quarter, part), weight_sems, part, 1 - side)

    def onward(kind, part):
        block = down_slice(2 * core + 1 - line if kind == 2 else quarter, part)
        return ctx_copy(block, block, weight_sems, 2 + 2 * kind + part, other_core if kind else other_line)

    cot_cross = side_copy(cot_in, cot_out, weight_sems, 8, 1 - side)

    def row_copy(away):
        to = lax.rem(rank + away, RANKS)
        return ctx_copy(att_ref.at[to], rows_out.at[rank], exchange_sems, away, to)

    @pl.when(at == 0)
    def _():
        greet(rank, side)
        for part in range(2):
            down_cross(part).start()
        cot_cross.start()
        val_t_ref[...] = jnp.zeros_like(val_t_ref)
        half = head_near.shape[0]
        for which, source in enumerate((head_near, head_far)):
            first = pl.ds(pl.multiple_of((side if which == 0 else 1 - side) * half, 16), half)
            weight_ref[first, :] = nt(source[...], pick_ref[...]).astype(BF)

    cosine, sine = cos_ref[...], sin_ref[...]
    unit, _ = normalize(tokens_ref[...].astype(jnp.float32))
    normed = (unit * gain_ref[...]).astype(BF)
    normed_ref[...] = normed
    raw = nn(normed, weight_ref[...])
    scale = HD**-0.5
    parts = [
        (turn(raw[:, j * LANES : (j + 1) * LANES], cosine, sine) * (scale if j < 2 else 1.0)).astype(BF) for j in range(3)
    ]
    value = raw[:, 3 * LANES :].astype(BF)
    for j in range(3):
        qkv_ref[:, j * LANES : (j + 1) * LANES] = parts[j]
    qkv_ref[:, 3 * LANES :] = value
    key_ref[here, :] = parts[2]
    val_t_ref[:, here] = value.T
    query = jnp.concatenate(parts[:2], axis=0)
    for band in range(key_ref.shape[0] // rows):
        @pl.when(at == band)
        def _():
            scores = nt(key_ref[0 : (band + 1) * rows, :], query)
            tail = scores[band * rows :, :]
            key_pos = lax.broadcasted_iota(jnp.int32, tail.shape, 0)
            query_pos = lax.broadcasted_iota(jnp.int32, tail.shape, 1) % rows
            tail = jnp.where(key_pos <= query_pos, tail, MASK_FILL)
            pieces = [scores[b * rows : (b + 1) * rows, :] for b in range(band)] + [tail]
            top = functools.reduce(jnp.maximum, [jnp.max(p, axis=0, keepdims=True) for p in pieces])
            total = 0.0
            acc = 0.0
            for b, p in enumerate(pieces):
                e = jnp.exp(p - top)
                total = total + jnp.sum(e, axis=0, keepdims=True)
                acc = acc + nn(val_t_ref[:, b * rows : (b + 1) * rows], e.astype(BF))
            acc = acc / total
            for h in range(2):
                turned = acc[:, h * rows : (h + 1) * rows].T.astype(BF)
                for i in range(blocks):
                    att_ref[band * blocks + i, :, h * LANES : (h + 1) * LANES] = turned[i * width : (i + 1) * width]
            lse_ref[0] = top + jnp.log(total)
            for i in range(blocks):
                to = band * blocks + i
                away = lax.rem(to - rank + RANKS, RANKS)

                @pl.when(away != 0)
                def _():
                    ctx_copy(att_ref.at[to], rows_out.at[rank], exchange_sems, away, to).start()

                @pl.when(away == 0)
                def _():
                    pltpu.make_async_copy(att_ref.at[to], rows_out.at[rank], local_sem).start()

    @pl.when(at == 1)
    def _():
        down_cross(0).wait_recv()
        onward(0, 0).start()
        onward(1, 0).start()

    @pl.when(at == 2)
    def _():
        down_cross(1).wait_recv()
        onward(0, 1).start()
        onward(1, 1).start()

    @pl.when(at == pl.num_programs(0) - 1)
    def _():
        for part in range(2):
            onward(0, part).wait_recv()
            onward(2, part).start()
        for part in range(2):
            onward(1, part).wait_recv()
            onward(2, part).wait_recv()
        for away in range(1, RANKS):
            row_copy(away).wait()
        pltpu.make_async_copy(att_ref.at[rank], rows_out.at[rank], local_sem).wait()
        cot_cross.wait()
        for part in range(2):
            down_cross(part).wait_send()
            for kind in range(3):
                onward(kind, part).wait_send()


def head_forward(tokens, gain, head_near, head_far, pick, cosine, sine, w_down, cotangent, rows=512):
    length, model = tokens.shape
    steps = length // rows
    width = length // RANKS
    hbm = pl.BlockSpec(memory_space=pl.ANY)
    dma = pltpu.SemaphoreType.DMA

    def block(cols):
        return pl.BlockSpec((rows, cols), lambda i: (i, 0))

    def whole(*dims):
        return pl.BlockSpec(dims, lambda i: (0,) * len(dims))

    return pl.pallas_call(
        forward_kernel,
        grid=(steps,),
        in_specs=[
            block(model), whole(1, model), whole(*head_near.shape), whole(*head_far.shape), whole(*pick.shape),
            block(LANES), block(LANES), hbm, hbm,
        ],
        out_specs=[
            block(model), block(4 * LANES), whole(RANKS, width, 2 * LANES),
            pl.BlockSpec((1, 1, 2 * rows), lambda i: (i, 0, 0)), hbm, hbm, hbm,
        ],
        out_shape=[
            jax.ShapeDtypeStruct((length, model), BF),
            jax.ShapeDtypeStruct((length, 4 * LANES), BF),
            jax.ShapeDtypeStruct((RANKS, width, 2 * LANES), BF),
            jax.ShapeDtypeStruct((steps, 1, 2 * rows), jnp.float32),
            jax.ShapeDtypeStruct((RANKS, width, 2 * LANES), BF),
            jax.ShapeDtypeStruct((w_down.shape[0] // 2, model), BF),
            jax.ShapeDtypeStruct(cotangent.shape, BF),
        ],
        scratch_shapes=[
            pltpu.VMEM((model, 4 * LANES), BF),
            pltpu.VMEM((length, LANES), BF),
            pltpu.VMEM((LANES, length), BF),
            dma((2, RANKS)),
            dma((2, 9)),
            dma,
        ],
        compiler_params=pltpu.CompilerParams(collective_id=2, has_side_effects=True, vmem_limit_bytes=VMEM_LIMIT),
    )(tokens, gain, head_near, head_far, pick, cosine, sine, w_down, cotangent)


def backward_kernel(
    rows_in, qkv_in, out_in, lse_ref, cos_in, sin_in, pick_ref, squeeze_ref, down_sent, gate_sent, branch_in, att_in,
    up_own, up_far, up_sib, normed_own, normed_far, normed_sib, normed_sib_far,
    down_keep_in, down_first, mixed_far, mixed_own_in, resid_in,
    res_ref, gate_first, out_sum_out, up_keep_out, up_sent_out, down_got_out, down_hops_out, mixed_ref,
    qkv_ref, out_ref, cos_ref, sin_ref, branch_ref, att_ref, down_keep, mixed_own, resid,
    up_keep, up_sent, down_got, down_in, load_sems, store_sems, out_keep, out_sent, out_got, out_side, out_sum, out_sems,
    down_acc, mixed_got, plane_sems, up_all, normed_all, core_sems, local_sems, weight_ref, grad_ref, key_t_ref, grad_key_ref, grad_val_ref, rows_ref, exchange_sems, line_sems, fetch_sems, local_sem,
):
    rank = lax.axis_index("ctx")
    side = lax.axis_index("fsdp")
    core = lax.rem(rank, CORES)
    line = lax.rem(lax.div(rank, CORES), LINES)
    plane = lax.div(rank, CORES * LINES)
    other_line = rank + CORES * (1 - 2 * line)
    other_core = rank + 1 - 2 * core
    first_loads = local_copies(((branch_in, branch_ref), (att_in, att_ref)), load_sems)
    head_loads = local_copies(
        ((qkv_in, qkv_ref), (out_in, out_ref), (cos_in, cos_ref), (sin_in, sin_ref)), load_sems, 2
    )
    down_loads = local_copies(
        [(down_keep_in, down_keep)] + [(down_first.at[slot], down_got.at[number]) for slot, number in enumerate(DOWN_EARLY)],
        load_sems,
        6,
    )
    mixed_loads = local_copies(((mixed_own_in, mixed_own), (resid_in, resid)), load_sems, 10)
    out_stores = local_copies(((out_sum, out_sum_out),), store_sems)
    up_stores = local_copies(((up_keep, up_keep_out), (up_sent, up_sent_out)), store_sems, 2)
    down_stores = local_copies(((down_got, down_got_out),), store_sems, 4)
    start(first_loads + head_loads)
    greet(rank, side)

    def row_copy(away):
        to = lax.rem(rank + away, RANKS)
        return ctx_copy(rows_in.at[to], grad_ref.at[rank], exchange_sems, away, to)

    own = pltpu.make_async_copy(rows_in.at[rank], grad_ref.at[rank], local_sem)
    own.start()
    for away in range(1, RANKS):
        row_copy(away).start()
    late = [
        ctx_copy(down_sent.at[number], down_got.at[number], line_sems, slot, other_line)
        for slot, number in enumerate(DOWN_LATE)
    ]
    lines = [
        ctx_copy(gate_sent.at[number], gate_first.at[slot], line_sems, len(DOWN_LATE) + slot, other_line)
        for slot, number in enumerate(GATE_EARLY)
    ]
    mixed_cross = side_copy(mixed_far, mixed_got, fetch_sems, 0, 1 - side)
    chain = Chain(rank, plane, plane_sems)
    down = Weight(down_keep, down_got, down_acc, down_in, 0)
    jobs = (
        (up_all, (up_own, up_far, up_sib, None), True),
        (normed_all, (normed_own, normed_far, normed_sib, normed_sib_far), False),
    )
    moves = chip_moves(jobs, core, other_core, core_sems, local_sems)
    start(late + lines + [mixed_cross] + moves[0] + moves[1] + down_loads + mixed_loads)

    length = qkv_ref.shape[0]
    width = grad_ref.shape[1]
    rows = CORES * width
    scale = HD**-0.5
    grad_key_ref[...] = jnp.zeros_like(grad_key_ref)
    grad_val_ref[...] = jnp.zeros_like(grad_val_ref)
    wait(first_loads + head_loads)
    for b in range(CHIPS):
        key_t_ref[:, b * rows : (b + 1) * rows] = qkv_ref[b * rows : (b + 1) * rows, 2 * LANES : 3 * LANES].T

    branch_t = branch_ref[...].T
    per_rank = out_keep.shape[2]
    for pair in range(HK // CORES):
        attended = 0.0
        for at_core in range(CORES):
            first = pair * CORES * LINES + at_core
            block = jnp.concatenate([att_ref[first + seq * CORES] for seq in range(LINES)], axis=0)
            attended = attended + nn(block, squeeze_ref[at_core])
        weight_ref[...] = nn(branch_t, attended.astype(BF)).astype(BF)
        columns = slice(pair * 4 * HD, (pair + 1) * 4 * HD)
        for at_plane in range(PLANES):
            for at_line in range(LINES):
                place = (at_plane * LINES + at_line) * CORES
                out_keep[at_line, at_plane, :, columns] = weight_ref[
                    pl.ds(pl.multiple_of((place + core) * per_rank, 16), per_rank), :
                ]
                out_sent[at_line, at_plane, :, columns] = weight_ref[
                    pl.ds(pl.multiple_of((place + 1 - core) * per_rank, 16), per_rank), :
                ]
    out_core = ctx_copy(out_sent, out_got, out_sems, 0, other_core)
    out_core.start()
    half_out = out_sum.shape[3]
    out_near = pl.ds(pl.multiple_of(side * half_out, LANES), half_out)
    out_away = pl.ds(pl.multiple_of((1 - side) * half_out, LANES), half_out)
    out_cross = side_copy(out_keep.at[:, :, :, out_away], out_side, out_sems, 1, 1 - side)

    wait(moves[0] + moves[1])
    split_lines(up_all, normed_all, up_keep, up_sent, line)
    out_core.wait()
    for at_line in range(LINES):
        for at_plane in range(PLANES):
            total = wide(out_keep[at_line, at_plane]) + wide(out_got[at_line, at_plane])
            out_keep[at_line, at_plane] = total.astype(BF)
    out_cross.start()
    start(up_stores)
    wait(down_loads)

    @pl.loop(0, CHIPS)
    def _(step):
        @pl.when(step == 3)
        def _():
            chain.hop(down, 0)

        @pl.when(step == 6)
        def _():
            for copy in late:
                copy.wait_recv()
            chain.hop(down, 1)

        turn_at = lax.div(step, LINES)
        low = jnp.where(plane < PLANES // 2, plane, PLANES - 1 - plane)
        nth = jnp.where((low == 1) & (turn_at < 2), 1 - turn_at, turn_at)
        plane_at = jnp.where(plane < PLANES // 2, nth, PLANES - 1 - nth)
        flip = lax.rem(step, LINES)
        chip = plane_at * LINES + jnp.where(flip == 0, line, 1 - line)
        here = pl.ds(pl.multiple_of(chip * rows, rows), rows)
        for at_core in range(CORES):
            source = chip * CORES + at_core
            away = lax.rem(rank - source + RANKS, RANKS)

            @pl.when(away == 0)
            def _():
                own.wait()

            @pl.when(away != 0)
            def _():
                ctx_copy(rows_in.at[source], grad_ref.at[source], exchange_sems, away, other_core).wait_recv()

        grad = jnp.concatenate(
            [grad_ref[chip * CORES + c, :, h * LANES : (h + 1) * LANES] for h in range(2) for c in range(CORES)], axis=0
        )
        query = jnp.concatenate([qkv_ref[here, 0:LANES], qkv_ref[here, LANES : 2 * LANES]], axis=0)
        out = jnp.concatenate([out_ref[here, 0:LANES], out_ref[here, LANES:]], axis=0)
        inner = jnp.sum((grad.astype(jnp.float32) * out.astype(jnp.float32)).T, axis=0, keepdims=True)
        lse = lse_ref[chip]
        for band in range(CHIPS):
            @pl.when(chip == band)
            def _():
                grad_query = 0.0
                for b in range(band + 1):
                    span = slice(b * rows, (b + 1) * rows)
                    scores = nt(qkv_ref[span, 2 * LANES : 3 * LANES], query)
                    prob = jnp.exp(scores - lse)
                    if b == band:
                        key_pos = lax.broadcasted_iota(jnp.int32, scores.shape, 0)
                        query_pos = lax.broadcasted_iota(jnp.int32, scores.shape, 1) % rows
                        prob = jnp.where(key_pos <= query_pos, prob, 0.0)
                    grad_prob = nt(qkv_ref[span, 3 * LANES :], grad)
                    grad_scores = (prob * (grad_prob - inner)).astype(BF)
                    grad_val_ref[span, :] += nn(prob.astype(BF), grad)
                    grad_key_ref[span, :] += nn(grad_scores, query)
                    grad_query = grad_query + nn(key_t_ref[:, span], grad_scores)
                for j in range(2):
                    back = grad_query[:, j * rows : (j + 1) * rows].T * scale
                    rows_ref[here, j * LANES : (j + 1) * LANES] = turn(back, cos_ref[here, :], -sin_ref[here, :]).astype(BF)

    for b in range(CHIPS):
        span = slice(b * rows, (b + 1) * rows)
        rows_ref[span, 2 * LANES : 3 * LANES] = turn(grad_key_ref[span, :], cos_ref[span, :], -sin_ref[span, :]).astype(BF)
        rows_ref[span, 3 * LANES :] = grad_val_ref[span, :].astype(BF)
        res_ref[span, :] = nn(rows_ref[span, :], pick_ref[...]).astype(BF)
    start(down_stores)
    out_cross.wait()
    for at_line in range(LINES):
        for at_plane in range(PLANES):
            total = wide(out_keep[at_line, at_plane, :, out_near]) + wide(out_side[at_line, at_plane])
            out_sum[at_line, at_plane] = total.astype(BF)
    start(out_stores)
    wait(mixed_loads)
    mixed_cross.wait()
    mixed_ref[...] = (resid[...] + mixed_own[...] + wide(mixed_got[...])).astype(BF)
    for away in range(1, RANKS):
        row_copy(away).wait_send()
    for copy in late:
        copy.wait_send()
    for copy in lines:
        copy.wait()
    chain.receive(down, 1)
    chain.sent(down, 0, 2)
    hops_store = local_copies(((down_in, down_hops_out),), store_sems, 5)
    start(hops_store)
    wait(out_stores + up_stores + down_stores + hops_store)


def head_backward(rows_in, qkv, out, lse, cosine, sine, pick, squeeze, down_sent, gate_sent, branch, attended, up, down, mixed):
    length = qkv.shape[0]
    rows = length // CHIPS
    model = branch.shape[1]
    out_shape = jax.ShapeDtypeStruct((LINES, PLANES, model // RANKS, HQ * HD), BF)
    out_half = jax.ShapeDtypeStruct((LINES, PLANES, model // RANKS, HK * HD), BF)
    lse = lse.reshape(-1, 2, lse.shape[2] // 2).transpose(1, 0, 2).reshape(2, CHIPS, rows)
    lse = lse.transpose(1, 0, 2).reshape(CHIPS, 1, 2 * rows)
    vmem = pl.BlockSpec(memory_space=pltpu.VMEM)
    hbm = pl.BlockSpec(memory_space=pl.ANY)
    dma = pltpu.SemaphoreType.DMA
    return pl.pallas_call(
        backward_kernel,
        in_specs=[hbm] * 3 + [vmem] + [hbm] * 2 + [vmem] * 2 + [hbm] * 16,
        out_specs=[vmem] + [hbm] * 6 + [vmem],
        out_shape=[
            jax.ShapeDtypeStruct((length, HEAD_COLS), BF),
            jax.ShapeDtypeStruct((len(GATE_EARLY),) + gate_sent.shape[1:], BF),
            out_half,
            jax.ShapeDtypeStruct(gate_sent.shape, BF),
            jax.ShapeDtypeStruct(gate_sent.shape, BF),
            jax.ShapeDtypeStruct(down_sent.shape, BF),
            jax.ShapeDtypeStruct((2 * (PLANES - 1),) + down_sent.shape[1:], BF),
            jax.ShapeDtypeStruct(mixed[0].shape, BF),
        ],
        scratch_shapes=[
            pltpu.VMEM(value.shape, value.dtype)
            for value in (qkv, out, cosine, sine, branch, attended, down[0], mixed[1], mixed[2])
            + (gate_sent, gate_sent, down_sent)
        ]
        + [
            pltpu.VMEM((2 * (PLANES - 1),) + down_sent.shape[1:], BF),
            dma((12,)),
            dma((6,)),
            pltpu.VMEM(out_shape.shape, BF),
            pltpu.VMEM(out_shape.shape, BF),
            pltpu.VMEM(out_shape.shape, BF),
            pltpu.VMEM(out_half.shape, BF),
            pltpu.VMEM(out_half.shape, BF),
            dma((2, 2)),
            pltpu.VMEM((PLANES - 1,) + down_sent.shape[1:], BF),
            pltpu.VMEM(mixed[0].shape, BF),
            dma((2, 2 * (PLANES - 1))),
            pltpu.VMEM((4 * mixed[0].shape[0], up[0].shape[2]), BF),
            pltpu.VMEM((4 * mixed[0].shape[0], model), BF),
            dma((2, 2)),
            dma((8,)),
            pltpu.VMEM((model, 4 * HD), BF),
            pltpu.VMEM(rows_in.shape, BF),
            pltpu.VMEM((LANES, length), BF),
            pltpu.VMEM((length, LANES), jnp.float32),
            pltpu.VMEM((length, LANES), jnp.float32),
            pltpu.VMEM((length, 4 * LANES), BF),
            dma((2, RANKS)),
            dma((2, len(DOWN_LATE) + len(GATE_EARLY))),
            dma((2, 1)),
            dma,
        ],
        compiler_params=pltpu.CompilerParams(collective_id=3, has_side_effects=True, vmem_limit_bytes=56 * 1024 * 1024),
    )(rows_in, qkv, out, lse, cosine, sine, pick, squeeze, down_sent, gate_sent, branch, attended, *up, *down, *mixed)


def pad_columns():
    half=HD//2
    lanes=np.arange(4*LANES); block=lanes//LANES; lane=lanes%LANES
    split=np.where(lane<half,lane,np.where((lane>=LANES//2)&(lane<LANES//2+half),lane-LANES//2+half,-1))
    plain=np.where(lane<HD,lane,-1)
    column=np.where(block<3,split,plain)
    return np.where(column>=0,column+block*HD,-1)

CORES, LINES, PLANES = 2, 2, 4
DOWN_EARLY, DOWN_LATE, GATE_EARLY = (3, 0, 2), (1,), (3, 0, 2)
CHIPS = LINES * PLANES
RANKS = CORES * CHIPS


def swap_fsdp(value):
    return lax.ppermute(value, "fsdp", [(0, 1), (1, 0)])


def swap_ctx(value, bit):
    return lax.ppermute(value, "ctx", [(i, i ^ bit) for i in range(RANKS)])


def swap_core(value):
    return swap_ctx(value, 1)


def swap_line(value):
    return swap_ctx(value, CORES)


def plane_up(value, sources):
    step = CORES * LINES
    return lax.ppermute(value, "ctx", [(z * step + i, z * step + step + i) for z in sources for i in range(step)])


def plane_down(value, sources):
    step = CORES * LINES
    return lax.ppermute(value, "ctx", [(z * step + i, z * step - step + i) for z in sources for i in range(step)])


def at(value, index, axis=0):
    return lax.dynamic_index_in_dim(value, index, axis, keepdims=False)


def in_order(which, mine, other):
    first = which == 0
    return jnp.concatenate([jnp.where(first, mine, other), jnp.where(first, other, mine)], axis=0)


def after(value, earlier):
    return lax.optimization_barrier((value, earlier))[0]


def rope_rows():
    lane = np.arange(LANES)
    half = LANES // 2
    entry = np.where(lane < half, lane, lane - half)
    used = entry < HD // 2
    rate = 1.0 / ROPE_BASE ** (jnp.asarray(entry, jnp.float32) * 2.0 / HD)
    factors = np.stack([used, np.where(lane < half, -1.0, 1.0) * used] + [0 * lane] * 5).astype(np.float32)
    return jnp.concatenate([rate[None], jnp.asarray(factors)], axis=0)


def mlp_kernel(
    kept, normed, grad_rows, gate_a, gate_b, up_a, up_b, gate_far, up_far, down_a, down_b, down_far, *refs
):
    sources, refs = refs[: len(kept)], refs[len(kept) :]
    inner_ref, grad_gate_ref, grad_up_ref, mixed_ref, back_ref = refs[:5]
    targets, refs = refs[5 : 5 + len(kept)], refs[5 + len(kept) :]
    down, mixed_acc, back_acc = refs[:3]
    step = pl.program_id(0)
    half_steps = pl.num_programs(0) // 2
    side = lax.axis_index("fsdp")
    if kept:
        rank = lax.axis_index("ctx")
        core = lax.rem(rank, CORES)
        other_core = rank + 1 - 2 * core
        copies = [
            ctx_copy(source.at[1 - core] if halved else source, target, refs[3], number, other_core)
            for number, (source, target, halved) in enumerate(zip(sources[:-1], targets[:-1], kept))
        ]
        per = sources[-1].shape[0] // CORES
        part = pl.ds(pl.multiple_of(core * per, 16), per)
        cross = side_copy(sources[-1].at[part], targets[-1].at[part], refs[3], len(kept) - 1, 1 - side)
        onward = ctx_copy(targets[-1].at[part], targets[-1].at[part], refs[3], len(kept), other_core)

        @pl.when(step == 0)
        def _():
            barrier = pltpu.get_barrier_semaphore()
            pl.semaphore_signal(barrier, inc=1, device_id={"ctx": other_core}, device_id_type=pl.DeviceIdType.MESH)
            pl.semaphore_signal(barrier, inc=1, device_id={"fsdp": 1 - side}, device_id_type=pl.DeviceIdType.MESH)
            pl.semaphore_wait(barrier, 2)
            for copy in copies + [cross]:
                copy.start()

        @pl.when(step == 2 * half_steps - 1)
        def _():
            cross.wait()
            onward.start()
            for copy in copies + [onward]:
                copy.wait()

    depth = gate_a.shape[0]
    near = pl.ds(pl.multiple_of(side * depth, LANES), depth)
    far = pl.ds(pl.multiple_of((1 - side) * depth, LANES), depth)

    @pl.when(step == 0)
    def _():
        mixed_acc[...] = jnp.zeros_like(mixed_acc)
        back_acc[...] = jnp.zeros_like(back_acc)

    @pl.when(step < half_steps)
    def _():
        down[:LANES, :] = down_a[...]
        down[LANES:, :] = down_b[...]

    @pl.when(step >= half_steps)
    def _():
        down[...] = down_far[...]

    gate_near = jnp.concatenate([gate_a[...], gate_b[...]], axis=1)
    up_near = jnp.concatenate([up_a[...], up_b[...]], axis=1)
    gate = nn(normed[:, near], gate_near) + nn(normed[:, far], gate_far[...])
    upper = nn(normed[:, near], up_near) + nn(normed[:, far], up_far[...])
    sigma = jax.nn.sigmoid(gate)
    active = gate * sigma
    inner = (active * upper).astype(BF)
    grad_inner = nt(grad_rows[...], down[...])
    grad_gate = (grad_inner * upper * sigma * (1.0 + gate * (1.0 - sigma))).astype(BF)
    grad_up = (grad_inner * active).astype(BF)
    for which in range(CORES):
        span = slice(which * LANES, (which + 1) * LANES)
        inner_ref[which] = inner[:, span]
        grad_gate_ref[which] = grad_gate[:, span]
        grad_up_ref[which] = grad_up[:, span]
    mixed_acc[...] += nn(inner, down[...])
    back_acc[:, near] += nt(grad_gate, gate_near) + nt(grad_up, up_near)
    back_acc[:, far] += nt(grad_gate, gate_far[...]) + nt(grad_up, up_far[...])

    @pl.when(step == 2 * half_steps - 1)
    def _():
        mixed_ref[...] = mixed_acc[...].astype(mixed_ref.dtype)
        back_ref[...] = back_acc[...].astype(back_ref.dtype)


def mlp_part(normed, grad_rows, weights, kind, halved=(), whole_rows=()):
    w_gate, w_up, far, w_down, down_far = weights
    rows, model = normed.shape
    depth, hidden = w_gate.shape
    half = hidden // 2
    steps = half // (2 * LANES)
    part = steps // 2
    kept = (True,) * len(halved) + (False,) * len(whole_rows)

    def side():
        return lax.axis_index("fsdp")

    def pair_of(j):
        return jnp.where(j < part, side() * part + j, (1 - side()) * part + j - part)

    def whole(shape):
        return pl.BlockSpec(shape, lambda j: (0, 0))

    def column(odd):
        return pl.BlockSpec((depth, LANES), lambda j: (0, 4 * pair_of(j) + 2 * odd + side()))

    def row(odd):
        return pl.BlockSpec((LANES, model), lambda j: (4 * jnp.minimum(j, part - 1) + 2 * odd + side(), 0))

    def far_column(which):
        return pl.BlockSpec((None, depth, 2 * LANES), lambda j: (which, 0, pair_of(j)))

    far_row = pl.BlockSpec((2 * LANES, model), lambda j: (jnp.maximum(j - part, 0), 0))

    def place(j):
        pair = pair_of(j)
        return (0, 0, lax.rem(pair, LINES) * PLANES + lax.div(pair, LINES))

    act = pl.BlockSpec((CORES, rows, LANES), place)
    act_shape = jax.ShapeDtypeStruct((CORES, rows, half // CORES), BF)
    hbm = pl.BlockSpec(memory_space=pl.ANY)
    params = dict(collective_id=5, has_side_effects=True) if kept else {}
    return pl.pallas_call(
        functools.partial(mlp_kernel, kept),
        grid=(steps,),
        in_specs=[
            whole((rows, model)), whole((rows, model)),
            column(0), column(1), column(0), column(1), far_column(0), far_column(1),
            row(0), row(1), far_row,
        ]
        + [hbm] * len(kept),
        out_specs=[act, act, act, whole((rows, model)), whole((rows, model))] + [hbm] * len(kept),
        out_shape=[act_shape, act_shape, act_shape]
        + [jax.ShapeDtypeStruct((rows, model), kind)] * 2
        + [jax.ShapeDtypeStruct(value.shape[1:], BF) for value in halved]
        + [jax.ShapeDtypeStruct(value.shape, BF) for value in whole_rows],
        scratch_shapes=[
            pltpu.VMEM((2 * LANES, model), BF),
            pltpu.VMEM((rows, model), jnp.float32),
            pltpu.VMEM((rows, model), jnp.float32),
        ]
        + ([pltpu.SemaphoreType.DMA((2, len(kept) + 1))] if kept else []),
        compiler_params=pltpu.CompilerParams(vmem_limit_bytes=VMEM_LIMIT, **params),
        cost_estimate=pl.CostEstimate(
            flops=12 * rows * model * half, bytes_accessed=6 * model * half, transcendentals=rows * half
        ),
    )(normed, grad_rows, w_gate, w_gate, w_up, w_up, far, far, w_down, w_down, down_far, *halved, *whole_rows)


def head_rows_of(info, number, out_near, out_far):
    heads = []
    for is_far in range(2):
        for at_plane in range(PLANES // 2):
            for at_core in range(CORES):
                plane = 2 * (info[0] if is_far == 0 else 1 - info[0]) + at_plane
                heads.append((plane, at_core, out_far if is_far else out_near, (2 * at_plane + at_core) * 2 * HD))
    return heads


def post_kernel(info, att, tokens, out_near, out_far, gain, resid_ref, normed_ref):
    width = att.shape[1]
    total = tokens[...].astype(jnp.float32)
    for plane, core, weight, first in head_rows_of(info, 0, out_near, out_far):
        both = [att[plane * CORES * LINES + seq * CORES + core] for seq in range(LINES)]
        for head in range(2):
            rows = jnp.concatenate([block[:, head * LANES : head * LANES + HD] for block in both], axis=0)
            total = total + nn(rows, weight[first + head * HD : first + (head + 1) * HD, :])
    resid_ref[...] = total
    normed_ref[...] = (normalize(total)[0] * gain[...]).astype(BF)


def local_call(kernel, info, operands, outs):
    def spec(shape):
        return pl.BlockSpec(shape, lambda i, info: (0,) * len(shape))

    return pl.pallas_call(
        kernel,
        grid_spec=pltpu.PrefetchScalarGridSpec(
            num_scalar_prefetch=1,
            grid=(1,),
            in_specs=[spec(operand.shape) for operand in operands],
            out_specs=[spec(out.shape) for out in outs],
        ),
        out_shape=outs,
        compiler_params=pltpu.CompilerParams(vmem_limit_bytes=VMEM_LIMIT),
    )(info, *operands)


def local_copies(pairs, sems, first=0):
    return [pltpu.make_async_copy(source, target, sems.at[first + i]) for i, (source, target) in enumerate(pairs)]


def start(copies):
    for copy in copies:
        copy.start()


def wait(copies):
    for copy in copies:
        copy.wait()


def chip_moves(jobs, core, other_core, core_sems, local_sems):
    moves = []
    for number, (target, parts, halved) in enumerate(jobs):
        rows = target.shape[0] // 4
        copies = []
        for which, source in enumerate(parts):
            place = target.at[pl.ds(which * rows, rows)]
            if source is None:
                copies.append(ctx_copy(parts[1].at[1 - core], place, core_sems, number, other_core))
            else:
                mine = source.at[core] if halved and which < 2 else source
                copies.append(pltpu.make_async_copy(mine, place, local_sems.at[4 * number + which]))
        moves.append(copies)
    return moves


def split_lines(source, normed, keep, sent, line):
    columns = keep.shape[1]
    for at_line in range(LINES):
        for at_plane in range(0, PLANES, 2):
            first = (at_line * PLANES + at_plane) * columns
            both = tn(source[:, first : first + 2 * columns], normed[...]).astype(BF)
            for i in range(2):
                block = both[i * columns : (i + 1) * columns]

                @pl.when(line == at_line)
                def _():
                    keep[at_plane + i] = block

                @pl.when(line != at_line)
                def _():
                    sent[at_plane + i] = block


def middle_kernel(
    back_far, inner_own, inner_far, inner_sib, gate_own, gate_far, gate_sib, normed_own, normed_far, normed_sib,
    normed_sib_far, cot_own, cot_far, cot_sib, cot_sib_far, back_in, resid_in, near_in, far_in, gain,
    down_keep, down_sent, down_first, gate_keep, gate_sent, grad_ref, branch_ref, att_ref, gain_ref,
    back_got, inner_all, gate_all, normed_all, cot_all, back_own, resid, out_near, out_far,
    side_sems, core_sems, local_sems, line_sems, load_sems,
):
    rank = lax.axis_index("ctx")
    side = lax.axis_index("fsdp")
    core = lax.rem(rank, CORES)
    line = lax.rem(lax.div(rank, CORES), LINES)
    other_line = rank + CORES * (1 - 2 * line)
    other_core = rank + 1 - 2 * core
    rows = normed_own.shape[0]
    greet(rank, side)
    cross = side_copy(back_far, back_got, side_sems, 0, 1 - side)
    cross.start()

    jobs = (
        (inner_all, (inner_own, inner_far, inner_sib, None), True),
        (cot_all, (cot_own, cot_far, cot_sib, cot_sib_far), False),
        (gate_all, (gate_own, gate_far, gate_sib, None), True),
        (normed_all, (normed_own, normed_far, normed_sib, normed_sib_far), False),
    )
    moves = chip_moves(jobs, core, other_core, core_sems, local_sems)
    loads = [
        pltpu.make_async_copy(source, target, load_sems.at[number])
        for number, (source, target) in enumerate(
            ((back_in, back_own), (resid_in, resid), (near_in, out_near), (far_in, out_far))
        )
    ]
    for copies in moves + [loads]:
        for copy in copies:
            copy.start()

    def landed(number):
        for copy in moves[number]:
            copy.wait()

    def lines(slot, number):
        return ctx_copy(down_sent.at[number], down_first.at[slot], line_sems, slot, other_line)

    landed(0)
    landed(1)
    per_chip = down_keep.shape[1]
    for at_plane in (3, 0, 2, 1):
        span = slice(at_plane * LINES * per_chip, (at_plane + 1) * LINES * per_chip)
        both = tn(cot_all[:, span], inner_all[...]).astype(BF)
        for at_line in range(LINES):
            block = both[at_line * per_chip : (at_line + 1) * per_chip]

            @pl.when(line == at_line)
            def _():
                down_keep[at_plane] = block

            @pl.when(line != at_line)
            def _():
                down_sent[at_plane] = block

        if at_plane in DOWN_EARLY:
            lines(DOWN_EARLY.index(at_plane), at_plane).start()

    landed(2)
    landed(3)
    split_lines(gate_all, normed_all, gate_keep, gate_sent, line)
    for copy in loads:
        copy.wait()
    cross.wait()
    grad_normed = back_own[...] + wide(back_got[...])
    unit, inv = normalize(resid[...])
    gain_ref[...] = jnp.sum(grad_normed * unit, axis=0, keepdims=True)
    grad = wide(cot_all[0:rows, :]) + norm_back(grad_normed, gain[...], unit, inv)
    grad_ref[...] = grad
    branch = grad.astype(BF)
    branch_ref[...] = branch
    width = att_ref.shape[1]
    blank = jnp.zeros((width, LANES - HD), BF)
    for plane, at_core, weight, first in head_rows_of((side,), 0, out_near, out_far):
        for head in range(2):
            back = nt(branch, weight[first + head * HD : first + (head + 1) * HD, :]).astype(BF)
            for seq in range(LINES):
                number = plane * CORES * LINES + seq * CORES + at_core
                att_ref[number, :, head * LANES : head * LANES + HD] = back[seq * width : (seq + 1) * width]
                att_ref[number, :, head * LANES + HD : (head + 1) * LANES] = blank
    for slot, number in enumerate(DOWN_EARLY):
        lines(slot, number).wait()


def middle(back_far, acts, normed, cot, back_own, resid, gain, out_near, out_far):
    rows, model = resid.shape
    half = acts[0].shape[2]
    per_chip, columns = model // CHIPS, half // CHIPS
    vmem = pl.BlockSpec(memory_space=pltpu.VMEM)
    hbm = pl.BlockSpec(memory_space=pl.ANY)
    dma = pltpu.SemaphoreType.DMA

    def low(*dims):
        return jax.ShapeDtypeStruct(dims, BF)

    outs = [
        low(PLANES, per_chip, half),
        low(PLANES, per_chip, half),
        low(len(DOWN_EARLY), per_chip, half),
        low(PLANES, columns, model),
        low(PLANES, columns, model),
        jax.ShapeDtypeStruct((rows, model), jnp.float32),
        low(rows, model),
        low(RANKS, rows // LINES, 2 * LANES),
        jax.ShapeDtypeStruct((1, model), jnp.float32),
    ]
    return pl.pallas_call(
        middle_kernel,
        in_specs=[hbm] * 19 + [vmem],
        out_specs=[vmem, vmem, hbm] + [vmem] * 6,
        out_shape=outs,
        scratch_shapes=[
            pltpu.VMEM((rows, model), BF),
            pltpu.VMEM((4 * rows, half), BF),
            pltpu.VMEM((4 * rows, half), BF),
            pltpu.VMEM((4 * rows, model), BF),
            pltpu.VMEM((4 * rows, model), BF),
            pltpu.VMEM((rows, model), jnp.float32),
            pltpu.VMEM((rows, model), jnp.float32),
            pltpu.VMEM(out_near.shape, BF),
            pltpu.VMEM(out_far.shape, BF),
            dma((2, 1)),
            dma((2, 4)),
            dma((16,)),
            dma((2, len(DOWN_EARLY))),
            dma((4,)),
        ],
        compiler_params=pltpu.CompilerParams(collective_id=4, has_side_effects=True, vmem_limit_bytes=VMEM_LIMIT),
    )(back_far, *acts, *normed, *cot, back_own, resid, out_near, out_far, gain)


def last_kernel(
    info, rows_in, tokens, gain, grad, query, key, value, query_far, key_far, value_far, thin, broad,
    out_ref, query_out, key_out, value_out, out_out, gate_out, up_out, down_out, total,
):
    side, core = info[0], info[1]
    half = query.shape[0]
    for is_far, weights in enumerate(((query, key, value), (query_far, key_far, value_far))):
        here = pl.ds(pl.multiple_of((side if is_far == 0 else 1 - side) * half, LANES), half)
        acc = 0.0
        for head in range(HK):
            first = head // CORES * CORES * LINES + head % CORES
            rows = jnp.concatenate([rows_in[first + seq * CORES] for seq in range(LINES)], axis=0)
            for weight, start, size in zip(weights, (0, 2 * HD, 3 * HD), (2 * HD, HD, HD)):
                acc = acc + nt(rows[:, start : start + size], weight[:, head * size : (head + 1) * size])
        total[:, here] = acc
    unit, inv = normalize(tokens[...].astype(jnp.float32))
    out_ref[...] = (grad[...] + norm_back(total[...], gain[...], unit, inv)).astype(BF)

    columns = gate_out.shape[1] // 2
    heads = wide(broad[4 * columns : 4 * columns + 2 * HD, :]).T
    query_out[...] = heads[:, :HD]
    key_out[...] = heads[:, HD : HD + HD // 2]
    value_out[...] = heads[:, HD + HD // 2 :]
    out_out[...] = wide(broad[4 * columns + 2 * HD :, :]).T
    for which, result in enumerate((gate_out, up_out)):
        for other in range(2):
            first = (2 * which + other) * columns
            place = pl.ds(pl.multiple_of((side if other == 0 else 1 - side) * columns, LANES), columns)
            result[:, place] = wide(broad[first : first + columns, :]).T
    span = thin.shape[2] // 4
    for which in range(2):
        at_core = core if which == 0 else 1 - core
        for at_line in range(LINES):
            for low in range(PLANES // 2):
                first = ((low * LINES + at_line) * CORES + at_core) * 2
                lanes = pl.ds(pl.multiple_of(at_line * 2 * span + side * span + low * LANES, LANES), LANES)
                block = wide(thin[which, :, lanes]).T
                down_out[pl.ds(pl.multiple_of((first + side) * LANES, LANES), LANES), :] = block
                lanes = slice((which * LINES + at_line) * span + low * LANES, (which * LINES + at_line) * span + (low + 1) * LANES)
                block = wide(thin[2, :, lanes]).T
                down_out[pl.ds(pl.multiple_of((first + 1 - side) * LANES, LANES), LANES), :] = block


def gather_kernel(
    tokens, head_in, w_gate, w_up, w_out, angle_ref, seq_out, head_out, far, out_far, cos_ref, sin_ref, sems_in, sems_up, sems_down, sems_core, weight_sems, column_sems, group_sems, local_sem
):
    rank = lax.axis_index("ctx")
    side = lax.axis_index("fsdp")
    core = lax.rem(rank, CORES)
    line = lax.rem(lax.div(rank, CORES), LINES)
    plane = lax.div(rank, CORES * LINES)
    step_rank = CORES * LINES
    last = PLANES - 1
    other_line = rank + CORES * (1 - 2 * line)
    other_core = rank + 1 - 2 * core
    greet(rank, side)

    def spot(at_plane, at_line):
        return at_plane * step_rank + at_line * CORES + core

    def move(index, send_sems, to, source=None):
        return pltpu.make_async_remote_copy(
            src_ref=seq_out.at[index] if source is None else source,
            dst_ref=seq_out.at[index],
            send_sem=send_sems.at[index],
            recv_sem=sems_in.at[index],
            device_id={"ctx": to},
            device_id_type=pl.DeviceIdType.MESH,
        )

    near, across = spot(plane, line), spot(plane, 1 - line)
    mine = tokens.at[line]
    to_line = pltpu.make_async_remote_copy(
        src_ref=tokens.at[1 - line],
        dst_ref=seq_out.at[near],
        send_sem=local_sem.at[1],
        recv_sem=sems_in.at[near],
        device_id={"ctx": other_line},
        device_id_type=pl.DeviceIdType.MESH,
    )
    landed_line = pltpu.make_async_remote_copy(
        src_ref=tokens.at[1 - line],
        dst_ref=seq_out.at[across],
        send_sem=local_sem.at[1],
        recv_sem=sems_in.at[across],
        device_id={"ctx": other_line},
        device_id_type=pl.DeviceIdType.MESH,
    )
    own = pltpu.make_async_copy(mine, seq_out.at[near], local_sem.at[0])

    def spread(index, up, down, source=None):
        if up:
            @pl.when(plane < last)
            def _():
                move(index, sems_up, rank + step_rank, source).start()

        if down:
            @pl.when(plane > 0)
            def _():
                move(index, sems_down, rank - step_rank, source).start()

        move(index, sems_core, other_core, source).start()

    to_line.start()
    spread(near, True, True, mine)
    own.start()

    head_cross = side_copy(head_in, head_out, weight_sems, 0, 1 - side)
    depth = w_gate.shape[0] // LINES
    rows = pl.ds(pl.multiple_of(line * depth, 16), depth)
    other_rows = pl.ds(pl.multiple_of((1 - line) * depth, 16), depth)
    groups = 4
    group_columns = far.shape[2] // groups
    per_group = group_columns // LANES

    def column(weight, number):
        there = pl.ds(number * LANES, LANES)
        here = pl.ds(pl.multiple_of((2 * number + 1 - side) * LANES, LANES), LANES)
        return side_copy(weight.at[rows, here], far.at[core, rows, there], column_sems, number, 1 - side)

    def send_group(group):
        for number in range(group * per_group, (group + 1) * per_group):
            @pl.when(core == 0)
            def _():
                column(w_gate, number).start()

            @pl.when(core != 0)
            def _():
                column(w_up, number).start()

    def group_copy(group, which_rows, kind, to):
        block = far.at[core, which_rows, pl.ds(group * group_columns, group_columns)]
        return ctx_copy(block, block, group_sems, kind * groups + group, to)

    def pass_group(group):
        for number in range(group * per_group, (group + 1) * per_group):
            column(w_gate, number).wait_recv()
        group_copy(group, rows, 0, other_line).start()
        group_copy(group, rows, 1, other_core).start()

    def pass_line(group):
        group_copy(group, rows, 0, other_line).wait_recv()
        group_copy(group, other_rows, 2, other_core).start()

    quarter = 2 * core + line
    out_rows = w_out.shape[0] // 4

    def out_slice(ref, which):
        return ref.at[pl.ds(pl.multiple_of(which * out_rows, 16), out_rows)]

    out_mine, out_got = out_slice(out_far, quarter), out_slice(out_far, 2 * core + 1 - line)
    out_cross = side_copy(out_slice(w_out, quarter), out_mine, weight_sems, 1, 1 - side)
    out_line = ctx_copy(out_mine, out_mine, weight_sems, 2, other_line)
    out_core = ctx_copy(out_mine, out_mine, weight_sems, 3, other_core)
    out_more = ctx_copy(out_got, out_got, weight_sems, 4, other_core)
    send_group(0)
    send_group(1)

    block = tokens.shape[1]

    @pl.loop(0, RANKS)
    def _(number):
        position = (number * block + lax.broadcasted_iota(jnp.int32, (block, LANES), 0)).astype(jnp.float32)
        angles = position * angle_ref[0:1, :]
        here = pl.ds(pl.multiple_of(number * block, block), block)
        cos_ref[here, :] = jnp.cos(angles) * angle_ref[1:2, :]
        sin_ref[here, :] = jnp.sin(angles) * angle_ref[2:3, :]

    def forward(index, up, down):
        move(index, sems_core, other_core).wait_recv()
        spread(index, up, down)

    landed_line.wait_recv()
    spread(across, True, True)

    def pass_on(away, at_line):
        @pl.when(plane >= away)
        def _():
            forward(spot(plane - away, at_line), True, False)

        @pl.when(plane + away <= last)
        def _():
            forward(spot(plane + away, at_line), False, True)

    pass_on(1, line)
    pass_group(0)
    send_group(2)
    pass_group(1)
    send_group(3)
    pass_on(1, 1 - line)
    pass_line(0)
    pass_on(2, line)
    pass_group(2)
    out_cross.start()
    pass_group(3)
    head_cross.start()
    pass_line(1)
    pass_on(2, 1 - line)
    pass_line(2)
    pass_on(3, line)
    out_cross.wait_recv()
    out_line.start()
    out_core.start()
    pass_line(3)
    pass_on(3, 1 - line)
    out_line.wait_recv()
    out_more.start()

    for at_plane in range(PLANES):
        for at_line in range(LINES):
            index = at_plane * step_rank + at_line * CORES + 1 - core
            move(index, sems_core, other_core).wait_recv()
    head_cross.wait_recv()
    out_core.wait_recv()
    out_more.wait_recv()
    for group in range(groups):
        group_copy(group, rows, 1, other_core).wait_recv()
        group_copy(group, other_rows, 2, other_core).wait_recv()

    own.wait()
    to_line.wait_send()
    for at_plane in range(PLANES):
        for at_line in range(LINES):
            index = at_plane * step_rank + at_line * CORES + core
            move(index, sems_core, other_core).wait_send()

            @pl.when((plane < last) & (at_plane <= plane))
            def _():
                move(index, sems_up, rank + step_rank).wait_send()

            @pl.when((plane > 0) & (at_plane >= plane))
            def _():
                move(index, sems_down, rank - step_rank).wait_send()

    for copy in (head_cross, out_cross, out_line, out_core, out_more):
        copy.wait_send()
    for number in range(groups * per_group):
        column(w_gate, number).wait_send()
    for group in range(groups):
        group_copy(group, rows, 0, other_line).wait_send()
        group_copy(group, rows, 1, other_core).wait_send()
        group_copy(group, other_rows, 2, other_core).wait_send()


def gather_all(tokens, head_rows, w_gate, w_up, w_out, angles):
    width, model = tokens.shape[1:]
    depth, hidden = w_gate.shape
    hbm = pl.BlockSpec(memory_space=pl.ANY)
    vmem = pl.BlockSpec(memory_space=pltpu.VMEM)
    dma = pltpu.SemaphoreType.DMA
    return pl.pallas_call(
        gather_kernel,
        in_specs=[hbm] * 5 + [vmem],
        out_specs=[hbm] * 4 + [vmem] * 2,
        out_shape=[
            jax.ShapeDtypeStruct((RANKS, width, model), BF),
            jax.ShapeDtypeStruct(head_rows.shape, BF),
            jax.ShapeDtypeStruct((2, depth, hidden // 2), BF),
            jax.ShapeDtypeStruct(w_out.shape, BF),
            jax.ShapeDtypeStruct((RANKS * width, LANES), jnp.float32),
            jax.ShapeDtypeStruct((RANKS * width, LANES), jnp.float32),
        ],
        scratch_shapes=[dma((RANKS,)), dma((RANKS,)), dma((RANKS,)), dma((RANKS,)), dma((2, 5)), dma((2, RANKS)), dma((2, 12)), dma((2,))],
        compiler_params=pltpu.CompilerParams(collective_id=1, has_side_effects=True, vmem_limit_bytes=VMEM_LIMIT),
    )(tokens, head_rows, w_gate, w_up, w_out, angles)


def ctx_copy(source, target, sems, number, rank):
    return pltpu.make_async_remote_copy(
        src_ref=source,
        dst_ref=target,
        send_sem=sems.at[0, number],
        recv_sem=sems.at[1, number],
        device_id={"ctx": rank},
        device_id_type=pl.DeviceIdType.MESH,
    )


def side_copy(source, target, sems, number, side):
    return pltpu.make_async_remote_copy(
        src_ref=source,
        dst_ref=target,
        send_sem=sems.at[0, number],
        recv_sem=sems.at[1, number],
        device_id={"fsdp": side},
        device_id_type=pl.DeviceIdType.MESH,
    )


def greet(rank, side):
    barrier = pltpu.get_barrier_semaphore()
    for away in range(1, RANKS):
        pl.semaphore_signal(
            barrier,
            inc=1,
            device_id={"ctx": lax.rem(rank + away, RANKS)},
            device_id_type=pl.DeviceIdType.MESH,
        )
    pl.semaphore_signal(barrier, inc=1, device_id={"fsdp": 1 - side}, device_id_type=pl.DeviceIdType.MESH)
    pl.semaphore_wait(barrier, RANKS)


def wide(value):
    return value.astype(jnp.float32)


@dataclasses.dataclass
class Weight:
    keep: Any
    got: Any
    acc: Any
    landed: Any
    number: int
    arrival: Any = None
    first: int = 0
    prior: Any = None


class Chain:
    def __init__(self, rank, plane, sems):
        self.rank, self.plane, self.sems = rank, plane, sems
        self.last = PLANES - 1

    def depth(self, direction):
        return self.plane if direction == 0 else self.last - self.plane

    def sends(self, direction, step):
        depth = self.depth(direction)
        return (depth <= step) & (depth < self.last)

    def takes(self, direction, step):
        depth = self.depth(direction)
        return (depth >= 1) & (depth <= step + 1)

    def message(self, weight, direction, step):
        slot = direction * self.last + step
        target = self.rank + CORES * LINES * (1 - 2 * direction)
        place = jnp.clip(step - direction * (self.last - self.plane), 0, self.last - 1)
        number = weight.number * 2 * self.last + slot
        return ctx_copy(weight.acc.at[place], weight.landed.at[slot], self.sems, number, target)

    def receive(self, weight, step):
        for direction in range(2):
            @pl.when(self.takes(direction, step))
            def _():
                self.message(weight, direction, step).wait_recv()

    def hop(self, weight, step):
        for direction in range(2):
            piece = self.plane + (self.last - step) * (1 - 2 * direction)
            place = step - direction * (self.last - self.plane)
            sends = self.sends(direction, step)
            if weight.arrival is not None:
                weight.arrival(piece, sends)
            if step > weight.first:
                @pl.when(self.takes(direction, step - 1))
                def _():
                    self.message(weight, direction, step - 1).wait_recv()

            if step:
                landed = weight.landed if step > weight.first else weight.prior
                slot = direction * self.last + step - 1

                @pl.when(self.takes(direction, step - 1) & sends)
                def _():
                    total = wide(weight.keep[piece]) + wide(weight.got[piece]) + wide(landed[slot])
                    weight.acc[place] = total.astype(BF)

            @pl.when(self.depth(direction) == 0)
            def _():
                weight.acc[place] = (wide(weight.keep[piece]) + wide(weight.got[piece])).astype(BF)

            @pl.when(sends)
            def _():
                self.message(weight, direction, step).start()

    def finish(self, weight, result):
        last, plane = self.last, self.plane
        self.receive(weight, last - 1)
        if weight.arrival is not None:
            weight.arrival(plane, plane >= 0)
        base = wide(weight.keep[plane]) + wide(weight.got[plane])
        above, below = weight.landed.at[last - 1], weight.landed.at[2 * last - 1]

        @pl.when(plane == 0)
        def _():
            result[...] = (base + wide(below[...])).astype(BF)

        @pl.when(plane == last)
        def _():
            result[...] = (base + wide(above[...])).astype(BF)

        @pl.when((plane > 0) & (plane < last))
        def _():
            result[...] = (base + wide(above[...]) + wide(below[...])).astype(BF)

    def sent(self, weight, first, end):
        for step in range(first, end):
            for direction in range(2):
                @pl.when(self.sends(direction, step))
                def _():
                    self.message(weight, direction, step).wait_send()


def reduce_kernel(
    rows_hbm, down_keep_in, down_got_in, down_hops_in, gate_keep_in, gate_first, gate_sent, up_keep_in, up_sent, out_sum_in,
    normed_in, head_weight, attn_gain, mlp_part, w_value, w_query,
    rows_out, thin, broad, gains_out, value_far, query_far,
    rows_in, down_keep, down_got, down_hops, gate_keep, up_keep, out_sum, load_sems, gate_got, up_got, out_got, down_acc, gate_acc, up_acc, out_acc,
    down_in, gate_in, up_in, out_in, down_mine, down_theirs, gate_mine, up_mine,
    normed_buf, head_grad, head_sent, head_got, head_two, head_side, head_last, gain_buf, gain_in,
    exchange_sems, plane_sems, sems, line_sems, fetch_sems, local_sems,
):
    rank = lax.axis_index("ctx")
    side = lax.axis_index("fsdp")
    core = lax.rem(rank, CORES)
    line = lax.rem(lax.div(rank, CORES), LINES)
    plane = lax.div(rank, CORES * LINES)
    step_rank = CORES * LINES
    last = PLANES - 1
    other_line = rank + CORES * (1 - 2 * line)
    other_core = rank + 1 - 2 * core
    down_loads = local_copies(
        ((down_keep_in, down_keep), (down_got_in, down_got), (down_hops_in, down_hops)), load_sems
    )
    gate_loads = local_copies(
        [(gate_keep_in, gate_keep)] + [(gate_first.at[slot], gate_got.at[number]) for slot, number in enumerate(GATE_EARLY)],
        load_sems,
        3,
    )
    row_loads = local_copies(((rows_hbm, rows_in),), load_sems, 7)
    out_loads = local_copies(((out_sum_in, out_sum),), load_sems, 8)
    up_loads = local_copies(((up_keep_in, up_keep),), load_sems, 9)
    start(down_loads + gate_loads + row_loads + out_loads + up_loads)
    greet(rank, side)


    def gate_line(number):
        return ctx_copy(gate_sent.at[number], gate_got.at[number], line_sems, number, other_line)

    def up_line(number):
        return ctx_copy(up_sent.at[number], up_got.at[number], line_sems, PLANES + number, other_line)

    model = head_grad.shape[1]
    half = model // 2
    near = pl.ds(pl.multiple_of(side * half, LANES), half)
    far = pl.ds(pl.multiple_of((1 - side) * half, LANES), half)
    out_line = ctx_copy(out_sum_in.at[1 - line], out_got, sems, 18, other_line)
    head_line = ctx_copy(head_sent, head_got, sems, 2, other_line)

    def gate_arrival(piece, wanted):
        late = functools.reduce(jnp.logical_and, [piece != number for number in GATE_EARLY])

        @pl.when(wanted & late)
        def _():
            gate_line(piece).wait_recv()

    def up_arrival(piece, wanted):
        @pl.when(wanted)
        def _():
            up_line(piece).wait_recv()

    chain = Chain(rank, plane, plane_sems)
    hop, finish = chain.hop, chain.finish
    down = Weight(down_keep, down_got, down_acc, down_in, 0, None, 2, down_hops)
    gate = Weight(gate_keep, gate_got, gate_acc, gate_in, 1, gate_arrival)
    up = Weight(up_keep, up_got, up_acc, up_in, 2, up_arrival)
    out = Weight(out_sum.at[line], out_got, out_acc, out_in, 3)
    gate_late = [number for number in range(PLANES) if number not in GATE_EARLY]
    for number in gate_late:
        gate_line(number).start()
    for number in (3, 0, 2, 1):
        up_line(number).start()

    def row_copy(away):
        to = lax.rem(rank + away, RANKS)
        return ctx_copy(rows_hbm.at[to], rows_out.at[rank], exchange_sems, away, to)

    def send_rows(same):
        for away in range(1, RANKS):
            to = lax.rem(rank + away, RANKS)
            crossing = lax.rem(lax.div(to, CORES), LINES) != line

            @pl.when(crossing != same)
            def _():
                row_copy(away).start()

    send_rows(True)
    wait(down_loads)
    hop(down, 2)
    wait(gate_loads)
    hop(gate, 0)
    own = pltpu.make_async_copy(rows_hbm.at[rank], rows_out.at[rank], local_sems.at[2])
    own.start()
    out_line.start()
    fetched = []
    for number, (source, target) in enumerate(((w_value, value_far), (w_query, query_far))):
        per = source.shape[0] // CORES
        part = pl.ds(pl.multiple_of(core * per, 16), per)
        cross = side_copy(source.at[part], target.at[part], fetch_sems, number, 1 - side)
        fetched.append((cross, ctx_copy(target.at[part], target.at[part], fetch_sems, 2 + number, other_core)))

    gain_partners = (None, other_core, other_line, rank + step_rank * (1 - 2 * lax.rem(plane, 2)),
                     rank + 2 * step_rank * (1 - 2 * lax.div(plane, 2)))

    def gain_copy(number):
        if number == 0:
            return side_copy(gain_buf.at[0], gain_in.at[0], sems, 3, 1 - side)
        return ctx_copy(gain_buf.at[number], gain_in.at[number], sems, 3 + number, gain_partners[number])

    def gain_hop(number):
        if number:
            gain_copy(number - 1).wait_recv()
            gain_buf[number] = gain_buf[number - 1] + gain_in[number - 1]
        if number < 5:
            gain_copy(number).start()

    chunks = normed_in.shape[0] // normed_buf.shape[1]
    chunk_rows = normed_buf.shape[1]
    blocks = chunk_rows // rows_in.shape[1]

    def chunk_copy(number):
        return pltpu.make_async_copy(
            normed_in.at[pl.ds(number * chunk_rows, chunk_rows)], normed_buf.at[number % 2], local_sems.at[number % 2]
        )

    chunk_copy(0).start()
    wait(row_loads)
    for number in range(chunks):
        if number + 1 < chunks:
            chunk_copy(number + 1).start()
        chunk_copy(number).wait()
        rows = jnp.concatenate([rows_in[number * blocks + i] for i in range(blocks)], axis=0)
        term = nn(rows.T, normed_buf[number % 2])
        head_grad[...] = term if number == 0 else head_grad[...] + term
    gain_buf[0] = jnp.zeros_like(gain_buf[0])
    gain_buf[0, 0:1, :] = jnp.sum(head_grad[...] * wide(head_weight[...]), axis=0, keepdims=True) / attn_gain[...]
    gain_buf[0, 1:2, :] = mlp_part[...]

    def half_columns(which):
        quarter = HD // 2
        first = pl.ds(pl.multiple_of(which * HD, 16), HD)
        key = pl.ds(pl.multiple_of(2 * HD + which * quarter, 16), quarter)
        value = pl.ds(pl.multiple_of(3 * HD + which * quarter, 16), quarter)
        return jnp.concatenate([head_grad[first, :], head_grad[key, :], head_grad[value, :]], axis=0)

    head_sent[...] = half_columns(1 - line).astype(BF)
    gain_hop(0)
    gain_hop(1)

    for cross, _ in fetched:
        cross.start()
    wait(out_loads + up_loads)
    hop(gate, 1)
    hop(up, 0)
    send_rows(False)
    head_line.start()
    hop(gate, 2)
    out_line.wait_recv()
    hop(out, 0)
    hop(up, 1)
    head_line.wait_recv()
    head_two[...] = (half_columns(line) + wide(head_got[...])).astype(BF)
    head_cross = side_copy(head_two.at[:, far], head_side, sems, 8, 1 - side)
    head_cross.start()
    gain_hop(2)
    gain_hop(3)
    head_cross.wait_recv()
    head_last[...] = (wide(head_two[:, near]) + wide(head_side[...])).astype(BF)
    turned = rank - CORES * line - core + CORES * core + line
    head_out = broad.at[pl.ds(4 * gate_mine.shape[0], head_last.shape[0])]
    head_turn = ctx_copy(head_last, head_out, sems, 9, turned)

    @pl.when(line != core)
    def _():
        head_turn.start()

    @pl.when(line == core)
    def _():
        head_out[...] = head_last[...]

    hop(up, 2)
    gain_hop(4)
    finish(down, down_mine)
    per_core = down_mine.shape[0] // CORES
    theirs = pl.ds(pl.multiple_of((1 - core) * per_core, 16), per_core)
    mine = pl.ds(pl.multiple_of(core * per_core, 16), per_core)
    down_core = ctx_copy(down_mine.at[theirs], down_theirs, sems, 10, other_core)
    down_core.start()
    hop(out, 1)
    finish(gate, gate_mine)
    columns = gate_mine.shape[0]
    gate_cross = side_copy(gate_mine.at[:, far], broad.at[pl.ds(columns, columns)], sems, 11, 1 - side)
    gate_cross.start()

    gain_hop(5)
    for cross, onward in fetched:
        cross.wait_recv()
        onward.start()
    gains_out[...] = gain_buf[5]

    down_core.wait_recv()
    crosses = []
    span = down_mine.shape[1] // 4
    for which in range(2):
        block = down_mine.at[mine] if which == 0 else down_theirs
        for at_line in range(LINES):
            lanes = pl.ds(pl.multiple_of(at_line * 2 * span + (1 - side) * span, LANES), span)
            cross = side_copy(
                block.at[:, lanes],
                thin.at[2, :, pl.ds((which * LINES + at_line) * span, span)],
                sems,
                13 + which * LINES + at_line,
                1 - side,
            )
            cross.start()
            crosses.append(cross)

    hop(out, 2)
    finish(up, up_mine)
    up_cross = side_copy(up_mine.at[:, far], broad.at[pl.ds(3 * columns, columns)], sems, 12, 1 - side)
    up_cross.start()
    finish(out, broad.at[pl.ds(4 * columns + head_last.shape[0], out_got.shape[1])])
    @pl.when(line != core)
    def _():
        head_turn.wait()

    thin[0] = down_mine[mine, :]
    thin[1] = down_theirs[...]
    broad[0:columns, :] = gate_mine[:, near]
    broad[2 * columns : 3 * columns, :] = up_mine[:, near]
    for away in range(1, RANKS):
        row_copy(away).wait()
    own.wait()
    for cross in crosses + [gate_cross, up_cross]:
        cross.wait()
    for copy in (out_line, head_line, head_cross, down_core):
        copy.wait_send()
    for cross, onward in fetched:
        cross.wait_send()
        onward.wait()
    for number in range(5):
        gain_copy(number).wait_send()
    for number in range(PLANES):
        up_line(number).wait_send()
    for number in gate_late:
        gate_line(number).wait_send()
    for weight in (down, gate, up, out):
        chain.sent(weight, weight.first, last)


def reduce_all(rows_in, down, gate, up, out_sum, head, attn_weights):
    (down_keep, down_got, down_hops), (gate_keep, gate_first, gate_sent), (up_keep, up_sent) = down, gate, up
    normed, head_weight, attn_gain, mlp_part = head
    head_cols, model = head_weight.shape
    half = model // 2
    hops = 2 * (PLANES - 1)
    vmem = pl.BlockSpec(memory_space=pltpu.VMEM)
    hbm = pl.BlockSpec(memory_space=pl.ANY)
    dma = pltpu.SemaphoreType.DMA

    def piece(keep):
        return keep.shape[1:]

    def out(dims):
        return jax.ShapeDtypeStruct(dims, BF)

    def low(*dims):
        return pltpu.VMEM(dims, BF)

    down_rows, down_cols = piece(down_keep)
    columns = gate_keep.shape[1]
    out_half = out_sum.shape[1:]
    keeps = (down_keep, gate_keep, up_keep, jax.ShapeDtypeStruct(out_half, BF))
    return pl.pallas_call(
        reduce_kernel,
        in_specs=[hbm] * 11 + [vmem] * 3 + [hbm] * 2,
        out_specs=[hbm] + [vmem] * 3 + [hbm] * 2,
        out_shape=[
            out(rows_in.shape),
            out((3, down_rows // CORES, down_cols)),
            out((4 * columns + head_cols // 2 + out_half[1], half)),
            jax.ShapeDtypeStruct((8, model), jnp.float32),
        ]
        + [jax.ShapeDtypeStruct(weight.shape, BF) for weight in attn_weights],
        scratch_shapes=[low(*value.shape) for value in (rows_in, down_keep, down_got, down_hops, gate_keep, up_keep, out_sum)]
        + [
            dma((10,)),
            low(*gate_keep.shape),
            low(*up_keep.shape),
            low(*out_half),
        ]
        + [low(PLANES - 1, *piece(keep)) for keep in keeps]
        + [low(hops, *piece(keep)) for keep in keeps]
        + [
            low(down_rows, down_cols),
            low(down_rows // CORES, down_cols),
            low(columns, model),
            low(columns, model),
            low(2, normed.shape[0] // PLANES, model),
            pltpu.VMEM((head_cols, model), jnp.float32),
            low(head_cols // 2, model),
            low(head_cols // 2, model),
            low(head_cols // 2, model),
            low(head_cols // 2, half),
            low(head_cols // 2, half),
            pltpu.VMEM((6, 8, model), jnp.float32),
            pltpu.VMEM((5, 8, model), jnp.float32),
            dma((2, RANKS)),
            dma((2, 4 * hops)),
            dma((2, 19)),
            dma((2, 2 * PLANES)),
            dma((2, 4)),
            dma((3,)),
        ],
        compiler_params=pltpu.CompilerParams(collective_id=0, has_side_effects=True, vmem_limit_bytes=58 * 1024 * 1024),
    )(
        rows_in, down_keep, down_got, down_hops, gate_keep, gate_first, gate_sent, up_keep, up_sent, out_sum,
        normed, head_weight, attn_gain, mlp_part, *attn_weights,
    )


def local_last(info, operands):
    rows, model = operands[1].shape
    half = model // 2
    columns, hidden = (operands[11].shape[0] - 2 * HD - model // RANKS) // 4, operands[10].shape[2] * 2

    def spec(shape):
        return pl.BlockSpec(shape, lambda i, info: (0,) * len(shape))

    shapes = [
        (half, HD), (half, HD // 2), (half, HD // 2), (half, model // RANKS), (half, 2 * columns), (half, 2 * columns),
        (hidden, model // RANKS),
    ]
    outs = [jax.ShapeDtypeStruct((rows, model), BF)] + [jax.ShapeDtypeStruct(shape, jnp.float32) for shape in shapes]
    return pl.pallas_call(
        last_kernel,
        grid_spec=pltpu.PrefetchScalarGridSpec(
            num_scalar_prefetch=1,
            grid=(1,),
            in_specs=[spec(operand.shape) for operand in operands],
            out_specs=[spec(out.shape) for out in outs],
            scratch_shapes=[pltpu.VMEM((rows, model), jnp.float32)],
        ),
        out_shape=outs,
        compiler_params=pltpu.CompilerParams(vmem_limit_bytes=VMEM_LIMIT),
    )(info, *operands)


def head_shards(
    tokens, attn_gain, w_query, w_key, w_value, w_out, mlp_gain, w_gate, w_up, w_down, cotangent
):
    seqs, width, model = tokens.shape
    length = width * RANKS
    rows = seqs * width
    half_model = model // 2
    hidden = w_gate.shape[1]
    half_hidden = hidden // 2
    part_hidden = half_hidden // CORES
    chunk = hidden // (2 * RANKS)
    rank = lax.axis_index("ctx")
    side = lax.axis_index("fsdp")
    core = rank % CORES
    line = (rank // CORES) % LINES
    plane = rank // (CORES * LINES)
    head = plane * CORES + core
    low_side = side == 0
    info = jnp.stack([side, core, line]).astype(jnp.int32)
    pick = jnp.asarray((pad_columns()[:, None] == np.arange(HEAD_COLS)[None, :]).astype(np.float32)).astype(BF)

    lane = np.arange(2 * LANES)
    column = np.where(lane % LANES < HD, lane // LANES * HD + lane % LANES, -1)
    columns = np.stack([np.where(column < 0, -1, column + i * 2 * HD) for i in range(CORES)])
    squeeze = jnp.asarray((columns[:, :, None] == np.arange(4 * HD)).astype(np.float32)).astype(BF)

    def head_slice(weight, size):
        return lax.dynamic_slice_in_dim(weight, head * size, size, 1)

    head_rows = jnp.concatenate(
        [head_slice(w_query, 2 * HD), head_slice(w_key, HD), head_slice(w_value, HD)], axis=1
    )
    tokens_seq, head_far, far, out_far, cosine, sine = gather_all(tokens, head_rows, w_gate, w_up, w_out, rope_rows())
    grad_down = cotangent.reshape(rows, model)
    attn_row, mlp_row = attn_gain[None], mlp_gain[None]
    normed_seq, qkv, attended_seq, lse, attended_blocks, down_far, grad_down_other = head_forward(
        tokens_seq.reshape(length, model), attn_row, head_rows, head_far, pick, cosine, sine, w_down, grad_down
    )
    attended_seq = attended_seq.reshape(length, 2 * LANES)
    head_weight = in_order(side, head_rows, head_far)
    weights = (w_gate, w_up, far, w_down, down_far)
    token_rows = tokens.reshape(rows, model)
    resid, normed_two = local_call(
        post_kernel,
        info,
        (attended_blocks, token_rows, w_out, out_far, mlp_row),
        [jax.ShapeDtypeStruct((rows, model), jnp.float32), jax.ShapeDtypeStruct((rows, model), BF)],
    )

    normed_other = swap_fsdp(normed_two)
    inner_own, gate_own, up_own, mixed_own, back_own = mlp_part(normed_two, grad_down, weights, jnp.float32)
    normed_other = after(normed_other, mixed_own)
    inner_far, gate_far, up_far, mixed_far, back_far, inner_sib, gate_sib, up_sib, *sib, key_far = mlp_part(
        normed_other, grad_down_other, weights, BF,
        (inner_own, gate_own, up_own), (normed_two, normed_other, grad_down, grad_down_other, w_key),
    )
    (
        down_keep, down_sent, down_first, gate_keep, gate_sent,
        grad_resid, grad_branch, grad_attended, mlp_gain_part,
    ) = middle(
        back_far,
        (inner_own, inner_far, inner_sib, gate_own, gate_far, gate_sib),
        (normed_two, normed_other, *sib[:2]),
        (grad_down, grad_down_other, *sib[2:]),
        back_own, resid, mlp_row, w_out, out_far,
    )

    grad_qkv, gate_first, out_sum, up_keep, up_sent, down_got, down_hops, mixed = head_backward(
        grad_attended, qkv, attended_seq, lse, cosine, sine, pick, squeeze, down_sent, gate_sent, grad_branch, attended_blocks,
        (up_own, up_far, up_sib, normed_two, normed_other, *sib[:2]),
        (down_keep, down_first),
        (mixed_far, mixed_own, resid),
    )
    grad_rows, thin, broad, gains, value_far, query_far = reduce_all(
        grad_qkv.reshape(RANKS, width, HEAD_COLS),
        (down_keep, down_got, down_hops),
        (gate_keep, gate_first, gate_sent),
        (up_keep, up_sent),
        out_sum,
        (normed_seq, head_weight.T, attn_row, mlp_gain_part),
        (w_value, w_query),
    )

    tokens_grad, w_query_grad, w_key_grad, w_value_grad, w_out_grad, w_gate_grad, w_up_grad, w_down_grad = local_last(
        info,
        (
            grad_rows, token_rows, attn_row, grad_resid, w_query, w_key, w_value, query_far, key_far, value_far, thin, broad,
        ),
    )
    return (
        mixed.reshape(seqs, width, model),
        tokens_grad.reshape(seqs, width, model),
        gains[0],
        w_query_grad,
        w_key_grad,
        w_value_grad,
        w_out_grad,
        gains[1],
        w_gate_grad,
        w_up_grad,
        w_down_grad,
    )


def solution(mesh):
    by_heads = mesh.shape["ctx"] == RANKS and mesh.shape["fsdp"] == 2
    placed = (
        P("fsdp", "ctx", None),
        P(),
        P("fsdp", None),
        P("fsdp", None),
        P("fsdp", None),
        P("fsdp", None),
        P(),
        P("fsdp", None),
        P("fsdp", None),
        P("fsdp", None),
        P("fsdp", "ctx", None),
    )
    return jax.shard_map(
        head_shards if by_heads else shards,
        mesh=mesh,
        in_specs=placed,
        out_specs=(
            P("fsdp", "ctx", None),
            P("fsdp", "ctx", None),
            P(),
            P("fsdp", "ctx"),
            P("fsdp", "ctx"),
            P("fsdp", "ctx"),
            P("fsdp", "ctx"),
            P(),
            P("fsdp", "ctx"),
            P("fsdp", "ctx"),
            P("fsdp", "ctx"),
        ),
        check_vma=False,
    )
```

```python
import dataclasses
import functools
from typing import Any

import jax
import jax.numpy as jnp
import numpy as np
from jax import lax
from jax.experimental import pallas as pl
from jax.experimental.pallas import tpu as pltpu
from jax.sharding import PartitionSpec as P

HQ = 16
HK = 8
HD = 96
MICRO = 2
LANES = 128
HEAD_COLS = 4 * HD
BF = jnp.bfloat16
VMEM_LIMIT = 62 * 1024 * 1024


EPSILON = 1e-05
ROPE_BASE = 100000.0
MASK_FILL = -1e30


def matmul(left, right):
    return jnp.dot(left, right, preferred_element_type=jnp.float32)


def times_transposed(left, right):
    return lax.dot_general(
        left, right, (((1,), (1,)), ((), ())), preferred_element_type=jnp.float32
    )


def transposed_times(left, right):
    return lax.dot_general(
        left, right, (((0,), (0,)), ((), ())), preferred_element_type=jnp.float32
    )


def normalize(values):
    inv_rms = lax.rsqrt(jnp.mean(values * values, axis=-1, keepdims=True) + EPSILON)
    return (values * inv_rms, inv_rms)


def norm_back(grad_normed, gain_row, unit_rows, inv_rms):
    scaled = grad_normed * gain_row
    return inv_rms * (scaled - unit_rows * jnp.mean(scaled * unit_rows, axis=-1, keepdims=True))


def rotate(values, cosine, sine_rows):
    half_dim = values.shape[-1] // 2
    front = values[..., :half_dim]
    back_half = values[..., half_dim:]
    return jnp.concatenate(
        [front * cosine - back_half * sine_rows, back_half * cosine + front * sine_rows], axis=-1
    )


def attend_forward(query_rows, key_rows, value_rows, allowed):
    width_ct = query_rows.shape[0]
    grouped = query_rows.reshape(width_ct, HK, HQ // HK, HD)
    key_heads = key_rows.reshape(-1, HK, HD)
    value_heads = value_rows.reshape(-1, HK, HD)
    scores = jnp.einsum("cgrd,lgd->grcl", grouped, key_heads, preferred_element_type=jnp.float32)
    scores = jnp.where(allowed, scores, MASK_FILL)
    row_top = jnp.max(scores, axis=-1, keepdims=True)
    shifted_exp = jnp.exp(scores - row_top)
    row_total = jnp.sum(shifted_exp, axis=-1, keepdims=True)
    prob_low = (shifted_exp / row_total).astype(jnp.bfloat16)
    attended = jnp.einsum(
        "grcl,lgd->cgrd", prob_low, value_heads, preferred_element_type=jnp.float32
    )
    return (attended.reshape(width_ct, HQ * HD), row_top + jnp.log(row_total))


def attend_backward(query_rows, key_rows, value_rows, allowed, log_total, grad_rows):
    width_ct = query_rows.shape[0]
    grouped = query_rows.reshape(width_ct, HK, HQ // HK, HD)
    key_heads = key_rows.reshape(-1, HK, HD)
    value_heads = value_rows.reshape(-1, HK, HD)
    scores = jnp.einsum("cgrd,lgd->grcl", grouped, key_heads, preferred_element_type=jnp.float32)
    prob_full = jnp.exp(jnp.where(allowed, scores, MASK_FILL) - log_total)
    prob_low = prob_full.astype(jnp.bfloat16)
    grad_heads = grad_rows.reshape(width_ct, HK, HQ // HK, HD)
    grad_prob = jnp.einsum(
        "cgrd,lgd->grcl", grad_heads, value_heads, preferred_element_type=jnp.float32
    )
    row_inner = jnp.sum(prob_full * grad_prob, axis=-1, keepdims=True)
    grad_scores = (prob_full * (grad_prob - row_inner)).astype(jnp.bfloat16)
    grad_query = jnp.einsum(
        "grcl,lgd->cgrd", grad_scores, key_heads, preferred_element_type=jnp.float32
    )
    grad_key = jnp.einsum(
        "grcl,cgrd->lgd", grad_scores, grouped, preferred_element_type=jnp.float32
    )
    grad_value = jnp.einsum(
        "grcl,cgrd->lgd", prob_low, grad_heads, preferred_element_type=jnp.float32
    )
    return (
        grad_query.reshape(width_ct, HQ * HD),
        grad_key.reshape(-1, HK * HD),
        grad_value.reshape(-1, HK * HD),
        row_inner,
    )


def reduce_grad(full_grad):
    partial_grad = lax.psum_scatter(
        full_grad.astype(jnp.bfloat16), "fsdp", scatter_dimension=0, tiled=True
    )
    return lax.psum_scatter(partial_grad, "ctx", scatter_dimension=1, tiled=True).astype(
        jnp.float32
    )


def shards(
    tokens, attn_gain, w_query, w_key, w_value, w_out, mlp_gain, w_gate, w_up, w_down, cotangent
):
    seq_local, width_ct, model_width = tokens.shape
    seq_block = seq_local // MICRO
    row_count = seq_block * width_ct
    length = width_ct * lax.axis_size("ctx")
    half_dim = HD // 2
    offset = lax.axis_index("ctx") * width_ct
    query_pos = offset + jnp.arange(width_ct, dtype=jnp.int32)
    key_pos = jnp.arange(length, dtype=jnp.int32)
    allowed = key_pos[None, :] <= query_pos[:, None]
    inv_freq = 1.0 / ROPE_BASE ** (jnp.arange(half_dim, dtype=jnp.float32) * 2.0 / HD)
    angles = query_pos.astype(jnp.float32)[:, None] * inv_freq[None, :]
    cos_one = jnp.cos(angles)[:, None, :]
    sin_one = jnp.sin(angles)[:, None, :]
    cos_rows = jnp.tile(cos_one, (seq_block, 1, 1))
    sin_rows = jnp.tile(sin_one, (seq_block, 1, 1))
    head_scale = HD ** (-0.5)
    mixed_list, token_grad_list = ([], [])
    kept_normed_one, kept_grad_query, kept_grad_key, kept_grad_value = ([], [], [], [])
    kept_attended, kept_grad_branch, kept_normed_two = ([], [], [])
    kept_grad_gate, kept_grad_upper, kept_inner, kept_grad_down = ([], [], [], [])
    attn_gain_acc = jnp.zeros((model_width,), jnp.float32)
    mlp_gain_acc = jnp.zeros((model_width,), jnp.float32)
    for micro_at in range(MICRO):
        first_seq = micro_at * seq_block
        inputs = (
            tokens[first_seq : first_seq + seq_block]
            .reshape(row_count, model_width)
            .astype(jnp.float32)
        )
        outer_grad = (
            cotangent[first_seq : first_seq + seq_block]
            .reshape(row_count, model_width)
            .astype(jnp.float32)
        )
        attn_all = (
            lax.all_gather(w_query, "fsdp", axis=0, tiled=True),
            lax.all_gather(w_key, "fsdp", axis=0, tiled=True),
            lax.all_gather(w_value, "fsdp", axis=0, tiled=True),
            lax.all_gather(w_out, "fsdp", axis=0, tiled=True),
        )
        unit_one, inv_one = normalize(inputs)
        normed_one = (unit_one * attn_gain).astype(jnp.bfloat16)
        query_raw = matmul(normed_one, attn_all[0]).reshape(row_count, HQ, HD)
        key_raw = matmul(normed_one, attn_all[1]).reshape(row_count, HK, HD)
        value_raw = matmul(normed_one, attn_all[2])
        queries = (
            (rotate(query_raw, cos_rows, sin_rows) * head_scale)
            .astype(jnp.bfloat16)
            .reshape(seq_block, width_ct, HQ * HD)
        )
        keys = (
            rotate(key_raw, cos_rows, sin_rows)
            .astype(jnp.bfloat16)
            .reshape(seq_block, width_ct, HK * HD)
        )
        values = value_raw.astype(jnp.bfloat16).reshape(seq_block, width_ct, HK * HD)
        key_all, value_all = (
            lax.all_gather(keys, "ctx", axis=1, tiled=True),
            lax.all_gather(values, "ctx", axis=1, tiled=True),
        )
        attended_parts, lse_parts = ([], [])
        seq_at = 0
        attended_one, lse_one = attend_forward(
            queries[seq_at], key_all[seq_at], value_all[seq_at], allowed
        )
        attended_parts.append(attended_one)
        lse_parts.append(lse_one)
        attended = attended_parts[0].astype(jnp.bfloat16)
        resid = inputs + matmul(attended, attn_all[3])
        unit_two, inv_two = normalize(resid)
        normed_two = (unit_two * mlp_gain).astype(jnp.bfloat16)
        gate_proj = matmul(normed_two, lax.all_gather(w_gate, "fsdp", axis=0, tiled=True))
        up_proj = matmul(normed_two, lax.all_gather(w_up, "fsdp", axis=0, tiled=True))
        sigma = jax.nn.sigmoid(gate_proj)
        active = gate_proj * sigma
        hidden_act = (active * up_proj).astype(jnp.bfloat16)
        down_out = matmul(hidden_act, lax.all_gather(w_down, "fsdp", axis=0, tiled=True))
        mixed_list.append((resid + down_out).astype(jnp.bfloat16))
        grad_down = outer_grad.astype(jnp.bfloat16)
        grad_hidden = times_transposed(
            grad_down, lax.all_gather(w_down, "fsdp", axis=0, tiled=True)
        )
        grad_gate = (grad_hidden * up_proj * sigma * (1.0 + gate_proj * (1.0 - sigma))).astype(
            jnp.bfloat16
        )
        grad_upper = (grad_hidden * active).astype(jnp.bfloat16)
        pair_pieces = lax.all_gather((w_gate, w_up), "fsdp", axis=0, tiled=True)
        grad_normed_two = times_transposed(grad_gate, pair_pieces[0]) + times_transposed(
            grad_upper, pair_pieces[1]
        )
        mlp_gain_acc = mlp_gain_acc + jnp.sum(grad_normed_two * unit_two, axis=0)
        grad_resid = outer_grad + norm_back(grad_normed_two, mlp_gain, unit_two, inv_two)
        grad_branch = grad_resid.astype(jnp.bfloat16)
        attn_back = (
            lax.all_gather(w_query, "fsdp", axis=0, tiled=True),
            lax.all_gather(w_key, "fsdp", axis=0, tiled=True),
            lax.all_gather(w_value, "fsdp", axis=0, tiled=True),
            lax.all_gather(w_out, "fsdp", axis=0, tiled=True),
        )
        grad_attended = times_transposed(grad_branch, attn_back[3]).astype(jnp.bfloat16)
        key_back, value_back = (
            lax.all_gather(keys, "ctx", axis=1, tiled=True),
            lax.all_gather(values, "ctx", axis=1, tiled=True),
        )
        query_parts, key_parts, value_parts = ([], [], [])
        seq_at = 0
        query_one = queries[seq_at]
        key_one = key_back[seq_at]
        value_one = value_back[seq_at]
        lse_one = lse_parts[seq_at]
        grad_query, grad_key, grad_value, row_inner = attend_backward(
            query_one, key_one, value_one, allowed, lse_one, grad_attended
        )
        own_key = lax.psum_scatter(
            grad_key.astype(jnp.bfloat16), "ctx", scatter_dimension=0, tiled=True
        ).astype(jnp.float32)
        own_value = lax.psum_scatter(
            grad_value.astype(jnp.bfloat16), "ctx", scatter_dimension=0, tiled=True
        ).astype(jnp.float32)
        query_parts.append(
            rotate((grad_query * head_scale).reshape(width_ct, HQ, HD), cos_one, -sin_one).reshape(
                width_ct, HQ * HD
            )
        )
        key_parts.append(
            rotate(own_key.reshape(width_ct, HK, HD), cos_one, -sin_one).reshape(width_ct, HK * HD)
        )
        value_parts.append(own_value)
        grad_query_raw = query_parts[0].astype(jnp.bfloat16)
        grad_key_raw = key_parts[0].astype(jnp.bfloat16)
        grad_value_raw = value_parts[0].astype(jnp.bfloat16)
        grad_normed_one = (
            times_transposed(grad_query_raw, attn_back[0])
            + times_transposed(grad_key_raw, attn_back[1])
            + times_transposed(grad_value_raw, attn_back[2])
        )
        attn_gain_acc = attn_gain_acc + jnp.sum(grad_normed_one * unit_one, axis=0)
        token_grad_list.append(
            (grad_resid + norm_back(grad_normed_one, attn_gain, unit_one, inv_one)).astype(
                jnp.bfloat16
            )
        )
        kept_normed_one.append(normed_one)
        kept_grad_query.append(grad_query_raw)
        kept_grad_key.append(grad_key_raw)
        kept_grad_value.append(grad_value_raw)
        kept_attended.append(attended)
        kept_grad_branch.append(grad_branch)
        kept_normed_two.append(normed_two)
        kept_grad_gate.append(grad_gate)
        kept_grad_upper.append(grad_upper)
        kept_inner.append(hidden_act)
        kept_grad_down.append(grad_down)
    normed_one_all = jnp.concatenate(kept_normed_one, axis=0)
    normed_two_all = jnp.concatenate(kept_normed_two, axis=0)
    w_query_grad = reduce_grad(
        transposed_times(normed_one_all, jnp.concatenate(kept_grad_query, axis=0))
    )
    w_key_grad = reduce_grad(
        transposed_times(normed_one_all, jnp.concatenate(kept_grad_key, axis=0))
    )
    w_value_grad = reduce_grad(
        transposed_times(normed_one_all, jnp.concatenate(kept_grad_value, axis=0))
    )
    w_out_grad = reduce_grad(
        transposed_times(
            jnp.concatenate(kept_attended, axis=0), jnp.concatenate(kept_grad_branch, axis=0)
        )
    )
    w_gate_grad = reduce_grad(
        transposed_times(normed_two_all, jnp.concatenate(kept_grad_gate, axis=0))
    )
    w_up_grad = reduce_grad(
        transposed_times(normed_two_all, jnp.concatenate(kept_grad_upper, axis=0))
    )
    w_down_grad = reduce_grad(
        transposed_times(
            jnp.concatenate(kept_inner, axis=0), jnp.concatenate(kept_grad_down, axis=0)
        )
    )
    attn_gain_grad, mlp_gain_grad = lax.psum((attn_gain_acc, mlp_gain_acc), ("ctx", "fsdp"))
    mixed = jnp.concatenate(mixed_list, axis=0).reshape(seq_local, width_ct, model_width)
    tokens_grad = jnp.concatenate(token_grad_list, axis=0).reshape(seq_local, width_ct, model_width)
    return (
        mixed,
        tokens_grad,
        attn_gain_grad,
        w_query_grad,
        w_key_grad,
        w_value_grad,
        w_out_grad,
        mlp_gain_grad,
        w_gate_grad,
        w_up_grad,
        w_down_grad,
    )


def nt(a,b):
    return lax.dot_general(a,b,(((1,),(1,)),((),())),preferred_element_type=jnp.float32)
def tn(a,b):
    return lax.dot_general(a,b,(((0,),(0,)),((),())),preferred_element_type=jnp.float32)
def nn(a,b):
    return jnp.dot(a,b,preferred_element_type=jnp.float32)

def turn(v,cosine,sine):
    return v*cosine+pltpu.roll(v,LANES//2,1)*sine

def forward_kernel(
    tokens_ref, gain_ref, head_near, head_far, pick_ref, cos_ref, sin_ref, w_down, cot_in,
    normed_ref, qkv_ref, att_ref, lse_ref, rows_out, down_far, cot_out,
    weight_ref, key_ref, val_t_ref, exchange_sems, weight_sems, local_sem,
):
    at = pl.program_id(0)
    rank = lax.axis_index("ctx")
    side = lax.axis_index("fsdp")
    core = lax.rem(rank, CORES)
    line = lax.rem(lax.div(rank, CORES), LINES)
    other_line = rank + CORES * (1 - 2 * line)
    other_core = rank + 1 - 2 * core
    rows = tokens_ref.shape[0]
    width = att_ref.shape[1]
    blocks = rows // width
    here = pl.ds(pl.multiple_of(at * rows, rows), rows)

    chunk = w_down.shape[0] // RANKS
    quarter = 2 * core + line

    def down_slice(which, part):
        return down_far.at[pl.ds(pl.multiple_of((2 * which + part) * chunk, chunk), chunk)]

    def down_cross(part):
        number = 2 * quarter + part
        source = w_down.at[pl.ds(pl.multiple_of((2 * number + 1 - side) * chunk, chunk), chunk)]
        return side_copy(source, down_slice(quarter, part), weight_sems, part, 1 - side)

    def onward(kind, part):
        block = down_slice(2 * core + 1 - line if kind == 2 else quarter, part)
        return ctx_copy(block, block, weight_sems, 2 + 2 * kind + part, other_core if kind else other_line)

    cot_cross = side_copy(cot_in, cot_out, weight_sems, 8, 1 - side)

    def row_copy(away):
        to = lax.rem(rank + away, RANKS)
        return ctx_copy(att_ref.at[to], rows_out.at[rank], exchange_sems, away, to)

    @pl.when(at == 0)
    def _():
        greet(rank, side)
        for part in range(2):
            down_cross(part).start()
        cot_cross.start()
        val_t_ref[...] = jnp.zeros_like(val_t_ref)
        half = head_near.shape[0]
        for which, source in enumerate((head_near, head_far)):
            first = pl.ds(pl.multiple_of((side if which == 0 else 1 - side) * half, 16), half)
            weight_ref[first, :] = nt(source[...], pick_ref[...]).astype(BF)

    cosine, sine = cos_ref[...], sin_ref[...]
    unit, _ = normalize(tokens_ref[...].astype(jnp.float32))
    normed = (unit * gain_ref[...]).astype(BF)
    normed_ref[...] = normed
    raw = nn(normed, weight_ref[...])
    scale = HD**-0.5
    parts = [
        (turn(raw[:, j * LANES : (j + 1) * LANES], cosine, sine) * (scale if j < 2 else 1.0)).astype(BF) for j in range(3)
    ]
    value = raw[:, 3 * LANES :].astype(BF)
    for j in range(3):
        qkv_ref[:, j * LANES : (j + 1) * LANES] = parts[j]
    qkv_ref[:, 3 * LANES :] = value
    key_ref[here, :] = parts[2]
    val_t_ref[:, here] = value.T
    query = jnp.concatenate(parts[:2], axis=0)
    for band in range(key_ref.shape[0] // rows):
        @pl.when(at == band)
        def _():
            scores = nt(key_ref[0 : (band + 1) * rows, :], query)
            tail = scores[band * rows :, :]
            key_pos = lax.broadcasted_iota(jnp.int32, tail.shape, 0)
            query_pos = lax.broadcasted_iota(jnp.int32, tail.shape, 1) % rows
            tail = jnp.where(key_pos <= query_pos, tail, MASK_FILL)
            pieces = [scores[b * rows : (b + 1) * rows, :] for b in range(band)] + [tail]
            top = functools.reduce(jnp.maximum, [jnp.max(p, axis=0, keepdims=True) for p in pieces])
            total = 0.0
            acc = 0.0
            for b, p in enumerate(pieces):
                e = jnp.exp(p - top)
                total = total + jnp.sum(e, axis=0, keepdims=True)
                acc = acc + nn(val_t_ref[:, b * rows : (b + 1) * rows], e.astype(BF))
            acc = acc / total
            for h in range(2):
                turned = acc[:, h * rows : (h + 1) * rows].T.astype(BF)
                for i in range(blocks):
                    att_ref[band * blocks + i, :, h * LANES : (h + 1) * LANES] = turned[i * width : (i + 1) * width]
            lse_ref[0] = top + jnp.log(total)
            for i in range(blocks):
                to = band * blocks + i
                away = lax.rem(to - rank + RANKS, RANKS)

                @pl.when(away != 0)
                def _():
                    ctx_copy(att_ref.at[to], rows_out.at[rank], exchange_sems, away, to).start()

                @pl.when(away == 0)
                def _():
                    pltpu.make_async_copy(att_ref.at[to], rows_out.at[rank], local_sem).start()

    @pl.when(at == 1)
    def _():
        down_cross(0).wait_recv()
        onward(0, 0).start()
        onward(1, 0).start()

    @pl.when(at == 2)
    def _():
        down_cross(1).wait_recv()
        onward(0, 1).start()
        onward(1, 1).start()

    @pl.when(at == pl.num_programs(0) - 1)
    def _():
        for part in range(2):
            onward(0, part).wait_recv()
            onward(2, part).start()
        for part in range(2):
            onward(1, part).wait_recv()
            onward(2, part).wait_recv()
        for away in range(1, RANKS):
            row_copy(away).wait()
        pltpu.make_async_copy(att_ref.at[rank], rows_out.at[rank], local_sem).wait()
        cot_cross.wait()
        for part in range(2):
            down_cross(part).wait_send()
            for kind in range(3):
                onward(kind, part).wait_send()


def head_forward(tokens, gain, head_near, head_far, pick, cosine, sine, w_down, cotangent, rows=512):
    length, model = tokens.shape
    steps = length // rows
    width = length // RANKS
    hbm = pl.BlockSpec(memory_space=pl.ANY)
    dma = pltpu.SemaphoreType.DMA

    def block(cols):
        return pl.BlockSpec((rows, cols), lambda i: (i, 0))

    def whole(*dims):
        return pl.BlockSpec(dims, lambda i: (0,) * len(dims))

    return pl.pallas_call(
        forward_kernel,
        grid=(steps,),
        in_specs=[
            block(model), whole(1, model), whole(*head_near.shape), whole(*head_far.shape), whole(*pick.shape),
            block(LANES), block(LANES), hbm, hbm,
        ],
        out_specs=[
            block(model), block(4 * LANES), whole(RANKS, width, 2 * LANES),
            pl.BlockSpec((1, 1, 2 * rows), lambda i: (i, 0, 0)), hbm, hbm, hbm,
        ],
        out_shape=[
            jax.ShapeDtypeStruct((length, model), BF),
            jax.ShapeDtypeStruct((length, 4 * LANES), BF),
            jax.ShapeDtypeStruct((RANKS, width, 2 * LANES), BF),
            jax.ShapeDtypeStruct((steps, 1, 2 * rows), jnp.float32),
            jax.ShapeDtypeStruct((RANKS, width, 2 * LANES), BF),
            jax.ShapeDtypeStruct((w_down.shape[0] // 2, model), BF),
            jax.ShapeDtypeStruct(cotangent.shape, BF),
        ],
        scratch_shapes=[
            pltpu.VMEM((model, 4 * LANES), BF),
            pltpu.VMEM((length, LANES), BF),
            pltpu.VMEM((LANES, length), BF),
            dma((2, RANKS)),
            dma((2, 9)),
            dma,
        ],
        compiler_params=pltpu.CompilerParams(collective_id=2, has_side_effects=True, vmem_limit_bytes=VMEM_LIMIT),
    )(tokens, gain, head_near, head_far, pick, cosine, sine, w_down, cotangent)


def backward_kernel(
    rows_in, qkv_in, out_in, lse_ref, cos_in, sin_in, pick_ref, squeeze_ref, down_sent, gate_sent, branch_in, att_in,
    up_own, up_far, up_sib, normed_own, normed_far, normed_sib, normed_sib_far,
    down_keep_in, down_first, mixed_far, mixed_own_in, resid_in,
    res_ref, gate_first, out_sum_out, up_keep_out, up_sent_out, down_got_out, down_hops_out, mixed_ref,
    qkv_ref, out_ref, cos_ref, sin_ref, branch_ref, att_ref, down_keep, mixed_own, resid,
    up_keep, up_sent, down_got, down_in, load_sems, store_sems, out_keep, out_sent, out_got, out_side, out_sum, out_sems,
    down_acc, mixed_got, plane_sems, up_all, normed_all, core_sems, local_sems, weight_ref, grad_ref, key_t_ref, grad_key_ref, grad_val_ref, rows_ref, exchange_sems, line_sems, fetch_sems, local_sem,
):
    rank = lax.axis_index("ctx")
    side = lax.axis_index("fsdp")
    core = lax.rem(rank, CORES)
    line = lax.rem(lax.div(rank, CORES), LINES)
    plane = lax.div(rank, CORES * LINES)
    other_line = rank + CORES * (1 - 2 * line)
    other_core = rank + 1 - 2 * core
    first_loads = local_copies(((branch_in, branch_ref), (att_in, att_ref)), load_sems)
    head_loads = local_copies(
        ((qkv_in, qkv_ref), (out_in, out_ref), (cos_in, cos_ref), (sin_in, sin_ref)), load_sems, 2
    )
    down_loads = local_copies(
        [(down_keep_in, down_keep)] + [(down_first.at[slot], down_got.at[number]) for slot, number in enumerate(DOWN_EARLY)],
        load_sems,
        6,
    )
    mixed_loads = local_copies(((mixed_own_in, mixed_own), (resid_in, resid)), load_sems, 10)
    out_stores = local_copies(((out_sum, out_sum_out),), store_sems)
    up_stores = local_copies(((up_keep, up_keep_out), (up_sent, up_sent_out)), store_sems, 2)
    down_stores = local_copies(((down_got, down_got_out),), store_sems, 4)
    start(first_loads + head_loads)
    greet(rank, side)

    def row_copy(away):
        to = lax.rem(rank + away, RANKS)
        return ctx_copy(rows_in.at[to], grad_ref.at[rank], exchange_sems, away, to)

    own = pltpu.make_async_copy(rows_in.at[rank], grad_ref.at[rank], local_sem)
    own.start()
    for away in range(1, RANKS):
        row_copy(away).start()
    late = [
        ctx_copy(down_sent.at[number], down_got.at[number], line_sems, slot, other_line)
        for slot, number in enumerate(DOWN_LATE)
    ]
    lines = [
        ctx_copy(gate_sent.at[number], gate_first.at[slot], line_sems, len(DOWN_LATE) + slot, other_line)
        for slot, number in enumerate(GATE_EARLY)
    ]
    mixed_cross = side_copy(mixed_far, mixed_got, fetch_sems, 0, 1 - side)
    chain = Chain(rank, plane, plane_sems)
    down = Weight(down_keep, down_got, down_acc, down_in, 0)
    jobs = (
        (up_all, (up_own, up_far, up_sib, None), True),
        (normed_all, (normed_own, normed_far, normed_sib, normed_sib_far), False),
    )
    moves = chip_moves(jobs, core, other_core, core_sems, local_sems)
    start(late + lines + [mixed_cross] + moves[0] + moves[1] + down_loads + mixed_loads)

    length = qkv_ref.shape[0]
    width = grad_ref.shape[1]
    rows = CORES * width
    scale = HD**-0.5
    grad_key_ref[...] = jnp.zeros_like(grad_key_ref)
    grad_val_ref[...] = jnp.zeros_like(grad_val_ref)
    wait(first_loads + head_loads)
    for b in range(CHIPS):
        key_t_ref[:, b * rows : (b + 1) * rows] = qkv_ref[b * rows : (b + 1) * rows, 2 * LANES : 3 * LANES].T

    branch_t = branch_ref[...].T
    per_rank = out_keep.shape[2]
    for pair in range(HK // CORES):
        attended = 0.0
        for at_core in range(CORES):
            first = pair * CORES * LINES + at_core
            block = jnp.concatenate([att_ref[first + seq * CORES] for seq in range(LINES)], axis=0)
            attended = attended + nn(block, squeeze_ref[at_core])
        weight_ref[...] = nn(branch_t, attended.astype(BF)).astype(BF)
        columns = slice(pair * 4 * HD, (pair + 1) * 4 * HD)
        for at_plane in range(PLANES):
            for at_line in range(LINES):
                place = (at_plane * LINES + at_line) * CORES
                out_keep[at_line, at_plane, :, columns] = weight_ref[
                    pl.ds(pl.multiple_of((place + core) * per_rank, 16), per_rank), :
                ]
                out_sent[at_line, at_plane, :, columns] = weight_ref[
                    pl.ds(pl.multiple_of((place + 1 - core) * per_rank, 16), per_rank), :
                ]
    out_core = ctx_copy(out_sent, out_got, out_sems, 0, other_core)
    out_core.start()
    half_out = out_sum.shape[3]
    out_near = pl.ds(pl.multiple_of(side * half_out, LANES), half_out)
    out_away = pl.ds(pl.multiple_of((1 - side) * half_out, LANES), half_out)
    out_cross = side_copy(out_keep.at[:, :, :, out_away], out_side, out_sems, 1, 1 - side)

    wait(moves[0] + moves[1])
    split_lines(up_all, normed_all, up_keep, up_sent, line)
    out_core.wait()
    for at_line in range(LINES):
        for at_plane in range(PLANES):
            total = wide(out_keep[at_line, at_plane]) + wide(out_got[at_line, at_plane])
            out_keep[at_line, at_plane] = total.astype(BF)
    out_cross.start()
    start(up_stores)
    wait(down_loads)

    @pl.loop(0, CHIPS)
    def _(step):
        @pl.when(step == 3)
        def _():
            chain.hop(down, 0)

        @pl.when(step == 6)
        def _():
            for copy in late:
                copy.wait_recv()
            chain.hop(down, 1)

        turn_at = lax.div(step, LINES)
        low = jnp.where(plane < PLANES // 2, plane, PLANES - 1 - plane)
        nth = jnp.where((low == 1) & (turn_at < 2), 1 - turn_at, turn_at)
        plane_at = jnp.where(plane < PLANES // 2, nth, PLANES - 1 - nth)
        flip = lax.rem(step, LINES)
        chip = plane_at * LINES + jnp.where(flip == 0, line, 1 - line)
        here = pl.ds(pl.multiple_of(chip * rows, rows), rows)
        for at_core in range(CORES):
            source = chip * CORES + at_core
            away = lax.rem(rank - source + RANKS, RANKS)

            @pl.when(away == 0)
            def _():
                own.wait()

            @pl.when(away != 0)
            def _():
                ctx_copy(rows_in.at[source], grad_ref.at[source], exchange_sems, away, other_core).wait_recv()

        grad = jnp.concatenate(
            [grad_ref[chip * CORES + c, :, h * LANES : (h + 1) * LANES] for h in range(2) for c in range(CORES)], axis=0
        )
        query = jnp.concatenate([qkv_ref[here, 0:LANES], qkv_ref[here, LANES : 2 * LANES]], axis=0)
        out = jnp.concatenate([out_ref[here, 0:LANES], out_ref[here, LANES:]], axis=0)
        inner = jnp.sum((grad.astype(jnp.float32) * out.astype(jnp.float32)).T, axis=0, keepdims=True)
        lse = lse_ref[chip]
        for band in range(CHIPS):
            @pl.when(chip == band)
            def _():
                grad_query = 0.0
                for b in range(band + 1):
                    span = slice(b * rows, (b + 1) * rows)
                    scores = nt(qkv_ref[span, 2 * LANES : 3 * LANES], query)
                    prob = jnp.exp(scores - lse)
                    if b == band:
                        key_pos = lax.broadcasted_iota(jnp.int32, scores.shape, 0)
                        query_pos = lax.broadcasted_iota(jnp.int32, scores.shape, 1) % rows
                        prob = jnp.where(key_pos <= query_pos, prob, 0.0)
                    grad_prob = nt(qkv_ref[span, 3 * LANES :], grad)
                    grad_scores = (prob * (grad_prob - inner)).astype(BF)
                    grad_val_ref[span, :] += nn(prob.astype(BF), grad)
                    grad_key_ref[span, :] += nn(grad_scores, query)
                    grad_query = grad_query + nn(key_t_ref[:, span], grad_scores)
                for j in range(2):
                    back = grad_query[:, j * rows : (j + 1) * rows].T * scale
                    rows_ref[here, j * LANES : (j + 1) * LANES] = turn(back, cos_ref[here, :], -sin_ref[here, :]).astype(BF)

    for b in range(CHIPS):
        span = slice(b * rows, (b + 1) * rows)
        rows_ref[span, 2 * LANES : 3 * LANES] = turn(grad_key_ref[span, :], cos_ref[span, :], -sin_ref[span, :]).astype(BF)
        rows_ref[span, 3 * LANES :] = grad_val_ref[span, :].astype(BF)
        res_ref[span, :] = nn(rows_ref[span, :], pick_ref[...]).astype(BF)
    start(down_stores)
    out_cross.wait()
    for at_line in range(LINES):
        for at_plane in range(PLANES):
            total = wide(out_keep[at_line, at_plane, :, out_near]) + wide(out_side[at_line, at_plane])
            out_sum[at_line, at_plane] = total.astype(BF)
    start(out_stores)
    wait(mixed_loads)
    mixed_cross.wait()
    mixed_ref[...] = (resid[...] + mixed_own[...] + wide(mixed_got[...])).astype(BF)
    for away in range(1, RANKS):
        row_copy(away).wait_send()
    for copy in late:
        copy.wait_send()
    for copy in lines:
        copy.wait()
    chain.receive(down, 1)
    chain.sent(down, 0, 2)
    hops_store = local_copies(((down_in, down_hops_out),), store_sems, 5)
    start(hops_store)
    wait(out_stores + up_stores + down_stores + hops_store)


def head_backward(rows_in, qkv, out, lse, cosine, sine, pick, squeeze, down_sent, gate_sent, branch, attended, up, down, mixed):
    length = qkv.shape[0]
    rows = length // CHIPS
    model = branch.shape[1]
    out_shape = jax.ShapeDtypeStruct((LINES, PLANES, model // RANKS, HQ * HD), BF)
    out_half = jax.ShapeDtypeStruct((LINES, PLANES, model // RANKS, HK * HD), BF)
    lse = lse.reshape(-1, 2, lse.shape[2] // 2).transpose(1, 0, 2).reshape(2, CHIPS, rows)
    lse = lse.transpose(1, 0, 2).reshape(CHIPS, 1, 2 * rows)
    vmem = pl.BlockSpec(memory_space=pltpu.VMEM)
    hbm = pl.BlockSpec(memory_space=pl.ANY)
    dma = pltpu.SemaphoreType.DMA
    return pl.pallas_call(
        backward_kernel,
        in_specs=[hbm] * 3 + [vmem] + [hbm] * 2 + [vmem] * 2 + [hbm] * 16,
        out_specs=[vmem] + [hbm] * 6 + [vmem],
        out_shape=[
            jax.ShapeDtypeStruct((length, HEAD_COLS), BF),
            jax.ShapeDtypeStruct((len(GATE_EARLY),) + gate_sent.shape[1:], BF),
            out_half,
            jax.ShapeDtypeStruct(gate_sent.shape, BF),
            jax.ShapeDtypeStruct(gate_sent.shape, BF),
            jax.ShapeDtypeStruct(down_sent.shape, BF),
            jax.ShapeDtypeStruct((2 * (PLANES - 1),) + down_sent.shape[1:], BF),
            jax.ShapeDtypeStruct(mixed[0].shape, BF),
        ],
        scratch_shapes=[
            pltpu.VMEM(value.shape, value.dtype)
            for value in (qkv, out, cosine, sine, branch, attended, down[0], mixed[1], mixed[2])
            + (gate_sent, gate_sent, down_sent)
        ]
        + [
            pltpu.VMEM((2 * (PLANES - 1),) + down_sent.shape[1:], BF),
            dma((12,)),
            dma((6,)),
            pltpu.VMEM(out_shape.shape, BF),
            pltpu.VMEM(out_shape.shape, BF),
            pltpu.VMEM(out_shape.shape, BF),
            pltpu.VMEM(out_half.shape, BF),
            pltpu.VMEM(out_half.shape, BF),
            dma((2, 2)),
            pltpu.VMEM((PLANES - 1,) + down_sent.shape[1:], BF),
            pltpu.VMEM(mixed[0].shape, BF),
            dma((2, 2 * (PLANES - 1))),
            pltpu.VMEM((4 * mixed[0].shape[0], up[0].shape[2]), BF),
            pltpu.VMEM((4 * mixed[0].shape[0], model), BF),
            dma((2, 2)),
            dma((8,)),
            pltpu.VMEM((model, 4 * HD), BF),
            pltpu.VMEM(rows_in.shape, BF),
            pltpu.VMEM((LANES, length), BF),
            pltpu.VMEM((length, LANES), jnp.float32),
            pltpu.VMEM((length, LANES), jnp.float32),
            pltpu.VMEM((length, 4 * LANES), BF),
            dma((2, RANKS)),
            dma((2, len(DOWN_LATE) + len(GATE_EARLY))),
            dma((2, 1)),
            dma,
        ],
        compiler_params=pltpu.CompilerParams(collective_id=3, has_side_effects=True, vmem_limit_bytes=VMEM_LIMIT),
    )(rows_in, qkv, out, lse, cosine, sine, pick, squeeze, down_sent, gate_sent, branch, attended, *up, *down, *mixed)


def pad_columns():
    half=HD//2
    lanes=np.arange(4*LANES); block=lanes//LANES; lane=lanes%LANES
    split=np.where(lane<half,lane,np.where((lane>=LANES//2)&(lane<LANES//2+half),lane-LANES//2+half,-1))
    plain=np.where(lane<HD,lane,-1)
    column=np.where(block<3,split,plain)
    return np.where(column>=0,column+block*HD,-1)

CORES, LINES, PLANES = 2, 2, 4
DOWN_EARLY, DOWN_LATE, GATE_EARLY = (3, 0, 2), (1,), (3, 0, 2)
CHIPS = LINES * PLANES
RANKS = CORES * CHIPS


def swap_fsdp(value):
    return lax.ppermute(value, "fsdp", [(0, 1), (1, 0)])


def swap_ctx(value, bit):
    return lax.ppermute(value, "ctx", [(i, i ^ bit) for i in range(RANKS)])


def swap_core(value):
    return swap_ctx(value, 1)


def swap_line(value):
    return swap_ctx(value, CORES)


def plane_up(value, sources):
    step = CORES * LINES
    return lax.ppermute(value, "ctx", [(z * step + i, z * step + step + i) for z in sources for i in range(step)])


def plane_down(value, sources):
    step = CORES * LINES
    return lax.ppermute(value, "ctx", [(z * step + i, z * step - step + i) for z in sources for i in range(step)])


def at(value, index, axis=0):
    return lax.dynamic_index_in_dim(value, index, axis, keepdims=False)


def in_order(which, mine, other):
    first = which == 0
    return jnp.concatenate([jnp.where(first, mine, other), jnp.where(first, other, mine)], axis=0)


def after(value, earlier):
    return lax.optimization_barrier((value, earlier))[0]


def rope_rows():
    lane = np.arange(LANES)
    half = LANES // 2
    entry = np.where(lane < half, lane, lane - half)
    used = entry < HD // 2
    rate = 1.0 / ROPE_BASE ** (jnp.asarray(entry, jnp.float32) * 2.0 / HD)
    factors = np.stack([used, np.where(lane < half, -1.0, 1.0) * used] + [0 * lane] * 5).astype(np.float32)
    return jnp.concatenate([rate[None], jnp.asarray(factors)], axis=0)


HALF, WHOLE, SIDE, WEIGHT = range(4)


def mlp_kernel(
    kinds, normed, grad_rows, gate_a, gate_b, up_a, up_b, gate_far, up_far, down_a, down_b, down_far, *refs
):
    sources, refs = refs[: len(kinds)], refs[len(kinds) :]
    inner_ref, grad_gate_ref, grad_up_ref, mixed_ref, back_ref = refs[:5]
    targets, refs = refs[5 : 5 + len(kinds)], refs[5 + len(kinds) :]
    down, mixed_acc, back_acc, sems = refs
    step = pl.program_id(0)
    half_steps = pl.num_programs(0) // 2
    side = lax.axis_index("fsdp")
    rank = lax.axis_index("ctx")
    core = lax.rem(rank, CORES)
    other_core = rank + 1 - 2 * core
    copies, onwards = [], []
    for number, (source, target, kind) in enumerate(zip(sources, targets, kinds)):
        if kind == SIDE:
            copies.append(side_copy(source, target, sems, number, 1 - side))
        elif kind == WEIGHT:
            per = source.shape[0] // CORES
            part = pl.ds(pl.multiple_of(core * per, 16), per)
            copies.append(side_copy(source.at[part], target.at[part], sems, number, 1 - side))
            onwards.append(ctx_copy(target.at[part], target.at[part], sems, len(kinds) + len(onwards), other_core))
        else:
            copies.append(ctx_copy(source.at[1 - core] if kind == HALF else source, target, sems, number, other_core))

    @pl.when(step == 0)
    def _():
        barrier = pltpu.get_barrier_semaphore()
        pl.semaphore_signal(barrier, inc=1, device_id={"ctx": other_core}, device_id_type=pl.DeviceIdType.MESH)
        pl.semaphore_signal(barrier, inc=1, device_id={"fsdp": 1 - side}, device_id_type=pl.DeviceIdType.MESH)
        pl.semaphore_wait(barrier, 2)
        start(copies)

    @pl.when(step == 2 * half_steps - 1)
    def _():
        wait(copies)
        start(onwards)
        wait(onwards)

    depth = gate_a.shape[0]
    near = pl.ds(pl.multiple_of(side * depth, LANES), depth)
    far = pl.ds(pl.multiple_of((1 - side) * depth, LANES), depth)

    @pl.when(step == 0)
    def _():
        mixed_acc[...] = jnp.zeros_like(mixed_acc)
        back_acc[...] = jnp.zeros_like(back_acc)

    @pl.when(step < half_steps)
    def _():
        down[:LANES, :] = down_a[...]
        down[LANES:, :] = down_b[...]

    @pl.when(step >= half_steps)
    def _():
        down[...] = down_far[...]

    gate_near = jnp.concatenate([gate_a[...], gate_b[...]], axis=1)
    up_near = jnp.concatenate([up_a[...], up_b[...]], axis=1)
    gate = nn(normed[:, near], gate_near) + nn(normed[:, far], gate_far[...])
    upper = nn(normed[:, near], up_near) + nn(normed[:, far], up_far[...])
    sigma = jax.nn.sigmoid(gate)
    active = gate * sigma
    inner = (active * upper).astype(BF)
    grad_inner = nt(grad_rows[...], down[...])
    grad_gate = (grad_inner * upper * sigma * (1.0 + gate * (1.0 - sigma))).astype(BF)
    grad_up = (grad_inner * active).astype(BF)
    for which in range(CORES):
        span = slice(which * LANES, (which + 1) * LANES)
        inner_ref[which] = inner[:, span]
        grad_gate_ref[which] = grad_gate[:, span]
        grad_up_ref[which] = grad_up[:, span]
    mixed_acc[...] += nn(inner, down[...])
    back_acc[:, near] += nt(grad_gate, gate_near) + nt(grad_up, up_near)
    back_acc[:, far] += nt(grad_gate, gate_far[...]) + nt(grad_up, up_far[...])

    @pl.when(step == 2 * half_steps - 1)
    def _():
        mixed_ref[...] = mixed_acc[...].astype(mixed_ref.dtype)
        back_ref[...] = back_acc[...].astype(back_ref.dtype)


def mlp_part(normed, grad_rows, weights, kind, number, travels):
    w_gate, w_up, far, w_down, down_far = weights
    rows, model = normed.shape
    depth, hidden = w_gate.shape
    half = hidden // 2
    steps = half // (2 * LANES)
    part = steps // 2
    kinds = tuple(how for how, _ in travels)
    arrays = [value for _, value in travels]

    def side():
        return lax.axis_index("fsdp")

    def pair_of(j):
        return jnp.where(j < part, side() * part + j, (1 - side()) * part + j - part)

    def whole(shape):
        return pl.BlockSpec(shape, lambda j: (0, 0))

    def column(odd):
        return pl.BlockSpec((depth, LANES), lambda j: (0, 4 * pair_of(j) + 2 * odd + side()))

    def row(odd):
        return pl.BlockSpec((LANES, model), lambda j: (4 * jnp.minimum(j, part - 1) + 2 * odd + side(), 0))

    def far_column(which):
        return pl.BlockSpec((None, depth, 2 * LANES), lambda j: (which, 0, pair_of(j)))

    far_row = pl.BlockSpec((2 * LANES, model), lambda j: (jnp.maximum(j - part, 0), 0))

    def place(j):
        pair = pair_of(j)
        return (0, 0, lax.rem(pair, LINES) * PLANES + lax.div(pair, LINES))

    act = pl.BlockSpec((CORES, rows, LANES), place)
    act_shape = jax.ShapeDtypeStruct((CORES, rows, half // CORES), BF)
    hbm = pl.BlockSpec(memory_space=pl.ANY)
    return pl.pallas_call(
        functools.partial(mlp_kernel, kinds),
        grid=(steps,),
        in_specs=[
            whole((rows, model)), whole((rows, model)),
            column(0), column(1), column(0), column(1), far_column(0), far_column(1),
            row(0), row(1), far_row,
        ]
        + [hbm] * len(kinds),
        out_specs=[act, act, act, whole((rows, model)), whole((rows, model))] + [hbm] * len(kinds),
        out_shape=[act_shape, act_shape, act_shape]
        + [jax.ShapeDtypeStruct((rows, model), kind)] * 2
        + [jax.ShapeDtypeStruct(value.shape[how == HALF :], BF) for how, value in travels],
        scratch_shapes=[
            pltpu.VMEM((2 * LANES, model), BF),
            pltpu.VMEM((rows, model), jnp.float32),
            pltpu.VMEM((rows, model), jnp.float32),
            pltpu.SemaphoreType.DMA((2, len(kinds) + 1)),
        ],
        compiler_params=pltpu.CompilerParams(
            collective_id=number, has_side_effects=True, vmem_limit_bytes=VMEM_LIMIT
        ),
        cost_estimate=pl.CostEstimate(
            flops=12 * rows * model * half, bytes_accessed=6 * model * half, transcendentals=rows * half
        ),
    )(normed, grad_rows, w_gate, w_gate, w_up, w_up, far, far, w_down, w_down, down_far, *arrays)


def head_rows_of(info, number, out_near, out_far):
    heads = []
    for is_far in range(2):
        for at_plane in range(PLANES // 2):
            for at_core in range(CORES):
                plane = 2 * (info[0] if is_far == 0 else 1 - info[0]) + at_plane
                heads.append((plane, at_core, out_far if is_far else out_near, (2 * at_plane + at_core) * 2 * HD))
    return heads


def post_kernel(info, att, tokens, out_near, out_far, gain, resid_ref, normed_ref):
    width = att.shape[1]
    total = tokens[...].astype(jnp.float32)
    for plane, core, weight, first in head_rows_of(info, 0, out_near, out_far):
        both = [att[plane * CORES * LINES + seq * CORES + core] for seq in range(LINES)]
        for head in range(2):
            rows = jnp.concatenate([block[:, head * LANES : head * LANES + HD] for block in both], axis=0)
            total = total + nn(rows, weight[first + head * HD : first + (head + 1) * HD, :])
    resid_ref[...] = total
    normed_ref[...] = (normalize(total)[0] * gain[...]).astype(BF)


def local_call(kernel, info, operands, outs):
    def spec(shape):
        return pl.BlockSpec(shape, lambda i, info: (0,) * len(shape))

    return pl.pallas_call(
        kernel,
        grid_spec=pltpu.PrefetchScalarGridSpec(
            num_scalar_prefetch=1,
            grid=(1,),
            in_specs=[spec(operand.shape) for operand in operands],
            out_specs=[spec(out.shape) for out in outs],
        ),
        out_shape=outs,
        compiler_params=pltpu.CompilerParams(vmem_limit_bytes=VMEM_LIMIT),
    )(info, *operands)


def local_copies(pairs, sems, first=0):
    return [pltpu.make_async_copy(source, target, sems.at[first + i]) for i, (source, target) in enumerate(pairs)]


def start(copies):
    for copy in copies:
        copy.start()


def wait(copies):
    for copy in copies:
        copy.wait()


def chip_moves(jobs, core, other_core, core_sems, local_sems):
    moves = []
    for number, (target, parts, halved) in enumerate(jobs):
        rows = target.shape[0] // 4
        copies = []
        for which, source in enumerate(parts):
            place = target.at[pl.ds(which * rows, rows)]
            if source is None:
                copies.append(ctx_copy(parts[1].at[1 - core], place, core_sems, number, other_core))
            else:
                mine = source.at[core] if halved and which < 2 else source
                copies.append(pltpu.make_async_copy(mine, place, local_sems.at[4 * number + which]))
        moves.append(copies)
    return moves


def split_lines(source, normed, keep, sent, line):
    columns = keep.shape[1]
    for at_line in range(LINES):
        for at_plane in range(0, PLANES, 2):
            first = (at_line * PLANES + at_plane) * columns
            both = tn(source[:, first : first + 2 * columns], normed[...]).astype(BF)
            for i in range(2):
                block = both[i * columns : (i + 1) * columns]

                @pl.when(line == at_line)
                def _():
                    keep[at_plane + i] = block

                @pl.when(line != at_line)
                def _():
                    sent[at_plane + i] = block


def middle_kernel(
    back_far, inner_own, inner_far, inner_sib, gate_own, gate_far, gate_sib, normed_own, normed_far, normed_sib,
    normed_sib_far, cot_own, cot_far, cot_sib, cot_sib_far, back_in, resid_in, near_in, far_in, gain,
    down_keep, down_sent, down_first, gate_keep, gate_sent, grad_ref, branch_ref, att_ref, gain_ref,
    back_got, inner_all, gate_all, normed_all, cot_all, back_own, resid, out_near, out_far,
    side_sems, core_sems, local_sems, line_sems, load_sems,
):
    rank = lax.axis_index("ctx")
    side = lax.axis_index("fsdp")
    core = lax.rem(rank, CORES)
    line = lax.rem(lax.div(rank, CORES), LINES)
    other_line = rank + CORES * (1 - 2 * line)
    other_core = rank + 1 - 2 * core
    rows = normed_own.shape[0]
    greet(rank, side)
    cross = side_copy(back_far, back_got, side_sems, 0, 1 - side)
    cross.start()

    jobs = (
        (inner_all, (inner_own, inner_far, inner_sib, None), True),
        (cot_all, (cot_own, cot_far, cot_sib, cot_sib_far), False),
        (gate_all, (gate_own, gate_far, gate_sib, None), True),
        (normed_all, (normed_own, normed_far, normed_sib, normed_sib_far), False),
    )
    moves = chip_moves(jobs, core, other_core, core_sems, local_sems)
    loads = [
        pltpu.make_async_copy(source, target, load_sems.at[number])
        for number, (source, target) in enumerate(
            ((back_in, back_own), (resid_in, resid), (near_in, out_near), (far_in, out_far))
        )
    ]
    for copies in moves + [loads]:
        for copy in copies:
            copy.start()

    def landed(number):
        for copy in moves[number]:
            copy.wait()

    def lines(slot, number):
        return ctx_copy(down_sent.at[number], down_first.at[slot], line_sems, slot, other_line)

    landed(0)
    landed(1)
    per_chip = down_keep.shape[1]
    for at_plane in (3, 0, 2, 1):
        span = slice(at_plane * LINES * per_chip, (at_plane + 1) * LINES * per_chip)
        both = tn(cot_all[:, span], inner_all[...]).astype(BF)
        for at_line in range(LINES):
            block = both[at_line * per_chip : (at_line + 1) * per_chip]

            @pl.when(line == at_line)
            def _():
                down_keep[at_plane] = block

            @pl.when(line != at_line)
            def _():
                down_sent[at_plane] = block

        if at_plane in DOWN_EARLY:
            lines(DOWN_EARLY.index(at_plane), at_plane).start()

    landed(2)
    landed(3)
    split_lines(gate_all, normed_all, gate_keep, gate_sent, line)
    for copy in loads:
        copy.wait()
    cross.wait()
    grad_normed = back_own[...] + wide(back_got[...])
    unit, inv = normalize(resid[...])
    gain_ref[...] = jnp.sum(grad_normed * unit, axis=0, keepdims=True)
    grad = wide(cot_all[0:rows, :]) + norm_back(grad_normed, gain[...], unit, inv)
    grad_ref[...] = grad
    branch = grad.astype(BF)
    branch_ref[...] = branch
    width = att_ref.shape[1]
    blank = jnp.zeros((width, LANES - HD), BF)
    for plane, at_core, weight, first in head_rows_of((side,), 0, out_near, out_far):
        for head in range(2):
            back = nt(branch, weight[first + head * HD : first + (head + 1) * HD, :]).astype(BF)
            for seq in range(LINES):
                number = plane * CORES * LINES + seq * CORES + at_core
                att_ref[number, :, head * LANES : head * LANES + HD] = back[seq * width : (seq + 1) * width]
                att_ref[number, :, head * LANES + HD : (head + 1) * LANES] = blank
    for slot, number in enumerate(DOWN_EARLY):
        lines(slot, number).wait()


def middle(back_far, acts, normed, cot, back_own, resid, gain, out_near, out_far):
    rows, model = resid.shape
    half = acts[0].shape[2]
    per_chip, columns = model // CHIPS, half // CHIPS
    vmem = pl.BlockSpec(memory_space=pltpu.VMEM)
    hbm = pl.BlockSpec(memory_space=pl.ANY)
    dma = pltpu.SemaphoreType.DMA

    def low(*dims):
        return jax.ShapeDtypeStruct(dims, BF)

    outs = [
        low(PLANES, per_chip, half),
        low(PLANES, per_chip, half),
        low(len(DOWN_EARLY), per_chip, half),
        low(PLANES, columns, model),
        low(PLANES, columns, model),
        jax.ShapeDtypeStruct((rows, model), jnp.float32),
        low(rows, model),
        low(RANKS, rows // LINES, 2 * LANES),
        jax.ShapeDtypeStruct((1, model), jnp.float32),
    ]
    return pl.pallas_call(
        middle_kernel,
        in_specs=[hbm] * 19 + [vmem],
        out_specs=[vmem, vmem, hbm] + [vmem] * 6,
        out_shape=outs,
        scratch_shapes=[
            pltpu.VMEM((rows, model), BF),
            pltpu.VMEM((4 * rows, half), BF),
            pltpu.VMEM((4 * rows, half), BF),
            pltpu.VMEM((4 * rows, model), BF),
            pltpu.VMEM((4 * rows, model), BF),
            pltpu.VMEM((rows, model), jnp.float32),
            pltpu.VMEM((rows, model), jnp.float32),
            pltpu.VMEM(out_near.shape, BF),
            pltpu.VMEM(out_far.shape, BF),
            dma((2, 1)),
            dma((2, 4)),
            dma((16,)),
            dma((2, len(DOWN_EARLY))),
            dma((4,)),
        ],
        compiler_params=pltpu.CompilerParams(collective_id=4, has_side_effects=True, vmem_limit_bytes=VMEM_LIMIT),
    )(back_far, *acts, *normed, *cot, back_own, resid, out_near, out_far, gain)


def last_kernel(info, thin, broad, query_out, key_out, value_out, out_out, gate_out, up_out, down_out):
    side, core = info[0], info[1]
    columns = gate_out.shape[1] // 2
    first = 4 * columns
    for result in (query_out, key_out, value_out, out_out):
        result[...] = wide(broad[first : first + result.shape[0], :])
        first += result.shape[0]
    for which, result in enumerate((gate_out, up_out)):
        for other in range(2):
            first = (2 * which + other) * columns
            place = pl.ds(pl.multiple_of((side if other == 0 else 1 - side) * columns, LANES), columns)
            result[:, place] = wide(broad[first : first + columns, :]).T
    span = thin.shape[2] // 4
    for which in range(2):
        at_core = core if which == 0 else 1 - core
        for at_line in range(LINES):
            for low in range(PLANES // 2):
                first = ((low * LINES + at_line) * CORES + at_core) * 2
                lanes = pl.ds(pl.multiple_of(at_line * 2 * span + side * span + low * LANES, LANES), LANES)
                down_out[:, pl.ds(pl.multiple_of((first + side) * LANES, LANES), LANES)] = wide(thin[which, :, lanes])
                start_at = (which * LINES + at_line) * span + low * LANES
                block = wide(thin[2, :, start_at : start_at + LANES])
                down_out[:, pl.ds(pl.multiple_of((first + 1 - side) * LANES, LANES), LANES)] = block


def gather_kernel(
    tokens, w_query, w_key, w_value, w_gate, w_up, w_out, angle_ref, attn_gain, mlp_gain,
    seq_out, head_in, head_out, far, out_far, cos_ref, sin_ref, attn_row, mlp_row, weight_refs, load_sems, sems_in, sems_up, sems_down, sems_core, weight_sems, column_sems, group_sems, local_sem
):
    rank = lax.axis_index("ctx")
    side = lax.axis_index("fsdp")
    core = lax.rem(rank, CORES)
    line = lax.rem(lax.div(rank, CORES), LINES)
    plane = lax.div(rank, CORES * LINES)
    step_rank = CORES * LINES
    last = PLANES - 1
    other_line = rank + CORES * (1 - 2 * line)
    other_core = rank + 1 - 2 * core
    greet(rank, side)

    def spot(at_plane, at_line):
        return at_plane * step_rank + at_line * CORES + core

    def move(index, send_sems, to, source=None):
        return pltpu.make_async_remote_copy(
            src_ref=seq_out.at[index] if source is None else source,
            dst_ref=seq_out.at[index],
            send_sem=send_sems.at[index],
            recv_sem=sems_in.at[index],
            device_id={"ctx": to},
            device_id_type=pl.DeviceIdType.MESH,
        )

    near, across = spot(plane, line), spot(plane, 1 - line)
    mine = tokens.at[line]
    to_line = pltpu.make_async_remote_copy(
        src_ref=tokens.at[1 - line],
        dst_ref=seq_out.at[near],
        send_sem=local_sem.at[1],
        recv_sem=sems_in.at[near],
        device_id={"ctx": other_line},
        device_id_type=pl.DeviceIdType.MESH,
    )
    landed_line = pltpu.make_async_remote_copy(
        src_ref=tokens.at[1 - line],
        dst_ref=seq_out.at[across],
        send_sem=local_sem.at[1],
        recv_sem=sems_in.at[across],
        device_id={"ctx": other_line},
        device_id_type=pl.DeviceIdType.MESH,
    )
    own = pltpu.make_async_copy(mine, seq_out.at[near], local_sem.at[0])

    def spread(index, up, down, source=None):
        if up:
            @pl.when(plane < last)
            def _():
                move(index, sems_up, rank + step_rank, source).start()

        if down:
            @pl.when(plane > 0)
            def _():
                move(index, sems_down, rank - step_rank, source).start()

        move(index, sems_core, other_core, source).start()

    loads = local_copies(zip((w_query, w_key, w_value), weight_refs), load_sems)
    start(loads)
    to_line.start()
    spread(near, True, True, mine)
    own.start()

    head_cross = side_copy(head_in, head_out, weight_sems, 0, 1 - side)
    depth = w_gate.shape[0] // LINES
    rows = pl.ds(pl.multiple_of(line * depth, 16), depth)
    other_rows = pl.ds(pl.multiple_of((1 - line) * depth, 16), depth)
    groups = 4
    group_columns = far.shape[2] // groups
    per_group = group_columns // LANES

    def column(weight, number):
        there = pl.ds(number * LANES, LANES)
        here = pl.ds(pl.multiple_of((2 * number + 1 - side) * LANES, LANES), LANES)
        return side_copy(weight.at[rows, here], far.at[core, rows, there], column_sems, number, 1 - side)

    def send_group(group):
        for number in range(group * per_group, (group + 1) * per_group):
            @pl.when(core == 0)
            def _():
                column(w_gate, number).start()

            @pl.when(core != 0)
            def _():
                column(w_up, number).start()

    def group_copy(group, which_rows, kind, to):
        block = far.at[core, which_rows, pl.ds(group * group_columns, group_columns)]
        return ctx_copy(block, block, group_sems, kind * groups + group, to)

    def pass_group(group):
        for number in range(group * per_group, (group + 1) * per_group):
            column(w_gate, number).wait_recv()
        group_copy(group, rows, 0, other_line).start()
        group_copy(group, rows, 1, other_core).start()

    def pass_line(group):
        group_copy(group, rows, 0, other_line).wait_recv()
        group_copy(group, other_rows, 2, other_core).start()

    quarter = 2 * core + line
    out_rows = w_out.shape[0] // 4

    def out_slice(ref, which):
        return ref.at[pl.ds(pl.multiple_of(which * out_rows, 16), out_rows)]

    out_mine, out_got = out_slice(out_far, quarter), out_slice(out_far, 2 * core + 1 - line)
    out_cross = side_copy(out_slice(w_out, quarter), out_mine, weight_sems, 1, 1 - side)
    out_line = ctx_copy(out_mine, out_mine, weight_sems, 2, other_line)
    out_core = ctx_copy(out_mine, out_mine, weight_sems, 3, other_core)
    out_more = ctx_copy(out_got, out_got, weight_sems, 4, other_core)
    send_group(0)
    send_group(1)

    head = plane * CORES + core
    columns = head_in.shape[1]
    wait(loads)
    picked = 0.0
    for weight, first, size in zip(weight_refs, (0, 2 * HD, 3 * HD), (2 * HD, HD, HD)):
        source = lax.broadcasted_iota(jnp.int32, (weight.shape[1], columns), 0) - head * size
        target = lax.broadcasted_iota(jnp.int32, (weight.shape[1], columns), 1) - first
        chosen = jnp.where((source == target) & (target >= 0) & (target < size), 1.0, 0.0).astype(BF)
        picked = picked + nn(weight[...], chosen)
    head_in[...] = picked.astype(BF)
    for source, target in ((attn_gain, attn_row), (mlp_gain, mlp_row)):
        for part in range(source.shape[0]):
            target[0:1, part * LANES : (part + 1) * LANES] = source[part : part + 1, :]
    block = tokens.shape[1]

    @pl.loop(0, RANKS)
    def _(number):
        position = (number * block + lax.broadcasted_iota(jnp.int32, (block, LANES), 0)).astype(jnp.float32)
        angles = position * angle_ref[0:1, :]
        here = pl.ds(pl.multiple_of(number * block, block), block)
        cos_ref[here, :] = jnp.cos(angles) * angle_ref[1:2, :]
        sin_ref[here, :] = jnp.sin(angles) * angle_ref[2:3, :]

    def forward(index, up, down):
        move(index, sems_core, other_core).wait_recv()
        spread(index, up, down)

    landed_line.wait_recv()
    spread(across, True, True)

    def pass_on(away, at_line):
        @pl.when(plane >= away)
        def _():
            forward(spot(plane - away, at_line), True, False)

        @pl.when(plane + away <= last)
        def _():
            forward(spot(plane + away, at_line), False, True)

    pass_on(1, line)
    pass_group(0)
    send_group(2)
    pass_group(1)
    send_group(3)
    pass_on(1, 1 - line)
    pass_line(0)
    pass_on(2, line)
    pass_group(2)
    out_cross.start()
    pass_group(3)
    head_cross.start()
    pass_line(1)
    pass_on(2, 1 - line)
    pass_line(2)
    pass_on(3, line)
    out_cross.wait_recv()
    out_line.start()
    out_core.start()
    pass_line(3)
    pass_on(3, 1 - line)
    out_line.wait_recv()
    out_more.start()

    for at_plane in range(PLANES):
        for at_line in range(LINES):
            index = at_plane * step_rank + at_line * CORES + 1 - core
            move(index, sems_core, other_core).wait_recv()
    head_cross.wait_recv()
    out_core.wait_recv()
    out_more.wait_recv()
    for group in range(groups):
        group_copy(group, rows, 1, other_core).wait_recv()
        group_copy(group, other_rows, 2, other_core).wait_recv()

    own.wait()
    to_line.wait_send()
    for at_plane in range(PLANES):
        for at_line in range(LINES):
            index = at_plane * step_rank + at_line * CORES + core
            move(index, sems_core, other_core).wait_send()

            @pl.when((plane < last) & (at_plane <= plane))
            def _():
                move(index, sems_up, rank + step_rank).wait_send()

            @pl.when((plane > 0) & (at_plane >= plane))
            def _():
                move(index, sems_down, rank - step_rank).wait_send()

    for copy in (head_cross, out_cross, out_line, out_core, out_more):
        copy.wait_send()
    for number in range(groups * per_group):
        column(w_gate, number).wait_send()
    for group in range(groups):
        group_copy(group, rows, 0, other_line).wait_send()
        group_copy(group, rows, 1, other_core).wait_send()
        group_copy(group, other_rows, 2, other_core).wait_send()


def gather_all(tokens, attn_weights, w_gate, w_up, w_out, angles, gains):
    width, model = tokens.shape[1:]
    depth, hidden = w_gate.shape
    hbm = pl.BlockSpec(memory_space=pl.ANY)
    vmem = pl.BlockSpec(memory_space=pltpu.VMEM)
    dma = pltpu.SemaphoreType.DMA
    return pl.pallas_call(
        gather_kernel,
        in_specs=[hbm] * 7 + [vmem] * 3,
        out_specs=[hbm, vmem] + [hbm] * 3 + [vmem] * 4,
        out_shape=[
            jax.ShapeDtypeStruct((RANKS, width, model), BF),
            jax.ShapeDtypeStruct((depth, HEAD_COLS), BF),
            jax.ShapeDtypeStruct((depth, HEAD_COLS), BF),
            jax.ShapeDtypeStruct((2, depth, hidden // 2), BF),
            jax.ShapeDtypeStruct(w_out.shape, BF),
            jax.ShapeDtypeStruct((RANKS * width, LANES), jnp.float32),
            jax.ShapeDtypeStruct((RANKS * width, LANES), jnp.float32),
            jax.ShapeDtypeStruct((1, model), jnp.float32),
            jax.ShapeDtypeStruct((1, model), jnp.float32),
        ],
        scratch_shapes=[[pltpu.VMEM(weight.shape, BF) for weight in attn_weights], dma((3,)), dma((RANKS,)), dma((RANKS,)), dma((RANKS,)), dma((RANKS,)), dma((2, 5)), dma((2, RANKS)), dma((2, 12)), dma((2,))],
        compiler_params=pltpu.CompilerParams(collective_id=1, has_side_effects=True, vmem_limit_bytes=VMEM_LIMIT),
    )(tokens, *attn_weights, w_gate, w_up, w_out, angles, *gains)


def ctx_copy(source, target, sems, number, rank):
    return pltpu.make_async_remote_copy(
        src_ref=source,
        dst_ref=target,
        send_sem=sems.at[0, number],
        recv_sem=sems.at[1, number],
        device_id={"ctx": rank},
        device_id_type=pl.DeviceIdType.MESH,
    )


def side_copy(source, target, sems, number, side):
    return pltpu.make_async_remote_copy(
        src_ref=source,
        dst_ref=target,
        send_sem=sems.at[0, number],
        recv_sem=sems.at[1, number],
        device_id={"fsdp": side},
        device_id_type=pl.DeviceIdType.MESH,
    )


def greet(rank, side):
    barrier = pltpu.get_barrier_semaphore()
    for away in range(1, RANKS):
        pl.semaphore_signal(
            barrier,
            inc=1,
            device_id={"ctx": lax.rem(rank + away, RANKS)},
            device_id_type=pl.DeviceIdType.MESH,
        )
    pl.semaphore_signal(barrier, inc=1, device_id={"fsdp": 1 - side}, device_id_type=pl.DeviceIdType.MESH)
    pl.semaphore_wait(barrier, RANKS)


def wide(value):
    return value.astype(jnp.float32)


@dataclasses.dataclass
class Weight:
    keep: Any
    got: Any
    acc: Any
    landed: Any
    number: int
    arrival: Any = None
    first: int = 0
    prior: Any = None


class Chain:
    def __init__(self, rank, plane, sems):
        self.rank, self.plane, self.sems = rank, plane, sems
        self.last = PLANES - 1

    def depth(self, direction):
        return self.plane if direction == 0 else self.last - self.plane

    def sends(self, direction, step):
        depth = self.depth(direction)
        return (depth <= step) & (depth < self.last)

    def takes(self, direction, step):
        depth = self.depth(direction)
        return (depth >= 1) & (depth <= step + 1)

    def message(self, weight, direction, step):
        slot = direction * self.last + step
        target = self.rank + CORES * LINES * (1 - 2 * direction)
        place = jnp.clip(step - direction * (self.last - self.plane), 0, self.last - 1)
        number = weight.number * 2 * self.last + slot
        return ctx_copy(weight.acc.at[place], weight.landed.at[slot], self.sems, number, target)

    def receive(self, weight, step):
        for direction in range(2):
            @pl.when(self.takes(direction, step))
            def _():
                self.message(weight, direction, step).wait_recv()

    def hop(self, weight, step):
        for direction in range(2):
            piece = self.plane + (self.last - step) * (1 - 2 * direction)
            place = step - direction * (self.last - self.plane)
            sends = self.sends(direction, step)
            if weight.arrival is not None:
                weight.arrival(piece, sends)
            if step > weight.first:
                @pl.when(self.takes(direction, step - 1))
                def _():
                    self.message(weight, direction, step - 1).wait_recv()

            if step:
                landed = weight.landed if step > weight.first else weight.prior
                slot = direction * self.last + step - 1

                @pl.when(self.takes(direction, step - 1) & sends)
                def _():
                    total = wide(weight.keep[piece]) + wide(weight.got[piece]) + wide(landed[slot])
                    weight.acc[place] = total.astype(BF)

            @pl.when(self.depth(direction) == 0)
            def _():
                weight.acc[place] = (wide(weight.keep[piece]) + wide(weight.got[piece])).astype(BF)

            @pl.when(sends)
            def _():
                self.message(weight, direction, step).start()

    def finish(self, weight, result):
        last, plane = self.last, self.plane
        self.receive(weight, last - 1)
        if weight.arrival is not None:
            weight.arrival(plane, plane >= 0)
        base = wide(weight.keep[plane]) + wide(weight.got[plane])
        above, below = weight.landed.at[last - 1], weight.landed.at[2 * last - 1]

        @pl.when(plane == 0)
        def _():
            result[...] = (base + wide(below[...])).astype(BF)

        @pl.when(plane == last)
        def _():
            result[...] = (base + wide(above[...])).astype(BF)

        @pl.when((plane > 0) & (plane < last))
        def _():
            result[...] = (base + wide(above[...]) + wide(below[...])).astype(BF)

    def sent(self, weight, first, end):
        for step in range(first, end):
            for direction in range(2):
                @pl.when(self.sends(direction, step))
                def _():
                    self.message(weight, direction, step).wait_send()


def reduce_kernel(
    rows_hbm, down_keep_in, down_got_in, down_hops_in, gate_keep_in, gate_first, gate_sent, up_keep_in, up_sent, out_sum_in,
    normed_in, head_near, head_far, attn_gain, mlp_part, w_value, w_query, w_key, key_far, tokens_in, grad_in,
    tokens_grad, thin, broad, gains_out, value_far, query_far,
    rows_out, query_buf, key_buf, value_buf, tokens, grad, total, weight_sems, rows_in, down_keep, down_got, down_hops, gate_keep, up_keep, out_sum, load_sems, gate_got, up_got, out_got, down_acc, gate_acc, up_acc, out_acc,
    down_in, gate_in, up_in, out_in, down_mine, down_theirs, gate_mine, up_mine,
    normed_buf, head_grad, head_sum, head_sent, head_got, head_two, head_side, head_last, gain_buf, gain_in,
    exchange_sems, plane_sems, sems, line_sems, fetch_sems, local_sems,
):
    rank = lax.axis_index("ctx")
    side = lax.axis_index("fsdp")
    core = lax.rem(rank, CORES)
    line = lax.rem(lax.div(rank, CORES), LINES)
    plane = lax.div(rank, CORES * LINES)
    step_rank = CORES * LINES
    last = PLANES - 1
    other_line = rank + CORES * (1 - 2 * line)
    other_core = rank + 1 - 2 * core
    down_loads = local_copies(
        ((down_keep_in, down_keep), (down_got_in, down_got), (down_hops_in, down_hops)), load_sems
    )
    gate_loads = local_copies(
        [(gate_keep_in, gate_keep)] + [(gate_first.at[slot], gate_got.at[number]) for slot, number in enumerate(GATE_EARLY)],
        load_sems,
        3,
    )
    row_loads = local_copies(((rows_hbm, rows_in),), load_sems, 7)
    out_loads = local_copies(((out_sum_in, out_sum),), load_sems, 8)
    up_loads = local_copies(((up_keep_in, up_keep),), load_sems, 9)
    near_loads = local_copies(((w_query, query_buf), (w_key, key_buf), (w_value, value_buf)), weight_sems)
    far_loads = local_copies(((query_far, query_buf), (key_far, key_buf), (value_far, value_buf)), weight_sems, 3)
    token_loads = local_copies(((tokens_in, tokens), (grad_in, grad)), weight_sems, 6)
    start(down_loads + gate_loads + row_loads + out_loads + up_loads + near_loads + token_loads)
    greet(rank, side)


    def gate_line(number):
        return ctx_copy(gate_sent.at[number], gate_got.at[number], line_sems, number, other_line)

    def up_line(number):
        return ctx_copy(up_sent.at[number], up_got.at[number], line_sems, PLANES + number, other_line)

    model = head_grad.shape[1]
    half = model // 2
    near = pl.ds(pl.multiple_of(side * half, LANES), half)
    far = pl.ds(pl.multiple_of((1 - side) * half, LANES), half)
    out_line = ctx_copy(out_sum_in.at[1 - line], out_got, sems, 18, other_line)
    head_cross = side_copy(head_sent, head_side, sems, 8, 1 - side)
    head_line = ctx_copy(head_two, head_got, sems, 2, other_line)

    def gate_arrival(piece, wanted):
        late = functools.reduce(jnp.logical_and, [piece != number for number in GATE_EARLY])

        @pl.when(wanted & late)
        def _():
            gate_line(piece).wait_recv()

    def up_arrival(piece, wanted):
        @pl.when(wanted)
        def _():
            up_line(piece).wait_recv()

    chain = Chain(rank, plane, plane_sems)
    hop, finish = chain.hop, chain.finish
    down = Weight(down_keep, down_got, down_acc, down_in, 0, None, 2, down_hops)
    gate = Weight(gate_keep, gate_got, gate_acc, gate_in, 1, gate_arrival)
    up = Weight(up_keep, up_got, up_acc, up_in, 2, up_arrival)
    out = Weight(out_sum.at[line], out_got, out_acc, out_in, 3)
    gate_late = [number for number in range(PLANES) if number not in GATE_EARLY]
    for number in gate_late:
        gate_line(number).start()
    for number in (3, 0, 2, 1):
        up_line(number).start()

    def row_copy(away):
        to = lax.rem(rank + away, RANKS)
        return ctx_copy(rows_hbm.at[to], rows_out.at[rank], exchange_sems, away, to)

    def send_rows(same):
        for away in range(1, RANKS):
            to = lax.rem(rank + away, RANKS)
            crossing = lax.rem(lax.div(to, CORES), LINES) != line

            @pl.when(crossing != same)
            def _():
                row_copy(away).start()

    send_rows(True)
    send_rows(False)
    wait(down_loads)
    hop(down, 2)
    wait(gate_loads)
    hop(gate, 0)
    own = pltpu.make_async_copy(rows_hbm.at[rank], rows_out.at[rank], local_sems.at[2])
    own.start()
    out_line.start()
    fetched = []
    for number, (source, target) in enumerate(((w_value, value_far), (w_query, query_far))):
        per = source.shape[0] // CORES
        part = pl.ds(pl.multiple_of(core * per, 16), per)
        cross = side_copy(source.at[part], target.at[part], fetch_sems, number, 1 - side)
        fetched.append((cross, ctx_copy(target.at[part], target.at[part], fetch_sems, 2 + number, other_core)))

    gain_partners = (None, other_core, other_line, rank + step_rank * (1 - 2 * lax.rem(plane, 2)),
                     rank + 2 * step_rank * (1 - 2 * lax.div(plane, 2)))

    def gain_copy(number):
        if number == 0:
            return side_copy(gain_buf.at[0], gain_in.at[0], sems, 3, 1 - side)
        return ctx_copy(gain_buf.at[number], gain_in.at[number], sems, 3 + number, gain_partners[number])

    def gain_hop(number):
        if number:
            gain_copy(number - 1).wait_recv()
            gain_buf[number] = gain_buf[number - 1] + gain_in[number - 1]
        if number < 5:
            gain_copy(number).start()

    chunks = normed_in.shape[0] // normed_buf.shape[1]
    chunk_rows = normed_buf.shape[1]
    blocks = chunk_rows // rows_in.shape[1]

    def chunk_copy(number):
        return pltpu.make_async_copy(
            normed_in.at[pl.ds(number * chunk_rows, chunk_rows)], normed_buf.at[number % 2], local_sems.at[number % 2]
        )

    chunk_copy(0).start()
    wait(row_loads)
    for number in range(chunks):
        if number + 1 < chunks:
            chunk_copy(number + 1).start()
        chunk_copy(number).wait()
        rows = jnp.concatenate([rows_in[number * blocks + i] for i in range(blocks)], axis=0)
        term = nn(rows.T, normed_buf[number % 2])
        head_grad[...] = term if number == 0 else head_grad[...] + term
    gain_buf[0] = jnp.zeros_like(gain_buf[0])
    for lanes, weight in ((near, head_near), (far, head_far)):
        term = jnp.sum(head_grad[:, lanes] * wide(weight[...]).T, axis=0, keepdims=True)
        gain_buf[0, 0:1, lanes] = term / attn_gain[:, lanes]
    gain_buf[0, 1:2, :] = mlp_part[...]

    def half_columns(which):
        quarter = HD // 2
        first = pl.ds(pl.multiple_of(which * HD, 16), HD)
        key = pl.ds(pl.multiple_of(2 * HD + which * quarter, 16), quarter)
        value = pl.ds(pl.multiple_of(3 * HD + which * quarter, 16), quarter)
        return jnp.concatenate([head_sum[first, :], head_sum[key, :], head_sum[value, :]], axis=0)

    head_sent[...] = head_grad[:, far].astype(BF)
    head_cross.start()
    gain_hop(0)
    gain_hop(1)

    for cross, _ in fetched:
        cross.start()
    wait(out_loads + up_loads)
    hop(gate, 1)
    hop(up, 0)
    head_cross.wait_recv()
    head_sum[...] = head_grad[:, near] + wide(head_side[...])
    head_two[...] = half_columns(1 - line).astype(BF)
    head_line.start()
    hop(gate, 2)
    out_line.wait_recv()
    hop(out, 0)
    hop(up, 1)
    gain_hop(2)
    gain_hop(3)
    for cross, onward in fetched:
        cross.wait_recv()
        onward.start()
    for away in range(1, RANKS):
        row_copy(away).wait_recv()
    own.wait()

    def row_gradients(lanes):
        acc = 0.0
        for head in range(HK):
            first = head // CORES * CORES * LINES + head % CORES
            rows = jnp.concatenate([rows_out[first + seq * CORES] for seq in range(LINES)], axis=0)
            for weight, begin, size in ((query_buf, 0, 2 * HD), (key_buf, 2 * HD, HD), (value_buf, 3 * HD, HD)):
                acc = acc + nt(rows[:, begin : begin + size], weight[:, head * size : (head + 1) * size])
        total[:, lanes] = acc

    wait(near_loads)
    row_gradients(near)
    for _, onward in fetched:
        onward.wait_recv()
    start(far_loads)
    head_line.wait_recv()
    head_last[...] = (half_columns(line) + wide(head_got[...])).astype(BF)
    turned = rank - CORES * line - core + CORES * core + line
    head_out = broad.at[pl.ds(4 * gate_mine.shape[0], head_last.shape[0])]
    head_turn = ctx_copy(head_last, head_out, sems, 9, turned)

    @pl.when(line != core)
    def _():
        head_turn.start()

    @pl.when(line == core)
    def _():
        head_out[...] = head_last[...]

    hop(up, 2)
    gain_hop(4)
    finish(down, down_mine)
    per_core = down_mine.shape[0] // CORES
    theirs = pl.ds(pl.multiple_of((1 - core) * per_core, 16), per_core)
    mine = pl.ds(pl.multiple_of(core * per_core, 16), per_core)
    down_core = ctx_copy(down_mine.at[theirs], down_theirs, sems, 10, other_core)
    down_core.start()
    hop(out, 1)
    finish(gate, gate_mine)
    columns = gate_mine.shape[0]
    gate_cross = side_copy(gate_mine.at[:, far], broad.at[pl.ds(columns, columns)], sems, 11, 1 - side)
    gate_cross.start()

    gain_hop(5)
    gains_out[...] = gain_buf[5]

    down_core.wait_recv()
    crosses = []
    span = down_mine.shape[1] // 4
    for which in range(2):
        block = down_mine.at[mine] if which == 0 else down_theirs
        for at_line in range(LINES):
            lanes = pl.ds(pl.multiple_of(at_line * 2 * span + (1 - side) * span, LANES), span)
            cross = side_copy(
                block.at[:, lanes],
                thin.at[2, :, pl.ds((which * LINES + at_line) * span, span)],
                sems,
                13 + which * LINES + at_line,
                1 - side,
            )
            cross.start()
            crosses.append(cross)

    hop(out, 2)
    wait(far_loads + token_loads)
    row_gradients(far)
    unit, inv = normalize(wide(tokens[...]))
    tokens_grad[...] = (grad[...] + norm_back(total[...], attn_gain[...], unit, inv)).astype(BF)
    finish(up, up_mine)
    up_cross = side_copy(up_mine.at[:, far], broad.at[pl.ds(3 * columns, columns)], sems, 12, 1 - side)
    up_cross.start()
    finish(out, broad.at[pl.ds(4 * columns + head_last.shape[0], out_got.shape[1])])
    @pl.when(line != core)
    def _():
        head_turn.wait()

    thin[0] = down_mine[mine, :]
    thin[1] = down_theirs[...]
    broad[0:columns, :] = gate_mine[:, near]
    broad[2 * columns : 3 * columns, :] = up_mine[:, near]
    for away in range(1, RANKS):
        row_copy(away).wait_send()
    for cross in crosses + [gate_cross, up_cross]:
        cross.wait()
    for copy in (out_line, head_line, head_cross, down_core):
        copy.wait_send()
    for cross, onward in fetched:
        cross.wait_send()
        onward.wait_send()
    for number in range(5):
        gain_copy(number).wait_send()
    for number in range(PLANES):
        up_line(number).wait_send()
    for number in gate_late:
        gate_line(number).wait_send()
    for weight in (down, gate, up, out):
        chain.sent(weight, weight.first, last)


def reduce_all(rows_in, down, gate, up, out_sum, head, attn_weights, w_key, key_far, tokens, grad):
    (down_keep, down_got, down_hops), (gate_keep, gate_first, gate_sent), (up_keep, up_sent) = down, gate, up
    normed, head_near, head_far, attn_gain, mlp_part = head
    head_cols, model = head_near.shape[1], normed.shape[1]
    half = model // 2
    hops = 2 * (PLANES - 1)
    vmem = pl.BlockSpec(memory_space=pltpu.VMEM)
    hbm = pl.BlockSpec(memory_space=pl.ANY)
    dma = pltpu.SemaphoreType.DMA

    def piece(keep):
        return keep.shape[1:]

    def out(dims):
        return jax.ShapeDtypeStruct(dims, BF)

    def low(*dims):
        return pltpu.VMEM(dims, BF)

    down_rows, down_cols = piece(down_keep)
    columns = gate_keep.shape[1]
    out_half = out_sum.shape[1:]
    keeps = (down_keep, gate_keep, up_keep, jax.ShapeDtypeStruct(out_half, BF))
    return pl.pallas_call(
        reduce_kernel,
        in_specs=[hbm] * 11 + [vmem] * 4 + [hbm] * 6,
        out_specs=[vmem] * 4 + [hbm] * 2,
        out_shape=[
            out(tokens.shape),
            out((3, down_rows // CORES, down_cols)),
            out((4 * columns + head_cols // 2 + out_half[1], half)),
            jax.ShapeDtypeStruct((8, model), jnp.float32),
        ]
        + [jax.ShapeDtypeStruct(weight.shape, BF) for weight in attn_weights],
        scratch_shapes=[
            low(*rows_in.shape),
            low(*attn_weights[1].shape),
            low(*w_key.shape),
            low(*w_key.shape),
            low(*tokens.shape),
            pltpu.VMEM(grad.shape, jnp.float32),
            pltpu.VMEM(grad.shape, jnp.float32),
            dma((8,)),
        ]
        + [low(*value.shape) for value in (rows_in, down_keep, down_got, down_hops, gate_keep, up_keep, out_sum)]
        + [
            dma((10,)),
            low(*gate_keep.shape),
            low(*up_keep.shape),
            low(*out_half),
        ]
        + [low(PLANES - 1, *piece(keep)) for keep in keeps]
        + [low(hops, *piece(keep)) for keep in keeps]
        + [
            low(down_rows, down_cols),
            low(down_rows // CORES, down_cols),
            low(columns, model),
            low(columns, model),
            low(2, normed.shape[0] // PLANES, model),
            pltpu.VMEM((head_cols, model), jnp.float32),
            pltpu.VMEM((head_cols, half), jnp.float32),
            low(head_cols, half),
            low(head_cols // 2, half),
            low(head_cols // 2, half),
            low(head_cols, half),
            low(head_cols // 2, half),
            pltpu.VMEM((6, 8, model), jnp.float32),
            pltpu.VMEM((5, 8, model), jnp.float32),
            dma((2, RANKS)),
            dma((2, 4 * hops)),
            dma((2, 19)),
            dma((2, 2 * PLANES)),
            dma((2, 4)),
            dma((3,)),
        ],
        compiler_params=pltpu.CompilerParams(collective_id=0, has_side_effects=True, vmem_limit_bytes=VMEM_LIMIT),
    )(
        rows_in, down_keep, down_got, down_hops, gate_keep, gate_first, gate_sent, up_keep, up_sent, out_sum,
        normed, head_near, head_far, attn_gain, mlp_part, *attn_weights, w_key, key_far, tokens, grad,
    )


def local_last(info, thin, broad):
    half = broad.shape[1]
    model = 2 * half
    columns, hidden = (broad.shape[0] - 2 * HD - model // RANKS) // 4, thin.shape[2] * 2
    shapes = [
        (HD, half), (HD // 2, half), (HD // 2, half), (model // RANKS, half), (half, 2 * columns), (half, 2 * columns),
        (model // RANKS, hidden),
    ]
    query, key, value, out, gate, up, down = local_call(
        last_kernel, info, (thin, broad), [jax.ShapeDtypeStruct(shape, jnp.float32) for shape in shapes]
    )
    return query.T, key.T, value.T, out.T, gate, up, down.T


def head_shards(
    tokens, attn_gain, w_query, w_key, w_value, w_out, mlp_gain, w_gate, w_up, w_down, cotangent
):
    seqs, width, model = tokens.shape
    length = width * RANKS
    rows = seqs * width
    half_model = model // 2
    hidden = w_gate.shape[1]
    half_hidden = hidden // 2
    part_hidden = half_hidden // CORES
    chunk = hidden // (2 * RANKS)
    rank = lax.axis_index("ctx")
    side = lax.axis_index("fsdp")
    core = rank % CORES
    line = (rank // CORES) % LINES
    plane = rank // (CORES * LINES)
    head = plane * CORES + core
    low_side = side == 0
    info = jnp.stack([side, core, line]).astype(jnp.int32)
    pick = jnp.asarray((pad_columns()[:, None] == np.arange(HEAD_COLS)[None, :]).astype(np.float32)).astype(BF)

    lane = np.arange(2 * LANES)
    column = np.where(lane % LANES < HD, lane // LANES * HD + lane % LANES, -1)
    columns = np.stack([np.where(column < 0, -1, column + i * 2 * HD) for i in range(CORES)])
    squeeze = jnp.asarray((columns[:, :, None] == np.arange(4 * HD)).astype(np.float32)).astype(BF)

    tokens_seq, head_rows, head_far, far, out_far, cosine, sine, attn_row, mlp_row = gather_all(
        tokens, (w_query, w_key, w_value), w_gate, w_up, w_out, rope_rows(),
        (attn_gain.reshape(-1, LANES), mlp_gain.reshape(-1, LANES)),
    )
    grad_down = cotangent.reshape(rows, model)
    normed_seq, qkv, attended_seq, lse, attended_blocks, down_far, grad_down_other = head_forward(
        tokens_seq.reshape(length, model), attn_row, head_rows, head_far, pick, cosine, sine, w_down, grad_down
    )
    attended_seq = attended_seq.reshape(length, 2 * LANES)
    weights = (w_gate, w_up, far, w_down, down_far)
    token_rows = tokens.reshape(rows, model)
    resid, normed_two = local_call(
        post_kernel,
        info,
        (attended_blocks, token_rows, w_out, out_far, mlp_row),
        [jax.ShapeDtypeStruct((rows, model), jnp.float32), jax.ShapeDtypeStruct((rows, model), BF)],
    )

    inner_own, gate_own, up_own, mixed_own, back_own, normed_other = mlp_part(
        normed_two, grad_down, weights, jnp.float32, 6, [(SIDE, normed_two)]
    )
    inner_far, gate_far, up_far, mixed_far, back_far, inner_sib, gate_sib, up_sib, *sib, key_far = mlp_part(
        normed_other, grad_down_other, weights, BF, 5,
        [(HALF, value) for value in (inner_own, gate_own, up_own)]
        + [(WHOLE, value) for value in (normed_two, normed_other, grad_down, grad_down_other)]
        + [(WEIGHT, w_key)],
    )
    (
        down_keep, down_sent, down_first, gate_keep, gate_sent,
        grad_resid, grad_branch, grad_attended, mlp_gain_part,
    ) = middle(
        back_far,
        (inner_own, inner_far, inner_sib, gate_own, gate_far, gate_sib),
        (normed_two, normed_other, *sib[:2]),
        (grad_down, grad_down_other, *sib[2:]),
        back_own, resid, mlp_row, w_out, out_far,
    )

    grad_qkv, gate_first, out_sum, up_keep, up_sent, down_got, down_hops, mixed = head_backward(
        grad_attended, qkv, attended_seq, lse, cosine, sine, pick, squeeze, down_sent, gate_sent, grad_branch, attended_blocks,
        (up_own, up_far, up_sib, normed_two, normed_other, *sib[:2]),
        (down_keep, down_first),
        (mixed_far, mixed_own, resid),
    )
    tokens_grad, thin, broad, gains, _, _ = reduce_all(
        grad_qkv.reshape(RANKS, width, HEAD_COLS),
        (down_keep, down_got, down_hops),
        (gate_keep, gate_first, gate_sent),
        (up_keep, up_sent),
        out_sum,
        (normed_seq, head_rows, head_far, attn_row, mlp_gain_part),
        (w_value, w_query),
        w_key, key_far, token_rows, grad_resid,
    )

    w_query_grad, w_key_grad, w_value_grad, w_out_grad, w_gate_grad, w_up_grad, w_down_grad = local_last(info, thin, broad)
    return (
        mixed.reshape(seqs, width, model),
        tokens_grad.reshape(seqs, width, model),
        gains[0],
        w_query_grad,
        w_key_grad,
        w_value_grad,
        w_out_grad,
        gains[1],
        w_gate_grad,
        w_up_grad,
        w_down_grad,
    )


def solution(mesh):
    by_heads = mesh.shape["ctx"] == RANKS and mesh.shape["fsdp"] == 2
    placed = (
        P("fsdp", "ctx", None),
        P(),
        P("fsdp", None),
        P("fsdp", None),
        P("fsdp", None),
        P("fsdp", None),
        P(),
        P("fsdp", None),
        P("fsdp", None),
        P("fsdp", None),
        P("fsdp", "ctx", None),
    )
    return jax.shard_map(
        head_shards if by_heads else shards,
        mesh=mesh,
        in_specs=placed,
        out_specs=(
            P("fsdp", "ctx", None),
            P("fsdp", "ctx", None),
            P(),
            P("fsdp", "ctx"),
            P("fsdp", "ctx"),
            P("fsdp", "ctx"),
            P("fsdp", "ctx"),
            P(),
            P("fsdp", "ctx"),
            P("fsdp", "ctx"),
            P("fsdp", "ctx"),
        ),
        check_vma=False,
    )
```

```python
import dataclasses
import functools
from typing import Any

import jax
import jax.numpy as jnp
import numpy as np
from jax import lax
from jax.experimental import pallas as pl
from jax.experimental.pallas import tpu as pltpu
from jax.sharding import PartitionSpec as P

HQ = 16
HK = 8
HD = 96
MICRO = 2
LANES = 128
HEAD_COLS = 4 * HD
BF = jnp.bfloat16
VMEM_LIMIT = 62 * 1024 * 1024


EPSILON = 1e-05
ROPE_BASE = 100000.0
MASK_FILL = -1e30


def matmul(left, right):
    return jnp.dot(left, right, preferred_element_type=jnp.float32)


def times_transposed(left, right):
    return lax.dot_general(
        left, right, (((1,), (1,)), ((), ())), preferred_element_type=jnp.float32
    )


def transposed_times(left, right):
    return lax.dot_general(
        left, right, (((0,), (0,)), ((), ())), preferred_element_type=jnp.float32
    )


def normalize(values):
    inv_rms = lax.rsqrt(jnp.mean(values * values, axis=-1, keepdims=True) + EPSILON)
    return (values * inv_rms, inv_rms)


def norm_back(grad_normed, gain_row, unit_rows, inv_rms):
    scaled = grad_normed * gain_row
    return inv_rms * (scaled - unit_rows * jnp.mean(scaled * unit_rows, axis=-1, keepdims=True))


def rotate(values, cosine, sine_rows):
    half_dim = values.shape[-1] // 2
    front = values[..., :half_dim]
    back_half = values[..., half_dim:]
    return jnp.concatenate(
        [front * cosine - back_half * sine_rows, back_half * cosine + front * sine_rows], axis=-1
    )


def attend_forward(query_rows, key_rows, value_rows, allowed):
    width_ct = query_rows.shape[0]
    grouped = query_rows.reshape(width_ct, HK, HQ // HK, HD)
    key_heads = key_rows.reshape(-1, HK, HD)
    value_heads = value_rows.reshape(-1, HK, HD)
    scores = jnp.einsum("cgrd,lgd->grcl", grouped, key_heads, preferred_element_type=jnp.float32)
    scores = jnp.where(allowed, scores, MASK_FILL)
    row_top = jnp.max(scores, axis=-1, keepdims=True)
    shifted_exp = jnp.exp(scores - row_top)
    row_total = jnp.sum(shifted_exp, axis=-1, keepdims=True)
    prob_low = (shifted_exp / row_total).astype(jnp.bfloat16)
    attended = jnp.einsum(
        "grcl,lgd->cgrd", prob_low, value_heads, preferred_element_type=jnp.float32
    )
    return (attended.reshape(width_ct, HQ * HD), row_top + jnp.log(row_total))


def attend_backward(query_rows, key_rows, value_rows, allowed, log_total, grad_rows):
    width_ct = query_rows.shape[0]
    grouped = query_rows.reshape(width_ct, HK, HQ // HK, HD)
    key_heads = key_rows.reshape(-1, HK, HD)
    value_heads = value_rows.reshape(-1, HK, HD)
    scores = jnp.einsum("cgrd,lgd->grcl", grouped, key_heads, preferred_element_type=jnp.float32)
    prob_full = jnp.exp(jnp.where(allowed, scores, MASK_FILL) - log_total)
    prob_low = prob_full.astype(jnp.bfloat16)
    grad_heads = grad_rows.reshape(width_ct, HK, HQ // HK, HD)
    grad_prob = jnp.einsum(
        "cgrd,lgd->grcl", grad_heads, value_heads, preferred_element_type=jnp.float32
    )
    row_inner = jnp.sum(prob_full * grad_prob, axis=-1, keepdims=True)
    grad_scores = (prob_full * (grad_prob - row_inner)).astype(jnp.bfloat16)
    grad_query = jnp.einsum(
        "grcl,lgd->cgrd", grad_scores, key_heads, preferred_element_type=jnp.float32
    )
    grad_key = jnp.einsum(
        "grcl,cgrd->lgd", grad_scores, grouped, preferred_element_type=jnp.float32
    )
    grad_value = jnp.einsum(
        "grcl,cgrd->lgd", prob_low, grad_heads, preferred_element_type=jnp.float32
    )
    return (
        grad_query.reshape(width_ct, HQ * HD),
        grad_key.reshape(-1, HK * HD),
        grad_value.reshape(-1, HK * HD),
        row_inner,
    )


def reduce_grad(full_grad):
    partial_grad = lax.psum_scatter(
        full_grad.astype(jnp.bfloat16), "fsdp", scatter_dimension=0, tiled=True
    )
    return lax.psum_scatter(partial_grad, "ctx", scatter_dimension=1, tiled=True).astype(
        jnp.float32
    )


def shards(
    tokens, attn_gain, w_query, w_key, w_value, w_out, mlp_gain, w_gate, w_up, w_down, cotangent
):
    seq_local, width_ct, model_width = tokens.shape
    seq_block = seq_local // MICRO
    row_count = seq_block * width_ct
    length = width_ct * lax.axis_size("ctx")
    half_dim = HD // 2
    offset = lax.axis_index("ctx") * width_ct
    query_pos = offset + jnp.arange(width_ct, dtype=jnp.int32)
    key_pos = jnp.arange(length, dtype=jnp.int32)
    allowed = key_pos[None, :] <= query_pos[:, None]
    inv_freq = 1.0 / ROPE_BASE ** (jnp.arange(half_dim, dtype=jnp.float32) * 2.0 / HD)
    angles = query_pos.astype(jnp.float32)[:, None] * inv_freq[None, :]
    cos_one = jnp.cos(angles)[:, None, :]
    sin_one = jnp.sin(angles)[:, None, :]
    cos_rows = jnp.tile(cos_one, (seq_block, 1, 1))
    sin_rows = jnp.tile(sin_one, (seq_block, 1, 1))
    head_scale = HD ** (-0.5)
    mixed_list, token_grad_list = ([], [])
    kept_normed_one, kept_grad_query, kept_grad_key, kept_grad_value = ([], [], [], [])
    kept_attended, kept_grad_branch, kept_normed_two = ([], [], [])
    kept_grad_gate, kept_grad_upper, kept_inner, kept_grad_down = ([], [], [], [])
    attn_gain_acc = jnp.zeros((model_width,), jnp.float32)
    mlp_gain_acc = jnp.zeros((model_width,), jnp.float32)
    for micro_at in range(MICRO):
        first_seq = micro_at * seq_block
        inputs = (
            tokens[first_seq : first_seq + seq_block]
            .reshape(row_count, model_width)
            .astype(jnp.float32)
        )
        outer_grad = (
            cotangent[first_seq : first_seq + seq_block]
            .reshape(row_count, model_width)
            .astype(jnp.float32)
        )
        attn_all = (
            lax.all_gather(w_query, "fsdp", axis=0, tiled=True),
            lax.all_gather(w_key, "fsdp", axis=0, tiled=True),
            lax.all_gather(w_value, "fsdp", axis=0, tiled=True),
            lax.all_gather(w_out, "fsdp", axis=0, tiled=True),
        )
        unit_one, inv_one = normalize(inputs)
        normed_one = (unit_one * attn_gain).astype(jnp.bfloat16)
        query_raw = matmul(normed_one, attn_all[0]).reshape(row_count, HQ, HD)
        key_raw = matmul(normed_one, attn_all[1]).reshape(row_count, HK, HD)
        value_raw = matmul(normed_one, attn_all[2])
        queries = (
            (rotate(query_raw, cos_rows, sin_rows) * head_scale)
            .astype(jnp.bfloat16)
            .reshape(seq_block, width_ct, HQ * HD)
        )
        keys = (
            rotate(key_raw, cos_rows, sin_rows)
            .astype(jnp.bfloat16)
            .reshape(seq_block, width_ct, HK * HD)
        )
        values = value_raw.astype(jnp.bfloat16).reshape(seq_block, width_ct, HK * HD)
        key_all, value_all = (
            lax.all_gather(keys, "ctx", axis=1, tiled=True),
            lax.all_gather(values, "ctx", axis=1, tiled=True),
        )
        attended_parts, lse_parts = ([], [])
        seq_at = 0
        attended_one, lse_one = attend_forward(
            queries[seq_at], key_all[seq_at], value_all[seq_at], allowed
        )
        attended_parts.append(attended_one)
        lse_parts.append(lse_one)
        attended = attended_parts[0].astype(jnp.bfloat16)
        resid = inputs + matmul(attended, attn_all[3])
        unit_two, inv_two = normalize(resid)
        normed_two = (unit_two * mlp_gain).astype(jnp.bfloat16)
        gate_proj = matmul(normed_two, lax.all_gather(w_gate, "fsdp", axis=0, tiled=True))
        up_proj = matmul(normed_two, lax.all_gather(w_up, "fsdp", axis=0, tiled=True))
        sigma = jax.nn.sigmoid(gate_proj)
        active = gate_proj * sigma
        hidden_act = (active * up_proj).astype(jnp.bfloat16)
        down_out = matmul(hidden_act, lax.all_gather(w_down, "fsdp", axis=0, tiled=True))
        mixed_list.append((resid + down_out).astype(jnp.bfloat16))
        grad_down = outer_grad.astype(jnp.bfloat16)
        grad_hidden = times_transposed(
            grad_down, lax.all_gather(w_down, "fsdp", axis=0, tiled=True)
        )
        grad_gate = (grad_hidden * up_proj * sigma * (1.0 + gate_proj * (1.0 - sigma))).astype(
            jnp.bfloat16
        )
        grad_upper = (grad_hidden * active).astype(jnp.bfloat16)
        pair_pieces = lax.all_gather((w_gate, w_up), "fsdp", axis=0, tiled=True)
        grad_normed_two = times_transposed(grad_gate, pair_pieces[0]) + times_transposed(
            grad_upper, pair_pieces[1]
        )
        mlp_gain_acc = mlp_gain_acc + jnp.sum(grad_normed_two * unit_two, axis=0)
        grad_resid = outer_grad + norm_back(grad_normed_two, mlp_gain, unit_two, inv_two)
        grad_branch = grad_resid.astype(jnp.bfloat16)
        attn_back = (
            lax.all_gather(w_query, "fsdp", axis=0, tiled=True),
            lax.all_gather(w_key, "fsdp", axis=0, tiled=True),
            lax.all_gather(w_value, "fsdp", axis=0, tiled=True),
            lax.all_gather(w_out, "fsdp", axis=0, tiled=True),
        )
        grad_attended = times_transposed(grad_branch, attn_back[3]).astype(jnp.bfloat16)
        key_back, value_back = (
            lax.all_gather(keys, "ctx", axis=1, tiled=True),
            lax.all_gather(values, "ctx", axis=1, tiled=True),
        )
        query_parts, key_parts, value_parts = ([], [], [])
        seq_at = 0
        query_one = queries[seq_at]
        key_one = key_back[seq_at]
        value_one = value_back[seq_at]
        lse_one = lse_parts[seq_at]
        grad_query, grad_key, grad_value, row_inner = attend_backward(
            query_one, key_one, value_one, allowed, lse_one, grad_attended
        )
        own_key = lax.psum_scatter(
            grad_key.astype(jnp.bfloat16), "ctx", scatter_dimension=0, tiled=True
        ).astype(jnp.float32)
        own_value = lax.psum_scatter(
            grad_value.astype(jnp.bfloat16), "ctx", scatter_dimension=0, tiled=True
        ).astype(jnp.float32)
        query_parts.append(
            rotate((grad_query * head_scale).reshape(width_ct, HQ, HD), cos_one, -sin_one).reshape(
                width_ct, HQ * HD
            )
        )
        key_parts.append(
            rotate(own_key.reshape(width_ct, HK, HD), cos_one, -sin_one).reshape(width_ct, HK * HD)
        )
        value_parts.append(own_value)
        grad_query_raw = query_parts[0].astype(jnp.bfloat16)
        grad_key_raw = key_parts[0].astype(jnp.bfloat16)
        grad_value_raw = value_parts[0].astype(jnp.bfloat16)
        grad_normed_one = (
            times_transposed(grad_query_raw, attn_back[0])
            + times_transposed(grad_key_raw, attn_back[1])
            + times_transposed(grad_value_raw, attn_back[2])
        )
        attn_gain_acc = attn_gain_acc + jnp.sum(grad_normed_one * unit_one, axis=0)
        token_grad_list.append(
            (grad_resid + norm_back(grad_normed_one, attn_gain, unit_one, inv_one)).astype(
                jnp.bfloat16
            )
        )
        kept_normed_one.append(normed_one)
        kept_grad_query.append(grad_query_raw)
        kept_grad_key.append(grad_key_raw)
        kept_grad_value.append(grad_value_raw)
        kept_attended.append(attended)
        kept_grad_branch.append(grad_branch)
        kept_normed_two.append(normed_two)
        kept_grad_gate.append(grad_gate)
        kept_grad_upper.append(grad_upper)
        kept_inner.append(hidden_act)
        kept_grad_down.append(grad_down)
    normed_one_all = jnp.concatenate(kept_normed_one, axis=0)
    normed_two_all = jnp.concatenate(kept_normed_two, axis=0)
    w_query_grad = reduce_grad(
        transposed_times(normed_one_all, jnp.concatenate(kept_grad_query, axis=0))
    )
    w_key_grad = reduce_grad(
        transposed_times(normed_one_all, jnp.concatenate(kept_grad_key, axis=0))
    )
    w_value_grad = reduce_grad(
        transposed_times(normed_one_all, jnp.concatenate(kept_grad_value, axis=0))
    )
    w_out_grad = reduce_grad(
        transposed_times(
            jnp.concatenate(kept_attended, axis=0), jnp.concatenate(kept_grad_branch, axis=0)
        )
    )
    w_gate_grad = reduce_grad(
        transposed_times(normed_two_all, jnp.concatenate(kept_grad_gate, axis=0))
    )
    w_up_grad = reduce_grad(
        transposed_times(normed_two_all, jnp.concatenate(kept_grad_upper, axis=0))
    )
    w_down_grad = reduce_grad(
        transposed_times(
            jnp.concatenate(kept_inner, axis=0), jnp.concatenate(kept_grad_down, axis=0)
        )
    )
    attn_gain_grad, mlp_gain_grad = lax.psum((attn_gain_acc, mlp_gain_acc), ("ctx", "fsdp"))
    mixed = jnp.concatenate(mixed_list, axis=0).reshape(seq_local, width_ct, model_width)
    tokens_grad = jnp.concatenate(token_grad_list, axis=0).reshape(seq_local, width_ct, model_width)
    return (
        mixed,
        tokens_grad,
        attn_gain_grad,
        w_query_grad,
        w_key_grad,
        w_value_grad,
        w_out_grad,
        mlp_gain_grad,
        w_gate_grad,
        w_up_grad,
        w_down_grad,
    )


def nt(a,b):
    return lax.dot_general(a,b,(((1,),(1,)),((),())),preferred_element_type=jnp.float32)
def tn(a,b):
    return lax.dot_general(a,b,(((0,),(0,)),((),())),preferred_element_type=jnp.float32)
def nn(a,b):
    return jnp.dot(a,b,preferred_element_type=jnp.float32)

def turn(v,cosine,sine):
    return v*cosine+pltpu.roll(v,LANES//2,1)*sine

def forward_kernel(
    tokens_ref, gain_ref, head_near, head_far, pick_ref, cos_ref, sin_ref, w_down, cot_in,
    normed_ref, qkv_ref, att_ref, lse_ref, rows_out, down_far, cot_out,
    weight_ref, key_ref, val_t_ref, exchange_sems, weight_sems, local_sem,
):
    at = pl.program_id(0)
    rank = lax.axis_index("ctx")
    side = lax.axis_index("fsdp")
    core = lax.rem(rank, CORES)
    line = lax.rem(lax.div(rank, CORES), LINES)
    other_line = rank + CORES * (1 - 2 * line)
    other_core = rank + 1 - 2 * core
    rows = tokens_ref.shape[0]
    width = att_ref.shape[1]
    blocks = rows // width
    here = pl.ds(pl.multiple_of(at * rows, rows), rows)

    chunk = w_down.shape[0] // RANKS
    quarter = 2 * core + line

    def down_slice(which, part):
        return down_far.at[pl.ds(pl.multiple_of((2 * which + part) * chunk, chunk), chunk)]

    def down_cross(part):
        number = 2 * quarter + part
        source = w_down.at[pl.ds(pl.multiple_of((2 * number + 1 - side) * chunk, chunk), chunk)]
        return side_copy(source, down_slice(quarter, part), weight_sems, part, 1 - side)

    def onward(kind, part):
        block = down_slice(2 * core + 1 - line if kind == 2 else quarter, part)
        return ctx_copy(block, block, weight_sems, 2 + 2 * kind + part, other_core if kind else other_line)

    cot_cross = side_copy(cot_in, cot_out, weight_sems, 8, 1 - side)

    def row_copy(away):
        to = lax.rem(rank + away, RANKS)
        return ctx_copy(att_ref.at[to], rows_out.at[rank], exchange_sems, away, to)

    @pl.when(at == 0)
    def _():
        greet(rank, side)
        for part in range(2):
            down_cross(part).start()
        cot_cross.start()
        val_t_ref[...] = jnp.zeros_like(val_t_ref)
        half = head_near.shape[0]
        for which, source in enumerate((head_near, head_far)):
            first = pl.ds(pl.multiple_of((side if which == 0 else 1 - side) * half, 16), half)
            weight_ref[first, :] = nt(source[...], pick_ref[...]).astype(BF)

    cosine, sine = cos_ref[...], sin_ref[...]
    unit, _ = normalize(tokens_ref[...].astype(jnp.float32))
    normed = (unit * gain_ref[...]).astype(BF)
    normed_ref[...] = normed
    raw = nn(normed, weight_ref[...])
    scale = HD**-0.5
    parts = [
        (turn(raw[:, j * LANES : (j + 1) * LANES], cosine, sine) * (scale if j < 2 else 1.0)).astype(BF) for j in range(3)
    ]
    value = raw[:, 3 * LANES :].astype(BF)
    for j in range(3):
        qkv_ref[:, j * LANES : (j + 1) * LANES] = parts[j]
    qkv_ref[:, 3 * LANES :] = value
    key_ref[here, :] = parts[2]
    val_t_ref[:, here] = value.T
    query = jnp.concatenate(parts[:2], axis=0)
    for band in range(key_ref.shape[0] // rows):
        @pl.when(at == band)
        def _():
            scores = nt(key_ref[0 : (band + 1) * rows, :], query)
            tail = scores[band * rows :, :]
            key_pos = lax.broadcasted_iota(jnp.int32, tail.shape, 0)
            query_pos = lax.broadcasted_iota(jnp.int32, tail.shape, 1) % rows
            tail = jnp.where(key_pos <= query_pos, tail, MASK_FILL)
            pieces = [scores[b * rows : (b + 1) * rows, :] for b in range(band)] + [tail]
            top = functools.reduce(jnp.maximum, [jnp.max(p, axis=0, keepdims=True) for p in pieces])
            total = 0.0
            acc = 0.0
            for b, p in enumerate(pieces):
                e = jnp.exp(p - top)
                total = total + jnp.sum(e, axis=0, keepdims=True)
                acc = acc + nn(val_t_ref[:, b * rows : (b + 1) * rows], e.astype(BF))
            acc = acc / total
            for h in range(2):
                turned = acc[:, h * rows : (h + 1) * rows].T.astype(BF)
                for i in range(blocks):
                    att_ref[band * blocks + i, :, h * LANES : (h + 1) * LANES] = turned[i * width : (i + 1) * width]
            lse_ref[0] = top + jnp.log(total)
            for i in range(blocks):
                to = band * blocks + i
                away = lax.rem(to - rank + RANKS, RANKS)

                @pl.when(away != 0)
                def _():
                    ctx_copy(att_ref.at[to], rows_out.at[rank], exchange_sems, away, to).start()

                @pl.when(away == 0)
                def _():
                    pltpu.make_async_copy(att_ref.at[to], rows_out.at[rank], local_sem).start()

    @pl.when(at == 1)
    def _():
        down_cross(0).wait_recv()
        onward(0, 0).start()
        onward(1, 0).start()

    @pl.when(at == 2)
    def _():
        down_cross(1).wait_recv()
        onward(0, 1).start()
        onward(1, 1).start()

    @pl.when(at == pl.num_programs(0) - 1)
    def _():
        for part in range(2):
            onward(0, part).wait_recv()
            onward(2, part).start()
        for part in range(2):
            onward(1, part).wait_recv()
            onward(2, part).wait_recv()
        for away in range(1, RANKS):
            row_copy(away).wait()
        pltpu.make_async_copy(att_ref.at[rank], rows_out.at[rank], local_sem).wait()
        cot_cross.wait()
        for part in range(2):
            down_cross(part).wait_send()
            for kind in range(3):
                onward(kind, part).wait_send()


def head_forward(tokens, gain, head_near, head_far, pick, cosine, sine, w_down, cotangent, rows=512):
    length, model = tokens.shape
    steps = length // rows
    width = length // RANKS
    hbm = pl.BlockSpec(memory_space=pl.ANY)
    dma = pltpu.SemaphoreType.DMA

    def block(cols):
        return pl.BlockSpec((rows, cols), lambda i: (i, 0))

    def whole(*dims):
        return pl.BlockSpec(dims, lambda i: (0,) * len(dims))

    return pl.pallas_call(
        forward_kernel,
        grid=(steps,),
        in_specs=[
            block(model), whole(1, model), whole(*head_near.shape), whole(*head_far.shape), whole(*pick.shape),
            block(LANES), block(LANES), hbm, hbm,
        ],
        out_specs=[
            block(model), block(4 * LANES), whole(RANKS, width, 2 * LANES),
            pl.BlockSpec((1, 1, 2 * rows), lambda i: (i, 0, 0)), hbm, hbm, hbm,
        ],
        out_shape=[
            jax.ShapeDtypeStruct((length, model), BF),
            jax.ShapeDtypeStruct((length, 4 * LANES), BF),
            jax.ShapeDtypeStruct((RANKS, width, 2 * LANES), BF),
            jax.ShapeDtypeStruct((steps, 1, 2 * rows), jnp.float32),
            jax.ShapeDtypeStruct((RANKS, width, 2 * LANES), BF),
            jax.ShapeDtypeStruct((w_down.shape[0] // 2, model), BF),
            jax.ShapeDtypeStruct(cotangent.shape, BF),
        ],
        scratch_shapes=[
            pltpu.VMEM((model, 4 * LANES), BF),
            pltpu.VMEM((length, LANES), BF),
            pltpu.VMEM((LANES, length), BF),
            dma((2, RANKS)),
            dma((2, 9)),
            dma,
        ],
        compiler_params=pltpu.CompilerParams(collective_id=2, has_side_effects=True, vmem_limit_bytes=VMEM_LIMIT),
    )(tokens, gain, head_near, head_far, pick, cosine, sine, w_down, cotangent)


def backward_kernel(
    rows_in, qkv_in, out_in, lse_ref, cos_in, sin_in, pick_ref, squeeze_ref, down_sent, gate_sent, branch_in, att_in,
    up_own, up_far, up_sib, normed_own, normed_far, normed_sib, normed_sib_far,
    down_keep_in, down_first, mixed_far, mixed_own_in, resid_in,
    res_ref, gate_first, out_sum_out, up_keep_out, up_sent_out, down_got_out, down_hops_out, mixed_ref,
    qkv_ref, out_ref, cos_ref, sin_ref, branch_ref, att_ref, down_keep, mixed_own, resid,
    up_keep, up_sent, down_got, down_in, load_sems, store_sems, out_keep, out_sent, out_got, out_side, out_sum, out_sems,
    down_acc, mixed_got, plane_sems, up_all, normed_all, core_sems, local_sems, weight_ref, grad_ref, key_t_ref, grad_key_ref, grad_val_ref, rows_ref, exchange_sems, line_sems, fetch_sems, local_sem,
):
    rank = lax.axis_index("ctx")
    side = lax.axis_index("fsdp")
    core = lax.rem(rank, CORES)
    line = lax.rem(lax.div(rank, CORES), LINES)
    plane = lax.div(rank, CORES * LINES)
    other_line = rank + CORES * (1 - 2 * line)
    other_core = rank + 1 - 2 * core
    first_loads = local_copies(((branch_in, branch_ref), (att_in, att_ref)), load_sems)
    head_loads = local_copies(
        ((qkv_in, qkv_ref), (out_in, out_ref), (cos_in, cos_ref), (sin_in, sin_ref)), load_sems, 2
    )
    down_loads = local_copies(
        [(down_keep_in, down_keep)] + [(down_first.at[slot], down_got.at[number]) for slot, number in enumerate(DOWN_EARLY)],
        load_sems,
        6,
    )
    mixed_loads = local_copies(((mixed_own_in, mixed_own), (resid_in, resid)), load_sems, 10)
    out_stores = local_copies(((out_sum, out_sum_out),), store_sems)
    up_stores = local_copies(((up_keep, up_keep_out), (up_sent, up_sent_out)), store_sems, 2)
    down_stores = local_copies(((down_got, down_got_out),), store_sems, 4)
    start(first_loads + head_loads)
    greet(rank, side)

    def row_copy(away):
        to = lax.rem(rank + away, RANKS)
        return ctx_copy(rows_in.at[to], grad_ref.at[rank], exchange_sems, away, to)

    own = pltpu.make_async_copy(rows_in.at[rank], grad_ref.at[rank], local_sem)
    own.start()
    for away in range(1, RANKS):
        row_copy(away).start()
    late = [
        ctx_copy(down_sent.at[number], down_got.at[number], line_sems, slot, other_line)
        for slot, number in enumerate(DOWN_LATE)
    ]
    lines = [
        ctx_copy(gate_sent.at[number], gate_first.at[slot], line_sems, len(DOWN_LATE) + slot, other_line)
        for slot, number in enumerate(GATE_EARLY)
    ]
    mixed_cross = side_copy(mixed_far, mixed_got, fetch_sems, 0, 1 - side)
    chain = Chain(rank, plane, plane_sems)
    down = Weight(down_keep, down_got, down_acc, down_in, 0)
    jobs = (
        (up_all, (up_own, up_far, up_sib, None), True),
        (normed_all, (normed_own, normed_far, normed_sib, normed_sib_far), False),
    )
    moves = chip_moves(jobs, core, other_core, core_sems, local_sems)
    start(late + lines + [mixed_cross] + moves[0] + moves[1] + down_loads + mixed_loads)

    length = qkv_ref.shape[0]
    width = grad_ref.shape[1]
    rows = CORES * width
    scale = HD**-0.5
    grad_key_ref[...] = jnp.zeros_like(grad_key_ref)
    grad_val_ref[...] = jnp.zeros_like(grad_val_ref)
    wait(first_loads + head_loads)
    for b in range(CHIPS):
        key_t_ref[:, b * rows : (b + 1) * rows] = qkv_ref[b * rows : (b + 1) * rows, 2 * LANES : 3 * LANES].T

    branch_t = branch_ref[...].T
    per_rank = out_keep.shape[2]
    for pair in range(HK // CORES):
        attended = 0.0
        for at_core in range(CORES):
            first = pair * CORES * LINES + at_core
            block = jnp.concatenate([att_ref[first + seq * CORES] for seq in range(LINES)], axis=0)
            attended = attended + nn(block, squeeze_ref[at_core])
        weight_ref[...] = nn(branch_t, attended.astype(BF)).astype(BF)
        columns = slice(pair * 4 * HD, (pair + 1) * 4 * HD)
        for at_plane in range(PLANES):
            for at_line in range(LINES):
                place = (at_plane * LINES + at_line) * CORES
                out_keep[at_line, at_plane, :, columns] = weight_ref[
                    pl.ds(pl.multiple_of((place + core) * per_rank, 16), per_rank), :
                ]
                out_sent[at_line, at_plane, :, columns] = weight_ref[
                    pl.ds(pl.multiple_of((place + 1 - core) * per_rank, 16), per_rank), :
                ]
    out_core = ctx_copy(out_sent, out_got, out_sems, 0, other_core)
    out_core.start()
    half_out = out_sum.shape[3]
    out_near = pl.ds(pl.multiple_of(side * half_out, LANES), half_out)
    out_away = pl.ds(pl.multiple_of((1 - side) * half_out, LANES), half_out)
    out_cross = side_copy(out_keep.at[:, :, :, out_away], out_side, out_sems, 1, 1 - side)

    wait(moves[0] + moves[1])
    split_lines(up_all, normed_all, up_keep, up_sent, line)
    out_core.wait()
    for at_line in range(LINES):
        for at_plane in range(PLANES):
            total = wide(out_keep[at_line, at_plane]) + wide(out_got[at_line, at_plane])
            out_keep[at_line, at_plane] = total.astype(BF)
    out_cross.start()
    start(up_stores)
    wait(down_loads)

    @pl.loop(0, CHIPS)
    def _(step):
        @pl.when(step == 3)
        def _():
            chain.hop(down, 0)

        @pl.when(step == 6)
        def _():
            for copy in late:
                copy.wait_recv()
            chain.hop(down, 1)

        turn_at = lax.div(step, LINES)
        low = jnp.where(plane < PLANES // 2, plane, PLANES - 1 - plane)
        nth = jnp.where((low == 1) & (turn_at < 2), 1 - turn_at, turn_at)
        plane_at = jnp.where(plane < PLANES // 2, nth, PLANES - 1 - nth)
        flip = lax.rem(step, LINES)
        chip = plane_at * LINES + jnp.where(flip == 0, line, 1 - line)
        here = pl.ds(pl.multiple_of(chip * rows, rows), rows)
        for at_core in range(CORES):
            source = chip * CORES + at_core
            away = lax.rem(rank - source + RANKS, RANKS)

            @pl.when(away == 0)
            def _():
                own.wait()

            @pl.when(away != 0)
            def _():
                ctx_copy(rows_in.at[source], grad_ref.at[source], exchange_sems, away, other_core).wait_recv()

        grad = jnp.concatenate(
            [grad_ref[chip * CORES + c, :, h * LANES : (h + 1) * LANES] for h in range(2) for c in range(CORES)], axis=0
        )
        query = jnp.concatenate([qkv_ref[here, 0:LANES], qkv_ref[here, LANES : 2 * LANES]], axis=0)
        out = jnp.concatenate([out_ref[here, 0:LANES], out_ref[here, LANES:]], axis=0)
        inner = jnp.sum((grad.astype(jnp.float32) * out.astype(jnp.float32)).T, axis=0, keepdims=True)
        lse = lse_ref[chip]
        for band in range(CHIPS):
            @pl.when(chip == band)
            def _():
                grad_query = 0.0
                for b in range(band + 1):
                    span = slice(b * rows, (b + 1) * rows)
                    scores = nt(qkv_ref[span, 2 * LANES : 3 * LANES], query)
                    prob = jnp.exp(scores - lse)
                    if b == band:
                        key_pos = lax.broadcasted_iota(jnp.int32, scores.shape, 0)
                        query_pos = lax.broadcasted_iota(jnp.int32, scores.shape, 1) % rows
                        prob = jnp.where(key_pos <= query_pos, prob, 0.0)
                    grad_prob = nt(qkv_ref[span, 3 * LANES :], grad)
                    grad_scores = (prob * (grad_prob - inner)).astype(BF)
                    grad_val_ref[span, :] += nn(prob.astype(BF), grad)
                    grad_key_ref[span, :] += nn(grad_scores, query)
                    grad_query = grad_query + nn(key_t_ref[:, span], grad_scores)
                for j in range(2):
                    back = grad_query[:, j * rows : (j + 1) * rows].T * scale
                    rows_ref[here, j * LANES : (j + 1) * LANES] = turn(back, cos_ref[here, :], -sin_ref[here, :]).astype(BF)

    for b in range(CHIPS):
        span = slice(b * rows, (b + 1) * rows)
        rows_ref[span, 2 * LANES : 3 * LANES] = turn(grad_key_ref[span, :], cos_ref[span, :], -sin_ref[span, :]).astype(BF)
        rows_ref[span, 3 * LANES :] = grad_val_ref[span, :].astype(BF)
        res_ref[span, :] = nn(rows_ref[span, :], pick_ref[...]).astype(BF)
    start(down_stores)
    out_cross.wait()
    for at_line in range(LINES):
        for at_plane in range(PLANES):
            total = wide(out_keep[at_line, at_plane, :, out_near]) + wide(out_side[at_line, at_plane])
            out_sum[at_line, at_plane] = total.astype(BF)
    start(out_stores)
    wait(mixed_loads)
    mixed_cross.wait()
    mixed_ref[...] = (resid[...] + mixed_own[...] + wide(mixed_got[...])).astype(BF)
    for away in range(1, RANKS):
        row_copy(away).wait_send()
    for copy in late:
        copy.wait_send()
    for copy in lines:
        copy.wait()
    chain.receive(down, 1)
    chain.sent(down, 0, 2)
    hops_store = local_copies(((down_in, down_hops_out),), store_sems, 5)
    start(hops_store)
    wait(out_stores + up_stores + down_stores + hops_store)


def head_backward(rows_in, qkv, out, lse, cosine, sine, pick, squeeze, down_sent, gate_sent, branch, attended, up, down, mixed):
    length = qkv.shape[0]
    rows = length // CHIPS
    model = branch.shape[1]
    out_shape = jax.ShapeDtypeStruct((LINES, PLANES, model // RANKS, HQ * HD), BF)
    out_half = jax.ShapeDtypeStruct((LINES, PLANES, model // RANKS, HK * HD), BF)
    lse = lse.reshape(-1, 2, lse.shape[2] // 2).transpose(1, 0, 2).reshape(2, CHIPS, rows)
    lse = lse.transpose(1, 0, 2).reshape(CHIPS, 1, 2 * rows)
    vmem = pl.BlockSpec(memory_space=pltpu.VMEM)
    hbm = pl.BlockSpec(memory_space=pl.ANY)
    dma = pltpu.SemaphoreType.DMA
    return pl.pallas_call(
        backward_kernel,
        in_specs=[hbm] * 3 + [vmem] + [hbm] * 2 + [vmem] * 2 + [hbm] * 16,
        out_specs=[vmem] + [hbm] * 6 + [vmem],
        out_shape=[
            jax.ShapeDtypeStruct((length, HEAD_COLS), BF),
            jax.ShapeDtypeStruct((len(GATE_EARLY),) + gate_sent.shape[1:], BF),
            out_half,
            jax.ShapeDtypeStruct(gate_sent.shape, BF),
            jax.ShapeDtypeStruct(gate_sent.shape, BF),
            jax.ShapeDtypeStruct(down_sent.shape, BF),
            jax.ShapeDtypeStruct((2 * (PLANES - 1),) + down_sent.shape[1:], BF),
            jax.ShapeDtypeStruct(mixed[0].shape, BF),
        ],
        scratch_shapes=[
            pltpu.VMEM(value.shape, value.dtype)
            for value in (qkv, out, cosine, sine, branch, attended, down[0], mixed[1], mixed[2])
            + (gate_sent, gate_sent, down_sent)
        ]
        + [
            pltpu.VMEM((2 * (PLANES - 1),) + down_sent.shape[1:], BF),
            dma((12,)),
            dma((6,)),
            pltpu.VMEM(out_shape.shape, BF),
            pltpu.VMEM(out_shape.shape, BF),
            pltpu.VMEM(out_shape.shape, BF),
            pltpu.VMEM(out_half.shape, BF),
            pltpu.VMEM(out_half.shape, BF),
            dma((2, 2)),
            pltpu.VMEM((PLANES - 1,) + down_sent.shape[1:], BF),
            pltpu.VMEM(mixed[0].shape, BF),
            dma((2, 2 * (PLANES - 1))),
            pltpu.VMEM((4 * mixed[0].shape[0], up[0].shape[2]), BF),
            pltpu.VMEM((4 * mixed[0].shape[0], model), BF),
            dma((2, 2)),
            dma((8,)),
            pltpu.VMEM((model, 4 * HD), BF),
            pltpu.VMEM(rows_in.shape, BF),
            pltpu.VMEM((LANES, length), BF),
            pltpu.VMEM((length, LANES), jnp.float32),
            pltpu.VMEM((length, LANES), jnp.float32),
            pltpu.VMEM((length, 4 * LANES), BF),
            dma((2, RANKS)),
            dma((2, len(DOWN_LATE) + len(GATE_EARLY))),
            dma((2, 1)),
            dma,
        ],
        compiler_params=pltpu.CompilerParams(collective_id=3, has_side_effects=True, vmem_limit_bytes=VMEM_LIMIT),
    )(rows_in, qkv, out, lse, cosine, sine, pick, squeeze, down_sent, gate_sent, branch, attended, *up, *down, *mixed)


def pad_columns():
    half=HD//2
    lanes=np.arange(4*LANES); block=lanes//LANES; lane=lanes%LANES
    split=np.where(lane<half,lane,np.where((lane>=LANES//2)&(lane<LANES//2+half),lane-LANES//2+half,-1))
    plain=np.where(lane<HD,lane,-1)
    column=np.where(block<3,split,plain)
    return np.where(column>=0,column+block*HD,-1)

CORES, LINES, PLANES = 2, 2, 4
DOWN_EARLY, DOWN_LATE, GATE_EARLY = (3, 0, 2), (1,), (3, 0, 2)
CHIPS = LINES * PLANES
RANKS = CORES * CHIPS


def swap_fsdp(value):
    return lax.ppermute(value, "fsdp", [(0, 1), (1, 0)])


def swap_ctx(value, bit):
    return lax.ppermute(value, "ctx", [(i, i ^ bit) for i in range(RANKS)])


def swap_core(value):
    return swap_ctx(value, 1)


def swap_line(value):
    return swap_ctx(value, CORES)


def plane_up(value, sources):
    step = CORES * LINES
    return lax.ppermute(value, "ctx", [(z * step + i, z * step + step + i) for z in sources for i in range(step)])


def plane_down(value, sources):
    step = CORES * LINES
    return lax.ppermute(value, "ctx", [(z * step + i, z * step - step + i) for z in sources for i in range(step)])


def at(value, index, axis=0):
    return lax.dynamic_index_in_dim(value, index, axis, keepdims=False)


def in_order(which, mine, other):
    first = which == 0
    return jnp.concatenate([jnp.where(first, mine, other), jnp.where(first, other, mine)], axis=0)


def after(value, earlier):
    return lax.optimization_barrier((value, earlier))[0]


def rope_rows():
    lane = np.arange(LANES)
    half = LANES // 2
    entry = np.where(lane < half, lane, lane - half)
    used = entry < HD // 2
    rate = 1.0 / ROPE_BASE ** (jnp.asarray(entry, jnp.float32) * 2.0 / HD)
    factors = np.stack([used, np.where(lane < half, -1.0, 1.0) * used] + [0 * lane] * 5).astype(np.float32)
    return jnp.concatenate([rate[None], jnp.asarray(factors)], axis=0)


HALF, WHOLE, SIDE, WEIGHT = range(4)


def mlp_kernel(
    kinds, normed, grad_rows, gate_a, gate_b, up_a, up_b, gate_far, up_far, down_a, down_b, down_far, *refs
):
    sources, refs = refs[: len(kinds)], refs[len(kinds) :]
    inner_ref, grad_gate_ref, grad_up_ref, mixed_ref, back_ref = refs[:5]
    targets, refs = refs[5 : 5 + len(kinds)], refs[5 + len(kinds) :]
    down, mixed_acc, back_acc, sems = refs
    step = pl.program_id(0)
    half_steps = pl.num_programs(0) // 2
    side = lax.axis_index("fsdp")
    rank = lax.axis_index("ctx")
    core = lax.rem(rank, CORES)
    other_core = rank + 1 - 2 * core
    copies, onwards = [], []
    for number, (source, target, kind) in enumerate(zip(sources, targets, kinds)):
        if kind == SIDE:
            copies.append(side_copy(source, target, sems, number, 1 - side))
        elif kind == WEIGHT:
            per = source.shape[0] // CORES
            part = pl.ds(pl.multiple_of(core * per, 16), per)
            copies.append(side_copy(source.at[part], target.at[part], sems, number, 1 - side))
            onwards.append(ctx_copy(target.at[part], target.at[part], sems, len(kinds) + len(onwards), other_core))
        else:
            copies.append(ctx_copy(source.at[1 - core] if kind == HALF else source, target, sems, number, other_core))

    @pl.when(step == 0)
    def _():
        barrier = pltpu.get_barrier_semaphore()
        pl.semaphore_signal(barrier, inc=1, device_id={"ctx": other_core}, device_id_type=pl.DeviceIdType.MESH)
        pl.semaphore_signal(barrier, inc=1, device_id={"fsdp": 1 - side}, device_id_type=pl.DeviceIdType.MESH)
        pl.semaphore_wait(barrier, 2)
        start(copies)

    @pl.when(step == 2 * half_steps - 1)
    def _():
        wait(copies)
        start(onwards)
        wait(onwards)

    depth = gate_a.shape[0]
    near = pl.ds(pl.multiple_of(side * depth, LANES), depth)
    far = pl.ds(pl.multiple_of((1 - side) * depth, LANES), depth)

    @pl.when(step == 0)
    def _():
        mixed_acc[...] = jnp.zeros_like(mixed_acc)
        back_acc[...] = jnp.zeros_like(back_acc)

    @pl.when(step < half_steps)
    def _():
        down[:LANES, :] = down_a[...]
        down[LANES:, :] = down_b[...]

    @pl.when(step >= half_steps)
    def _():
        down[...] = down_far[...]

    gate_near = jnp.concatenate([gate_a[...], gate_b[...]], axis=1)
    up_near = jnp.concatenate([up_a[...], up_b[...]], axis=1)
    gate = nn(normed[:, near], gate_near) + nn(normed[:, far], gate_far[...])
    upper = nn(normed[:, near], up_near) + nn(normed[:, far], up_far[...])
    sigma = jax.nn.sigmoid(gate)
    active = gate * sigma
    inner = (active * upper).astype(BF)
    grad_inner = nt(grad_rows[...], down[...])
    grad_gate = (grad_inner * upper * sigma * (1.0 + gate * (1.0 - sigma))).astype(BF)
    grad_up = (grad_inner * active).astype(BF)
    for which in range(CORES):
        span = slice(which * LANES, (which + 1) * LANES)
        inner_ref[which] = inner[:, span]
        grad_gate_ref[which] = grad_gate[:, span]
        grad_up_ref[which] = grad_up[:, span]
    mixed_acc[...] += nn(inner, down[...])
    back_acc[:, near] += nt(grad_gate, gate_near) + nt(grad_up, up_near)
    back_acc[:, far] += nt(grad_gate, gate_far[...]) + nt(grad_up, up_far[...])

    @pl.when(step == 2 * half_steps - 1)
    def _():
        mixed_ref[...] = mixed_acc[...].astype(mixed_ref.dtype)
        back_ref[...] = back_acc[...].astype(back_ref.dtype)


def mlp_part(normed, grad_rows, weights, kind, number, travels):
    w_gate, w_up, far, w_down, down_far = weights
    rows, model = normed.shape
    depth, hidden = w_gate.shape
    half = hidden // 2
    steps = half // (2 * LANES)
    part = steps // 2
    kinds = tuple(how for how, _ in travels)
    arrays = [value for _, value in travels]

    def side():
        return lax.axis_index("fsdp")

    def pair_of(j):
        return jnp.where(j < part, side() * part + j, (1 - side()) * part + j - part)

    def whole(shape):
        return pl.BlockSpec(shape, lambda j: (0, 0))

    def column(odd):
        return pl.BlockSpec((depth, LANES), lambda j: (0, 4 * pair_of(j) + 2 * odd + side()))

    def row(odd):
        return pl.BlockSpec((LANES, model), lambda j: (4 * jnp.minimum(j, part - 1) + 2 * odd + side(), 0))

    def far_column(which):
        return pl.BlockSpec((None, depth, 2 * LANES), lambda j: (which, 0, pair_of(j)))

    far_row = pl.BlockSpec((2 * LANES, model), lambda j: (jnp.maximum(j - part, 0), 0))

    def place(j):
        pair = pair_of(j)
        return (0, 0, lax.rem(pair, LINES) * PLANES + lax.div(pair, LINES))

    act = pl.BlockSpec((CORES, rows, LANES), place)
    act_shape = jax.ShapeDtypeStruct((CORES, rows, half // CORES), BF)
    hbm = pl.BlockSpec(memory_space=pl.ANY)
    return pl.pallas_call(
        functools.partial(mlp_kernel, kinds),
        grid=(steps,),
        in_specs=[
            whole((rows, model)), whole((rows, model)),
            column(0), column(1), column(0), column(1), far_column(0), far_column(1),
            row(0), row(1), far_row,
        ]
        + [hbm] * len(kinds),
        out_specs=[act, act, act, whole((rows, model)), whole((rows, model))] + [hbm] * len(kinds),
        out_shape=[act_shape, act_shape, act_shape]
        + [jax.ShapeDtypeStruct((rows, model), kind)] * 2
        + [jax.ShapeDtypeStruct(value.shape[how == HALF :], BF) for how, value in travels],
        scratch_shapes=[
            pltpu.VMEM((2 * LANES, model), BF),
            pltpu.VMEM((rows, model), jnp.float32),
            pltpu.VMEM((rows, model), jnp.float32),
            pltpu.SemaphoreType.DMA((2, len(kinds) + 1)),
        ],
        compiler_params=pltpu.CompilerParams(
            collective_id=number, has_side_effects=True, vmem_limit_bytes=VMEM_LIMIT
        ),
        cost_estimate=pl.CostEstimate(
            flops=12 * rows * model * half, bytes_accessed=6 * model * half, transcendentals=rows * half
        ),
    )(normed, grad_rows, w_gate, w_gate, w_up, w_up, far, far, w_down, w_down, down_far, *arrays)


def head_rows_of(info, number, out_near, out_far):
    heads = []
    for is_far in range(2):
        for at_plane in range(PLANES // 2):
            for at_core in range(CORES):
                plane = 2 * (info[0] if is_far == 0 else 1 - info[0]) + at_plane
                heads.append((plane, at_core, out_far if is_far else out_near, (2 * at_plane + at_core) * 2 * HD))
    return heads


def post_kernel(info, att, tokens, out_near, out_far, gain, resid_ref, normed_ref):
    width = att.shape[1]
    total = tokens[...].astype(jnp.float32)
    for plane, core, weight, first in head_rows_of(info, 0, out_near, out_far):
        both = [att[plane * CORES * LINES + seq * CORES + core] for seq in range(LINES)]
        for head in range(2):
            rows = jnp.concatenate([block[:, head * LANES : head * LANES + HD] for block in both], axis=0)
            total = total + nn(rows, weight[first + head * HD : first + (head + 1) * HD, :])
    resid_ref[...] = total
    normed_ref[...] = (normalize(total)[0] * gain[...]).astype(BF)


def local_call(kernel, info, operands, outs):
    def spec(shape):
        return pl.BlockSpec(shape, lambda i, info: (0,) * len(shape))

    return pl.pallas_call(
        kernel,
        grid_spec=pltpu.PrefetchScalarGridSpec(
            num_scalar_prefetch=1,
            grid=(1,),
            in_specs=[spec(operand.shape) for operand in operands],
            out_specs=[spec(out.shape) for out in outs],
        ),
        out_shape=outs,
        compiler_params=pltpu.CompilerParams(vmem_limit_bytes=VMEM_LIMIT),
    )(info, *operands)


def local_copies(pairs, sems, first=0):
    return [pltpu.make_async_copy(source, target, sems.at[first + i]) for i, (source, target) in enumerate(pairs)]


def start(copies):
    for copy in copies:
        copy.start()


def wait(copies):
    for copy in copies:
        copy.wait()


def chip_moves(jobs, core, other_core, core_sems, local_sems):
    moves = []
    for number, (target, parts, halved) in enumerate(jobs):
        rows = target.shape[0] // 4
        copies = []
        for which, source in enumerate(parts):
            place = target.at[pl.ds(which * rows, rows)]
            if source is None:
                copies.append(ctx_copy(parts[1].at[1 - core], place, core_sems, number, other_core))
            else:
                mine = source.at[core] if halved and which < 2 else source
                copies.append(pltpu.make_async_copy(mine, place, local_sems.at[4 * number + which]))
        moves.append(copies)
    return moves


def split_lines(source, normed, keep, sent, line):
    columns = keep.shape[1]
    for at_line in range(LINES):
        for at_plane in range(0, PLANES, 2):
            first = (at_line * PLANES + at_plane) * columns
            both = tn(source[:, first : first + 2 * columns], normed[...]).astype(BF)
            for i in range(2):
                block = both[i * columns : (i + 1) * columns]

                @pl.when(line == at_line)
                def _():
                    keep[at_plane + i] = block

                @pl.when(line != at_line)
                def _():
                    sent[at_plane + i] = block


def middle_kernel(
    back_far, inner_own, inner_far, inner_sib, gate_own, gate_far, gate_sib, normed_own, normed_far, normed_sib,
    normed_sib_far, cot_own, cot_far, cot_sib, cot_sib_far, back_in, resid_in, near_in, far_in, gain,
    down_keep, down_sent, down_first, gate_keep, gate_sent, grad_ref, branch_ref, att_ref, gain_ref,
    back_got, inner_all, gate_all, normed_all, cot_all, back_own, resid, out_near, out_far,
    side_sems, core_sems, local_sems, line_sems, load_sems,
):
    rank = lax.axis_index("ctx")
    side = lax.axis_index("fsdp")
    core = lax.rem(rank, CORES)
    line = lax.rem(lax.div(rank, CORES), LINES)
    other_line = rank + CORES * (1 - 2 * line)
    other_core = rank + 1 - 2 * core
    rows = normed_own.shape[0]
    greet_near(rank, side, False)
    cross = side_copy(back_far, back_got, side_sems, 0, 1 - side)
    cross.start()

    jobs = (
        (inner_all, (inner_own, inner_far, inner_sib, None), True),
        (cot_all, (cot_own, cot_far, cot_sib, cot_sib_far), False),
        (gate_all, (gate_own, gate_far, gate_sib, None), True),
        (normed_all, (normed_own, normed_far, normed_sib, normed_sib_far), False),
    )
    moves = chip_moves(jobs, core, other_core, core_sems, local_sems)
    loads = [
        pltpu.make_async_copy(source, target, load_sems.at[number])
        for number, (source, target) in enumerate(
            ((back_in, back_own), (resid_in, resid), (near_in, out_near), (far_in, out_far))
        )
    ]
    for copies in moves + [loads]:
        for copy in copies:
            copy.start()

    def landed(number):
        for copy in moves[number]:
            copy.wait()

    def lines(slot, number):
        return ctx_copy(down_sent.at[number], down_first.at[slot], line_sems, slot, other_line)

    landed(0)
    landed(1)
    per_chip = down_keep.shape[1]
    for at_plane in (3, 0, 2, 1):
        span = slice(at_plane * LINES * per_chip, (at_plane + 1) * LINES * per_chip)
        both = tn(cot_all[:, span], inner_all[...]).astype(BF)
        for at_line in range(LINES):
            block = both[at_line * per_chip : (at_line + 1) * per_chip]

            @pl.when(line == at_line)
            def _():
                down_keep[at_plane] = block

            @pl.when(line != at_line)
            def _():
                down_sent[at_plane] = block

        if at_plane in DOWN_EARLY:
            lines(DOWN_EARLY.index(at_plane), at_plane).start()

    landed(2)
    landed(3)
    split_lines(gate_all, normed_all, gate_keep, gate_sent, line)
    for copy in loads:
        copy.wait()
    cross.wait()
    grad_normed = back_own[...] + wide(back_got[...])
    unit, inv = normalize(resid[...])
    gain_ref[...] = jnp.sum(grad_normed * unit, axis=0, keepdims=True)
    grad = wide(cot_all[0:rows, :]) + norm_back(grad_normed, gain[...], unit, inv)
    grad_ref[...] = grad
    branch = grad.astype(BF)
    branch_ref[...] = branch
    width = att_ref.shape[1]
    blank = jnp.zeros((width, LANES - HD), BF)
    for plane, at_core, weight, first in head_rows_of((side,), 0, out_near, out_far):
        for head in range(2):
            back = nt(branch, weight[first + head * HD : first + (head + 1) * HD, :]).astype(BF)
            for seq in range(LINES):
                number = plane * CORES * LINES + seq * CORES + at_core
                att_ref[number, :, head * LANES : head * LANES + HD] = back[seq * width : (seq + 1) * width]
                att_ref[number, :, head * LANES + HD : (head + 1) * LANES] = blank
    for slot, number in enumerate(DOWN_EARLY):
        lines(slot, number).wait()


def middle(back_far, acts, normed, cot, back_own, resid, gain, out_near, out_far):
    rows, model = resid.shape
    half = acts[0].shape[2]
    per_chip, columns = model // CHIPS, half // CHIPS
    vmem = pl.BlockSpec(memory_space=pltpu.VMEM)
    hbm = pl.BlockSpec(memory_space=pl.ANY)
    dma = pltpu.SemaphoreType.DMA

    def low(*dims):
        return jax.ShapeDtypeStruct(dims, BF)

    outs = [
        low(PLANES, per_chip, half),
        low(PLANES, per_chip, half),
        low(len(DOWN_EARLY), per_chip, half),
        low(PLANES, columns, model),
        low(PLANES, columns, model),
        jax.ShapeDtypeStruct((rows, model), jnp.float32),
        low(rows, model),
        low(RANKS, rows // LINES, 2 * LANES),
        jax.ShapeDtypeStruct((1, model), jnp.float32),
    ]
    return pl.pallas_call(
        middle_kernel,
        in_specs=[hbm] * 19 + [vmem],
        out_specs=[vmem, vmem, hbm] + [vmem] * 6,
        out_shape=outs,
        scratch_shapes=[
            pltpu.VMEM((rows, model), BF),
            pltpu.VMEM((4 * rows, half), BF),
            pltpu.VMEM((4 * rows, half), BF),
            pltpu.VMEM((4 * rows, model), BF),
            pltpu.VMEM((4 * rows, model), BF),
            pltpu.VMEM((rows, model), jnp.float32),
            pltpu.VMEM((rows, model), jnp.float32),
            pltpu.VMEM(out_near.shape, BF),
            pltpu.VMEM(out_far.shape, BF),
            dma((2, 1)),
            dma((2, 4)),
            dma((16,)),
            dma((2, len(DOWN_EARLY))),
            dma((4,)),
        ],
        compiler_params=pltpu.CompilerParams(collective_id=4, has_side_effects=True, vmem_limit_bytes=VMEM_LIMIT),
    )(back_far, *acts, *normed, *cot, back_own, resid, out_near, out_far, gain)


def last_kernel(info, thin, broad, query_out, key_out, value_out, out_out, gate_out, up_out, down_out):
    side, core = info[0], info[1]
    columns = gate_out.shape[1] // 2
    first = 4 * columns
    for result in (query_out, key_out, value_out, out_out):
        result[...] = wide(broad[first : first + result.shape[0], :])
        first += result.shape[0]
    for which, result in enumerate((gate_out, up_out)):
        for other in range(2):
            first = (2 * which + other) * columns
            place = pl.ds(pl.multiple_of((side if other == 0 else 1 - side) * columns, LANES), columns)
            result[:, place] = wide(broad[first : first + columns, :]).T
    span = thin.shape[2] // 4
    for which in range(2):
        at_core = core if which == 0 else 1 - core
        for at_line in range(LINES):
            for low in range(PLANES // 2):
                first = ((low * LINES + at_line) * CORES + at_core) * 2
                lanes = pl.ds(pl.multiple_of(at_line * 2 * span + side * span + low * LANES, LANES), LANES)
                down_out[:, pl.ds(pl.multiple_of((first + side) * LANES, LANES), LANES)] = wide(thin[which, :, lanes])
                start_at = (which * LINES + at_line) * span + low * LANES
                block = wide(thin[2, :, start_at : start_at + LANES])
                down_out[:, pl.ds(pl.multiple_of((first + 1 - side) * LANES, LANES), LANES)] = block


def gather_kernel(
    tokens, w_query, w_key, w_value, w_gate, w_up, w_out, angle_ref, attn_gain, mlp_gain,
    seq_out, head_in, head_out, far, out_far, cos_ref, sin_ref, attn_row, mlp_row, weight_refs, load_sems, sems_in, sems_up, sems_down, sems_core, weight_sems, column_sems, group_sems, local_sem
):
    rank = lax.axis_index("ctx")
    side = lax.axis_index("fsdp")
    core = lax.rem(rank, CORES)
    line = lax.rem(lax.div(rank, CORES), LINES)
    plane = lax.div(rank, CORES * LINES)
    step_rank = CORES * LINES
    last = PLANES - 1
    other_line = rank + CORES * (1 - 2 * line)
    other_core = rank + 1 - 2 * core
    greet_near(rank, side, True)

    def spot(at_plane, at_line):
        return at_plane * step_rank + at_line * CORES + core

    def move(index, send_sems, to, source=None):
        return pltpu.make_async_remote_copy(
            src_ref=seq_out.at[index] if source is None else source,
            dst_ref=seq_out.at[index],
            send_sem=send_sems.at[index],
            recv_sem=sems_in.at[index],
            device_id={"ctx": to},
            device_id_type=pl.DeviceIdType.MESH,
        )

    near, across = spot(plane, line), spot(plane, 1 - line)
    mine = tokens.at[line]
    to_line = pltpu.make_async_remote_copy(
        src_ref=tokens.at[1 - line],
        dst_ref=seq_out.at[near],
        send_sem=local_sem.at[1],
        recv_sem=sems_in.at[near],
        device_id={"ctx": other_line},
        device_id_type=pl.DeviceIdType.MESH,
    )
    landed_line = pltpu.make_async_remote_copy(
        src_ref=tokens.at[1 - line],
        dst_ref=seq_out.at[across],
        send_sem=local_sem.at[1],
        recv_sem=sems_in.at[across],
        device_id={"ctx": other_line},
        device_id_type=pl.DeviceIdType.MESH,
    )
    own = pltpu.make_async_copy(mine, seq_out.at[near], local_sem.at[0])

    def spread(index, up, down, source=None):
        if up:
            @pl.when(plane < last)
            def _():
                move(index, sems_up, rank + step_rank, source).start()

        if down:
            @pl.when(plane > 0)
            def _():
                move(index, sems_down, rank - step_rank, source).start()

        move(index, sems_core, other_core, source).start()

    loads = local_copies(zip((w_query, w_key, w_value), weight_refs), load_sems)
    start(loads)
    to_line.start()
    spread(near, True, True, mine)
    own.start()

    head_cross = side_copy(head_in, head_out, weight_sems, 0, 1 - side)
    depth = w_gate.shape[0] // LINES
    rows = pl.ds(pl.multiple_of(line * depth, 16), depth)
    other_rows = pl.ds(pl.multiple_of((1 - line) * depth, 16), depth)
    groups = 4
    group_columns = far.shape[2] // groups
    per_group = group_columns // LANES

    def column(weight, number):
        there = pl.ds(number * LANES, LANES)
        here = pl.ds(pl.multiple_of((2 * number + 1 - side) * LANES, LANES), LANES)
        return side_copy(weight.at[rows, here], far.at[core, rows, there], column_sems, number, 1 - side)

    def send_group(group):
        for number in range(group * per_group, (group + 1) * per_group):
            @pl.when(core == 0)
            def _():
                column(w_gate, number).start()

            @pl.when(core != 0)
            def _():
                column(w_up, number).start()

    def group_copy(group, which_rows, kind, to):
        block = far.at[core, which_rows, pl.ds(group * group_columns, group_columns)]
        return ctx_copy(block, block, group_sems, kind * groups + group, to)

    def pass_group(group):
        for number in range(group * per_group, (group + 1) * per_group):
            column(w_gate, number).wait_recv()
        group_copy(group, rows, 0, other_line).start()
        group_copy(group, rows, 1, other_core).start()

    def pass_line(group):
        group_copy(group, rows, 0, other_line).wait_recv()
        group_copy(group, other_rows, 2, other_core).start()

    quarter = 2 * core + line
    out_rows = w_out.shape[0] // 4

    def out_slice(ref, which):
        return ref.at[pl.ds(pl.multiple_of(which * out_rows, 16), out_rows)]

    out_mine, out_got = out_slice(out_far, quarter), out_slice(out_far, 2 * core + 1 - line)
    out_cross = side_copy(out_slice(w_out, quarter), out_mine, weight_sems, 1, 1 - side)
    out_line = ctx_copy(out_mine, out_mine, weight_sems, 2, other_line)
    out_core = ctx_copy(out_mine, out_mine, weight_sems, 3, other_core)
    out_more = ctx_copy(out_got, out_got, weight_sems, 4, other_core)
    send_group(0)
    send_group(1)

    head = plane * CORES + core
    columns = head_in.shape[1]
    wait(loads)
    picked = 0.0
    for weight, first, size in zip(weight_refs, (0, 2 * HD, 3 * HD), (2 * HD, HD, HD)):
        source = lax.broadcasted_iota(jnp.int32, (weight.shape[1], columns), 0) - head * size
        target = lax.broadcasted_iota(jnp.int32, (weight.shape[1], columns), 1) - first
        chosen = jnp.where((source == target) & (target >= 0) & (target < size), 1.0, 0.0).astype(BF)
        picked = picked + nn(weight[...], chosen)
    head_in[...] = picked.astype(BF)
    for source, target in ((attn_gain, attn_row), (mlp_gain, mlp_row)):
        for part in range(source.shape[0]):
            target[0:1, part * LANES : (part + 1) * LANES] = source[part : part + 1, :]
    block = tokens.shape[1]

    @pl.loop(0, RANKS)
    def _(number):
        position = (number * block + lax.broadcasted_iota(jnp.int32, (block, LANES), 0)).astype(jnp.float32)
        angles = position * angle_ref[0:1, :]
        here = pl.ds(pl.multiple_of(number * block, block), block)
        cos_ref[here, :] = jnp.cos(angles) * angle_ref[1:2, :]
        sin_ref[here, :] = jnp.sin(angles) * angle_ref[2:3, :]

    def forward(index, up, down):
        move(index, sems_core, other_core).wait_recv()
        spread(index, up, down)

    landed_line.wait_recv()
    spread(across, True, True)

    def pass_on(away, at_line):
        @pl.when(plane >= away)
        def _():
            forward(spot(plane - away, at_line), True, False)

        @pl.when(plane + away <= last)
        def _():
            forward(spot(plane + away, at_line), False, True)

    pass_on(1, line)
    pass_group(0)
    send_group(2)
    pass_group(1)
    send_group(3)
    pass_on(1, 1 - line)
    pass_line(0)
    pass_on(2, line)
    pass_group(2)
    out_cross.start()
    pass_group(3)
    head_cross.start()
    pass_line(1)
    pass_on(2, 1 - line)
    pass_line(2)
    pass_on(3, line)
    out_cross.wait_recv()
    out_line.start()
    out_core.start()
    pass_line(3)
    pass_on(3, 1 - line)
    out_line.wait_recv()
    out_more.start()

    for at_plane in range(PLANES):
        for at_line in range(LINES):
            index = at_plane * step_rank + at_line * CORES + 1 - core
            move(index, sems_core, other_core).wait_recv()
    head_cross.wait_recv()
    out_core.wait_recv()
    out_more.wait_recv()
    for group in range(groups):
        group_copy(group, rows, 1, other_core).wait_recv()
        group_copy(group, other_rows, 2, other_core).wait_recv()

    own.wait()
    to_line.wait_send()
    for at_plane in range(PLANES):
        for at_line in range(LINES):
            index = at_plane * step_rank + at_line * CORES + core
            move(index, sems_core, other_core).wait_send()

            @pl.when((plane < last) & (at_plane <= plane))
            def _():
                move(index, sems_up, rank + step_rank).wait_send()

            @pl.when((plane > 0) & (at_plane >= plane))
            def _():
                move(index, sems_down, rank - step_rank).wait_send()

    for copy in (head_cross, out_cross, out_line, out_core, out_more):
        copy.wait_send()
    for number in range(groups * per_group):
        column(w_gate, number).wait_send()
    for group in range(groups):
        group_copy(group, rows, 0, other_line).wait_send()
        group_copy(group, rows, 1, other_core).wait_send()
        group_copy(group, other_rows, 2, other_core).wait_send()


def gather_all(tokens, attn_weights, w_gate, w_up, w_out, angles, gains):
    width, model = tokens.shape[1:]
    depth, hidden = w_gate.shape
    hbm = pl.BlockSpec(memory_space=pl.ANY)
    vmem = pl.BlockSpec(memory_space=pltpu.VMEM)
    dma = pltpu.SemaphoreType.DMA
    return pl.pallas_call(
        gather_kernel,
        in_specs=[hbm] * 7 + [vmem] * 3,
        out_specs=[hbm, vmem] + [hbm] * 3 + [vmem] * 4,
        out_shape=[
            jax.ShapeDtypeStruct((RANKS, width, model), BF),
            jax.ShapeDtypeStruct((depth, HEAD_COLS), BF),
            jax.ShapeDtypeStruct((depth, HEAD_COLS), BF),
            jax.ShapeDtypeStruct((2, depth, hidden // 2), BF),
            jax.ShapeDtypeStruct(w_out.shape, BF),
            jax.ShapeDtypeStruct((RANKS * width, LANES), jnp.float32),
            jax.ShapeDtypeStruct((RANKS * width, LANES), jnp.float32),
            jax.ShapeDtypeStruct((1, model), jnp.float32),
            jax.ShapeDtypeStruct((1, model), jnp.float32),
        ],
        scratch_shapes=[[pltpu.VMEM(weight.shape, BF) for weight in attn_weights], dma((3,)), dma((RANKS,)), dma((RANKS,)), dma((RANKS,)), dma((RANKS,)), dma((2, 5)), dma((2, RANKS)), dma((2, 12)), dma((2,))],
        compiler_params=pltpu.CompilerParams(collective_id=1, has_side_effects=True, vmem_limit_bytes=VMEM_LIMIT),
    )(tokens, *attn_weights, w_gate, w_up, w_out, angles, *gains)


def ctx_copy(source, target, sems, number, rank):
    return pltpu.make_async_remote_copy(
        src_ref=source,
        dst_ref=target,
        send_sem=sems.at[0, number],
        recv_sem=sems.at[1, number],
        device_id={"ctx": rank},
        device_id_type=pl.DeviceIdType.MESH,
    )


def side_copy(source, target, sems, number, side):
    return pltpu.make_async_remote_copy(
        src_ref=source,
        dst_ref=target,
        send_sem=sems.at[0, number],
        recv_sem=sems.at[1, number],
        device_id={"fsdp": side},
        device_id_type=pl.DeviceIdType.MESH,
    )


def greet(rank, side):
    barrier = pltpu.get_barrier_semaphore()
    for away in range(1, RANKS):
        pl.semaphore_signal(
            barrier,
            inc=1,
            device_id={"ctx": lax.rem(rank + away, RANKS)},
            device_id_type=pl.DeviceIdType.MESH,
        )
    pl.semaphore_signal(barrier, inc=1, device_id={"fsdp": 1 - side}, device_id_type=pl.DeviceIdType.MESH)
    pl.semaphore_wait(barrier, RANKS)


def greet_near(rank, side, planes):
    barrier = pltpu.get_barrier_semaphore()
    core = lax.rem(rank, CORES)
    line = lax.rem(lax.div(rank, CORES), LINES)
    plane = lax.div(rank, CORES * LINES)

    def signal(where):
        pl.semaphore_signal(barrier, inc=1, device_id=where, device_id_type=pl.DeviceIdType.MESH)

    signal({"ctx": rank + 1 - 2 * core})
    signal({"ctx": rank + CORES * (1 - 2 * line)})
    signal({"fsdp": 1 - side})
    expected = 3
    if planes:
        @pl.when(plane > 0)
        def _():
            signal({"ctx": rank - CORES * LINES})

        @pl.when(plane < PLANES - 1)
        def _():
            signal({"ctx": rank + CORES * LINES})

        expected = 4 + jnp.where((plane > 0) & (plane < PLANES - 1), 1, 0)
    pl.semaphore_wait(barrier, expected)


def wide(value):
    return value.astype(jnp.float32)


@dataclasses.dataclass
class Weight:
    keep: Any
    got: Any
    acc: Any
    landed: Any
    number: int
    arrival: Any = None
    first: int = 0
    prior: Any = None


class Chain:
    def __init__(self, rank, plane, sems):
        self.rank, self.plane, self.sems = rank, plane, sems
        self.last = PLANES - 1

    def depth(self, direction):
        return self.plane if direction == 0 else self.last - self.plane

    def sends(self, direction, step):
        depth = self.depth(direction)
        return (depth <= step) & (depth < self.last)

    def takes(self, direction, step):
        depth = self.depth(direction)
        return (depth >= 1) & (depth <= step + 1)

    def message(self, weight, direction, step):
        slot = direction * self.last + step
        target = self.rank + CORES * LINES * (1 - 2 * direction)
        place = jnp.clip(step - direction * (self.last - self.plane), 0, self.last - 1)
        number = weight.number * 2 * self.last + slot
        return ctx_copy(weight.acc.at[place], weight.landed.at[slot], self.sems, number, target)

    def receive(self, weight, step):
        for direction in range(2):
            @pl.when(self.takes(direction, step))
            def _():
                self.message(weight, direction, step).wait_recv()

    def hop(self, weight, step):
        for direction in range(2):
            piece = self.plane + (self.last - step) * (1 - 2 * direction)
            place = step - direction * (self.last - self.plane)
            sends = self.sends(direction, step)
            if weight.arrival is not None:
                weight.arrival(piece, sends)
            if step > weight.first:
                @pl.when(self.takes(direction, step - 1))
                def _():
                    self.message(weight, direction, step - 1).wait_recv()

            if step:
                landed = weight.landed if step > weight.first else weight.prior
                slot = direction * self.last + step - 1

                @pl.when(self.takes(direction, step - 1) & sends)
                def _():
                    total = wide(weight.keep[piece]) + wide(weight.got[piece]) + wide(landed[slot])
                    weight.acc[place] = total.astype(BF)

            @pl.when(self.depth(direction) == 0)
            def _():
                weight.acc[place] = (wide(weight.keep[piece]) + wide(weight.got[piece])).astype(BF)

            @pl.when(sends)
            def _():
                self.message(weight, direction, step).start()

    def finish(self, weight, result):
        last, plane = self.last, self.plane
        self.receive(weight, last - 1)
        if weight.arrival is not None:
            weight.arrival(plane, plane >= 0)
        base = wide(weight.keep[plane]) + wide(weight.got[plane])
        above, below = weight.landed.at[last - 1], weight.landed.at[2 * last - 1]

        @pl.when(plane == 0)
        def _():
            result[...] = (base + wide(below[...])).astype(BF)

        @pl.when(plane == last)
        def _():
            result[...] = (base + wide(above[...])).astype(BF)

        @pl.when((plane > 0) & (plane < last))
        def _():
            result[...] = (base + wide(above[...]) + wide(below[...])).astype(BF)

    def sent(self, weight, first, end):
        for step in range(first, end):
            for direction in range(2):
                @pl.when(self.sends(direction, step))
                def _():
                    self.message(weight, direction, step).wait_send()


def reduce_kernel(
    rows_hbm, down_keep_in, down_got_in, down_hops_in, gate_keep_in, gate_first, gate_sent, up_keep_in, up_sent, out_sum_in,
    normed_in, head_near, head_far, attn_gain, mlp_part, w_value, w_query, w_key, key_far, tokens_in, grad_in,
    tokens_grad, thin, broad, gains_out, value_far, query_far,
    rows_out, query_buf, key_buf, value_buf, tokens, grad, total, weight_sems, rows_in, down_keep, down_got, down_hops, gate_keep, up_keep, out_sum, load_sems, gate_got, up_got, out_got, down_acc, gate_acc, up_acc, out_acc,
    down_in, gate_in, up_in, out_in, down_mine, down_theirs, gate_mine, up_mine,
    normed_buf, head_grad, head_sum, head_sent, head_got, head_two, head_side, head_last, gain_buf, gain_in,
    exchange_sems, plane_sems, sems, line_sems, fetch_sems, local_sems,
):
    rank = lax.axis_index("ctx")
    side = lax.axis_index("fsdp")
    core = lax.rem(rank, CORES)
    line = lax.rem(lax.div(rank, CORES), LINES)
    plane = lax.div(rank, CORES * LINES)
    step_rank = CORES * LINES
    last = PLANES - 1
    other_line = rank + CORES * (1 - 2 * line)
    other_core = rank + 1 - 2 * core
    down_loads = local_copies(
        ((down_keep_in, down_keep), (down_got_in, down_got), (down_hops_in, down_hops)), load_sems
    )
    gate_loads = local_copies(
        [(gate_keep_in, gate_keep)] + [(gate_first.at[slot], gate_got.at[number]) for slot, number in enumerate(GATE_EARLY)],
        load_sems,
        3,
    )
    row_loads = local_copies(((rows_hbm, rows_in),), load_sems, 7)
    out_loads = local_copies(((out_sum_in, out_sum),), load_sems, 8)
    up_loads = local_copies(((up_keep_in, up_keep),), load_sems, 9)
    near_loads = local_copies(((w_query, query_buf), (w_key, key_buf), (w_value, value_buf)), weight_sems)
    far_loads = local_copies(((query_far, query_buf), (key_far, key_buf), (value_far, value_buf)), weight_sems, 3)
    token_loads = local_copies(((tokens_in, tokens), (grad_in, grad)), weight_sems, 6)
    start(down_loads + gate_loads + row_loads + out_loads + up_loads + near_loads + token_loads)
    greet(rank, side)


    def gate_line(number):
        return ctx_copy(gate_sent.at[number], gate_got.at[number], line_sems, number, other_line)

    def up_line(number):
        return ctx_copy(up_sent.at[number], up_got.at[number], line_sems, PLANES + number, other_line)

    model = head_grad.shape[1]
    half = model // 2
    near = pl.ds(pl.multiple_of(side * half, LANES), half)
    far = pl.ds(pl.multiple_of((1 - side) * half, LANES), half)
    out_line = ctx_copy(out_sum_in.at[1 - line], out_got, sems, 18, other_line)
    head_cross = side_copy(head_sent, head_side, sems, 8, 1 - side)
    head_line = ctx_copy(head_two, head_got, sems, 2, other_line)

    def gate_arrival(piece, wanted):
        late = functools.reduce(jnp.logical_and, [piece != number for number in GATE_EARLY])

        @pl.when(wanted & late)
        def _():
            gate_line(piece).wait_recv()

    def up_arrival(piece, wanted):
        @pl.when(wanted)
        def _():
            up_line(piece).wait_recv()

    chain = Chain(rank, plane, plane_sems)
    hop, finish = chain.hop, chain.finish
    down = Weight(down_keep, down_got, down_acc, down_in, 0, None, 2, down_hops)
    gate = Weight(gate_keep, gate_got, gate_acc, gate_in, 1, gate_arrival)
    half_rows = up_keep.shape[1] // 2
    ups = []
    for which in range(2):
        part = pl.ds(which * half_rows, half_rows)
        views = [ref.at[:, part] for ref in (up_keep, up_got, up_acc, up_in)]
        ups.append(Weight(*views, 2 + 2 * which, up_arrival if which == 0 else None))

    def hop_ups(step):
        for weight in ups:
            hop(weight, step)

    out = Weight(out_sum.at[line], out_got, out_acc, out_in, 3)
    gate_late = [number for number in range(PLANES) if number not in GATE_EARLY]
    for number in gate_late:
        gate_line(number).start()
    for number in (3, 0, 2, 1):
        up_line(number).start()

    def row_copy(away):
        to = lax.rem(rank + away, RANKS)
        return ctx_copy(rows_hbm.at[to], rows_out.at[rank], exchange_sems, away, to)

    def send_rows(same):
        for away in range(1, RANKS):
            to = lax.rem(rank + away, RANKS)
            crossing = lax.rem(lax.div(to, CORES), LINES) != line

            @pl.when(crossing != same)
            def _():
                row_copy(away).start()

    send_rows(True)
    wait(down_loads)
    hop(down, 2)
    wait(gate_loads)
    hop(gate, 0)
    own = pltpu.make_async_copy(rows_hbm.at[rank], rows_out.at[rank], local_sems.at[2])
    own.start()
    fetched = []
    for number, (source, target) in enumerate(((w_value, value_far), (w_query, query_far))):
        per = source.shape[0] // CORES
        part = pl.ds(pl.multiple_of(core * per, 16), per)
        cross = side_copy(source.at[part], target.at[part], fetch_sems, number, 1 - side)
        fetched.append((cross, ctx_copy(target.at[part], target.at[part], fetch_sems, 2 + number, other_core)))

    gain_partners = (None, other_core, other_line, rank + step_rank * (1 - 2 * lax.rem(plane, 2)),
                     rank + 2 * step_rank * (1 - 2 * lax.div(plane, 2)))

    def gain_copy(number):
        if number == 0:
            return side_copy(gain_buf.at[0], gain_in.at[0], sems, 3, 1 - side)
        return ctx_copy(gain_buf.at[number], gain_in.at[number], sems, 3 + number, gain_partners[number])

    def gain_hop(number):
        if number:
            gain_copy(number - 1).wait_recv()
            gain_buf[number] = gain_buf[number - 1] + gain_in[number - 1]
        if number < 5:
            gain_copy(number).start()

    chunks = normed_in.shape[0] // normed_buf.shape[1]
    chunk_rows = normed_buf.shape[1]
    blocks = chunk_rows // rows_in.shape[1]

    def chunk_copy(number):
        return pltpu.make_async_copy(
            normed_in.at[pl.ds(number * chunk_rows, chunk_rows)], normed_buf.at[number % 2], local_sems.at[number % 2]
        )

    chunk_copy(0).start()
    wait(row_loads)
    for number in range(chunks):
        if number + 1 < chunks:
            chunk_copy(number + 1).start()
        chunk_copy(number).wait()
        rows = jnp.concatenate([rows_in[number * blocks + i] for i in range(blocks)], axis=0)
        term = nn(rows.T, normed_buf[number % 2])
        head_grad[...] = term if number == 0 else head_grad[...] + term
    gain_buf[0] = jnp.zeros_like(gain_buf[0])
    for lanes, weight in ((near, head_near), (far, head_far)):
        term = jnp.sum(head_grad[:, lanes] * wide(weight[...]).T, axis=0, keepdims=True)
        gain_buf[0, 0:1, lanes] = term / attn_gain[:, lanes]
    gain_buf[0, 1:2, :] = mlp_part[...]

    def half_columns(which):
        quarter = HD // 2
        first = pl.ds(pl.multiple_of(which * HD, 16), HD)
        key = pl.ds(pl.multiple_of(2 * HD + which * quarter, 16), quarter)
        value = pl.ds(pl.multiple_of(3 * HD + which * quarter, 16), quarter)
        return jnp.concatenate([head_sum[first, :], head_sum[key, :], head_sum[value, :]], axis=0)

    head_sent[...] = head_grad[:, far].astype(BF)
    head_cross.start()
    gain_hop(0)
    gain_hop(1)

    for cross, _ in fetched:
        cross.start()
    wait(out_loads + up_loads)
    hop(gate, 1)
    hop_ups(0)
    send_rows(False)
    out_line.start()
    head_cross.wait_recv()
    head_sum[...] = head_grad[:, near] + wide(head_side[...])
    head_two[...] = half_columns(1 - line).astype(BF)
    head_line.start()
    hop(gate, 2)
    hop_ups(1)
    gain_hop(2)
    gain_hop(3)
    hop_ups(2)
    out_line.wait_recv()
    hop(out, 0)
    finish(down, down_mine)
    per_core = down_mine.shape[0] // CORES
    theirs = pl.ds(pl.multiple_of((1 - core) * per_core, 16), per_core)
    mine = pl.ds(pl.multiple_of(core * per_core, 16), per_core)
    down_core = ctx_copy(down_mine.at[theirs], down_theirs, sems, 10, other_core)
    down_core.start()
    for cross, onward in fetched:
        cross.wait_recv()
        onward.start()
    for away in range(1, RANKS):
        row_copy(away).wait_recv()
    own.wait()

    def row_gradients(lanes):
        acc = 0.0
        for head in range(HK):
            first = head // CORES * CORES * LINES + head % CORES
            rows = jnp.concatenate([rows_out[first + seq * CORES] for seq in range(LINES)], axis=0)
            for weight, begin, size in ((query_buf, 0, 2 * HD), (key_buf, 2 * HD, HD), (value_buf, 3 * HD, HD)):
                acc = acc + nt(rows[:, begin : begin + size], weight[:, head * size : (head + 1) * size])
        total[:, lanes] = acc

    wait(near_loads)
    row_gradients(near)
    for _, onward in fetched:
        onward.wait_recv()
    start(far_loads)
    head_line.wait_recv()
    head_last[...] = (half_columns(line) + wide(head_got[...])).astype(BF)
    turned = rank - CORES * line - core + CORES * core + line
    head_out = broad.at[pl.ds(4 * gate_mine.shape[0], head_last.shape[0])]
    head_turn = ctx_copy(head_last, head_out, sems, 9, turned)

    @pl.when(line != core)
    def _():
        head_turn.start()

    @pl.when(line == core)
    def _():
        head_out[...] = head_last[...]

    gain_hop(4)
    hop(out, 1)
    finish(gate, gate_mine)
    columns = gate_mine.shape[0]
    gate_cross = side_copy(gate_mine.at[:, far], broad.at[pl.ds(columns, columns)], sems, 11, 1 - side)
    gate_cross.start()

    gain_hop(5)
    gains_out[...] = gain_buf[5]

    down_core.wait_recv()
    crosses = []
    span = down_mine.shape[1] // 4
    for which in range(2):
        block = down_mine.at[mine] if which == 0 else down_theirs
        for at_line in range(LINES):
            lanes = pl.ds(pl.multiple_of(at_line * 2 * span + (1 - side) * span, LANES), span)
            cross = side_copy(
                block.at[:, lanes],
                thin.at[2, :, pl.ds((which * LINES + at_line) * span, span)],
                sems,
                13 + which * LINES + at_line,
                1 - side,
            )
            cross.start()
            crosses.append(cross)

    hop(out, 2)
    for which, weight in enumerate(ups):
        finish(weight, up_mine.at[pl.ds(which * half_rows, half_rows)])
    up_cross = side_copy(up_mine.at[:, far], broad.at[pl.ds(3 * columns, columns)], sems, 12, 1 - side)
    up_cross.start()
    wait(far_loads + token_loads)
    row_gradients(far)
    unit, inv = normalize(wide(tokens[...]))
    tokens_grad[...] = (grad[...] + norm_back(total[...], attn_gain[...], unit, inv)).astype(BF)
    finish(out, broad.at[pl.ds(4 * columns + head_last.shape[0], out_got.shape[1])])
    @pl.when(line != core)
    def _():
        head_turn.wait()

    thin[0] = down_mine[mine, :]
    thin[1] = down_theirs[...]
    broad[0:columns, :] = gate_mine[:, near]
    broad[2 * columns : 3 * columns, :] = up_mine[:, near]
    for away in range(1, RANKS):
        row_copy(away).wait_send()
    for cross in crosses + [gate_cross, up_cross]:
        cross.wait()
    for copy in (out_line, head_line, head_cross, down_core):
        copy.wait_send()
    for cross, onward in fetched:
        cross.wait_send()
        onward.wait_send()
    for number in range(5):
        gain_copy(number).wait_send()
    for number in range(PLANES):
        up_line(number).wait_send()
    for number in gate_late:
        gate_line(number).wait_send()
    for weight in (down, gate, *ups, out):
        chain.sent(weight, weight.first, last)


def reduce_all(rows_in, down, gate, up, out_sum, head, attn_weights, w_key, key_far, tokens, grad):
    (down_keep, down_got, down_hops), (gate_keep, gate_first, gate_sent), (up_keep, up_sent) = down, gate, up
    normed, head_near, head_far, attn_gain, mlp_part = head
    head_cols, model = head_near.shape[1], normed.shape[1]
    half = model // 2
    hops = 2 * (PLANES - 1)
    vmem = pl.BlockSpec(memory_space=pltpu.VMEM)
    hbm = pl.BlockSpec(memory_space=pl.ANY)
    dma = pltpu.SemaphoreType.DMA

    def piece(keep):
        return keep.shape[1:]

    def out(dims):
        return jax.ShapeDtypeStruct(dims, BF)

    def low(*dims):
        return pltpu.VMEM(dims, BF)

    down_rows, down_cols = piece(down_keep)
    columns = gate_keep.shape[1]
    out_half = out_sum.shape[1:]
    keeps = (down_keep, gate_keep, up_keep, jax.ShapeDtypeStruct(out_half, BF))
    return pl.pallas_call(
        reduce_kernel,
        in_specs=[hbm] * 11 + [vmem] * 4 + [hbm] * 6,
        out_specs=[vmem] * 4 + [hbm] * 2,
        out_shape=[
            out(tokens.shape),
            out((3, down_rows // CORES, down_cols)),
            out((4 * columns + head_cols // 2 + out_half[1], half)),
            jax.ShapeDtypeStruct((8, model), jnp.float32),
        ]
        + [jax.ShapeDtypeStruct(weight.shape, BF) for weight in attn_weights],
        scratch_shapes=[
            low(*rows_in.shape),
            low(*attn_weights[1].shape),
            low(*w_key.shape),
            low(*w_key.shape),
            low(*tokens.shape),
            pltpu.VMEM(grad.shape, jnp.float32),
            pltpu.VMEM(grad.shape, jnp.float32),
            dma((8,)),
        ]
        + [low(*value.shape) for value in (rows_in, down_keep, down_got, down_hops, gate_keep, up_keep, out_sum)]
        + [
            dma((10,)),
            low(*gate_keep.shape),
            low(*up_keep.shape),
            low(*out_half),
        ]
        + [low(PLANES - 1, *piece(keep)) for keep in keeps]
        + [low(hops, *piece(keep)) for keep in keeps]
        + [
            low(down_rows, down_cols),
            low(down_rows // CORES, down_cols),
            low(columns, model),
            low(columns, model),
            low(2, normed.shape[0] // PLANES, model),
            pltpu.VMEM((head_cols, model), jnp.float32),
            pltpu.VMEM((head_cols, half), jnp.float32),
            low(head_cols, half),
            low(head_cols // 2, half),
            low(head_cols // 2, half),
            low(head_cols, half),
            low(head_cols // 2, half),
            pltpu.VMEM((6, 8, model), jnp.float32),
            pltpu.VMEM((5, 8, model), jnp.float32),
            dma((2, RANKS)),
            dma((2, 5 * hops)),
            dma((2, 19)),
            dma((2, 2 * PLANES)),
            dma((2, 4)),
            dma((3,)),
        ],
        compiler_params=pltpu.CompilerParams(collective_id=0, has_side_effects=True, vmem_limit_bytes=VMEM_LIMIT),
    )(
        rows_in, down_keep, down_got, down_hops, gate_keep, gate_first, gate_sent, up_keep, up_sent, out_sum,
        normed, head_near, head_far, attn_gain, mlp_part, *attn_weights, w_key, key_far, tokens, grad,
    )


def local_last(info, thin, broad):
    half = broad.shape[1]
    model = 2 * half
    columns, hidden = (broad.shape[0] - 2 * HD - model // RANKS) // 4, thin.shape[2] * 2
    shapes = [
        (HD, half), (HD // 2, half), (HD // 2, half), (model // RANKS, half), (half, 2 * columns), (half, 2 * columns),
        (model // RANKS, hidden),
    ]
    query, key, value, out, gate, up, down = local_call(
        last_kernel, info, (thin, broad), [jax.ShapeDtypeStruct(shape, jnp.float32) for shape in shapes]
    )
    return query.T, key.T, value.T, out.T, gate, up, down.T


def head_shards(
    tokens, attn_gain, w_query, w_key, w_value, w_out, mlp_gain, w_gate, w_up, w_down, cotangent
):
    seqs, width, model = tokens.shape
    length = width * RANKS
    rows = seqs * width
    half_model = model // 2
    hidden = w_gate.shape[1]
    half_hidden = hidden // 2
    part_hidden = half_hidden // CORES
    chunk = hidden // (2 * RANKS)
    rank = lax.axis_index("ctx")
    side = lax.axis_index("fsdp")
    core = rank % CORES
    line = (rank // CORES) % LINES
    plane = rank // (CORES * LINES)
    head = plane * CORES + core
    low_side = side == 0
    info = jnp.stack([side, core, line]).astype(jnp.int32)
    pick = jnp.asarray((pad_columns()[:, None] == np.arange(HEAD_COLS)[None, :]).astype(np.float32)).astype(BF)

    lane = np.arange(2 * LANES)
    column = np.where(lane % LANES < HD, lane // LANES * HD + lane % LANES, -1)
    columns = np.stack([np.where(column < 0, -1, column + i * 2 * HD) for i in range(CORES)])
    squeeze = jnp.asarray((columns[:, :, None] == np.arange(4 * HD)).astype(np.float32)).astype(BF)

    tokens_seq, head_rows, head_far, far, out_far, cosine, sine, attn_row, mlp_row = gather_all(
        tokens, (w_query, w_key, w_value), w_gate, w_up, w_out, rope_rows(),
        (attn_gain.reshape(-1, LANES), mlp_gain.reshape(-1, LANES)),
    )
    grad_down = cotangent.reshape(rows, model)
    normed_seq, qkv, attended_seq, lse, attended_blocks, down_far, grad_down_other = head_forward(
        tokens_seq.reshape(length, model), attn_row, head_rows, head_far, pick, cosine, sine, w_down, grad_down
    )
    attended_seq = attended_seq.reshape(length, 2 * LANES)
    weights = (w_gate, w_up, far, w_down, down_far)
    token_rows = tokens.reshape(rows, model)
    resid, normed_two = local_call(
        post_kernel,
        info,
        (attended_blocks, token_rows, w_out, out_far, mlp_row),
        [jax.ShapeDtypeStruct((rows, model), jnp.float32), jax.ShapeDtypeStruct((rows, model), BF)],
    )

    inner_own, gate_own, up_own, mixed_own, back_own, normed_other = mlp_part(
        normed_two, grad_down, weights, jnp.float32, 6, [(SIDE, normed_two)]
    )
    inner_far, gate_far, up_far, mixed_far, back_far, inner_sib, gate_sib, up_sib, *sib, key_far = mlp_part(
        normed_other, grad_down_other, weights, BF, 5,
        [(HALF, value) for value in (inner_own, gate_own, up_own)]
        + [(WHOLE, value) for value in (normed_two, normed_other, grad_down, grad_down_other)]
        + [(WEIGHT, w_key)],
    )
    (
        down_keep, down_sent, down_first, gate_keep, gate_sent,
        grad_resid, grad_branch, grad_attended, mlp_gain_part,
    ) = middle(
        back_far,
        (inner_own, inner_far, inner_sib, gate_own, gate_far, gate_sib),
        (normed_two, normed_other, *sib[:2]),
        (grad_down, grad_down_other, *sib[2:]),
        back_own, resid, mlp_row, w_out, out_far,
    )

    grad_qkv, gate_first, out_sum, up_keep, up_sent, down_got, down_hops, mixed = head_backward(
        grad_attended, qkv, attended_seq, lse, cosine, sine, pick, squeeze, down_sent, gate_sent, grad_branch, attended_blocks,
        (up_own, up_far, up_sib, normed_two, normed_other, *sib[:2]),
        (down_keep, down_first),
        (mixed_far, mixed_own, resid),
    )
    tokens_grad, thin, broad, gains, _, _ = reduce_all(
        grad_qkv.reshape(RANKS, width, HEAD_COLS),
        (down_keep, down_got, down_hops),
        (gate_keep, gate_first, gate_sent),
        (up_keep, up_sent),
        out_sum,
        (normed_seq, head_rows, head_far, attn_row, mlp_gain_part),
        (w_value, w_query),
        w_key, key_far, token_rows, grad_resid,
    )

    w_query_grad, w_key_grad, w_value_grad, w_out_grad, w_gate_grad, w_up_grad, w_down_grad = local_last(info, thin, broad)
    return (
        mixed.reshape(seqs, width, model),
        tokens_grad.reshape(seqs, width, model),
        gains[0],
        w_query_grad,
        w_key_grad,
        w_value_grad,
        w_out_grad,
        gains[1],
        w_gate_grad,
        w_up_grad,
        w_down_grad,
    )


def solution(mesh):
    by_heads = mesh.shape["ctx"] == RANKS and mesh.shape["fsdp"] == 2
    placed = (
        P("fsdp", "ctx", None),
        P(),
        P("fsdp", None),
        P("fsdp", None),
        P("fsdp", None),
        P("fsdp", None),
        P(),
        P("fsdp", None),
        P("fsdp", None),
        P("fsdp", None),
        P("fsdp", "ctx", None),
    )
    return jax.shard_map(
        head_shards if by_heads else shards,
        mesh=mesh,
        in_specs=placed,
        out_specs=(
            P("fsdp", "ctx", None),
            P("fsdp", "ctx", None),
            P(),
            P("fsdp", "ctx"),
            P("fsdp", "ctx"),
            P("fsdp", "ctx"),
            P("fsdp", "ctx"),
            P(),
            P("fsdp", "ctx"),
            P("fsdp", "ctx"),
            P("fsdp", "ctx"),
        ),
        check_vma=False,
    )
```
